32 devices in a mesh: section: 2 (over core), fsdp: 4 (over y, x), rep: 4 (over z).
Axes of the slice: x: 2, y: 2, z: 4, core: 2. Of those that a mesh axis runs over, the one named last changes fastest.
Arguments:
- inputs: bfloat16 [64, 256, 384], P(('fsdp', 'rep')), may hold values from -6 to 6
- conditioning: bfloat16 [64, 384], P(('fsdp', 'rep')), may hold values from -6 to 6
- cotangent: bfloat16 [64, 256, 384], P(('fsdp', 'rep')), may hold values from -6 to 6
- micro_sizes: int32 [16, 2], P(('fsdp', 'rep')), may hold values from 1 to 2, as said below
- relative_bias_index: int32 [256, 256], replicated, may hold values from 0 to 960
- w_ada: bfloat16 [2, 384, 2304], P('section', 'fsdp'), may hold values from -0.3125 to 0.3125
- w_qkv: bfloat16 [2, 384, 1152], P('section', 'fsdp'), may hold values from -0.3125 to 0.3125
- w_proj: bfloat16 [2, 384, 384], P('section', 'fsdp'), may hold values from -1.25 to 1.25
- w_fc1: bfloat16 [2, 384, 1536], P('section', 'fsdp'), may hold values from -0.3125 to 0.3125
- w_fc2: bfloat16 [2, 1536, 384], P('section', 'fsdp'), may hold values from -0.15625 to 0.15625
- b_ada: bfloat16 [2, 2304], P('section', 'fsdp'), may hold values from -3 to 3
- b_qv: bfloat16 [2, 768], P('section', 'fsdp'), may hold values from -3 to 3
- b_proj: bfloat16 [2, 384], P('section', 'fsdp'), may hold values from -3 to 3
- b_fc1: bfloat16 [2, 1536], P('section', 'fsdp'), may hold values from -3 to 3
- b_fc2: bfloat16 [2, 384], P('section', 'fsdp'), may hold values from -3 to 3
- bias_table: bfloat16 [2, 6, 961], P('section'), may hold values from -5 to 5
Outputs:
- activations: bfloat16 [2, 64, 256, 384], P('section', ('fsdp', 'rep'))
- input_grads: float32 [2, 64, 256, 384], P('section', ('fsdp', 'rep'))
- cond_grad: float32 [64, 384], P(('fsdp', 'rep'))
- g_w_ada: float32 [2, 384, 2304], P('section', 'fsdp')
- g_w_qkv: float32 [2, 384, 1152], P('section', 'fsdp')
- g_w_proj: float32 [2, 384, 384], P('section', 'fsdp')
- g_w_fc1: float32 [2, 384, 1536], P('section', 'fsdp')
- g_w_fc2: float32 [2, 1536, 384], P('section', 'fsdp')
- g_b_ada: float32 [2, 2304], P('section', 'fsdp')
- g_b_qv: float32 [2, 768], P('section', 'fsdp')
- g_b_proj: float32 [2, 384], P('section', 'fsdp')
- g_b_fc1: float32 [2, 1536], P('section', 'fsdp')
- g_b_fc2: float32 [2, 384], P('section', 'fsdp')
- g_table: float32 [2, 6, 961], P('section')
The draws below stay inside these ranges and needn't reach their ends.
Inputs may be any that keep to these rules, and one draw needn't show every extreme that they name: Only the first micro_sizes[g, m] of the 2 slots of micro-batch m of group g hold live samples; some micro-batch is full in every draw.
All inputs are finite; a program needn't handle non-finite values.
Results may differ from the reference program's by a relative error of at most 0.035.
Values may be sent and summed in bfloat16 or wider, within the bound.
No kernel may reach another device: no remote copies, remote signals or barrier semaphores. Data moves between devices by JAX's collectives and lax.ppermute only.
A program may use at most 128 MiB of HBM per device.

```python
import math
import jax
import jax.numpy as jnp
from jax import lax

HEADS = 6
D = 384
FF = 1536
L = 256
REL = 961
MICRO = 2
CAP = 2
SAMP_DEV = 4
GROUPS = 16
SAMPLES = 64


def draw_micro_sizes(key, part):
    key = jax.random.fold_in(key, 5)
    size_key, pick_key = jax.random.split(key)
    drawn = jax.random.randint(size_key, (GROUPS * MICRO,), 1, CAP + 1)
    chosen = jax.random.randint(pick_key, (), 0, GROUPS * MICRO)
    drawn = jnp.where(jnp.arange(GROUPS * MICRO) == chosen, CAP, drawn)
    return drawn.reshape(GROUPS, MICRO).astype(jnp.int32)


def plant(array, rng, smallest, largest):
    place = [jax.random.randint(jax.random.fold_in(rng, axis), (), 0, length) for axis, length in enumerate(array.shape)]
    longest = array.shape.index(max(array.shape))
    next_to = place[:longest] + [(place[longest] + 1) % array.shape[longest]] + place[longest + 1:]
    return array.at[tuple(place)].set(smallest).at[tuple(next_to)].set(largest)


def level_of(key, shape, cuts, smallest, largest):
    def one(axis_at, parts):
        draws = jax.random.uniform(jax.random.fold_in(jax.random.fold_in(key, 6), axis_at), (parts,), jnp.float32, smallest / len(cuts), largest / len(cuts))
        return jnp.repeat(jnp.exp(draws), shape[axis_at] // parts).reshape((-1,) + (1,) * (len(shape) - axis_at - 1))

    level = one(*cuts[0])
    for cut in cuts[1:]:
        level = level * one(*cut)
    return level


def noise(own_key, dims, width, bound, shards=(), dtype=jnp.bfloat16):
    array = width * jax.random.normal(own_key, dims, jnp.float32)
    if shards:
        array = array * level_of(own_key, dims, shards, -0.22, 0.18)
    return jnp.clip(array, -bound, bound).astype(dtype)


def setup_inputs(seed: int = 0) -> dict:
    seeds = jax.random.split(jax.random.key(seed), 17)
    return {
        "inputs": noise(seeds[0], (SAMPLES, L, D), 1.0, 6.0, ((0, 16),)),
        "conditioning": noise(seeds[1], (SAMPLES, D), 1.0, 6.0, ((0, 16),)),
        "cotangent": noise(seeds[2], (SAMPLES, L, D), 1.0, 6.0, ((0, 16),)),
        "micro_sizes": draw_micro_sizes(jax.random.fold_in(seeds[16], 71), 0),
        "relative_bias_index": plant(jax.random.randint(seeds[4], (L, L), 0, REL), jax.random.fold_in(seeds[4], 1), 0, REL - 1).astype(jnp.int32),
        "w_ada": noise(seeds[5], (2, D, 6 * D), D ** -0.5, 0.3125, ((0, 2), (1, 4))),
        "w_qkv": noise(seeds[6], (2, D, 3 * D), D ** -0.5, 0.3125, ((0, 2), (1, 4))),
        "w_proj": noise(seeds[7], (2, D, D), (D * 16 // L) ** -0.5, 1.25, ((0, 2), (1, 4))),
        "w_fc1": noise(seeds[8], (2, D, FF), D ** -0.5, 0.3125, ((0, 2), (1, 4))),
        "w_fc2": noise(seeds[9], (2, FF, D), FF ** -0.5, 0.15625, ((0, 2), (1, 4))),
        "b_ada": noise(seeds[10], (2, 6 * D), 0.5, 3.0, ((0, 2), (1, 4))),
        "b_qv": noise(seeds[11], (2, 2 * D), 0.5, 3.0, ((0, 2), (1, 4))),
        "b_proj": noise(seeds[12], (2, D), 0.5, 3.0, ((0, 2), (1, 4))),
        "b_fc1": noise(seeds[13], (2, FF), 0.5, 3.0, ((0, 2), (1, 4))),
        "b_fc2": noise(seeds[14], (2, D), 0.5, 3.0, ((0, 2), (1, 4))),
        "bias_table": noise(seeds[15], (2, HEADS, REL), 1.0, 5.0, ((0, 2),)),
    }


@jax.custom_vjp
def low(v):
    return lax.optimization_barrier(v.astype(jnp.bfloat16)).astype(jnp.float32)

@jax.custom_vjp
def low_back(v):
    return v

def low_keep(v):
    return (low(v), None)

def low_pass(kept, grad):
    return (grad,)

def back_keep(v):
    return (v, None)

def back_low(kept, grad):
    return (low(grad),)
low.defvjp(low_keep, low_pass)
low_back.defvjp(back_keep, back_low)
EPSILON = 1e-06
PRECISE = lax.Precision.HIGHEST

def norm_rows(v):
    centre = v - lax.optimization_barrier(jnp.mean(v, axis=-1, keepdims=True))
    spread = lax.optimization_barrier(jnp.mean(centre * centre, axis=-1, keepdims=True))
    return centre * lax.rsqrt(spread + EPSILON)

def gelu_tanh(v):
    return 0.5 * v * (1.0 + jnp.tanh(0.7978845608028654 * (v + 0.044715 * v * v * v)))

def diffusion_transformer_layer(layer_input_rows, condition_row_set, parameter_pair, relative_bias_index):
    w_ada, w_qkv, w_proj, w_fc1, w_fc2, b_ada, b_qv, b_proj, b_fc1, b_fc2, bias_table = parameter_pair
    batch_size, length, model_width = layer_input_rows.shape
    head_count = bias_table.shape[0]
    head_dim = model_width // head_count
    modulation = low_back(jnp.dot(low(jax.nn.silu(condition_row_set)), w_ada, precision=PRECISE) + b_ada)
    pieces = [modulation[:, None, i * model_width:(i + 1) * model_width] for i in range(6)]
    normed_one = low(norm_rows(layer_input_rows) * (1.0 + pieces[1]) + pieces[0])
    projected = jnp.einsum('bld,de->ble', normed_one, w_qkv, precision=PRECISE)
    queries = low_back(low(projected[..., :model_width] + b_qv[:model_width]))
    key_heads = low_back(low(projected[..., model_width:2 * model_width]))
    value_heads = low_back(low(projected[..., 2 * model_width:] + b_qv[model_width:]))
    queries = queries.reshape(batch_size, length, head_count, head_dim)
    key_heads = key_heads.reshape(batch_size, length, head_count, head_dim)
    value_heads = value_heads.reshape(batch_size, length, head_count, head_dim)
    scores = jnp.einsum('bqhe,bkhe->bhqk', queries, key_heads, precision=PRECISE) * head_dim ** (-0.5)
    scores = low_back(scores + bias_table[:, relative_bias_index][None])
    probs = low(jax.nn.softmax(scores, axis=-1))
    attended = jnp.einsum('bhqk,bkhe->bqhe', probs, value_heads, precision=PRECISE)
    attended = low_back(low(attended.reshape(batch_size, length, model_width)))
    branch = low_back(jnp.einsum('bld,de->ble', attended, w_proj, precision=PRECISE) + b_proj)
    middle = layer_input_rows + pieces[2] * branch
    normed_two = low(norm_rows(middle) * (1.0 + pieces[4]) + pieces[3])
    hidden_pre = low_back(jnp.einsum('bld,df->blf', normed_two, w_fc1, precision=PRECISE) + b_fc1)
    hidden_act = low(gelu_tanh(hidden_pre))
    out_branch = low_back(jnp.einsum('blf,fd->bld', hidden_act, w_fc2, precision=PRECISE) + b_fc2)
    return middle + pieces[5] * out_branch

def reference(inputs, conditioning, cotangent, micro_sizes, relative_bias_index, w_ada, w_qkv, w_proj, w_fc1, w_fc2, b_ada, b_qv, b_proj, b_fc1, b_fc2, bias_table):
    parameter_pair = tuple((p.astype(jnp.float32) for p in (w_ada, w_qkv, w_proj, w_fc1, w_fc2, b_ada, b_qv, b_proj, b_fc1, b_fc2, bias_table)))
    slot_index = jnp.arange(SAMP_DEV)
    slot_micro = slot_index // CAP
    slot_sizes = lax.optimization_barrier(jnp.sum(jnp.where(slot_micro[None, :, None] == jnp.arange(MICRO)[None, None, :], micro_sizes[:, None, :], 0), axis=2))
    live_mask = ((slot_index % CAP)[None, :] < slot_sizes).astype(jnp.float32).reshape(SAMPLES)
    block_size = math.gcd(SAMPLES, max(1, 4096 // L))
    block_count = SAMPLES // block_size

    def two_layers(pars, layer_input_rows, condition_row_set, mid_probe):
        first_parameters = tuple((p[0] for p in pars))
        second_parameters = tuple((p[1] for p in pars))
        first_layer_output = diffusion_transformer_layer(layer_input_rows, condition_row_set, first_parameters, relative_bias_index)
        handed_onward = low_back(low(first_layer_output) + mid_probe)
        second_layer_output = diffusion_transformer_layer(handed_onward, condition_row_set, second_parameters, relative_bias_index)
        return (first_layer_output, second_layer_output)

    def block_step(grad_total, block_data):
        layer_input_rows, condition_row_set, grad_rows, live_rows = block_data
        layer_input_rows = layer_input_rows.astype(jnp.float32)
        condition_row_set = condition_row_set.astype(jnp.float32)
        mid_probe = jnp.zeros_like(layer_input_rows)
        outputs, pull_back = jax.vjp(two_layers, parameter_pair, layer_input_rows, condition_row_set, mid_probe)
        first_layer_output, second_layer_output = outputs
        grad_full = grad_rows.astype(jnp.float32) * live_rows[:, None, None]
        d_par, d_in, d_cond, d_mid = pull_back((jnp.zeros_like(first_layer_output), grad_full))
        grad_total = jax.tree.map(jnp.add, grad_total, d_par)
        return (grad_total, (first_layer_output.astype(jnp.bfloat16), second_layer_output.astype(jnp.bfloat16), d_in, d_mid, d_cond))
    zero_grads = tuple((jnp.zeros_like(p) for p in parameter_pair))
    block_inputs = (inputs.reshape(block_count, block_size, L, D), conditioning.reshape(block_count, block_size, D), cotangent.reshape(block_count, block_size, L, D), live_mask.reshape(block_count, block_size))
    grad_total, results = lax.scan(block_step, zero_grads, block_inputs)
    first_layer_output, second_layer_output, d_in, d_mid, d_cond = results
    activations = jnp.stack([first_layer_output.reshape(SAMPLES, L, D), second_layer_output.reshape(SAMPLES, L, D)])
    input_grads = jnp.stack([d_in.reshape(SAMPLES, L, D), d_mid.reshape(SAMPLES, L, D)])
    cond_grad = d_cond.reshape(SAMPLES, D)
    return (activations, input_grads, cond_grad, grad_total[0], grad_total[1], grad_total[2], grad_total[3], grad_total[4], grad_total[5], grad_total[6], grad_total[7], grad_total[8], grad_total[9], grad_total[10])
```

```python
import functools

import jax
import jax.numpy as jnp
from jax import lax
from jax.experimental import pallas as pl
from jax.experimental.pallas import tpu as pltpu
from jax.sharding import PartitionSpec as P

EPSILON = 1e-06
F32 = jnp.float32
BF16 = jnp.bfloat16
VMEM_BYTES = 58 * 1024 * 1024
LOW = 32


def dot(a, b):
    return jnp.dot(a, b, preferred_element_type=F32)


def dot_rows(a, b):
    return lax.dot_general(a, b, (((1,), (1,)), ((), ())), preferred_element_type=F32)


def dot_cols(a, b):
    return lax.dot_general(a, b, (((0,), (0,)), ((), ())), preferred_element_type=F32)


def norm_parts(v):
    centre = v - jnp.mean(v, axis=-1, keepdims=True)
    inverse = lax.rsqrt(jnp.mean(centre * centre, axis=-1, keepdims=True) + EPSILON)
    return centre * inverse, inverse


def norm_back(d_normed, scale, normed, inverse):
    d = d_normed * (1.0 + scale)
    return inverse * (
        d
        - jnp.mean(d, axis=-1, keepdims=True)
        - normed * jnp.mean(d * normed, axis=-1, keepdims=True)
    )


def col_sum(v):
    return jnp.sum(v, axis=0, keepdims=True)


def half_masks(width):
    lane = lax.broadcasted_iota(jnp.int32, (1, width), 1)
    first = jnp.where(lane < width // 2, 1.0, 0.0)
    return first.astype(BF16), (1.0 - first).astype(BF16)


def attention_copies(pack, w_qkv, w_proj, sems, first_sem, shard, pieces):
    model = w_proj.shape[0]
    q = model // pieces
    copies = []
    for p in range(pieces):
        off = pl.multiple_of((shard ^ p) * q, 16) if pieces > 1 else 0
        for c in range(4):
            source = pack.at[pl.ds((4 * p + c) * q, q), :]
            if c < 3:
                target = w_qkv.at[pl.ds(off, q), pl.ds(c * model, model)]
            else:
                target = w_proj.at[pl.ds(off, q), :]
            copies.append(
                pltpu.make_async_copy(source, target, sems.at[first_sem + len(copies)])
            )
    return copies


def mlp_copies(pack, w_fc1, w_fc2, sems, first_sem, shard, pieces):
    model = w_fc1.shape[0]
    q = model // pieces
    copies = []
    for p in range(pieces):
        off = pl.multiple_of((shard ^ p) * q, 16) if pieces > 1 else 0
        for c in range(4):
            copies.append(
                pltpu.make_async_copy(
                    pack.at[pl.ds((8 * p + c) * q, q), :],
                    w_fc1.at[pl.ds(off, q), pl.ds(c * model, model)],
                    sems.at[first_sem + len(copies)],
                )
            )
        copies.append(
            pltpu.make_async_copy(
                pack.at[pl.ds((8 * p + 4) * q, 4 * q), :],
                w_fc2.at[pl.ds(off * 4, 4 * q), :],
                sems.at[first_sem + len(copies)],
            )
        )
    return copies


def start_from(section, layer, own_copies, other_copies):
    @pl.when(section == layer)
    def _():
        for copy in own_copies:
            copy.start()

    @pl.when(section != layer)
    def _():
        for copy in other_copies:
            copy.start()


def wait_all(copies):
    for copy in copies:
        copy.wait()


def pack_attention(out_ref, g_qkv, g_proj, shard, pieces):
    model = g_proj.shape[0]
    q = model // pieces
    for p in range(pieces):
        off = pl.multiple_of((shard ^ p) * q, 16) if pieces > 1 else 0
        for c in range(3):
            out_ref[(4 * p + c) * q : (4 * p + c + 1) * q, :] = g_qkv[
                pl.ds(off, q), c * model : (c + 1) * model
            ]
        out_ref[(4 * p + 3) * q : (4 * p + 4) * q, :] = g_proj[pl.ds(off, q), :]


def pack_mlp(out_ref, g_fc1, g_fc2, shard, pieces):
    model = g_fc1.shape[0]
    q = model // pieces
    for p in range(pieces):
        off = pl.multiple_of((shard ^ p) * q, 16) if pieces > 1 else 0
        for c in range(4):
            out_ref[(8 * p + c) * q : (8 * p + c + 1) * q, :] = g_fc1[
                pl.ds(off, q), c * model : (c + 1) * model
            ]
        out_ref[(8 * p + 4) * q : (8 * p + 8) * q, :] = g_fc2[
            pl.ds(pl.multiple_of(off * 4, 16), 4 * q), :
        ]


def attention_forward(b, length, h, mod, bias, w_qkv, w_proj, b_qkv, b_proj, qkv, probs, att, branch, middle):
    model = w_proj.shape[0]
    heads = bias.shape[0]
    pair = 2 * model // heads
    rows = pl.ds(pl.multiple_of(b * length, length), length)
    masks = half_masks(pair)
    x = h[rows, :].astype(F32)
    normed, _ = norm_parts(x)
    normed_low = (normed * (1.0 + mod[b, 1:2, :]) + mod[b, 0:1, :]).astype(BF16)
    qkv[rows, :] = (dot(normed_low, w_qkv[...]) + b_qkv[...]).astype(BF16)
    for j in range(heads // 2):
        q_pair = qkv[rows, j * pair : (j + 1) * pair] * BF16((pair // 2) ** (-0.5))
        k_pair = qkv[rows, model + j * pair : model + (j + 1) * pair]
        v_pair = qkv[rows, 2 * model + j * pair : 2 * model + (j + 1) * pair]
        total = None
        for e in range(2):
            scores = dot_rows(q_pair * masks[e], k_pair) + bias[2 * j + e].astype(F32)
            raised = jnp.exp(scores - jnp.max(scores, axis=-1, keepdims=True))
            p = (raised * (1.0 / jnp.sum(raised, axis=-1, keepdims=True))).astype(BF16)
            probs[b, 2 * j + e] = p
            part = dot(p, v_pair * masks[e])
            total = part if total is None else total + part
        att[rows, j * pair : (j + 1) * pair] = total.astype(BF16)
    out = dot(att[rows, :], w_proj[...]) + b_proj[...]
    branch[rows, :] = out
    middle[rows, :] = x + mod[b, 2:3, :] * out


def mlp_forward(b, length, middle, mod, w_fc1, w_fc2, b_fc1, b_fc2, act, slope, out_branch, layer_out):
    model = w_fc1.shape[0]
    rows = pl.ds(pl.multiple_of(b * length, length), length)
    mid = middle[rows, :]
    normed, _ = norm_parts(mid)
    normed_low = (normed * (1.0 + mod[b, 4:5, :]) + mod[b, 3:4, :]).astype(BF16)
    total = b_fc2[...]
    for c in range(w_fc1.shape[1] // model):
        cols = slice(c * model, (c + 1) * model)
        v = dot(normed_low, w_fc1[:, cols]) + b_fc1[:, cols]
        square = v * v
        t = jnp.tanh(0.7978845608028654 * v * (1.0 + 0.044715 * square))
        half = 0.5 * (1.0 + t)
        a = (v * half).astype(BF16)
        act[rows, cols] = a
        slope[rows, cols] = (
            half
            + 0.5 * v * (1.0 - t * t) * (0.7978845608028654 + (3 * 0.044715 * 0.7978845608028654) * square)
        ).astype(BF16)
        total = total + dot(a, w_fc2[cols, :])
    out_branch[rows, :] = total
    layer_out[rows, :] = (mid + mod[b, 5:6, :] * total).astype(layer_out.dtype)


def mlp_backward(b, length, grad, middle, mod, w_fc1, w_fc2, act, slope, out_branch, d_middle, small, normed_low, d_pre, d_ob):
    model = w_fc1.shape[0]
    rows = pl.ds(pl.multiple_of(b * length, length), length)
    g = grad[rows, :].astype(F32)
    small[b, 2:3, :] = col_sum(g * out_branch[rows, :])
    d_out = g * mod[b, 5:6, :]
    d_out_low = d_out.astype(BF16)
    d_ob[rows, :] = d_out_low
    small[b, 3:4, :] = col_sum(d_out_low.astype(F32))
    normed, inverse = norm_parts(middle[rows, :])
    normed_low[rows, :] = (normed * (1.0 + mod[b, 4:5, :]) + mod[b, 3:4, :]).astype(BF16)
    d_normed = None
    for c in range(w_fc1.shape[1] // model):
        cols = slice(c * model, (c + 1) * model)
        d_act = dot_rows(d_out_low, w_fc2[cols, :])
        d_low = (d_act * slope[rows, cols].astype(F32)).astype(BF16)
        d_pre[rows, cols] = d_low
        small[b, 4 + c : 5 + c, :] = col_sum(d_low.astype(F32))
        part = dot_rows(d_low, w_fc1[:, cols])
        d_normed = part if d_normed is None else d_normed + part
    small[b, 0:1, :] = col_sum(d_normed)
    small[b, 1:2, :] = col_sum(d_normed * normed)
    d_middle[rows, :] = norm_back(d_normed, mod[b, 4:5, :], normed, inverse) + g


def mlp_weight_grads(normed_low, d_pre, act, d_ob, g_fc1, g_fc2):
    model = g_fc1.shape[0]
    for c in range(g_fc1.shape[1] // model):
        cols = slice(c * model, (c + 1) * model)
        g_fc1[:, cols] = dot_cols(normed_low[...], d_pre[:, cols]).astype(BF16)
        g_fc2[cols, :] = dot_cols(act[:, cols], d_ob[...]).astype(BF16)


def attention_backward(b, length, h, mod, w_qkv, w_proj, qkv, probs, att, branch, d_middle, d_in, small, score_sum, normed_low, d_qkv, d_br):
    model = w_proj.shape[0]
    heads = probs.shape[1]
    pair = 2 * model // heads
    scale = F32((pair // 2) ** (-0.5))
    rows = pl.ds(pl.multiple_of(b * length, length), length)
    masks = half_masks(pair)
    d_mid = d_middle[rows, :]
    small[b, 2:3, :] = col_sum(d_mid * branch[rows, :])
    d_branch = (d_mid * mod[b, 2:3, :]).astype(BF16)
    d_br[rows, :] = d_branch
    small[b, 5:6, :] = col_sum(d_branch.astype(F32))
    d_att = dot_rows(d_branch, w_proj[...]).astype(BF16)
    for j in range(heads // 2):
        q_pair = qkv[rows, j * pair : (j + 1) * pair]
        k_pair = qkv[rows, model + j * pair : model + (j + 1) * pair]
        v_pair = qkv[rows, 2 * model + j * pair : 2 * model + (j + 1) * pair]
        d_pair = d_att[:, j * pair : (j + 1) * pair]
        d_q = d_k = d_v = None
        for e in range(2):
            p_low = probs[b, 2 * j + e]
            p = p_low.astype(F32)
            d_here = d_pair * masks[e]
            d_p = dot_rows(d_here, v_pair)
            d_s = (p * (d_p - jnp.sum(d_p * p, axis=-1, keepdims=True))).astype(BF16)
            score_sum[2 * j + e] += d_s.astype(F32)
            v_part = dot_cols(p_low, d_here)
            q_part = dot(d_s, k_pair * masks[e])
            k_part = dot_cols(d_s, q_pair * masks[e])
            d_v = v_part if d_v is None else d_v + v_part
            d_q = q_part if d_q is None else d_q + q_part
            d_k = k_part if d_k is None else d_k + k_part
        d_qkv[rows, j * pair : (j + 1) * pair] = (d_q * scale).astype(BF16)
        d_qkv[rows, model + j * pair : model + (j + 1) * pair] = (d_k * scale).astype(BF16)
        d_qkv[rows, 2 * model + j * pair : 2 * model + (j + 1) * pair] = d_v.astype(BF16)
    small[b, 3:4, :] = col_sum(d_qkv[rows, :model].astype(F32))
    small[b, 4:5, :] = col_sum(d_qkv[rows, 2 * model :].astype(F32))
    small[b, 6:8, :] = jnp.zeros((2, model), F32)
    d_normed = dot_rows(d_qkv[rows, :], w_qkv[...])
    normed, inverse = norm_parts(h[rows, :].astype(F32))
    normed_low[rows, :] = (normed * (1.0 + mod[b, 1:2, :]) + mod[b, 0:1, :]).astype(BF16)
    small[b, 0:1, :] = col_sum(d_normed)
    small[b, 1:2, :] = col_sum(d_normed * normed)
    d_in[rows, :] = (norm_back(d_normed, mod[b, 1:2, :], normed, inverse) + d_mid).astype(d_in.dtype)


def attention_weight_grads(normed_low, d_qkv, att, d_br, g_qkv, g_proj):
    model = g_proj.shape[0]
    for c in range(3):
        cols = slice(c * model, (c + 1) * model)
        g_qkv[:, cols] = dot_cols(normed_low[...], d_qkv[:, cols]).astype(BF16)
    g_proj[...] = dot_cols(att[...], d_br[...]).astype(BF16)


def each_sample(count, body):
    def step(b, carry):
        body(b)
        return carry

    lax.fori_loop(0, count, step, 0)


def forward_attention_kernel(layer, pieces, length, pos, h, mod, bias, own, other, b_qkv, b_proj,
                             qkv, probs, att, branch, middle, w_qkv, w_proj, sems):
    section, shard = pos[0], pos[1]
    mine = attention_copies(own, w_qkv, w_proj, sems, 0, shard, pieces)
    theirs = attention_copies(other, w_qkv, w_proj, sems, 0, shard, pieces)
    start_from(section, layer, mine, theirs)
    wait_all(mine)
    each_sample(
        h.shape[0] // length,
        lambda b: attention_forward(b, length, h, mod, bias, w_qkv, w_proj, b_qkv, b_proj, qkv, probs, att, branch, middle),
    )


def forward_mlp_kernel(layer, pieces, length, pos, middle, mod, own, other, b_fc1, b_fc2,
                       act, slope, out_branch, layer_out, w_fc1, w_fc2, sems):
    section, shard = pos[0], pos[1]
    mine = mlp_copies(own, w_fc1, w_fc2, sems, 0, shard, pieces)
    theirs = mlp_copies(other, w_fc1, w_fc2, sems, 0, shard, pieces)
    start_from(section, layer, mine, theirs)
    wait_all(mine)
    each_sample(
        middle.shape[0] // length,
        lambda b: mlp_forward(b, length, middle, mod, w_fc1, w_fc2, b_fc1, b_fc2, act, slope, out_branch, layer_out),
    )


def both_kernel(layer, pieces, length, pos, h, grad, mod, bias, own_a, other_a, own_m, other_m,
                b_qkv, b_proj, b_fc1, b_fc2,
                layer_out, d_in, small_a, small_m, scores, pack_a, pack_m,
                w_qkv, w_proj, w_fc1, w_fc2, qkv, probs, att, branch, middle, act, slope, out_branch,
                d_middle, normed_low, d_pre, d_ob, d_qkv, score_sum, g_qkv, g_proj, g_fc1, g_fc2, sems):
    section, shard = pos[0], pos[1]
    mine_a = attention_copies(own_a, w_qkv, w_proj, sems, 0, shard, pieces)
    theirs_a = attention_copies(other_a, w_qkv, w_proj, sems, 0, shard, pieces)
    mine_m = mlp_copies(own_m, w_fc1, w_fc2, sems, len(mine_a), shard, pieces)
    theirs_m = mlp_copies(other_m, w_fc1, w_fc2, sems, len(mine_a), shard, pieces)
    start_from(section, layer, mine_a + mine_m, theirs_a + theirs_m)
    wait_all(mine_a)
    samples = h.shape[0] // length
    each_sample(
        samples,
        lambda b: attention_forward(b, length, h, mod, bias, w_qkv, w_proj, b_qkv, b_proj, qkv, probs, att, branch, middle),
    )
    wait_all(mine_m)

    def mlp(b):
        mlp_forward(b, length, middle, mod, w_fc1, w_fc2, b_fc1, b_fc2, act, slope, out_branch, layer_out)
        mlp_backward(b, length, grad, middle, mod, w_fc1, w_fc2, act, slope, out_branch, d_middle, small_m, normed_low, d_pre, d_ob)

    each_sample(samples, mlp)
    mlp_weight_grads(normed_low, d_pre, act, d_ob, g_fc1, g_fc2)
    pack_mlp(pack_m, g_fc1, g_fc2, shard, pieces)
    score_sum[...] = jnp.zeros_like(score_sum)
    each_sample(
        samples,
        lambda b: attention_backward(b, length, h, mod, w_qkv, w_proj, qkv, probs, att, branch, d_middle, d_in, small_a, score_sum, normed_low, d_qkv, d_ob),
    )
    scores[...] = score_sum[...].astype(BF16)
    attention_weight_grads(normed_low, d_qkv, att, d_ob, g_qkv, g_proj)
    pack_attention(pack_a, g_qkv, g_proj, shard, pieces)


def backward_mlp_kernel(layer, pieces, length, pos, grad, middle, mod, own, other, act, slope, out_branch,
                        d_middle, small, pack, w_fc1, w_fc2, normed_low, d_pre, d_ob, g_fc1, g_fc2, sems):
    section, shard = pos[0], pos[1]
    mine = mlp_copies(own, w_fc1, w_fc2, sems, 0, shard, pieces)
    theirs = mlp_copies(other, w_fc1, w_fc2, sems, 0, shard, pieces)
    start_from(section, layer, mine, theirs)
    wait_all(mine)
    each_sample(
        middle.shape[0] // length,
        lambda b: mlp_backward(b, length, grad, middle, mod, w_fc1, w_fc2, act, slope, out_branch, d_middle, small, normed_low, d_pre, d_ob),
    )
    mlp_weight_grads(normed_low, d_pre, act, d_ob, g_fc1, g_fc2)
    pack_mlp(pack, g_fc1, g_fc2, shard, pieces)


def backward_attention_kernel(layer, pieces, length, pos, h, mod, own, other, qkv, probs, att, branch, d_middle,
                              d_in, small, scores, pack, w_qkv, w_proj, normed_low, d_qkv, d_br, score_sum, g_qkv, g_proj, sems):
    section, shard = pos[0], pos[1]
    mine = attention_copies(own, w_qkv, w_proj, sems, 0, shard, pieces)
    theirs = attention_copies(other, w_qkv, w_proj, sems, 0, shard, pieces)
    start_from(section, layer, mine, theirs)
    score_sum[...] = jnp.zeros_like(score_sum)
    wait_all(mine)
    each_sample(
        h.shape[0] // length,
        lambda b: attention_backward(b, length, h, mod, w_qkv, w_proj, qkv, probs, att, branch, d_middle, d_in, small, score_sum, normed_low, d_qkv, d_br),
    )
    scores[...] = score_sum[...].astype(BF16)
    attention_weight_grads(normed_low, d_qkv, att, d_br, g_qkv, g_proj)
    pack_attention(pack, g_qkv, g_proj, shard, pieces)


def call(kernel, pos, operands, in_hbm, outs, scratch, sems=0):
    specs = [pl.BlockSpec(memory_space=pltpu.SMEM)]
    for i in range(len(operands)):
        specs.append(pl.BlockSpec(memory_space=pl.ANY if i in in_hbm else pltpu.VMEM))
    shapes = [pltpu.VMEM(shape, dtype) for shape, dtype in scratch]
    if sems:
        shapes.append(pltpu.SemaphoreType.DMA((sems,)))
    return pl.pallas_call(
        kernel,
        out_shape=[jax.ShapeDtypeStruct(shape, dtype) for shape, dtype in outs],
        in_specs=specs,
        out_specs=[pl.BlockSpec(memory_space=pltpu.VMEM) for _ in outs],
        scratch_shapes=shapes,
        compiler_params=pltpu.CompilerParams(vmem_limit_bytes=VMEM_BYTES),
    )(pos, *operands)


def forward_attention(layer, pieces, pos, h, mod, bias, own, other, b_qkv, b_proj):
    samples, length, model = mod.shape[0], bias.shape[1], h.shape[1]
    rows, heads = h.shape[0], bias.shape[0]
    return call(
        functools.partial(forward_attention_kernel, layer, pieces, length),
        pos, (h, mod, bias, own, other, b_qkv, b_proj), (3, 4),
        [((rows, 3 * model), BF16), ((samples, heads, length, length), BF16), ((rows, model), BF16),
         ((rows, model), F32), ((rows, model), F32)],
        [((model, 3 * model), BF16), ((model, model), BF16)], 4 * pieces,
    )


def forward_mlp(layer, pieces, length, pos, middle, mod, own, other, b_fc1, b_fc2):
    rows, model = middle.shape
    hidden = b_fc1.shape[1]
    return call(
        functools.partial(forward_mlp_kernel, layer, pieces, length),
        pos, (middle, mod, own, other, b_fc1, b_fc2), (2, 3),
        [((rows, hidden), BF16), ((rows, hidden), BF16), ((rows, model), F32), ((rows, model), BF16)],
        [((model, hidden), BF16), ((hidden, model), BF16)], 5 * pieces,
    )


def both_ways(layer, pieces, pos, h, grad, mod, bias, own_a, other_a, own_m, other_m, b_qkv, b_proj, b_fc1, b_fc2):
    samples, length = mod.shape[0], bias.shape[1]
    rows, model = h.shape
    hidden, heads = b_fc1.shape[1], bias.shape[0]
    return call(
        functools.partial(both_kernel, layer, pieces, length),
        pos, (h, grad, mod, bias, own_a, other_a, own_m, other_m, b_qkv, b_proj, b_fc1, b_fc2), (4, 5, 6, 7),
        [((rows, model), BF16), ((rows, model), BF16), ((samples, 8, model), F32), ((samples, 8, model), F32),
         ((heads, length, length), BF16), ((4 * model, model), BF16), ((8 * model, model), BF16)],
        [((model, 3 * model), BF16), ((model, model), BF16), ((model, hidden), BF16), ((hidden, model), BF16),
         ((rows, 3 * model), BF16), ((samples, heads, length, length), BF16), ((rows, model), BF16),
         ((rows, model), F32), ((rows, model), F32), ((rows, hidden), BF16), ((rows, hidden), BF16), ((rows, model), F32),
         ((rows, model), F32), ((rows, model), BF16), ((rows, hidden), BF16), ((rows, model), BF16),
         ((rows, 3 * model), BF16), ((heads, length, length), F32),
         ((model, 3 * model), BF16), ((model, model), BF16), ((model, hidden), BF16), ((hidden, model), BF16)],
        9 * pieces,
    )


def backward_mlp(layer, pieces, length, pos, grad, middle, mod, own, other, act, slope, out_branch):
    rows, model = middle.shape
    hidden, samples = act.shape[1], mod.shape[0]
    return call(
        functools.partial(backward_mlp_kernel, layer, pieces, length),
        pos, (grad, middle, mod, own, other, act, slope, out_branch), (3, 4),
        [((rows, model), F32), ((samples, 8, model), F32), ((8 * model, model), BF16)],
        [((model, hidden), BF16), ((hidden, model), BF16), ((rows, model), BF16), ((rows, hidden), BF16),
         ((rows, model), BF16), ((model, hidden), BF16), ((hidden, model), BF16)],
        5 * pieces,
    )


def backward_attention(layer, pieces, pos, h, mod, own, other, qkv, probs, att, branch, d_middle):
    rows, model = h.shape
    samples, heads, length = probs.shape[:3]
    return call(
        functools.partial(backward_attention_kernel, layer, pieces, length),
        pos, (h, mod, own, other, qkv, probs, att, branch, d_middle), (2, 3),
        [((rows, model), F32), ((samples, 8, model), F32), ((heads, length, length), BF16), ((4 * model, model), BF16)],
        [((model, 3 * model), BF16), ((model, model), BF16), ((rows, model), BF16), ((rows, 3 * model), BF16),
         ((rows, model), BF16), ((heads, length, length), F32), ((model, 3 * model), BF16), ((model, model), BF16)],
        4 * pieces,
    )


def lookup_kernel(table, index, out, work):
    heads, length = out.shape[0], out.shape[1]
    high_count = table.shape[0] // 8
    values = table[...]
    low_id = lax.broadcasted_iota(jnp.int32, (LOW, length), 0)

    def step(i, carry):
        block = index[pl.ds(pl.multiple_of(i * 8, 8), 8), :]
        for r in range(8):
            entry = block[r : r + 1, :]
            picks = jnp.where(low_id == (entry & (LOW - 1)), 1.0, 0.0).astype(BF16)
            found = dot(values, picks).reshape(high_count, 8, length)
            high = jnp.broadcast_to(entry >> 5, (8, length))
            bit = high_count // 2
            while bit:
                chosen = (high & bit) != 0
                found = jnp.where(chosen[None], found[bit : 2 * bit], found[:bit])
                bit //= 2
            for head in range(heads):
                work[head, pl.ds(i * 8 + r, 1), :] = found[0, head : head + 1, :]
        return carry

    lax.fori_loop(0, length // 8, step, 0)
    out[...] = work[...].astype(BF16)


def lookup(table, index):
    heads, entries = table.shape
    high_count = LOW
    padded = jnp.pad(table, ((0, 8 - heads), (0, high_count * LOW - entries)))
    rows = jnp.transpose(padded.reshape(8, high_count, LOW), (1, 0, 2)).reshape(high_count * 8, LOW)
    length = index.shape[0]
    return pl.pallas_call(
        lookup_kernel,
        out_shape=jax.ShapeDtypeStruct((heads, length, length), BF16),
        scratch_shapes=[pltpu.VMEM((heads, length, length), F32)],
        compiler_params=pltpu.CompilerParams(vmem_limit_bytes=VMEM_BYTES),
    )(rows, index)


def table_kernel(scores, index, out):
    heads, length = scores.shape[0], scores.shape[1]
    out[...] = jnp.zeros_like(out)
    ids = lax.broadcasted_iota(jnp.int32, (LOW, length), 0)

    def step(i, carry):
        rows = pl.ds(pl.multiple_of(i * 16, 16), 16)
        entries = index[rows, :]
        block = [scores[head, rows, :].astype(F32) for head in range(heads)]
        total = None
        for r in range(16):
            entry = entries[r : r + 1, :]
            low = jnp.where(ids == (entry & (LOW - 1)), 1.0, 0.0).astype(BF16)
            high = ids == (entry >> 5)
            left = jnp.concatenate(
                [jnp.where(high, block[head][r : r + 1, :], 0.0) for head in range(heads)], axis=0
            ).astype(BF16)
            part = dot_rows(left, low)
            total = part if total is None else total + part
        out[...] += total
        return carry

    lax.fori_loop(0, length // 16, step, 0)


def table_gradient(scores, index):
    heads = scores.shape[0]
    return pl.pallas_call(
        table_kernel,
        out_shape=jax.ShapeDtypeStruct((heads * LOW, LOW), F32),
        compiler_params=pltpu.CompilerParams(vmem_limit_bytes=VMEM_BYTES),
    )(scores, index)


def swap_section(value):
    return lax.ppermute(value, "section", [(0, 1), (1, 0)])


def pairs_of(count, step):
    return [(i, i ^ step) for i in range(count)]


def by_rank(pieces, rank):
    stack = jnp.stack(pieces)
    count = len(pieces)
    bit = 1
    while bit < count:
        moved = jnp.stack([stack[i ^ bit] for i in range(count)])
        stack = jnp.where((rank & bit) != 0, moved, stack)
        bit *= 2
    return stack


def one_section_pairs(layer, count, step):
    return [(layer * count + i, layer * count + (i ^ step)) for i in range(count)]


def reduce_grads(pack, layer, shards, rank):
    other = lax.ppermute(pack, "section", [(1 - layer, layer)])
    size = pack.shape[0] // shards
    sums = [
        pack[p * size : (p + 1) * size].astype(F32) + other[p * size : (p + 1) * size].astype(F32)
        for p in range(shards)
    ]
    total = sums[0]
    got = [
        lax.ppermute(sums[p].astype(BF16), ("section", "fsdp"), one_section_pairs(layer, shards, p))
        for p in range(1, shards)
    ]
    for piece in got:
        total = total + piece.astype(F32)
    replicas = lax.axis_size("rep")
    parts = total.reshape(replicas, size // replicas, -1)
    low_parts = parts.astype(BF16)
    mine = lax.dynamic_index_in_dim(parts, rank, 0, keepdims=False)
    names = ("section", "rep")
    got = [
        lax.ppermute(
            lax.dynamic_index_in_dim(low_parts, rank ^ j, 0, keepdims=False),
            names, one_section_pairs(layer, replicas, j),
        )
        for j in range(1, replicas)
    ]
    for piece in got:
        mine = mine + piece.astype(F32)
    mine = mine.astype(BF16)
    quarters = [mine] + [
        lax.ppermute(mine, names, one_section_pairs(layer, replicas, j)) for j in range(1, replicas)
    ]
    return by_rank(quarters, rank).reshape(size, -1)


def unpack_attention(pack):
    q = pack.shape[0] // 4
    return jnp.concatenate([pack[c * q : (c + 1) * q] for c in range(3)], axis=1), pack[3 * q :]


def unpack_mlp(pack):
    q = pack.shape[0] // 8
    return jnp.concatenate([pack[c * q : (c + 1) * q] for c in range(4)], axis=1), pack[4 * q :]


def pack_attention_shard(w_qkv, w_proj):
    model = w_proj.shape[1]
    return jnp.concatenate([w_qkv[:, c * model : (c + 1) * model] for c in range(3)] + [w_proj], axis=0)


def pack_mlp_shard(w_fc1, w_fc2):
    model = w_fc2.shape[1]
    return jnp.concatenate([w_fc1[:, c * model : (c + 1) * model] for c in range(4)] + [w_fc2], axis=0)


def per_device(inputs, conditioning, cotangent, micro_sizes, relative_bias_index,
               w_ada, w_qkv, w_proj, w_fc1, w_fc2, b_ada, b_qv, b_proj, b_fc1, b_fc2, bias_table):
    section = lax.axis_index("section")
    shard = lax.axis_index("fsdp")
    rank = lax.axis_index("rep")
    shards, replicas = lax.axis_size("fsdp"), lax.axis_size("rep")
    direct = shards == 4 and replicas == 4
    pieces = shards if direct else 1
    is_first = section == 0
    samples, length, model = inputs.shape
    heads, entries = bias_table.shape[1:]
    half = samples // 2
    pos = jnp.stack([section, shard]).astype(jnp.int32)

    def mine(first, second):
        return jnp.where(is_first, first, second)

    def own_samples(array):
        return lax.dynamic_slice_in_dim(array, section * half, half, 0)

    def in_order(own, other):
        return jnp.where(is_first, jnp.concatenate([own, other]), jnp.concatenate([other, own]))

    row = jnp.concatenate([conditioning.reshape(-1), b_ada[0], b_qv[0], b_proj[0], b_fc1[0], b_fc2[0]])
    pack_a = pack_attention_shard(w_qkv[0], w_proj[0])
    pack_m = pack_mlp_shard(w_fc1[0], w_fc2[0])
    cond_size = conditioning.size
    if direct:
        rows = [row] + [lax.ppermute(row, "fsdp", pairs_of(shards, p)) for p in range(1, shards)]
        all_a = [pack_a] + [lax.ppermute(pack_a, "fsdp", pairs_of(shards, p)) for p in range(1, shards)]
        cond_pieces = jnp.stack([r[:cond_size].reshape(samples, model) for r in rows])
        acts = jax.nn.silu(cond_pieces.astype(F32)).astype(BF16)
        width = model // shards
        acts = lax.dynamic_slice_in_dim(acts, shard * width, width, 2)
        partial = lax.dot_general(acts, w_ada[0], (((2,), (0,)), ((), ())), preferred_element_type=F32)
        modulation = partial[0]
        for p in range(1, shards):
            modulation = modulation + lax.ppermute(partial[p], "fsdp", pairs_of(shards, p))
        all_m = [pack_m] + [lax.ppermute(pack_m, "fsdp", pairs_of(shards, p)) for p in range(1, shards)]
        own_a = jnp.concatenate(all_a)
        own_m = jnp.concatenate(all_m)
        bias_rows = by_rank([r[cond_size:] for r in rows], shard)
        w_ada_all = lax.all_gather(w_ada[0], "fsdp", axis=0, tiled=True)
    else:
        bias_rows = lax.all_gather(row[cond_size:], "fsdp", axis=0)
        gathered_a = lax.all_gather(pack_a, "fsdp", axis=0)
        gathered_m = lax.all_gather(pack_m, "fsdp", axis=0)
        q = model // shards
        own_a = jnp.transpose(gathered_a.reshape(shards, 4, q, model), (1, 0, 2, 3)).reshape(4 * model, model)
        fc1 = jnp.transpose(gathered_m[:, : 4 * q].reshape(shards, 4, q, model), (1, 0, 2, 3))
        own_m = jnp.concatenate([fc1.reshape(4 * model, model), gathered_m[:, 4 * q :].reshape(4 * model, model)])
        w_ada_all = lax.all_gather(w_ada[0], "fsdp", axis=0, tiled=True)
        acts = jax.nn.silu(conditioning.astype(F32)).astype(BF16)
        modulation = dot(acts, w_ada_all)
    cuts = [b_ada.shape[1], b_qv.shape[1], b_proj.shape[1], b_fc1.shape[1], b_fc2.shape[1]]
    biases, at = [], 0
    for cut in cuts:
        biases.append(bias_rows[:, at : at + cut].reshape(1, -1).astype(F32))
        at += cut
    modulation = modulation + biases[0]
    bias_line = jnp.concatenate(biases[1:], axis=1)
    other_line = swap_section(bias_line)
    other_samples = lax.dynamic_slice_in_dim(modulation, (1 - section) * half, half, 0)
    other_mod = swap_section(other_samples)
    own_mod = own_samples(modulation)
    other_a = swap_section(own_a)
    other_m = swap_section(own_m)
    bias_own = lookup(bias_table[0], relative_bias_index)
    bias_other = swap_section(bias_own)

    def layer_values(layer):
        pick = (lambda a, b: mine(a, b)) if layer == 0 else (lambda a, b: mine(b, a))
        line = pick(bias_line, other_line)
        mod = pick(own_mod, other_mod).reshape(half, 6, model)
        b_qkv = jnp.concatenate([line[:, :model], jnp.zeros((1, model), F32), line[:, model : 2 * model]], axis=1)
        at = 2 * model
        hidden = w_fc1.shape[2]
        return (
            mod, pick(bias_own, bias_other), b_qkv, line[:, at : at + model],
            line[:, at + model : at + model + hidden], line[:, at + model + hidden :],
        )

    mod0, bias0, b_qkv0, b_proj0, b_fc10, b_fc20 = layer_values(0)
    mod1, bias1, b_qkv1, b_proj1, b_fc11, b_fc21 = layer_values(1)

    live = (jnp.arange(half)[:, None, None] < lax.dynamic_index_in_dim(micro_sizes[0], section, 0)).astype(BF16)
    h0 = own_samples(inputs).reshape(half * length, model)
    grad1 = (own_samples(cotangent) * live).reshape(half * length, model)

    qkv, probs, att, branch, middle = forward_attention(0, pieces, pos, h0, mod0, bias0, own_a, other_a, b_qkv0, b_proj0)
    act, slope, out_branch, h1 = forward_mlp(0, pieces, length, pos, middle, mod0, own_m, other_m, b_fc10, b_fc20)
    out1, d_h1, small_a1, small_m1, scores1, grads_a1, grads_m1 = both_ways(
        1, pieces, pos, h1, grad1, mod1, bias1, own_a, other_a, own_m, other_m, b_qkv1, b_proj1, b_fc11, b_fc21
    )
    d_middle, small_m0, grads_m0 = backward_mlp(0, pieces, length, pos, d_h1, middle, mod0, own_m, other_m, act, slope, out_branch)
    d_h0, small_a0, scores0, grads_a0 = backward_attention(0, pieces, pos, h0, mod0, own_a, other_a, qkv, probs, att, branch, d_middle)

    if direct:
        done1 = reduce_grads(jnp.concatenate([
            x for p in range(pieces)
            for x in (grads_a1[p * model : (p + 1) * model], grads_m1[2 * p * model : 2 * (p + 1) * model])
        ]), 1, shards, rank)
        done_a0 = reduce_grads(grads_a0, 0, shards, rank)
        done_m0 = reduce_grads(grads_m0, 0, shards, rank)
        total_a = mine(done_a0, done1[:model])
        total_m = mine(done_m0, done1[model:])
        g_qkv, g_proj = unpack_attention(total_a.astype(F32))
        g_fc1, g_fc2 = unpack_mlp(total_m.astype(F32))
    else:
        def whole(pack0, pack1):
            return (mine(pack0, pack1).astype(F32) + swap_section(mine(pack1, pack0)).astype(F32)).astype(BF16)

        grads = unpack_attention(whole(grads_a0, grads_a1)) + unpack_mlp(whole(grads_m0, grads_m1))
        grads = [lax.psum_scatter(g, "fsdp", scatter_dimension=0, tiled=True) for g in grads]
        g_qkv, g_proj, g_fc1, g_fc2 = [g.astype(F32) for g in lax.psum(tuple(grads), "rep")]

    other_out = swap_section(mine(out1, h1))
    activations = in_order(mine(h1, out1).reshape(half, length, model), other_out.reshape(half, length, model))
    other_in = swap_section(mine(d_h1, d_h0.astype(BF16)))
    input_grads = in_order(
        mine(d_h0, d_h1.astype(F32)).reshape(half, length, model),
        other_in.astype(F32).reshape(half, length, model),
    )

    tables = [table_gradient(scores, relative_bias_index) for scores in (scores0, scores1)]
    smalls = [
        jnp.concatenate([small_a0[:, :3], small_m0, small_a0[:, 3:]], axis=1),
        jnp.concatenate([small_a1[:, :3], small_m1, small_a1[:, 3:]], axis=1),
    ]
    small = in_order(mine(smalls[0], smalls[1]), swap_section(mine(smalls[1], smalls[0])))
    table = mine(tables[0], tables[1]) + swap_section(mine(tables[1], tables[0]))
    low = small[:, :6].astype(BF16)
    w_rows = w_ada_all.reshape(model, 6, model)
    d_act = sum(dot_rows(low[:, i], w_rows[:, i]) for i in range(6))
    cond = conditioning.astype(F32)
    gate = jax.nn.sigmoid(cond)
    cond_part = d_act * (gate * (1.0 + cond * (1.0 - gate)))
    cond_grad = cond_part + swap_section(cond_part)

    bias_sum = jnp.sum(small[:, 6:], axis=0).astype(BF16)
    packed = jnp.concatenate([
        low.reshape(-1, model), bias_sum, table.astype(BF16).reshape(-1, model)
    ], axis=0)
    every = lax.all_gather(packed, ("fsdp", "rep"), axis=0)
    groups = shards * replicas
    mod_rows = samples * 6
    d_mod = every[:, :mod_rows].reshape(groups * samples, 6 * model)
    cond_all = lax.all_gather(conditioning, ("fsdp", "rep"), axis=0, tiled=True)
    width = model // shards
    act_all = jax.nn.silu(cond_all.astype(F32)).astype(BF16)
    act_cols = lax.dynamic_slice_in_dim(act_all, shard * width, width, 1)
    g_ada = dot_cols(act_cols, d_mod)
    summed = jnp.sum(every[:, mod_rows:].astype(F32), axis=0)
    g_b_ada = jnp.sum(d_mod.astype(F32), axis=0)
    g_b_fc2, g_b_fc1 = summed[0], summed[1:5].reshape(-1)
    g_b_qv, g_b_proj = summed[5:7].reshape(-1), summed[7]
    g_table = summed[10:].reshape(heads, LOW * LOW)[:, :entries]

    def own_part(vector):
        size = vector.shape[0] // shards
        return lax.dynamic_slice_in_dim(vector, shard * size, size, 0)[None]

    return (
        activations[None], input_grads[None], cond_grad,
        g_ada[None], g_qkv[None], g_proj[None], g_fc1[None], g_fc2[None],
        own_part(g_b_ada), own_part(g_b_qv), own_part(g_b_proj), own_part(g_b_fc1), own_part(g_b_fc2),
        g_table[None],
    )


def solution(mesh):
    batch = ("fsdp", "rep")
    matrix = P("section", "fsdp", None)
    vector = P("section", "fsdp")
    return jax.shard_map(
        per_device,
        mesh=mesh,
        in_specs=(
            P(batch, None, None), P(batch, None), P(batch, None, None), P(batch, None), P(),
            matrix, matrix, matrix, matrix, matrix, vector, vector, vector, vector, vector,
            P("section", None, None),
        ),
        out_specs=(
            P("section", batch, None, None), P("section", batch, None, None), P(batch, None),
            matrix, matrix, matrix, matrix, matrix, vector, vector, vector, vector, vector,
            P("section", None, None),
        ),
        check_vma=False,
    )
```

```python
import functools

import jax
import jax.numpy as jnp
from jax import lax
from jax.experimental import pallas as pl
from jax.experimental.pallas import tpu as pltpu
from jax.sharding import PartitionSpec as P

EPSILON = 1e-06
F32 = jnp.float32
BF16 = jnp.bfloat16
VMEM_BYTES = 58 * 1024 * 1024
LOW_BITS = 6
LOW = 1 << LOW_BITS
HIGH = 16


def dot(a, b):
    return jnp.dot(a, b, preferred_element_type=F32)


def dot_rows(a, b):
    return lax.dot_general(a, b, (((1,), (1,)), ((), ())), preferred_element_type=F32)


def dot_cols(a, b):
    return lax.dot_general(a, b, (((0,), (0,)), ((), ())), preferred_element_type=F32)


def norm_parts(v):
    centre = v - jnp.mean(v, axis=-1, keepdims=True)
    inverse = lax.rsqrt(jnp.mean(centre * centre, axis=-1, keepdims=True) + EPSILON)
    return centre * inverse, inverse


def norm_back(d_normed, scale, normed, inverse):
    d = d_normed * (1.0 + scale)
    return inverse * (
        d
        - jnp.mean(d, axis=-1, keepdims=True)
        - normed * jnp.mean(d * normed, axis=-1, keepdims=True)
    )


def col_sum(v):
    return jnp.sum(v, axis=0, keepdims=True)


def half_masks(width):
    lane = lax.broadcasted_iota(jnp.int32, (1, width), 1)
    first = jnp.where(lane < width // 2, 1.0, 0.0)
    return first.astype(BF16), (1.0 - first).astype(BF16)


def block_targets(mats, off, q):
    w_qkv, w_proj, w_fc1, w_fc2 = mats
    model = w_proj.shape[0]
    targets = [w_qkv.at[pl.ds(off, q), pl.ds(c * model, model)] for c in range(3)]
    targets.append(w_proj.at[pl.ds(off, q), :])
    targets += [w_fc1.at[pl.ds(off, q), pl.ds(c * model, model)] for c in range(4)]
    targets.append(w_fc2.at[pl.ds(off * 4, 4 * q), :])
    return targets


def weight_count(refs):
    return 9 if refs == 2 else 31


def weight_loads(layer, section, shard, refs, mats, sems):
    model = mats[1].shape[0]
    plans = []
    own_layer = section == layer
    if len(refs) == 2:
        targets = block_targets(mats, 0, model)
        for i, target in enumerate(targets):
            rows = pl.ds(i * model, 4 * model if i == 8 else model)
            plans.append((own_layer, refs[0].at[rows, :], refs[1].at[rows, :], target, i < 4))
    else:
        own, other, mine, theirs = refs[:4], refs[4:8], refs[8:11], refs[11:14]
        q = own[0].shape[0]
        off = pl.multiple_of(shard * q, 16)
        whole = [
            mats[0].at[pl.ds(off, q), :], mats[1].at[pl.ds(off, q), :],
            mats[2].at[pl.ds(off, q), :], mats[3].at[pl.ds(pl.multiple_of(off * 4, 16), 4 * q), :],
        ]
        for i in range(4):
            plans.append((own_layer, own[i], other[i], whole[i], i < 2))
        for p in range(1, 4):
            targets = block_targets(mats, pl.multiple_of((shard ^ p) * q, 16), q)
            for i, target in enumerate(targets):
                at = i if i < 6 else i - 6
                rows = pl.ds(at * q, 4 * q if i == 8 else q)
                half = 0 if i < 6 else 1
                plans.append((section == half, mine[p - 1].at[rows, :], theirs[p - 1].at[rows, :], target, i < 4))
    waits = ([], [])
    for i, (condition, first, second, target, early) in enumerate(plans):
        one = pltpu.make_async_copy(first, target, sems.at[i])
        two = pltpu.make_async_copy(second, target, sems.at[i])
        pl.when(condition)(one.start)
        pl.when(jnp.logical_not(condition))(two.start)
        waits[0 if early else 1].append(one)
    return waits


def wait_all(copies):
    for copy in copies:
        copy.wait()


def pack_attention(out_ref, g_qkv, g_proj, shard, pieces, stride, first):
    model = g_proj.shape[0]
    q = model // pieces
    for p in range(pieces):
        off = pl.multiple_of((shard ^ p) * q, 16) if pieces > 1 else 0
        at = (stride * p + first) * q
        for c in range(3):
            out_ref[at + c * q : at + (c + 1) * q, :] = g_qkv[pl.ds(off, q), c * model : (c + 1) * model]
        out_ref[at + 3 * q : at + 4 * q, :] = g_proj[pl.ds(off, q), :]


def pack_mlp(out_ref, g_fc1, g_fc2, shard, pieces, stride, first):
    model = g_fc1.shape[0]
    q = model // pieces
    for p in range(pieces):
        off = pl.multiple_of((shard ^ p) * q, 16) if pieces > 1 else 0
        at = (stride * p + first) * q
        for c in range(4):
            out_ref[at + c * q : at + (c + 1) * q, :] = g_fc1[pl.ds(off, q), c * model : (c + 1) * model]
        out_ref[at + 4 * q : at + 8 * q, :] = g_fc2[pl.ds(pl.multiple_of(off * 4, 16), 4 * q), :]


class Modulation:
    def __init__(self, line, model):
        self.line, self.model = line, model

    def __getitem__(self, key):
        b, rows, _ = key
        return self.line[:, pl.ds(pl.multiple_of((6 * b + rows.start) * self.model, 128), self.model)]


def bias_at(line, samples, model, start, size):
    return line[:, (6 * samples + start) * model : (6 * samples + start + size) * model]


def attention_forward(b, length, h, mod, bias, w_qkv, w_proj, b_qkv, b_proj, qkv, probs, att, branch, middle):
    model = w_proj.shape[0]
    heads = bias.shape[0]
    pair = 2 * model // heads
    rows = pl.ds(pl.multiple_of(b * length, length), length)
    masks = half_masks(pair)
    x = h[rows, :].astype(F32)
    normed, _ = norm_parts(x)
    normed_low = (normed * (1.0 + mod[b, 1:2, :]) + mod[b, 0:1, :]).astype(BF16)
    qkv[rows, :] = (dot(normed_low, w_qkv[...]) + b_qkv[...]).astype(BF16)
    for j in range(heads // 2):
        q_pair = qkv[rows, j * pair : (j + 1) * pair] * BF16((pair // 2) ** (-0.5))
        k_pair = qkv[rows, model + j * pair : model + (j + 1) * pair]
        v_pair = qkv[rows, 2 * model + j * pair : 2 * model + (j + 1) * pair]
        total = None
        for e in range(2):
            scores = dot_rows(q_pair * masks[e], k_pair) + bias[2 * j + e].astype(F32)
            raised = jnp.exp(scores - jnp.max(scores, axis=-1, keepdims=True))
            p = (raised * (1.0 / jnp.sum(raised, axis=-1, keepdims=True))).astype(BF16)
            probs[b, 2 * j + e] = p
            part = dot(p, v_pair * masks[e])
            total = part if total is None else total + part
        att[rows, j * pair : (j + 1) * pair] = total.astype(BF16)
    out = dot(att[rows, :], w_proj[...]) + b_proj[...]
    branch[rows, :] = out
    middle[rows, :] = x + mod[b, 2:3, :] * out


def mlp_forward(b, length, middle, mod, w_fc1, w_fc2, b_fc1, b_fc2, act, slope, out_branch, layer_out):
    model = w_fc1.shape[0]
    rows = pl.ds(pl.multiple_of(b * length, length), length)
    mid = middle[rows, :]
    normed, _ = norm_parts(mid)
    normed_low = (normed * (1.0 + mod[b, 4:5, :]) + mod[b, 3:4, :]).astype(BF16)
    total = b_fc2[...]
    for c in range(w_fc1.shape[1] // model):
        cols = slice(c * model, (c + 1) * model)
        v = dot(normed_low, w_fc1[:, cols]) + b_fc1[:, cols]
        square = v * v
        t = jnp.tanh(0.7978845608028654 * v * (1.0 + 0.044715 * square))
        half = 0.5 * (1.0 + t)
        a = (v * half).astype(BF16)
        act[rows, cols] = a
        slope[rows, cols] = (
            half
            + 0.5 * v * (1.0 - t * t) * (0.7978845608028654 + (3 * 0.044715 * 0.7978845608028654) * square)
        ).astype(BF16)
        total = total + dot(a, w_fc2[cols, :])
    out_branch[rows, :] = total
    layer_out[rows, :] = (mid + mod[b, 5:6, :] * total).astype(layer_out.dtype)


def mlp_backward(b, length, grad, middle, mod, w_fc1, w_fc2, act, slope, out_branch, d_middle, small, normed_low, d_pre, d_ob):
    model = w_fc1.shape[0]
    rows = pl.ds(pl.multiple_of(b * length, length), length)
    g = grad[rows, :].astype(F32)
    small[b, 2:3, :] = col_sum(g * out_branch[rows, :])
    d_out = g * mod[b, 5:6, :]
    d_out_low = d_out.astype(BF16)
    d_ob[rows, :] = d_out_low
    small[b, 3:4, :] = col_sum(d_out_low.astype(F32))
    normed, inverse = norm_parts(middle[rows, :])
    normed_low[rows, :] = (normed * (1.0 + mod[b, 4:5, :]) + mod[b, 3:4, :]).astype(BF16)
    d_normed = None
    for c in range(w_fc1.shape[1] // model):
        cols = slice(c * model, (c + 1) * model)
        d_act = dot_rows(d_out_low, w_fc2[cols, :])
        d_low = (d_act * slope[rows, cols].astype(F32)).astype(BF16)
        d_pre[rows, cols] = d_low
        small[b, 4 + c : 5 + c, :] = col_sum(d_low.astype(F32))
        part = dot_rows(d_low, w_fc1[:, cols])
        d_normed = part if d_normed is None else d_normed + part
    small[b, 0:1, :] = col_sum(d_normed)
    small[b, 1:2, :] = col_sum(d_normed * normed)
    d_middle[rows, :] = norm_back(d_normed, mod[b, 4:5, :], normed, inverse) + g


def mlp_weight_grads(normed_low, d_pre, act, d_ob, g_fc1, g_fc2):
    model = g_fc1.shape[0]
    for c in range(g_fc1.shape[1] // model):
        cols = slice(c * model, (c + 1) * model)
        g_fc1[:, cols] = dot_cols(normed_low[...], d_pre[:, cols]).astype(BF16)
        g_fc2[cols, :] = dot_cols(act[:, cols], d_ob[...]).astype(BF16)


def attention_backward(b, length, h, mod, w_qkv, w_proj, qkv, probs, att, branch, d_middle, d_in, small, score_sum, normed_low, d_qkv, d_br):
    model = w_proj.shape[0]
    heads = probs.shape[1]
    pair = 2 * model // heads
    scale = F32((pair // 2) ** (-0.5))
    rows = pl.ds(pl.multiple_of(b * length, length), length)
    masks = half_masks(pair)
    d_mid = d_middle[rows, :]
    small[b, 2:3, :] = col_sum(d_mid * branch[rows, :])
    d_branch = (d_mid * mod[b, 2:3, :]).astype(BF16)
    d_br[rows, :] = d_branch
    small[b, 5:6, :] = col_sum(d_branch.astype(F32))
    d_att = dot_rows(d_branch, w_proj[...]).astype(BF16)
    for j in range(heads // 2):
        q_pair = qkv[rows, j * pair : (j + 1) * pair]
        k_pair = qkv[rows, model + j * pair : model + (j + 1) * pair]
        v_pair = qkv[rows, 2 * model + j * pair : 2 * model + (j + 1) * pair]
        d_pair = d_att[:, j * pair : (j + 1) * pair]
        d_q = d_k = d_v = None
        for e in range(2):
            p_low = probs[b, 2 * j + e]
            p = p_low.astype(F32)
            d_here = d_pair * masks[e]
            d_p = dot_rows(d_here, v_pair)
            d_s = (p * (d_p - jnp.sum(d_p * p, axis=-1, keepdims=True))).astype(BF16)
            score_sum[2 * j + e] += d_s.astype(F32)
            v_part = dot_cols(p_low, d_here)
            q_part = dot(d_s, k_pair * masks[e])
            k_part = dot_cols(d_s, q_pair * masks[e])
            d_v = v_part if d_v is None else d_v + v_part
            d_q = q_part if d_q is None else d_q + q_part
            d_k = k_part if d_k is None else d_k + k_part
        d_qkv[rows, j * pair : (j + 1) * pair] = (d_q * scale).astype(BF16)
        d_qkv[rows, model + j * pair : model + (j + 1) * pair] = (d_k * scale).astype(BF16)
        d_qkv[rows, 2 * model + j * pair : 2 * model + (j + 1) * pair] = d_v.astype(BF16)
    small[b, 3:4, :] = col_sum(d_qkv[rows, :model].astype(F32))
    small[b, 4:5, :] = col_sum(d_qkv[rows, 2 * model :].astype(F32))
    small[b, 6:8, :] = jnp.zeros((2, model), F32)
    d_normed = dot_rows(d_qkv[rows, :], w_qkv[...])
    normed, inverse = norm_parts(h[rows, :].astype(F32))
    normed_low[rows, :] = (normed * (1.0 + mod[b, 1:2, :]) + mod[b, 0:1, :]).astype(BF16)
    small[b, 0:1, :] = col_sum(d_normed)
    small[b, 1:2, :] = col_sum(d_normed * normed)
    d_in[rows, :] = (norm_back(d_normed, mod[b, 1:2, :], normed, inverse) + d_mid).astype(d_in.dtype)


def attention_weight_grads(normed_low, d_qkv, att, d_br, g_qkv, g_proj):
    model = g_proj.shape[0]
    for c in range(3):
        cols = slice(c * model, (c + 1) * model)
        g_qkv[:, cols] = dot_cols(normed_low[...], d_qkv[:, cols]).astype(BF16)
    g_proj[...] = dot_cols(att[...], d_br[...]).astype(BF16)


def each_sample(count, body):
    def step(b, carry):
        body(b)
        return carry

    lax.fori_loop(0, count, step, 0)


def set_line(line, layer, section, own_line, other_line):
    line[...] = jnp.where(section == layer, own_line[...], other_line[...])


def start_bias(layer, section, own, other, bias, sem):
    one = pltpu.make_async_copy(own, bias, sem)
    two = pltpu.make_async_copy(other, bias, sem)
    pl.when(section == layer)(one.start)
    pl.when(section != layer)(two.start)
    return one


def line_biases(line, samples, model):
    q_bias = bias_at(line, samples, model, 0, 1)
    v_bias = bias_at(line, samples, model, 1, 1)
    b_qkv = jnp.concatenate([q_bias, jnp.zeros_like(q_bias), v_bias], axis=1)
    return b_qkv, bias_at(line, samples, model, 2, 1), bias_at(line, samples, model, 3, 4), bias_at(line, samples, model, 7, 1)


def forward_kernel(layer, length, n_weights, pos, h, own_line, other_line, own_bias, other_bias, *rest):
    refs, rest = rest[:n_weights], rest[n_weights:]
    (qkv, probs, att, branch, middle, act, slope, out_branch, layer_out,
     w_qkv, w_proj, w_fc1, w_fc2, bias, line, sems) = rest
    section, shard = pos[0], pos[1]
    model = h.shape[1]
    samples = h.shape[0] // length
    got_bias = start_bias(layer, section, own_bias, other_bias, bias, sems.at[weight_count(n_weights)])
    for_attention, for_mlp = weight_loads(layer, section, shard, refs, (w_qkv, w_proj, w_fc1, w_fc2), sems)
    set_line(line, layer, section, own_line, other_line)
    mod = Modulation(line, model)
    b_qkv, b_proj, b_fc1, b_fc2 = line_biases(line, samples, model)
    got_bias.wait()
    wait_all(for_attention)
    each_sample(
        samples,
        lambda b: attention_forward(b, length, h, mod, bias, w_qkv, w_proj, b_qkv, b_proj, qkv, probs, att, branch, middle),
    )
    wait_all(for_mlp)
    each_sample(
        samples,
        lambda b: mlp_forward(b, length, middle, mod, w_fc1, w_fc2, b_fc1, b_fc2, act, slope, out_branch, layer_out),
    )


def both_kernel(layer, pieces, length, n_weights, pos, h, grad, own_line, other_line, own_bias, other_bias, *rest):
    refs, rest = rest[:n_weights], rest[n_weights:]
    (layer_out, d_in, small_a, small_m, scores, pack,
     w_qkv, w_proj, w_fc1, w_fc2, bias, line, qkv, probs, att, branch, middle, act, slope, out_branch,
     d_middle, normed_low, d_pre, d_ob, d_qkv, score_sum, g_qkv, g_proj, g_fc1, g_fc2, sems) = rest
    section, shard = pos[0], pos[1]
    model = h.shape[1]
    samples = h.shape[0] // length
    got_bias = start_bias(layer, section, own_bias, other_bias, bias, sems.at[weight_count(n_weights)])
    for_attention, for_mlp = weight_loads(layer, section, shard, refs, (w_qkv, w_proj, w_fc1, w_fc2), sems)
    set_line(line, layer, section, own_line, other_line)
    mod = Modulation(line, model)
    b_qkv, b_proj, b_fc1, b_fc2 = line_biases(line, samples, model)
    got_bias.wait()
    wait_all(for_attention)
    each_sample(
        samples,
        lambda b: attention_forward(b, length, h, mod, bias, w_qkv, w_proj, b_qkv, b_proj, qkv, probs, att, branch, middle),
    )
    wait_all(for_mlp)

    def mlp(b):
        mlp_forward(b, length, middle, mod, w_fc1, w_fc2, b_fc1, b_fc2, act, slope, out_branch, layer_out)
        mlp_backward(b, length, grad, middle, mod, w_fc1, w_fc2, act, slope, out_branch, d_middle, small_m, normed_low, d_pre, d_ob)

    each_sample(samples, mlp)
    mlp_weight_grads(normed_low, d_pre, act, d_ob, g_fc1, g_fc2)
    pack_mlp(pack, g_fc1, g_fc2, shard, pieces, 12, 4)
    score_sum[...] = jnp.zeros_like(score_sum)
    each_sample(
        samples,
        lambda b: attention_backward(b, length, h, mod, w_qkv, w_proj, qkv, probs, att, branch, d_middle, d_in, small_a, score_sum, normed_low, d_qkv, d_ob),
    )
    scores[...] = score_sum[...].astype(BF16)
    attention_weight_grads(normed_low, d_qkv, att, d_ob, g_qkv, g_proj)
    pack_attention(pack, g_qkv, g_proj, shard, pieces, 12, 0)


def backward_mlp_kernel(layer, pieces, length, n_weights, pos, grad, middle, own_line, other_line, act, slope, out_branch, *rest):
    refs, rest = rest[:n_weights], rest[n_weights:]
    (d_middle, small, pack,
     w_qkv, w_proj, w_fc1, w_fc2, line, normed_low, d_pre, d_ob, g_fc1, g_fc2, sems) = rest
    section, shard = pos[0], pos[1]
    for_attention, for_mlp = weight_loads(layer, section, shard, refs, (w_qkv, w_proj, w_fc1, w_fc2), sems)
    set_line(line, layer, section, own_line, other_line)
    mod = Modulation(line, middle.shape[1])
    wait_all(for_mlp)
    each_sample(
        middle.shape[0] // length,
        lambda b: mlp_backward(b, length, grad, middle, mod, w_fc1, w_fc2, act, slope, out_branch, d_middle, small, normed_low, d_pre, d_ob),
    )
    mlp_weight_grads(normed_low, d_pre, act, d_ob, g_fc1, g_fc2)
    pack_mlp(pack, g_fc1, g_fc2, shard, pieces, 8, 0)
    wait_all(for_attention)


def backward_attention_kernel(layer, pieces, length, n_weights, n_after, pos, h, own_line, other_line, qkv, probs, att, branch, d_middle, *rest):
    refs, rest = rest[:n_weights], rest[n_weights + n_after :]
    (d_in, small, scores, pack,
     w_qkv, w_proj, w_fc1, w_fc2, line, normed_low, d_qkv, d_br, score_sum, g_qkv, g_proj, sems) = rest
    section, shard = pos[0], pos[1]
    for_attention, for_mlp = weight_loads(layer, section, shard, refs, (w_qkv, w_proj, w_fc1, w_fc2), sems)
    set_line(line, layer, section, own_line, other_line)
    mod = Modulation(line, h.shape[1])
    score_sum[...] = jnp.zeros_like(score_sum)
    wait_all(for_attention)
    each_sample(
        h.shape[0] // length,
        lambda b: attention_backward(b, length, h, mod, w_qkv, w_proj, qkv, probs, att, branch, d_middle, d_in, small, score_sum, normed_low, d_qkv, d_br),
    )
    scores[...] = score_sum[...].astype(BF16)
    attention_weight_grads(normed_low, d_qkv, att, d_br, g_qkv, g_proj)
    pack_attention(pack, g_qkv, g_proj, shard, pieces, 4, 0)
    wait_all(for_mlp)


def call(kernel, pos, operands, in_hbm, outs, scratch, sems=0):
    specs = [pl.BlockSpec(memory_space=pltpu.SMEM)]
    specs += [pl.BlockSpec(memory_space=pltpu.VMEM) for _ in operands]
    specs += [pl.BlockSpec(memory_space=pl.ANY) for _ in in_hbm]
    shapes = [pltpu.VMEM(shape, dtype) for shape, dtype in scratch]
    if sems:
        shapes.append(pltpu.SemaphoreType.DMA((sems,)))
    return pl.pallas_call(
        kernel,
        out_shape=[jax.ShapeDtypeStruct(shape, dtype) for shape, dtype in outs],
        in_specs=specs,
        out_specs=[pl.BlockSpec(memory_space=pltpu.VMEM) for _ in outs],
        scratch_shapes=shapes,
        compiler_params=pltpu.CompilerParams(vmem_limit_bytes=VMEM_BYTES),
    )(pos, *operands, *in_hbm)


class Sizes:
    def __init__(self, samples, length, model, heads, hidden, pieces):
        self.samples, self.length, self.model = samples, length, model
        self.heads, self.hidden, self.pieces = heads, hidden, pieces
        self.rows = samples * length
        self.line = ((1, (6 * samples + 4 + hidden // model) * model), F32)
        self.weights = [
            ((model, 3 * model), BF16), ((model, model), BF16), ((model, hidden), BF16), ((hidden, model), BF16),
        ]
        self.bias = ((heads, length, length), BF16)
        self.probs = ((samples, heads, length, length), BF16)
        self.low = ((self.rows, model), BF16)
        self.full = ((self.rows, model), F32)
        self.qkv = ((self.rows, 3 * model), BF16)
        self.wide = ((self.rows, hidden), BF16)
        self.small = ((samples, 8, model), F32)


def forward_layer(layer, z, pos, h, lines, biases, weights):
    def kernel(pos_ref, h_ref, a, b, *rest):
        forward_kernel(layer, z.length, len(weights), pos_ref, h_ref, a, b, *rest)

    return call(
        kernel, pos, (h, *lines), (*biases, *weights),
        [z.qkv, z.probs, z.low, z.full, z.full, z.wide, z.wide, z.full, z.low],
        [*z.weights, z.bias, z.line], weight_count(len(weights)) + 1,
    )


def both_ways(layer, z, pos, h, grad, lines, biases, weights):
    return call(
        functools.partial(both_kernel, layer, z.pieces, z.length, len(weights)),
        pos, (h, grad, *lines), (*biases, *weights),
        [z.low, z.low, z.small, z.small, z.bias, ((12 * z.model, z.model), BF16)],
        [*z.weights, z.bias, z.line, z.qkv, z.probs, z.low, z.full, z.full, z.wide, z.wide, z.full,
         z.full, z.low, z.wide, z.low, z.qkv, (z.bias[0], F32), *z.weights],
        weight_count(len(weights)) + 1,
    )


def backward_mlp(layer, z, pos, grad, middle, lines, act, slope, out_branch, weights):
    return call(
        functools.partial(backward_mlp_kernel, layer, z.pieces, z.length, len(weights)),
        pos, (grad, middle, *lines, act, slope, out_branch), weights,
        [z.full, z.small, ((8 * z.model, z.model), BF16)],
        [*z.weights, z.line, z.low, z.wide, z.low, *z.weights[2:]],
        weight_count(len(weights)),
    )


def backward_attention(layer, z, pos, h, lines, qkv, probs, att, branch, d_middle, weights, after):
    return call(
        functools.partial(backward_attention_kernel, layer, z.pieces, z.length, len(weights), len(after)),
        pos, (h, *lines, qkv, probs, att, branch, d_middle), (*weights, *after),
        [z.full, z.small, z.bias, ((4 * z.model, z.model), BF16)],
        [*z.weights, z.line, z.low, z.qkv, z.low, (z.bias[0], F32), *z.weights[:2]],
        weight_count(len(weights)),
    )


def half_kernel(pos, *refs):
    own, other, outs = refs[:4], refs[4:8], refs[8:]
    section = pos[0]
    model = outs[0].shape[1]
    q = own[0].shape[0]
    for layer in range(2):
        out = outs[layer]
        for source, here in ((own, section == layer), (other, section != layer)):
            qkv, proj, fc1, fc2 = source

            @pl.when(jnp.logical_and(here, section == 0))
            def _():
                for c in range(3):
                    out[c * q : (c + 1) * q, :] = qkv[:, c * model : (c + 1) * model]
                out[3 * q : 4 * q, :] = proj[...]
                for c in range(2):
                    out[(4 + c) * q : (5 + c) * q, :] = fc1[:, c * model : (c + 1) * model]

            @pl.when(jnp.logical_and(here, section == 1))
            def _():
                for c in range(2):
                    out[c * q : (c + 1) * q, :] = fc1[:, (2 + c) * model : (3 + c) * model]
                out[2 * q : 6 * q, :] = fc2[...]


def halves(pos, own, other):
    q, model = own[1].shape
    shape = ((6 * q, model), BF16)
    return call(half_kernel, pos, (*own, *other), (), [shape, shape], [])


def lookup_kernel(table, index, out, work):
    heads, length = out.shape[0], out.shape[1]
    high_count = table.shape[0] // 8
    values = table[...]
    low_id = lax.broadcasted_iota(jnp.int32, (LOW, length), 0)

    def step(i, carry):
        block = index[pl.ds(pl.multiple_of(i * 8, 8), 8), :]
        for r in range(8):
            entry = block[r : r + 1, :]
            picks = jnp.where(low_id == (entry & (LOW - 1)), 1.0, 0.0).astype(BF16)
            found = dot(values, picks).reshape(high_count, 8, length)
            high = jnp.broadcast_to(entry >> LOW_BITS, (8, length))
            bit = high_count // 2
            while bit:
                chosen = (high & bit) != 0
                found = jnp.where(chosen[None], found[bit : 2 * bit], found[:bit])
                bit //= 2
            for head in range(heads):
                work[head, pl.ds(i * 8 + r, 1), :] = found[0, head : head + 1, :]
        return carry

    lax.fori_loop(0, length // 8, step, 0)
    out[...] = work[...].astype(BF16)


def lookup(table, index):
    heads, entries = table.shape
    high_count = HIGH
    padded = jnp.pad(table, ((0, 8 - heads), (0, high_count * LOW - entries)))
    rows = jnp.transpose(padded.reshape(8, high_count, LOW), (1, 0, 2)).reshape(high_count * 8, LOW)
    length = index.shape[0]
    return pl.pallas_call(
        lookup_kernel,
        out_shape=jax.ShapeDtypeStruct((heads, length, length), BF16),
        scratch_shapes=[pltpu.VMEM((heads, length, length), F32)],
        compiler_params=pltpu.CompilerParams(vmem_limit_bytes=VMEM_BYTES),
    )(rows, index)


def table_kernel(scores_a, scores_b, index, *rest):
    out = rest[-1]
    heads, length = scores_a.shape[0], scores_a.shape[1]
    out[...] = jnp.zeros_like(out)
    low_ids = lax.broadcasted_iota(jnp.int32, (LOW, length), 0)
    high_ids = lax.broadcasted_iota(jnp.int32, (HIGH, length), 0)

    def step(i, carry):
        rows = pl.ds(pl.multiple_of(i * 16, 16), 16)
        entries = index[rows, :]
        block = [scores[head, rows, :].astype(F32) for scores in (scores_a, scores_b) for head in range(heads)]
        total = None
        for r in range(16):
            entry = entries[r : r + 1, :]
            low = jnp.where(low_ids == (entry & (LOW - 1)), 1.0, 0.0).astype(BF16)
            high = high_ids == (entry >> LOW_BITS)
            left = jnp.concatenate([jnp.where(high, part[r : r + 1, :], 0.0) for part in block], axis=0).astype(BF16)
            part = dot_rows(left, low)
            total = part if total is None else total + part
        out[...] += total
        return carry

    lax.fori_loop(0, length // 16, step, 0)


def table_gradients(scores_a, scores_b, index, after):
    heads = scores_a.shape[0]
    total = pl.pallas_call(
        table_kernel,
        out_shape=jax.ShapeDtypeStruct((2 * heads * HIGH, LOW), F32),
        in_specs=[pl.BlockSpec(memory_space=pltpu.VMEM)] * 3 + [pl.BlockSpec(memory_space=pl.ANY)] * len(after),
        out_specs=pl.BlockSpec(memory_space=pltpu.VMEM),
        compiler_params=pltpu.CompilerParams(vmem_limit_bytes=VMEM_BYTES),
    )(scores_a, scores_b, index, *after)
    return total[: heads * HIGH], total[heads * HIGH :]


def swap_section(value):
    return lax.ppermute(value, "section", [(0, 1), (1, 0)])


def pairs_of(count, step):
    return [(i, i ^ step) for i in range(count)]


def by_rank(pieces, rank):
    stack = jnp.stack(pieces)
    count = len(pieces)
    bit = 1
    while bit < count:
        moved = jnp.stack([stack[i ^ bit] for i in range(count)])
        stack = jnp.where((rank & bit) != 0, moved, stack)
        bit *= 2
    return stack


def one_section_pairs(layer, count, step):
    return [(layer * count + i, layer * count + (i ^ step)) for i in range(count)]


def section_sums(pack, layer, shards):
    other = lax.ppermute(pack, "section", [(1 - layer, layer)])
    size = pack.shape[0] // shards
    return [
        pack[p * size : (p + 1) * size].astype(F32) + other[p * size : (p + 1) * size].astype(F32)
        for p in range(shards)
    ]


def send_pieces(sums, layer):
    shards = len(sums)
    low = [x.astype(BF16) for x in sums[1:]]
    got = [
        lax.ppermute(low[p - 1], ("section", "fsdp"), one_section_pairs(layer, shards, p))
        for p in range(1, shards)
    ]
    return low, got


def add_pieces(own, got):
    total = own
    for piece in got:
        total = total + piece.astype(F32)
    return total


def replica_total(total, layer, rank):
    replicas = lax.axis_size("rep")
    size = total.shape[0]
    parts = total.reshape(replicas, size // replicas, -1)
    low_parts = parts.astype(BF16)
    mine = lax.dynamic_index_in_dim(parts, rank, 0, keepdims=False)
    names = ("section", "rep")
    got = [
        lax.ppermute(
            lax.dynamic_index_in_dim(low_parts, rank ^ j, 0, keepdims=False),
            names, one_section_pairs(layer, replicas, j),
        )
        for j in range(1, replicas)
    ]
    mine = add_pieces(mine, got).astype(BF16)
    quarters = [mine] + [
        lax.ppermute(mine, names, one_section_pairs(layer, replicas, j)) for j in range(1, replicas)
    ]
    return by_rank(quarters, rank).reshape(size, -1)


def unpack_attention(pack):
    q = pack.shape[0] // 4
    return jnp.concatenate([pack[c * q : (c + 1) * q] for c in range(3)], axis=1), pack[3 * q :]


def unpack_mlp(pack):
    q = pack.shape[0] // 8
    return jnp.concatenate([pack[c * q : (c + 1) * q] for c in range(4)], axis=1), pack[4 * q :]


def from_peers(value, axis):
    return [lax.ppermute(value, axis, pairs_of(lax.axis_size(axis), p)) for p in range(1, lax.axis_size(axis))]


def pair_sum(values):
    while len(values) > 1:
        values = [values[i] + values[i + 1] for i in range(0, len(values), 2)]
    return values[0]


def per_device(inputs, conditioning, cotangent, micro_sizes, relative_bias_index,
               w_ada, w_qkv, w_proj, w_fc1, w_fc2, b_ada, b_qv, b_proj, b_fc1, b_fc2, bias_table):
    section = lax.axis_index("section")
    shard = lax.axis_index("fsdp")
    rank = lax.axis_index("rep")
    shards, replicas = lax.axis_size("fsdp"), lax.axis_size("rep")
    direct = shards == 4 and replicas == 4
    is_first = section == 0
    samples, length, model = inputs.shape
    heads, entries = bias_table.shape[1:]
    half = samples // 2
    z = Sizes(half, length, model, heads, 4 * model, shards if direct else 1)
    pos = jnp.stack([section, shard]).astype(jnp.int32)

    def mine(first, second):
        return jnp.where(is_first, first, second)

    def own_samples(array):
        return lax.dynamic_slice_in_dim(array, section * half, half, 0)

    def in_order(own, other):
        return jnp.where(is_first, jnp.concatenate([own, other]), jnp.concatenate([other, own]))

    own_raw = [w_qkv[0], w_proj[0], w_fc1[0], w_fc2[0]]
    cond_size = conditioning.size
    width = model // shards
    w_ada_all = lax.all_gather(w_ada[0], "fsdp", axis=0, tiled=True)
    if direct:
        row = jnp.concatenate([conditioning.reshape(1, -1), b_ada, b_qv, b_proj, b_fc1, b_fc2], axis=1)
        rows = [row] + from_peers(row, "fsdp")
        other_raw = [swap_section(w) for w in own_raw]
        half0, half1 = halves(pos, own_raw, other_raw)
        got0 = from_peers(half0, "fsdp")
        cond_pieces = jnp.stack([r[0, :cond_size].reshape(samples, model) for r in rows])
        acts = jax.nn.silu(cond_pieces.astype(F32)).astype(BF16)
        acts = lax.dynamic_slice_in_dim(acts, shard * width, width, 2)
        partial = lax.dot_general(acts, w_ada[0], (((2,), (0,)), ((), ())), preferred_element_type=F32)
        modulation = partial[0]
        for p in range(1, shards):
            modulation = modulation + lax.ppermute(partial[p], "fsdp", pairs_of(shards, p))
        got1 = from_peers(half1, "fsdp")
        weights0 = own_raw + other_raw + got0 + [swap_section(w) for w in got0]
        weights1 = own_raw + other_raw + got1 + [swap_section(w) for w in got1]
        bias_rows = by_rank([r[0, cond_size:] for r in rows], shard)
    else:
        row = jnp.concatenate([b_ada, b_qv, b_proj, b_fc1, b_fc2], axis=1)
        bias_rows = lax.all_gather(row[0], "fsdp", axis=0)
        whole = [lax.all_gather(w, "fsdp", axis=0, tiled=True) for w in own_raw]
        own_whole = jnp.concatenate(
            [whole[0][:, c * model : (c + 1) * model] for c in range(3)] + [whole[1]]
            + [whole[2][:, c * model : (c + 1) * model] for c in range(4)] + [whole[3]]
        )
        weights0 = weights1 = [own_whole, swap_section(own_whole)]
        acts = jax.nn.silu(conditioning.astype(F32)).astype(BF16)
        modulation = dot(acts, w_ada_all)
    cuts = [b_ada.shape[1], b_qv.shape[1], b_proj.shape[1], b_fc1.shape[1], b_fc2.shape[1]]
    biases, at = [], 0
    for cut in cuts:
        biases.append(bias_rows[:, at : at + cut].reshape(1, -1).astype(F32))
        at += cut
    modulation = modulation + biases[0]
    other_samples = lax.dynamic_slice_in_dim(modulation, (1 - section) * half, half, 0)
    own_line = jnp.concatenate([own_samples(modulation).reshape(1, -1)] + biases[1:], axis=1)
    other_line = swap_section(jnp.concatenate([other_samples.reshape(1, -1)] + biases[1:], axis=1))
    lines = (own_line, other_line)
    bias_own = lookup(bias_table[0], relative_bias_index)
    bias_heads = (bias_own, swap_section(bias_own))

    live = (jnp.arange(half)[:, None, None] < lax.dynamic_index_in_dim(micro_sizes[0], section, 0)).astype(BF16)
    h0 = own_samples(inputs).reshape(half * length, model)
    grad1 = (own_samples(cotangent) * live).reshape(half * length, model)

    qkv, probs, att, branch, middle, act, slope, out_branch, h1 = forward_layer(0, z, pos, h0, lines, bias_heads, weights0)
    out1, d_h1, small_a1, small_m1, scores1, pack1 = both_ways(1, z, pos, h1, grad1, lines, bias_heads, weights1)
    d_middle, small_m0, pack_m0 = backward_mlp(0, z, pos, d_h1, middle, lines, act, slope, out_branch, weights0)
    if direct:
        sums1 = section_sums(pack1, 1, shards)
        low1, got1 = send_pieces(sums1, 1)
        after = low1
    else:
        after = []
    d_h0, small_a0, scores0, pack_a0 = backward_attention(
        0, z, pos, h0, lines, qkv, probs, att, branch, d_middle, weights0, after
    )

    if direct:
        sums_m0 = section_sums(pack_m0, 0, shards)
        low_m0, got_m0 = send_pieces(sums_m0, 0)
        sums_a0 = section_sums(pack_a0, 0, shards)
        low_a0, got_a0 = send_pieces(sums_a0, 0)
        done1 = replica_total(add_pieces(sums1[0], got1), 1, rank)
        total0 = jnp.concatenate([add_pieces(sums_a0[0], got_a0), add_pieces(sums_m0[0], got_m0)])
        done0 = replica_total(total0, 0, rank)
        done = mine(done0, done1).astype(F32)
        g_qkv, g_proj = unpack_attention(done[:model])
        g_fc1, g_fc2 = unpack_mlp(done[model:])
        after = got1 + low_a0 + low_m0
    else:
        pack0 = jnp.concatenate([pack_a0, pack_m0])
        total = (mine(pack0, pack1).astype(F32) + swap_section(mine(pack1, pack0)).astype(F32)).astype(BF16)
        grads = unpack_attention(total[: 4 * model]) + unpack_mlp(total[4 * model :])
        grads = [lax.psum_scatter(g, "fsdp", scatter_dimension=0, tiled=True) for g in grads]
        g_qkv, g_proj, g_fc1, g_fc2 = [g.astype(F32) for g in lax.psum(tuple(grads), "rep")]

    other_out = swap_section(mine(out1, h1))
    activations = in_order(mine(h1, out1).reshape(half, length, model), other_out.reshape(half, length, model))
    other_in = swap_section(mine(d_h1, d_h0.astype(BF16)))
    input_grads = in_order(
        mine(d_h0, d_h1.astype(F32)).reshape(half, length, model),
        other_in.astype(F32).reshape(half, length, model),
    )

    tables = table_gradients(scores0, scores1, relative_bias_index, after)
    smalls = [
        jnp.concatenate([small_a0[:, :3], small_m0, small_a0[:, 3:]], axis=1),
        jnp.concatenate([small_a1[:, :3], small_m1, small_a1[:, 3:]], axis=1),
    ]
    small = in_order(mine(smalls[0], smalls[1]), swap_section(mine(smalls[1], smalls[0])))
    table = mine(tables[0], tables[1]) + swap_section(mine(tables[1], tables[0]))
    low = small[:, :6].astype(BF16)
    w_rows = w_ada_all.reshape(model, 6, model)
    d_act = sum(dot_rows(low[:, i], w_rows[:, i]) for i in range(6))
    cond = conditioning.astype(F32)
    gate = jax.nn.sigmoid(cond)
    cond_part = d_act * (gate * (1.0 + cond * (1.0 - gate)))
    cond_grad = cond_part + swap_section(cond_part)

    kept = jnp.concatenate([low, conditioning[:, None]], axis=1).reshape(-1, model)
    summed = jnp.concatenate([jnp.sum(small[:, 6:14], axis=0), table.reshape(-1, model)])
    if direct:
        both = jnp.concatenate([kept, summed.astype(BF16)])
        plane = [both] + from_peers(both, "fsdp")
        count = kept.shape[0]
        summed = pair_sum([p[count:].astype(F32) for p in plane])
        both = jnp.concatenate([p[:count] for p in plane] + [summed.astype(BF16)])
        every = [both] + from_peers(both, "rep")
        count = count * shards
        summed = pair_sum([p[count:].astype(F32) for p in every])
        kept = by_rank([p[:count] for p in every], rank).reshape(-1, 7, model)
    else:
        kept = lax.all_gather(kept, ("fsdp", "rep"), axis=0, tiled=True).reshape(-1, 7, model)
        summed = lax.psum(summed, ("fsdp", "rep"))
    act_all = jax.nn.silu(kept[:, 6].astype(F32)).astype(BF16)
    act_cols = lax.dynamic_slice_in_dim(act_all, shard * width, width, 1)
    g_ada = jnp.concatenate([dot_cols(act_cols, kept[:, i]) for i in range(6)], axis=1)
    g_b_ada = jnp.sum(kept[:, :6].astype(F32), axis=0).reshape(-1)
    g_b_fc2, g_b_fc1 = summed[0], summed[1:5].reshape(-1)
    g_b_qv, g_b_proj = summed[5:7].reshape(-1), summed[7]
    g_table = summed[8:].reshape(heads, HIGH * LOW)[:, :entries]

    def own_part(vector):
        size = vector.shape[0] // shards
        return lax.dynamic_slice_in_dim(vector, shard * size, size, 0)[None]

    return (
        activations[None], input_grads[None], cond_grad,
        g_ada[None], g_qkv[None], g_proj[None], g_fc1[None], g_fc2[None],
        own_part(g_b_ada), own_part(g_b_qv), own_part(g_b_proj), own_part(g_b_fc1), own_part(g_b_fc2),
        g_table[None],
    )


def solution(mesh):
    batch = ("fsdp", "rep")
    matrix = P("section", "fsdp", None)
    vector = P("section", "fsdp")
    return jax.shard_map(
        per_device,
        mesh=mesh,
        in_specs=(
            P(batch, None, None), P(batch, None), P(batch, None, None), P(batch, None), P(),
            matrix, matrix, matrix, matrix, matrix, vector, vector, vector, vector, vector,
            P("section", None, None),
        ),
        out_specs=(
            P("section", batch, None, None), P("section", batch, None, None), P(batch, None),
            matrix, matrix, matrix, matrix, matrix, vector, vector, vector, vector, vector,
            P("section", None, None),
        ),
        check_vma=False,
    )
```

```python
import functools

import jax
import jax.numpy as jnp
from jax import lax
from jax.experimental import pallas as pl
from jax.experimental.pallas import tpu as pltpu
from jax.sharding import PartitionSpec as P

EPSILON = 1e-06
F32 = jnp.float32
BF16 = jnp.bfloat16
VMEM_BYTES = 58 * 1024 * 1024
LOW_BITS = 6
LOW = 1 << LOW_BITS
HIGH = 16


def dot(a, b):
    return jnp.dot(a, b, preferred_element_type=F32)


def dot_rows(a, b):
    return lax.dot_general(a, b, (((1,), (1,)), ((), ())), preferred_element_type=F32)


def dot_cols(a, b):
    return lax.dot_general(a, b, (((0,), (0,)), ((), ())), preferred_element_type=F32)


def norm_parts(v):
    centre = v - jnp.mean(v, axis=-1, keepdims=True)
    inverse = lax.rsqrt(jnp.mean(centre * centre, axis=-1, keepdims=True) + EPSILON)
    return centre * inverse, inverse


def norm_back(d_normed, scale, normed, inverse):
    d = d_normed * (1.0 + scale)
    return inverse * (
        d
        - jnp.mean(d, axis=-1, keepdims=True)
        - normed * jnp.mean(d * normed, axis=-1, keepdims=True)
    )


def col_sum(v):
    return jnp.sum(v, axis=0, keepdims=True)


def half_masks(width):
    lane = lax.broadcasted_iota(jnp.int32, (1, width), 1)
    first = jnp.where(lane < width // 2, 1.0, 0.0)
    return first.astype(BF16), (1.0 - first).astype(BF16)


def block_targets(mats, off, q):
    w_qkv, w_proj, w_fc1, w_fc2 = mats
    model = w_proj.shape[0]
    targets = [w_qkv.at[pl.ds(off, q), pl.ds(c * model, model)] for c in range(3)]
    targets.append(w_proj.at[pl.ds(off, q), :])
    targets += [w_fc1.at[pl.ds(off, q), pl.ds(c * model, model)] for c in range(4)]
    targets.append(w_fc2.at[pl.ds(off * 4, 4 * q), :])
    return targets


def weight_count(refs):
    return 9 if refs == 2 else 36


def weight_loads(layer, section, shard, refs, mats, sems):
    model = mats[1].shape[0]
    plans = []
    if len(refs) == 2:
        for i, target in enumerate(block_targets(mats, 0, model)):
            rows = pl.ds(i * model, 4 * model if i == 8 else model)
            plans.append((refs[0].at[rows, :], refs[1].at[rows, :], target, i < 4))
    else:
        count = len(refs) // 2
        q = refs[0].shape[0] // 12
        for p in range(4):
            targets = block_targets(mats, pl.multiple_of((shard ^ p) * q, 16), q)
            for i, target in enumerate(targets):
                which, at = p, i
                if p == 3 and i >= 6:
                    which, at = 4, i - 6
                rows = pl.ds(at * q, 4 * q if i == 8 else q)
                plans.append((refs[which].at[rows, :], refs[count + which].at[rows, :], target, i < 4))
    ones = [pltpu.make_async_copy(x[0], x[2], sems.at[i]) for i, x in enumerate(plans)]
    twos = [pltpu.make_async_copy(x[1], x[2], sems.at[i]) for i, x in enumerate(plans)]

    @pl.when(section == layer)
    def _():
        for copy in ones:
            copy.start()

    @pl.when(section != layer)
    def _():
        for copy in twos:
            copy.start()

    return (
        [copy for copy, x in zip(ones, plans) if x[3]],
        [copy for copy, x in zip(ones, plans) if not x[3]],
    )


def wait_all(copies):
    for copy in copies:
        copy.wait()


def put_half(refs, section, half, at, value):
    keep, send = refs
    rows = slice(at, at + value.shape[0])

    @pl.when(section == half)
    def _():
        keep[rows, :] = value

    @pl.when(section != half)
    def _():
        send[rows, :] = value


def pack_attention(refs, section, g_qkv, g_proj, shard, pieces, stride, first):
    model = g_proj.shape[0]
    q = model // pieces
    for p in range(pieces):
        off = pl.multiple_of((shard ^ p) * q, 16) if pieces > 1 else 0
        at = (stride * p + first) * q
        for c in range(3):
            value = g_qkv[pl.ds(off, q), c * model : (c + 1) * model]
            put_half(refs, section, c // 2, at + (c % 2) * q, value)
        put_half(refs, section, 1, at + q, g_proj[pl.ds(off, q), :])


def pack_mlp(refs, section, g_fc1, g_fc2, shard, pieces, stride, first):
    model = g_fc1.shape[0]
    q = model // pieces
    for p in range(pieces):
        off = pl.multiple_of((shard ^ p) * q, 16) if pieces > 1 else 0
        at = (stride * p + first) * q
        for c in range(4):
            value = g_fc1[pl.ds(off, q), c * model : (c + 1) * model]
            put_half(refs, section, 0, at + c * q, value)
        put_half(refs, section, 1, at, g_fc2[pl.ds(pl.multiple_of(off * 4, 16), 4 * q), :])


class Modulation:
    def __init__(self, line, model):
        self.line, self.model = line, model

    def __getitem__(self, key):
        b, rows, _ = key
        return self.line[:, pl.ds(pl.multiple_of((6 * b + rows.start) * self.model, 128), self.model)]


def bias_at(line, samples, model, start, size):
    return line[:, (6 * samples + start) * model : (6 * samples + start + size) * model]


def attention_forward(b, length, h, mod, bias, w_qkv, w_proj, b_qkv, b_proj, qkv, probs, att, branch, middle):
    model = w_proj.shape[0]
    heads = bias.shape[0]
    pair = 2 * model // heads
    rows = pl.ds(pl.multiple_of(b * length, length), length)
    masks = half_masks(pair)
    x = h[rows, :].astype(F32)
    normed, _ = norm_parts(x)
    normed_low = (normed * (1.0 + mod[b, 1:2, :]) + mod[b, 0:1, :]).astype(BF16)
    qkv[rows, :] = (dot(normed_low, w_qkv[...]) + b_qkv[...]).astype(BF16)
    for j in range(heads // 2):
        q_pair = qkv[rows, j * pair : (j + 1) * pair] * BF16((pair // 2) ** (-0.5))
        k_pair = qkv[rows, model + j * pair : model + (j + 1) * pair]
        v_pair = qkv[rows, 2 * model + j * pair : 2 * model + (j + 1) * pair]
        total = None
        for e in range(2):
            scores = dot_rows(q_pair * masks[e], k_pair) + bias[2 * j + e].astype(F32)
            raised = jnp.exp(scores - jnp.max(scores, axis=-1, keepdims=True))
            p = (raised * (1.0 / jnp.sum(raised, axis=-1, keepdims=True))).astype(BF16)
            probs[b, 2 * j + e] = p
            part = dot(p, v_pair * masks[e])
            total = part if total is None else total + part
        att[rows, j * pair : (j + 1) * pair] = total.astype(BF16)
    out = dot(att[rows, :], w_proj[...]) + b_proj[...]
    branch[rows, :] = out
    middle[rows, :] = x + mod[b, 2:3, :] * out


def mlp_forward(b, length, middle, mod, w_fc1, w_fc2, b_fc1, b_fc2, act, slope, out_branch, layer_out):
    model = w_fc1.shape[0]
    rows = pl.ds(pl.multiple_of(b * length, length), length)
    mid = middle[rows, :]
    normed, _ = norm_parts(mid)
    normed_low = (normed * (1.0 + mod[b, 4:5, :]) + mod[b, 3:4, :]).astype(BF16)
    total = b_fc2[...]
    for c in range(w_fc1.shape[1] // model):
        cols = slice(c * model, (c + 1) * model)
        v = dot(normed_low, w_fc1[:, cols]) + b_fc1[:, cols]
        square = v * v
        t = jnp.tanh(0.7978845608028654 * v * (1.0 + 0.044715 * square))
        half = 0.5 * (1.0 + t)
        a = (v * half).astype(BF16)
        act[rows, cols] = a
        slope[rows, cols] = (
            half
            + 0.5 * v * (1.0 - t * t) * (0.7978845608028654 + (3 * 0.044715 * 0.7978845608028654) * square)
        ).astype(BF16)
        total = total + dot(a, w_fc2[cols, :])
    out_branch[rows, :] = total
    layer_out[rows, :] = (mid + mod[b, 5:6, :] * total).astype(layer_out.dtype)


def mlp_backward(b, length, grad, middle, mod, w_fc1, w_fc2, act, slope, out_branch, d_middle, small, normed_low, d_pre, d_ob):
    model = w_fc1.shape[0]
    rows = pl.ds(pl.multiple_of(b * length, length), length)
    g = grad[rows, :].astype(F32)
    small[b, 2:3, :] = col_sum(g * out_branch[rows, :])
    d_out = g * mod[b, 5:6, :]
    d_out_low = d_out.astype(BF16)
    d_ob[rows, :] = d_out_low
    small[b, 3:4, :] = col_sum(d_out_low.astype(F32))
    normed, inverse = norm_parts(middle[rows, :])
    normed_low[rows, :] = (normed * (1.0 + mod[b, 4:5, :]) + mod[b, 3:4, :]).astype(BF16)
    d_normed = None
    for c in range(w_fc1.shape[1] // model):
        cols = slice(c * model, (c + 1) * model)
        d_act = dot_rows(d_out_low, w_fc2[cols, :])
        d_low = (d_act * slope[rows, cols].astype(F32)).astype(BF16)
        d_pre[rows, cols] = d_low
        small[b, 4 + c : 5 + c, :] = col_sum(d_low.astype(F32))
        part = dot_rows(d_low, w_fc1[:, cols])
        d_normed = part if d_normed is None else d_normed + part
    small[b, 0:1, :] = col_sum(d_normed)
    small[b, 1:2, :] = col_sum(d_normed * normed)
    d_middle[rows, :] = norm_back(d_normed, mod[b, 4:5, :], normed, inverse) + g


def mlp_weight_grads(normed_low, d_pre, act, d_ob, g_fc1, g_fc2):
    model = g_fc1.shape[0]
    for c in range(g_fc1.shape[1] // model):
        cols = slice(c * model, (c + 1) * model)
        g_fc1[:, cols] = dot_cols(normed_low[...], d_pre[:, cols]).astype(BF16)
        g_fc2[cols, :] = dot_cols(act[:, cols], d_ob[...]).astype(BF16)


def attention_backward(b, length, h, mod, w_qkv, w_proj, qkv, probs, att, branch, d_middle, d_in, small, score_sum, normed_low, d_qkv, d_br):
    model = w_proj.shape[0]
    heads = probs.shape[1]
    pair = 2 * model // heads
    scale = F32((pair // 2) ** (-0.5))
    rows = pl.ds(pl.multiple_of(b * length, length), length)
    masks = half_masks(pair)
    d_mid = d_middle[rows, :]
    small[b, 2:3, :] = col_sum(d_mid * branch[rows, :])
    d_branch = (d_mid * mod[b, 2:3, :]).astype(BF16)
    d_br[rows, :] = d_branch
    small[b, 5:6, :] = col_sum(d_branch.astype(F32))
    d_att = dot_rows(d_branch, w_proj[...]).astype(BF16)
    for j in range(heads // 2):
        q_pair = qkv[rows, j * pair : (j + 1) * pair]
        k_pair = qkv[rows, model + j * pair : model + (j + 1) * pair]
        v_pair = qkv[rows, 2 * model + j * pair : 2 * model + (j + 1) * pair]
        d_pair = d_att[:, j * pair : (j + 1) * pair]
        d_q = d_k = d_v = None
        for e in range(2):
            p_low = probs[b, 2 * j + e]
            p = p_low.astype(F32)
            d_here = d_pair * masks[e]
            d_p = dot_rows(d_here, v_pair)
            d_s = (p * (d_p - jnp.sum(d_p * p, axis=-1, keepdims=True))).astype(BF16)
            score_sum[2 * j + e] += d_s.astype(F32)
            v_part = dot_cols(p_low, d_here)
            q_part = dot(d_s, k_pair * masks[e])
            k_part = dot_cols(d_s, q_pair * masks[e])
            d_v = v_part if d_v is None else d_v + v_part
            d_q = q_part if d_q is None else d_q + q_part
            d_k = k_part if d_k is None else d_k + k_part
        d_qkv[rows, j * pair : (j + 1) * pair] = (d_q * scale).astype(BF16)
        d_qkv[rows, model + j * pair : model + (j + 1) * pair] = (d_k * scale).astype(BF16)
        d_qkv[rows, 2 * model + j * pair : 2 * model + (j + 1) * pair] = d_v.astype(BF16)
    small[b, 3:4, :] = col_sum(d_qkv[rows, :model].astype(F32))
    small[b, 4:5, :] = col_sum(d_qkv[rows, 2 * model :].astype(F32))
    small[b, 6:8, :] = jnp.zeros((2, model), F32)
    d_normed = dot_rows(d_qkv[rows, :], w_qkv[...])
    normed, inverse = norm_parts(h[rows, :].astype(F32))
    normed_low[rows, :] = (normed * (1.0 + mod[b, 1:2, :]) + mod[b, 0:1, :]).astype(BF16)
    small[b, 0:1, :] = col_sum(d_normed)
    small[b, 1:2, :] = col_sum(d_normed * normed)
    d_in[rows, :] = (norm_back(d_normed, mod[b, 1:2, :], normed, inverse) + d_mid).astype(d_in.dtype)


def attention_weight_grads(normed_low, d_qkv, att, d_br, g_qkv, g_proj):
    model = g_proj.shape[0]
    for c in range(3):
        cols = slice(c * model, (c + 1) * model)
        g_qkv[:, cols] = dot_cols(normed_low[...], d_qkv[:, cols]).astype(BF16)
    g_proj[...] = dot_cols(att[...], d_br[...]).astype(BF16)


def each_sample(count, body):
    def step(b, carry):
        body(b)
        return carry

    lax.fori_loop(0, count, step, 0)


def set_line(line, layer, section, own_line, other_line):
    line[...] = jnp.where(section == layer, own_line[...], other_line[...])


def start_bias(layer, section, own, other, bias, sem):
    one = pltpu.make_async_copy(own, bias, sem)
    two = pltpu.make_async_copy(other, bias, sem)
    pl.when(section == layer)(one.start)
    pl.when(section != layer)(two.start)
    return one


def line_biases(line, samples, model):
    q_bias = bias_at(line, samples, model, 0, 1)
    v_bias = bias_at(line, samples, model, 1, 1)
    b_qkv = jnp.concatenate([q_bias, jnp.zeros_like(q_bias), v_bias], axis=1)
    return b_qkv, bias_at(line, samples, model, 2, 1), bias_at(line, samples, model, 3, 4), bias_at(line, samples, model, 7, 1)


def forward_kernel(layer, length, n_weights, pos, h, own_line, other_line, own_bias, other_bias, *rest):
    refs, rest = rest[:n_weights], rest[n_weights:]
    (qkv, probs, att, branch, middle, act, slope, out_branch, layer_out,
     w_qkv, w_proj, w_fc1, w_fc2, bias, line, sems) = rest
    section, shard = pos[0], pos[1]
    model = h.shape[1]
    samples = h.shape[0] // length
    got_bias = start_bias(layer, section, own_bias, other_bias, bias, sems.at[weight_count(n_weights)])
    for_attention, for_mlp = weight_loads(layer, section, shard, refs, (w_qkv, w_proj, w_fc1, w_fc2), sems)
    set_line(line, layer, section, own_line, other_line)
    mod = Modulation(line, model)
    b_qkv, b_proj, b_fc1, b_fc2 = line_biases(line, samples, model)
    got_bias.wait()
    wait_all(for_attention)
    each_sample(
        samples,
        lambda b: attention_forward(b, length, h, mod, bias, w_qkv, w_proj, b_qkv, b_proj, qkv, probs, att, branch, middle),
    )
    wait_all(for_mlp)
    each_sample(
        samples,
        lambda b: mlp_forward(b, length, middle, mod, w_fc1, w_fc2, b_fc1, b_fc2, act, slope, out_branch, layer_out),
    )


def both_kernel(layer, pieces, length, n_weights, pos, h, grad, own_line, other_line, own_bias, other_bias, *rest):
    refs, rest = rest[:n_weights], rest[n_weights:]
    (layer_out, d_in, small_a, small_m, scores, keep, send,
     w_qkv, w_proj, w_fc1, w_fc2, bias, line, qkv, probs, att, branch, middle, act, slope, out_branch,
     d_middle, normed_low, d_pre, d_ob, d_qkv, score_sum, g_qkv, g_proj, g_fc1, g_fc2, sems) = rest
    section, shard = pos[0], pos[1]
    model = h.shape[1]
    samples = h.shape[0] // length
    got_bias = start_bias(layer, section, own_bias, other_bias, bias, sems.at[weight_count(n_weights)])
    for_attention, for_mlp = weight_loads(layer, section, shard, refs, (w_qkv, w_proj, w_fc1, w_fc2), sems)
    set_line(line, layer, section, own_line, other_line)
    mod = Modulation(line, model)
    b_qkv, b_proj, b_fc1, b_fc2 = line_biases(line, samples, model)
    got_bias.wait()
    wait_all(for_attention)
    each_sample(
        samples,
        lambda b: attention_forward(b, length, h, mod, bias, w_qkv, w_proj, b_qkv, b_proj, qkv, probs, att, branch, middle),
    )
    wait_all(for_mlp)

    def mlp(b):
        mlp_forward(b, length, middle, mod, w_fc1, w_fc2, b_fc1, b_fc2, act, slope, out_branch, layer_out)
        mlp_backward(b, length, grad, middle, mod, w_fc1, w_fc2, act, slope, out_branch, d_middle, small_m, normed_low, d_pre, d_ob)

    each_sample(samples, mlp)
    mlp_weight_grads(normed_low, d_pre, act, d_ob, g_fc1, g_fc2)
    pack_mlp((keep, send), section, g_fc1, g_fc2, shard, pieces, 6, 2)
    score_sum[...] = jnp.zeros_like(score_sum)
    each_sample(
        samples,
        lambda b: attention_backward(b, length, h, mod, w_qkv, w_proj, qkv, probs, att, branch, d_middle, d_in, small_a, score_sum, normed_low, d_qkv, d_ob),
    )
    scores[...] = score_sum[...].astype(BF16)
    attention_weight_grads(normed_low, d_qkv, att, d_ob, g_qkv, g_proj)
    pack_attention((keep, send), section, g_qkv, g_proj, shard, pieces, 6, 0)


def backward_mlp_kernel(layer, pieces, length, n_weights, pos, grad, middle, own_line, other_line, act, slope, out_branch, *rest):
    refs, rest = rest[:n_weights], rest[n_weights:]
    (d_middle, small, keep, send,
     w_qkv, w_proj, w_fc1, w_fc2, line, normed_low, d_pre, d_ob, g_fc1, g_fc2, sems) = rest
    section, shard = pos[0], pos[1]
    for_attention, for_mlp = weight_loads(layer, section, shard, refs, (w_qkv, w_proj, w_fc1, w_fc2), sems)
    set_line(line, layer, section, own_line, other_line)
    mod = Modulation(line, middle.shape[1])
    wait_all(for_mlp)
    each_sample(
        middle.shape[0] // length,
        lambda b: mlp_backward(b, length, grad, middle, mod, w_fc1, w_fc2, act, slope, out_branch, d_middle, small, normed_low, d_pre, d_ob),
    )
    mlp_weight_grads(normed_low, d_pre, act, d_ob, g_fc1, g_fc2)
    pack_mlp((keep, send), section, g_fc1, g_fc2, shard, pieces, 4, 0)
    wait_all(for_attention)


def backward_attention_kernel(layer, pieces, length, n_weights, n_after, pos, h, own_line, other_line, qkv, probs, att, branch, d_middle, *rest):
    refs, rest = rest[:n_weights], rest[n_weights + n_after :]
    (d_in, small, scores, keep, send,
     w_qkv, w_proj, w_fc1, w_fc2, line, normed_low, d_qkv, d_br, score_sum, g_qkv, g_proj, sems) = rest
    section, shard = pos[0], pos[1]
    for_attention, for_mlp = weight_loads(layer, section, shard, refs, (w_qkv, w_proj, w_fc1, w_fc2), sems)
    set_line(line, layer, section, own_line, other_line)
    mod = Modulation(line, h.shape[1])
    score_sum[...] = jnp.zeros_like(score_sum)
    wait_all(for_attention)
    each_sample(
        h.shape[0] // length,
        lambda b: attention_backward(b, length, h, mod, w_qkv, w_proj, qkv, probs, att, branch, d_middle, d_in, small, score_sum, normed_low, d_qkv, d_br),
    )
    scores[...] = score_sum[...].astype(BF16)
    attention_weight_grads(normed_low, d_qkv, att, d_br, g_qkv, g_proj)
    pack_attention((keep, send), section, g_qkv, g_proj, shard, pieces, 2, 0)
    wait_all(for_mlp)


def call(kernel, pos, operands, in_hbm, outs, scratch, sems=0):
    specs = [pl.BlockSpec(memory_space=pltpu.SMEM)]
    specs += [pl.BlockSpec(memory_space=pltpu.VMEM) for _ in operands]
    specs += [pl.BlockSpec(memory_space=pl.ANY) for _ in in_hbm]
    shapes = [pltpu.VMEM(shape, dtype) for shape, dtype in scratch]
    if sems:
        shapes.append(pltpu.SemaphoreType.DMA((sems,)))
    return pl.pallas_call(
        kernel,
        out_shape=[jax.ShapeDtypeStruct(shape, dtype) for shape, dtype in outs],
        in_specs=specs,
        out_specs=[pl.BlockSpec(memory_space=pltpu.VMEM) for _ in outs],
        scratch_shapes=shapes,
        compiler_params=pltpu.CompilerParams(vmem_limit_bytes=VMEM_BYTES),
    )(pos, *operands, *in_hbm)


class Sizes:
    def __init__(self, samples, length, model, heads, hidden, pieces):
        self.samples, self.length, self.model = samples, length, model
        self.heads, self.hidden, self.pieces = heads, hidden, pieces
        self.rows = samples * length
        self.line = ((1, (6 * samples + 4 + hidden // model) * model), F32)
        self.weights = [
            ((model, 3 * model), BF16), ((model, model), BF16), ((model, hidden), BF16), ((hidden, model), BF16),
        ]
        self.bias = ((heads, length, length), BF16)
        self.probs = ((samples, heads, length, length), BF16)
        self.low = ((self.rows, model), BF16)
        self.full = ((self.rows, model), F32)
        self.qkv = ((self.rows, 3 * model), BF16)
        self.wide = ((self.rows, hidden), BF16)
        self.small = ((samples, 8, model), F32)

    def pack(self, blocks):
        return [((blocks * self.model, self.model), BF16)] * 2


def forward_layer(layer, z, pos, h, lines, biases, weights):
    def kernel(pos_ref, h_ref, a, b, *rest):
        forward_kernel(layer, z.length, len(weights), pos_ref, h_ref, a, b, *rest)

    return call(
        kernel, pos, (h, *lines), (*biases, *weights),
        [z.qkv, z.probs, z.low, z.full, z.full, z.wide, z.wide, z.full, z.low],
        [*z.weights, z.bias, z.line], weight_count(len(weights)) + 1,
    )


def both_ways(layer, z, pos, h, grad, lines, biases, weights):
    return call(
        functools.partial(both_kernel, layer, z.pieces, z.length, len(weights)),
        pos, (h, grad, *lines), (*biases, *weights),
        [z.low, z.low, z.small, z.small, z.bias, *z.pack(6)],
        [*z.weights, z.bias, z.line, z.qkv, z.probs, z.low, z.full, z.full, z.wide, z.wide, z.full,
         z.full, z.low, z.wide, z.low, z.qkv, (z.bias[0], F32), *z.weights],
        weight_count(len(weights)) + 1,
    )


def backward_mlp(layer, z, pos, grad, middle, lines, act, slope, out_branch, weights):
    return call(
        functools.partial(backward_mlp_kernel, layer, z.pieces, z.length, len(weights)),
        pos, (grad, middle, *lines, act, slope, out_branch), weights,
        [z.full, z.small, *z.pack(4)],
        [*z.weights, z.line, z.low, z.wide, z.low, *z.weights[2:]],
        weight_count(len(weights)),
    )


def backward_attention(layer, z, pos, h, lines, qkv, probs, att, branch, d_middle, weights, earlier):
    return call(
        functools.partial(backward_attention_kernel, layer, z.pieces, z.length, len(weights), len(earlier)),
        pos, (h, *lines, qkv, probs, att, branch, d_middle), (*weights, *earlier),
        [z.full, z.small, z.bias, *z.pack(2)],
        [*z.weights, z.line, z.low, z.qkv, z.low, (z.bias[0], F32), *z.weights[:2]],
        weight_count(len(weights)),
    )


def pack_kernel(pos, qkv, proj, fc1, fc2, out):
    q, model = proj.shape
    for c in range(3):
        out[c * q : (c + 1) * q, :] = qkv[:, c * model : (c + 1) * model]
    out[3 * q : 4 * q, :] = proj[...]
    for c in range(4):
        out[(4 + c) * q : (5 + c) * q, :] = fc1[:, c * model : (c + 1) * model]
    out[8 * q : 12 * q, :] = fc2[...]


def pack_shard(pos, own):
    q, model = own[1].shape
    return call(pack_kernel, pos, own, (), [((12 * q, model), BF16)], [])[0]


def after(values, others):
    return pl.pallas_call(
        lambda *refs: None,
        out_shape=[jax.ShapeDtypeStruct(v.shape, v.dtype) for v in values],
        in_specs=[pl.BlockSpec(memory_space=pl.ANY)] * (len(values) + len(others)),
        out_specs=[pl.BlockSpec(memory_space=pl.ANY)] * len(values),
        input_output_aliases={i: i for i in range(len(values))},
    )(*values, *others)


def lookup_kernel(table, index, *rest):
    out, work = rest[-2:]
    heads, length = out.shape[0], out.shape[1]
    high_count = table.shape[0] // 8
    values = table[...]
    low_id = lax.broadcasted_iota(jnp.int32, (LOW, length), 0)

    def step(i, carry):
        block = index[pl.ds(pl.multiple_of(i * 8, 8), 8), :]
        for r in range(8):
            entry = block[r : r + 1, :]
            picks = jnp.where(low_id == (entry & (LOW - 1)), 1.0, 0.0).astype(BF16)
            found = dot(values, picks).reshape(high_count, 8, length)
            high = jnp.broadcast_to(entry >> LOW_BITS, (8, length))
            bit = high_count // 2
            while bit:
                chosen = (high & bit) != 0
                found = jnp.where(chosen[None], found[bit : 2 * bit], found[:bit])
                bit //= 2
            for head in range(heads):
                work[head, pl.ds(i * 8 + r, 1), :] = found[0, head : head + 1, :]
        return carry

    lax.fori_loop(0, length // 8, step, 0)
    out[...] = work[...].astype(BF16)


def lookup(table, index, earlier):
    heads, entries = table.shape
    high_count = HIGH
    padded = jnp.pad(table, ((0, 8 - heads), (0, high_count * LOW - entries)))
    rows = jnp.transpose(padded.reshape(8, high_count, LOW), (1, 0, 2)).reshape(high_count * 8, LOW)
    length = index.shape[0]
    return pl.pallas_call(
        lookup_kernel,
        out_shape=jax.ShapeDtypeStruct((heads, length, length), BF16),
        in_specs=[pl.BlockSpec(memory_space=pltpu.VMEM)] * 2 + [pl.BlockSpec(memory_space=pl.ANY)] * len(earlier),
        out_specs=pl.BlockSpec(memory_space=pltpu.VMEM),
        scratch_shapes=[pltpu.VMEM((heads, length, length), F32)],
        compiler_params=pltpu.CompilerParams(vmem_limit_bytes=VMEM_BYTES),
    )(rows, index, *earlier)


def table_kernel(scores, index, *rest):
    out = rest[-1]
    heads, length = scores.shape[0], scores.shape[1]
    out[...] = jnp.zeros_like(out)
    low_ids = lax.broadcasted_iota(jnp.int32, (LOW, length), 0)
    high_ids = lax.broadcasted_iota(jnp.int32, (HIGH, length), 0)

    def step(i, carry):
        rows = pl.ds(pl.multiple_of(i * 16, 16), 16)
        entries = index[rows, :]
        block = [scores[head, rows, :].astype(F32) for head in range(heads)]
        total = None
        for r in range(16):
            entry = entries[r : r + 1, :]
            low = jnp.where(low_ids == (entry & (LOW - 1)), 1.0, 0.0).astype(BF16)
            high = high_ids == (entry >> LOW_BITS)
            left = jnp.concatenate([jnp.where(high, part[r : r + 1, :], 0.0) for part in block], axis=0).astype(BF16)
            part = dot_rows(left, low)
            total = part if total is None else total + part
        out[...] += total
        return carry

    lax.fori_loop(0, length // 16, step, 0)


def table_gradient(scores, index, earlier):
    heads = scores.shape[0]
    return pl.pallas_call(
        table_kernel,
        out_shape=jax.ShapeDtypeStruct((heads * HIGH, LOW), F32),
        in_specs=[pl.BlockSpec(memory_space=pltpu.VMEM)] * 2 + [pl.BlockSpec(memory_space=pl.ANY)] * len(earlier),
        out_specs=pl.BlockSpec(memory_space=pltpu.VMEM),
        compiler_params=pltpu.CompilerParams(vmem_limit_bytes=VMEM_BYTES),
    )(scores, index, *earlier)


def swap_section(value):
    return lax.ppermute(value, "section", [(0, 1), (1, 0)])


def pairs_of(count, step):
    return [(i, i ^ step) for i in range(count)]


def by_rank(pieces, rank):
    stack = jnp.stack(pieces)
    count = len(pieces)
    bit = 1
    while bit < count:
        moved = jnp.stack([stack[i ^ bit] for i in range(count)])
        stack = jnp.where((rank & bit) != 0, moved, stack)
        bit *= 2
    return stack


def section_sums(keep, send, shards):
    other = swap_section(send)
    size = keep.shape[0] // shards
    return [
        keep[p * size : (p + 1) * size].astype(F32) + other[p * size : (p + 1) * size].astype(F32)
        for p in range(shards)
    ]


def low_pieces(sums):
    return [x.astype(BF16) for x in sums[1:]]


def to_peers(messages, axis):
    count = lax.axis_size(axis)
    return [lax.ppermute(messages[p - 1], axis, pairs_of(count, p)) for p in range(1, count)]


def add_pieces(own, got):
    total = own
    for piece in got:
        total = total + piece.astype(F32)
    return total


def replica_parts(total, rank):
    replicas = lax.axis_size("rep")
    parts = total.reshape(replicas, total.shape[0] // replicas, -1)
    low = parts.astype(BF16)
    mine = lax.dynamic_index_in_dim(parts, rank, 0, keepdims=False)
    return mine, [lax.dynamic_index_in_dim(low, rank ^ j, 0, keepdims=False) for j in range(1, replicas)]


def replica_whole(mine, rank):
    quarters = [mine] + from_peers(mine, "rep")
    return by_rank(quarters, rank).reshape(-1, mine.shape[1])


def unpack(pack):
    q = pack.shape[0] // 12
    unit = [pack[c * q : (c + 1) * q] for c in range(8)]
    return (
        jnp.concatenate([unit[0], unit[1], unit[6]], axis=1), unit[7],
        jnp.concatenate(unit[2:6], axis=1), pack[8 * q :],
    )


def pad_rows(value):
    return jnp.pad(value, ((0, -value.shape[0] % 16), (0, 0)))


def from_peers(value, axis):
    return [lax.ppermute(value, axis, pairs_of(lax.axis_size(axis), p)) for p in range(1, lax.axis_size(axis))]


def pair_sum(values):
    while len(values) > 1:
        values = [values[i] + values[i + 1] for i in range(0, len(values), 2)]
    return values[0]


def per_device(inputs, conditioning, cotangent, micro_sizes, relative_bias_index,
               w_ada, w_qkv, w_proj, w_fc1, w_fc2, b_ada, b_qv, b_proj, b_fc1, b_fc2, bias_table):
    section = lax.axis_index("section")
    shard = lax.axis_index("fsdp")
    rank = lax.axis_index("rep")
    shards, replicas = lax.axis_size("fsdp"), lax.axis_size("rep")
    direct = shards == 4 and replicas == 4
    is_first = section == 0
    samples, length, model = inputs.shape
    heads, entries = bias_table.shape[1:]
    half = samples // 2
    z = Sizes(half, length, model, heads, 4 * model, shards if direct else 1)
    pos = jnp.stack([section, shard]).astype(jnp.int32)

    def mine(first, second):
        return jnp.where(is_first, first, second)

    def own_samples(array):
        return lax.dynamic_slice_in_dim(array, section * half, half, 0)

    def in_order(own, other):
        return jnp.where(is_first, jnp.concatenate([own, other]), jnp.concatenate([other, own]))

    own_raw = [w_qkv[0], w_proj[0], w_fc1[0], w_fc2[0]]
    cond_size = conditioning.size
    width = model // shards
    if direct:
        row = jnp.concatenate([conditioning.reshape(1, -1), b_ada, b_qv, b_proj, b_fc1, b_fc2], axis=1)
        rows = [row] + from_peers(row, "fsdp")
        own_pack = pack_shard(pos, own_raw)
        middle_row = own_pack.shape[0] // 2
        got_x = lax.ppermute(own_pack, "fsdp", pairs_of(shards, 1))
        got_y = lax.ppermute(own_pack, "fsdp", pairs_of(shards, 2))
        got_first = lax.ppermute(got_x[:middle_row], "fsdp", pairs_of(shards, 2))
        got_second = lax.ppermute(got_y[middle_row:], "fsdp", pairs_of(shards, 1))
        own_weights = [own_pack, got_x, got_y, got_first, got_second]
        weights = own_weights + [swap_section(w) for w in own_weights]
        cond_pieces = jnp.stack([r[0, :cond_size].reshape(samples, model) for r in rows])
        acts = jax.nn.silu(cond_pieces.astype(F32)).astype(BF16)
        acts = lax.dynamic_slice_in_dim(acts, shard * width, width, 2)
        partial = lax.dot_general(acts, w_ada[0], (((2,), (0,)), ((), ())), preferred_element_type=F32)
        modulation = partial[0]
        for p in range(1, shards):
            modulation = modulation + lax.ppermute(partial[p], "fsdp", pairs_of(shards, p))
        bias_rows = by_rank([r[0, cond_size:] for r in rows], shard)
        bias_own = lookup(bias_table[0], relative_bias_index, [own_pack, partial])
    else:
        row = jnp.concatenate([b_ada, b_qv, b_proj, b_fc1, b_fc2], axis=1)
        bias_rows = lax.all_gather(row[0], "fsdp", axis=0)
        whole = [lax.all_gather(w, "fsdp", axis=0, tiled=True) for w in own_raw]
        own_whole = pack_shard(pos, whole)
        weights = [own_whole, swap_section(own_whole)]
        acts = jax.nn.silu(conditioning.astype(F32)).astype(BF16)
        modulation = dot(acts, lax.all_gather(w_ada[0], "fsdp", axis=0, tiled=True))
        bias_own = lookup(bias_table[0], relative_bias_index, [])
    cuts = [b_ada.shape[1], b_qv.shape[1], b_proj.shape[1], b_fc1.shape[1], b_fc2.shape[1]]
    biases, at = [], 0
    for cut in cuts:
        biases.append(bias_rows[:, at : at + cut].reshape(1, -1).astype(F32))
        at += cut
    modulation = modulation + biases[0]
    other_samples = lax.dynamic_slice_in_dim(modulation, (1 - section) * half, half, 0)
    own_line = jnp.concatenate([own_samples(modulation).reshape(1, -1)] + biases[1:], axis=1)
    other_line = swap_section(jnp.concatenate([other_samples.reshape(1, -1)] + biases[1:], axis=1))
    lines = (own_line, other_line)
    bias_heads = (bias_own, swap_section(bias_own))

    live = (jnp.arange(half)[:, None, None] < lax.dynamic_index_in_dim(micro_sizes[0], section, 0)).astype(BF16)
    h0 = own_samples(inputs).reshape(half * length, model)
    grad1 = (own_samples(cotangent) * live).reshape(half * length, model)

    qkv, probs, att, branch, middle, act, slope, out_branch, h1 = forward_layer(0, z, pos, h0, lines, bias_heads, weights)
    w_ada_later = after([w_ada[0]], [h1])[0]
    w_ada_all = lax.all_gather(w_ada_later, "fsdp", axis=0, tiled=True)
    out1, d_h1, small_a1, small_m1, scores1, keep1, send1 = both_ways(1, z, pos, h1, grad1, lines, bias_heads, weights)
    d_middle, small_m0, keep_m0, send_m0 = backward_mlp(0, z, pos, d_h1, middle, lines, act, slope, out_branch, weights)
    pieces = z.pieces
    sums1 = section_sums(keep1, send1, pieces)
    sums_m0 = section_sums(keep_m0, send_m0, pieces)
    low1, low_m0 = low_pieces(sums1), low_pieces(sums_m0)
    table1 = table_gradient(scores1, relative_bias_index, low1)
    d_h0, small_a0, scores0, keep_a0, send_a0 = backward_attention(
        0, z, pos, h0, lines, qkv, probs, att, branch, d_middle, weights, [table1, w_ada_all, *low_m0]
    )
    sums_a0 = section_sums(keep_a0, send_a0, pieces)
    if direct:
        got1 = to_peers(low1, "fsdp")
        got_m0 = to_peers(low_m0, "fsdp")
        part1, others1 = replica_parts(add_pieces(sums1[0], got1), rank)
        table0 = table_gradient(scores0, relative_bias_index, others1)
        half1 = replica_whole(add_pieces(part1, to_peers(others1, "rep")).astype(BF16), rank)
    else:
        table0 = table_gradient(scores0, relative_bias_index, [])

    other_out = swap_section(mine(out1, h1))
    activations = in_order(mine(h1, out1).reshape(half, length, model), other_out.reshape(half, length, model))
    other_in = swap_section(mine(d_h1, d_h0.astype(BF16)))
    input_grads = in_order(
        mine(d_h0, d_h1.astype(F32)).reshape(half, length, model),
        other_in.astype(F32).reshape(half, length, model),
    )

    tables = (table0, table1)
    smalls = [
        jnp.concatenate([small_a0[:, :3], small_m0, small_a0[:, 3:]], axis=1),
        jnp.concatenate([small_a1[:, :3], small_m1, small_a1[:, 3:]], axis=1),
    ]
    small = in_order(mine(smalls[0], smalls[1]), swap_section(mine(smalls[1], smalls[0])))
    table = mine(tables[0], tables[1]) + swap_section(mine(tables[1], tables[0]))
    low = small[:, :6].astype(BF16)
    w_rows = w_ada_all.reshape(model, 6, model)
    d_act = sum(dot_rows(low[:, i], w_rows[:, i]) for i in range(6))
    cond = conditioning.astype(F32)
    gate = jax.nn.sigmoid(cond)
    cond_part = d_act * (gate * (1.0 + cond * (1.0 - gate)))
    cond_grad = cond_part + swap_section(cond_part)

    kept = jnp.concatenate([low, conditioning[:, None]], axis=1).reshape(-1, model)
    summed = jnp.concatenate([jnp.sum(small[:, 6:14], axis=0), table.reshape(-1, model)])
    if direct:
        both = pad_rows(jnp.concatenate([kept, summed.astype(BF16)]))
        low_a0 = low_pieces(sums_a0)
        size, count, end = sums_a0[0].shape[0], kept.shape[0], kept.shape[0] + summed.shape[0]
        got = to_peers([jnp.concatenate([x, both]) for x in low_a0], "fsdp")
        total0 = jnp.concatenate([
            add_pieces(sums_a0[0], [x[:size] for x in got]), add_pieces(sums_m0[0], got_m0)
        ])
        plane = [both] + [x[size:] for x in got]
        summed = pair_sum([p[count:end].astype(F32) for p in plane])
        both = pad_rows(jnp.concatenate([p[:count] for p in plane] + [summed.astype(BF16)]))
        part0, others0 = replica_parts(total0, rank)
        got = to_peers([jnp.concatenate([x, both]) for x in others0], "rep")
        size = part0.shape[0]
        half0 = replica_whole(add_pieces(part0, [x[:size] for x in got]).astype(BF16), rank)
        every = [both] + [x[size:] for x in got]
        count, end = count * shards, count * shards + summed.shape[0]
        summed = pair_sum([p[count:end].astype(F32) for p in every])
        kept = by_rank([p[:count] for p in every], rank).reshape(-1, 7, model)
        grads = [g.astype(F32) for g in unpack(in_order(mine(half0, half1), swap_section(mine(half1, half0))))]
    else:
        kept = lax.all_gather(kept, ("fsdp", "rep"), axis=0, tiled=True).reshape(-1, 7, model)
        summed = lax.psum(summed, ("fsdp", "rep"))
        half0 = jnp.concatenate([sums_a0[0], sums_m0[0]]).astype(BF16)
        half1 = sums1[0].astype(BF16)
        whole = unpack(in_order(mine(half0, half1), swap_section(mine(half1, half0))))
        whole = [lax.psum_scatter(g, "fsdp", scatter_dimension=0, tiled=True) for g in whole]
        grads = [g.astype(F32) for g in lax.psum(tuple(whole), "rep")]
    g_qkv, g_proj, g_fc1, g_fc2 = grads
    act_all = jax.nn.silu(kept[:, 6].astype(F32)).astype(BF16)
    act_cols = lax.dynamic_slice_in_dim(act_all, shard * width, width, 1)
    g_ada = jnp.concatenate([dot_cols(act_cols, kept[:, i]) for i in range(6)], axis=1)
    g_b_ada = jnp.sum(kept[:, :6].astype(F32), axis=0).reshape(-1)
    g_b_fc2, g_b_fc1 = summed[0], summed[1:5].reshape(-1)
    g_b_qv, g_b_proj = summed[5:7].reshape(-1), summed[7]
    g_table = summed[8:].reshape(heads, HIGH * LOW)[:, :entries]

    def own_part(vector):
        size = vector.shape[0] // shards
        return lax.dynamic_slice_in_dim(vector, shard * size, size, 0)[None]

    return (
        activations[None], input_grads[None], cond_grad,
        g_ada[None], g_qkv[None], g_proj[None], g_fc1[None], g_fc2[None],
        own_part(g_b_ada), own_part(g_b_qv), own_part(g_b_proj), own_part(g_b_fc1), own_part(g_b_fc2),
        g_table[None],
    )


def solution(mesh):
    batch = ("fsdp", "rep")
    matrix = P("section", "fsdp", None)
    vector = P("section", "fsdp")
    return jax.shard_map(
        per_device,
        mesh=mesh,
        in_specs=(
            P(batch, None, None), P(batch, None), P(batch, None, None), P(batch, None), P(),
            matrix, matrix, matrix, matrix, matrix, vector, vector, vector, vector, vector,
            P("section", None, None),
        ),
        out_specs=(
            P("section", batch, None, None), P("section", batch, None, None), P(batch, None),
            matrix, matrix, matrix, matrix, matrix, vector, vector, vector, vector, vector,
            P("section", None, None),
        ),
        check_vma=False,
    )
```

```python
import functools

import jax
import jax.numpy as jnp
from jax import lax
from jax.experimental import pallas as pl
from jax.experimental.pallas import tpu as pltpu
from jax.sharding import PartitionSpec as P

EPSILON = 1e-06
F32 = jnp.float32
BF16 = jnp.bfloat16
VMEM_BYTES = 58 * 1024 * 1024
LOW_BITS = 6
LOW = 1 << LOW_BITS
HIGH = 16


def dot(a, b):
    return jnp.dot(a, b, preferred_element_type=F32)


def dot_rows(a, b):
    return lax.dot_general(a, b, (((1,), (1,)), ((), ())), preferred_element_type=F32)


def dot_cols(a, b):
    return lax.dot_general(a, b, (((0,), (0,)), ((), ())), preferred_element_type=F32)


def norm_parts(v):
    centre = v - jnp.mean(v, axis=-1, keepdims=True)
    inverse = lax.rsqrt(jnp.mean(centre * centre, axis=-1, keepdims=True) + EPSILON)
    return centre * inverse, inverse


def norm_back(d_normed, scale, normed, inverse):
    d = d_normed * (1.0 + scale)
    return inverse * (
        d
        - jnp.mean(d, axis=-1, keepdims=True)
        - normed * jnp.mean(d * normed, axis=-1, keepdims=True)
    )


def col_sum(v):
    return jnp.sum(v, axis=0, keepdims=True)


def half_masks(width):
    lane = lax.broadcasted_iota(jnp.int32, (1, width), 1)
    first = jnp.where(lane < width // 2, 1.0, 0.0)
    return first.astype(BF16), (1.0 - first).astype(BF16)


def block_targets(mats, off, q):
    w_qkv, w_proj, w_fc1, w_fc2 = mats
    model = w_proj.shape[0]
    targets = [w_qkv.at[pl.ds(off, q), pl.ds(c * model, model)] for c in range(3)]
    targets.append(w_proj.at[pl.ds(off, q), :])
    targets += [w_fc1.at[pl.ds(off, q), pl.ds(c * model, model)] for c in range(4)]
    targets.append(w_fc2.at[pl.ds(off * 4, 4 * q), :])
    return targets


def weight_count(refs):
    return 9 if refs == 2 else 36


def weight_loads(layer, section, shard, refs, mats, sems):
    model = mats[1].shape[0]
    plans = []
    if len(refs) == 2:
        for i, target in enumerate(block_targets(mats, 0, model)):
            rows = pl.ds(i * model, 4 * model if i == 8 else model)
            plans.append((refs[0].at[rows, :], refs[1].at[rows, :], target, i < 4))
    else:
        count = len(refs) // 2
        q = refs[0].shape[0] // 12
        for p in range(4):
            targets = block_targets(mats, pl.multiple_of((shard ^ p) * q, 16), q)
            for i, target in enumerate(targets):
                which, at = p, i
                if p == 3 and i >= 6:
                    which, at = 4, i - 6
                rows = pl.ds(at * q, 4 * q if i == 8 else q)
                plans.append((refs[which].at[rows, :], refs[count + which].at[rows, :], target, i < 4))
    ones = [pltpu.make_async_copy(x[0], x[2], sems.at[i]) for i, x in enumerate(plans)]
    twos = [pltpu.make_async_copy(x[1], x[2], sems.at[i]) for i, x in enumerate(plans)]

    @pl.when(section == layer)
    def _():
        for copy in ones:
            copy.start()

    @pl.when(section != layer)
    def _():
        for copy in twos:
            copy.start()

    return (
        [copy for copy, x in zip(ones, plans) if x[3]],
        [copy for copy, x in zip(ones, plans) if not x[3]],
    )


def wait_all(copies):
    for copy in copies:
        copy.wait()


def put_half(refs, section, half, at, value):
    keep, send = refs
    rows = slice(at, at + value.shape[0])

    @pl.when(section == half)
    def _():
        keep[rows, :] = value

    @pl.when(section != half)
    def _():
        send[rows, :] = value


def pack_attention(refs, section, g_qkv, g_proj, shard, pieces, stride, first):
    model = g_proj.shape[0]
    q = model // pieces
    for p in range(pieces):
        off = pl.multiple_of((shard ^ p) * q, 16) if pieces > 1 else 0
        at = (stride * p + first) * q
        for c in range(3):
            value = g_qkv[pl.ds(off, q), c * model : (c + 1) * model]
            put_half(refs, section, c // 2, at + (c % 2) * q, value)
        put_half(refs, section, 1, at + q, g_proj[pl.ds(off, q), :])


def pack_mlp(refs, section, g_fc1, g_fc2, shard, pieces, stride, first):
    model = g_fc1.shape[0]
    q = model // pieces
    for p in range(pieces):
        off = pl.multiple_of((shard ^ p) * q, 16) if pieces > 1 else 0
        at = (stride * p + first) * q
        for c in range(4):
            value = g_fc1[pl.ds(off, q), c * model : (c + 1) * model]
            put_half(refs, section, 0, at + c * q, value)
        put_half(refs, section, 1, at, g_fc2[pl.ds(pl.multiple_of(off * 4, 16), 4 * q), :])


class Modulation:
    def __init__(self, line, model):
        self.line, self.model = line, model

    def __getitem__(self, key):
        b, rows, _ = key
        return self.line[:, pl.ds(pl.multiple_of((6 * b + rows.start) * self.model, 128), self.model)]


def bias_at(line, samples, model, start, size):
    return line[:, (6 * samples + start) * model : (6 * samples + start + size) * model]


def attention_forward(b, length, h, mod, bias, w_qkv, w_proj, b_qkv, b_proj, qkv, probs, att, branch, middle):
    model = w_proj.shape[0]
    heads = bias.shape[0]
    pair = 2 * model // heads
    rows = pl.ds(pl.multiple_of(b * length, length), length)
    masks = half_masks(pair)
    x = h[rows, :].astype(F32)
    normed, _ = norm_parts(x)
    normed_low = (normed * (1.0 + mod[b, 1:2, :]) + mod[b, 0:1, :]).astype(BF16)
    qkv[rows, :] = (dot(normed_low, w_qkv[...]) + b_qkv[...]).astype(BF16)
    for j in range(heads // 2):
        q_pair = qkv[rows, j * pair : (j + 1) * pair] * BF16((pair // 2) ** (-0.5))
        k_pair = qkv[rows, model + j * pair : model + (j + 1) * pair]
        v_pair = qkv[rows, 2 * model + j * pair : 2 * model + (j + 1) * pair]
        total = None
        for e in range(2):
            scores = dot_rows(q_pair * masks[e], k_pair) + bias[2 * j + e].astype(F32)
            raised = jnp.exp(scores - jnp.max(scores, axis=-1, keepdims=True))
            p = (raised * (1.0 / jnp.sum(raised, axis=-1, keepdims=True))).astype(BF16)
            probs[b, 2 * j + e] = p
            part = dot(p, v_pair * masks[e])
            total = part if total is None else total + part
        att[rows, j * pair : (j + 1) * pair] = total.astype(BF16)
    out = dot(att[rows, :], w_proj[...]) + b_proj[...]
    branch[rows, :] = out
    middle[rows, :] = x + mod[b, 2:3, :] * out


def mlp_forward(b, length, middle, mod, w_fc1, w_fc2, b_fc1, b_fc2, act, slope, out_branch, layer_out):
    model = w_fc1.shape[0]
    rows = pl.ds(pl.multiple_of(b * length, length), length)
    mid = middle[rows, :]
    normed, _ = norm_parts(mid)
    normed_low = (normed * (1.0 + mod[b, 4:5, :]) + mod[b, 3:4, :]).astype(BF16)
    total = b_fc2[...]
    for c in range(w_fc1.shape[1] // model):
        cols = slice(c * model, (c + 1) * model)
        v = dot(normed_low, w_fc1[:, cols]) + b_fc1[:, cols]
        square = v * v
        t = jnp.tanh(0.7978845608028654 * v * (1.0 + 0.044715 * square))
        half = 0.5 * (1.0 + t)
        a = (v * half).astype(BF16)
        act[rows, cols] = a
        slope[rows, cols] = (
            half
            + 0.5 * v * (1.0 - t * t) * (0.7978845608028654 + (3 * 0.044715 * 0.7978845608028654) * square)
        ).astype(BF16)
        total = total + dot(a, w_fc2[cols, :])
    out_branch[rows, :] = total
    layer_out[rows, :] = (mid + mod[b, 5:6, :] * total).astype(layer_out.dtype)


def mlp_backward(b, length, grad, middle, mod, w_fc1, w_fc2, act, slope, out_branch, d_middle, small, normed_low, d_pre, d_ob):
    model = w_fc1.shape[0]
    rows = pl.ds(pl.multiple_of(b * length, length), length)
    g = grad[rows, :].astype(F32)
    small[b, 2:3, :] = col_sum(g * out_branch[rows, :])
    d_out = g * mod[b, 5:6, :]
    d_out_low = d_out.astype(BF16)
    d_ob[rows, :] = d_out_low
    small[b, 3:4, :] = col_sum(d_out_low.astype(F32))
    normed, inverse = norm_parts(middle[rows, :])
    normed_low[rows, :] = (normed * (1.0 + mod[b, 4:5, :]) + mod[b, 3:4, :]).astype(BF16)
    d_normed = None
    for c in range(w_fc1.shape[1] // model):
        cols = slice(c * model, (c + 1) * model)
        d_act = dot_rows(d_out_low, w_fc2[cols, :])
        d_low = (d_act * slope[rows, cols].astype(F32)).astype(BF16)
        d_pre[rows, cols] = d_low
        small[b, 4 + c : 5 + c, :] = col_sum(d_low.astype(F32))
        part = dot_rows(d_low, w_fc1[:, cols])
        d_normed = part if d_normed is None else d_normed + part
    small[b, 0:1, :] = col_sum(d_normed)
    small[b, 1:2, :] = col_sum(d_normed * normed)
    d_middle[rows, :] = norm_back(d_normed, mod[b, 4:5, :], normed, inverse) + g


def mlp_weight_grads(normed_low, d_pre, act, d_ob, g_fc1, g_fc2):
    model = g_fc1.shape[0]
    for c in range(g_fc1.shape[1] // model):
        cols = slice(c * model, (c + 1) * model)
        g_fc1[:, cols] = dot_cols(normed_low[...], d_pre[:, cols]).astype(BF16)
        g_fc2[cols, :] = dot_cols(act[:, cols], d_ob[...]).astype(BF16)


def attention_backward(b, length, h, mod, w_qkv, w_proj, qkv, probs, att, branch, d_middle, d_in, small, score_sum, normed_low, d_qkv, d_br):
    model = w_proj.shape[0]
    heads = probs.shape[1]
    pair = 2 * model // heads
    scale = F32((pair // 2) ** (-0.5))
    rows = pl.ds(pl.multiple_of(b * length, length), length)
    masks = half_masks(pair)
    d_mid = d_middle[rows, :]
    small[b, 2:3, :] = col_sum(d_mid * branch[rows, :])
    d_branch = (d_mid * mod[b, 2:3, :]).astype(BF16)
    d_br[rows, :] = d_branch
    small[b, 5:6, :] = col_sum(d_branch.astype(F32))
    d_att = dot_rows(d_branch, w_proj[...]).astype(BF16)
    for j in range(heads // 2):
        q_pair = qkv[rows, j * pair : (j + 1) * pair]
        k_pair = qkv[rows, model + j * pair : model + (j + 1) * pair]
        v_pair = qkv[rows, 2 * model + j * pair : 2 * model + (j + 1) * pair]
        d_pair = d_att[:, j * pair : (j + 1) * pair]
        d_q = d_k = d_v = None
        for e in range(2):
            p_low = probs[b, 2 * j + e]
            p = p_low.astype(F32)
            d_here = d_pair * masks[e]
            d_p = dot_rows(d_here, v_pair)
            d_s = (p * (d_p - jnp.sum(d_p * p, axis=-1, keepdims=True))).astype(BF16)
            score_sum[2 * j + e] += d_s.astype(F32)
            v_part = dot_cols(p_low, d_here)
            q_part = dot(d_s, k_pair * masks[e])
            k_part = dot_cols(d_s, q_pair * masks[e])
            d_v = v_part if d_v is None else d_v + v_part
            d_q = q_part if d_q is None else d_q + q_part
            d_k = k_part if d_k is None else d_k + k_part
        d_qkv[rows, j * pair : (j + 1) * pair] = (d_q * scale).astype(BF16)
        d_qkv[rows, model + j * pair : model + (j + 1) * pair] = (d_k * scale).astype(BF16)
        d_qkv[rows, 2 * model + j * pair : 2 * model + (j + 1) * pair] = d_v.astype(BF16)
    small[b, 3:4, :] = col_sum(d_qkv[rows, :model].astype(F32))
    small[b, 4:5, :] = col_sum(d_qkv[rows, 2 * model :].astype(F32))
    small[b, 6:8, :] = jnp.zeros((2, model), F32)
    d_normed = dot_rows(d_qkv[rows, :], w_qkv[...])
    normed, inverse = norm_parts(h[rows, :].astype(F32))
    normed_low[rows, :] = (normed * (1.0 + mod[b, 1:2, :]) + mod[b, 0:1, :]).astype(BF16)
    small[b, 0:1, :] = col_sum(d_normed)
    small[b, 1:2, :] = col_sum(d_normed * normed)
    d_in[rows, :] = (norm_back(d_normed, mod[b, 1:2, :], normed, inverse) + d_mid).astype(d_in.dtype)


def attention_weight_grads(normed_low, d_qkv, att, d_br, g_qkv, g_proj):
    model = g_proj.shape[0]
    for c in range(3):
        cols = slice(c * model, (c + 1) * model)
        g_qkv[:, cols] = dot_cols(normed_low[...], d_qkv[:, cols]).astype(BF16)
    g_proj[...] = dot_cols(att[...], d_br[...]).astype(BF16)


def each_sample(count, body):
    def step(b, carry):
        body(b)
        return carry

    lax.fori_loop(0, count, step, 0)


def add_table(scores, index, out):
    heads, length = scores.shape[0], scores.shape[1]
    low_ids = lax.broadcasted_iota(jnp.int32, (LOW, length), 0)
    high_ids = lax.broadcasted_iota(jnp.int32, (HIGH, length), 0)

    def step(i, carry):
        rows = pl.ds(pl.multiple_of(i * 16, 16), 16)
        entries = index[rows, :]
        block = [scores[head, rows, :].astype(F32) for head in range(heads)]
        total = carry
        for r in range(16):
            entry = entries[r : r + 1, :]
            low = jnp.where(low_ids == (entry & (LOW - 1)), 1.0, 0.0).astype(BF16)
            high = high_ids == (entry >> LOW_BITS)
            left = jnp.concatenate([jnp.where(high, part[r : r + 1, :], 0.0) for part in block], axis=0).astype(BF16)
            total = total + dot_rows(left, low)
        return total

    total = lax.fori_loop(0, length // 16, step, jnp.zeros((heads * HIGH, LOW), F32))
    out[...] = jnp.concatenate([total[head * HIGH : (head + 1) * HIGH] for head in range(heads)], axis=1)


def table_kernel(scores, index, *rest):
    add_table(scores, index, rest[-1])


def table_gradient(scores, index, earlier):
    heads = scores.shape[0]
    return pl.pallas_call(
        table_kernel,
        out_shape=jax.ShapeDtypeStruct((HIGH, heads * LOW), F32),
        in_specs=[pl.BlockSpec(memory_space=pltpu.VMEM)] * 2 + [pl.BlockSpec(memory_space=pl.ANY)] * len(earlier),
        out_specs=pl.BlockSpec(memory_space=pltpu.VMEM),
        compiler_params=pltpu.CompilerParams(vmem_limit_bytes=VMEM_BYTES),
    )(scores, index, *earlier)


def set_line(line, layer, section, own_line, other_line):
    line[...] = jnp.where(section == layer, own_line[...], other_line[...])


def start_bias(layer, section, own, other, bias, sem):
    one = pltpu.make_async_copy(own, bias, sem)
    two = pltpu.make_async_copy(other, bias, sem)
    pl.when(section == layer)(one.start)
    pl.when(section != layer)(two.start)
    return one


def line_biases(line, samples, model):
    q_bias = bias_at(line, samples, model, 0, 1)
    v_bias = bias_at(line, samples, model, 1, 1)
    b_qkv = jnp.concatenate([q_bias, jnp.zeros_like(q_bias), v_bias], axis=1)
    return b_qkv, bias_at(line, samples, model, 2, 1), bias_at(line, samples, model, 3, 4), bias_at(line, samples, model, 7, 1)


def forward_kernel(layer, length, n_weights, n_after, pos, h, own_line, other_line, own_bias, other_bias, *rest):
    refs, rest = rest[:n_weights], rest[n_weights + n_after :]
    (qkv, probs, att, branch, middle, act, slope, out_branch, layer_out,
     w_qkv, w_proj, w_fc1, w_fc2, bias, line, sems) = rest
    section, shard = pos[0], pos[1]
    model = h.shape[1]
    samples = h.shape[0] // length
    got_bias = start_bias(layer, section, own_bias, other_bias, bias, sems.at[weight_count(n_weights)])
    for_attention, for_mlp = weight_loads(layer, section, shard, refs, (w_qkv, w_proj, w_fc1, w_fc2), sems)
    set_line(line, layer, section, own_line, other_line)
    mod = Modulation(line, model)
    b_qkv, b_proj, b_fc1, b_fc2 = line_biases(line, samples, model)
    got_bias.wait()
    wait_all(for_attention)
    each_sample(
        samples,
        lambda b: attention_forward(b, length, h, mod, bias, w_qkv, w_proj, b_qkv, b_proj, qkv, probs, att, branch, middle),
    )
    wait_all(for_mlp)
    each_sample(
        samples,
        lambda b: mlp_forward(b, length, middle, mod, w_fc1, w_fc2, b_fc1, b_fc2, act, slope, out_branch, layer_out),
    )


def both_kernel(layer, pieces, length, n_weights, pos, h, grad, own_line, other_line, own_bias, other_bias, *rest):
    refs, rest = rest[:n_weights], rest[n_weights:]
    (layer_out, d_in, small_a, small_m, scores, keep, send,
     w_qkv, w_proj, w_fc1, w_fc2, bias, line, qkv, probs, att, branch, middle, act, slope, out_branch,
     d_middle, normed_low, d_pre, d_ob, d_qkv, score_sum, g_qkv, g_proj, g_fc1, g_fc2, sems) = rest
    section, shard = pos[0], pos[1]
    model = h.shape[1]
    samples = h.shape[0] // length
    got_bias = start_bias(layer, section, own_bias, other_bias, bias, sems.at[weight_count(n_weights)])
    for_attention, for_mlp = weight_loads(layer, section, shard, refs, (w_qkv, w_proj, w_fc1, w_fc2), sems)
    set_line(line, layer, section, own_line, other_line)
    mod = Modulation(line, model)
    b_qkv, b_proj, b_fc1, b_fc2 = line_biases(line, samples, model)
    got_bias.wait()
    wait_all(for_attention)
    each_sample(
        samples,
        lambda b: attention_forward(b, length, h, mod, bias, w_qkv, w_proj, b_qkv, b_proj, qkv, probs, att, branch, middle),
    )
    wait_all(for_mlp)

    def mlp(b):
        mlp_forward(b, length, middle, mod, w_fc1, w_fc2, b_fc1, b_fc2, act, slope, out_branch, layer_out)
        mlp_backward(b, length, grad, middle, mod, w_fc1, w_fc2, act, slope, out_branch, d_middle, small_m, normed_low, d_pre, d_ob)

    each_sample(samples, mlp)
    mlp_weight_grads(normed_low, d_pre, act, d_ob, g_fc1, g_fc2)
    pack_mlp((keep, send), section, g_fc1, g_fc2, shard, pieces, 6, 2)
    score_sum[...] = jnp.zeros_like(score_sum)
    each_sample(
        samples,
        lambda b: attention_backward(b, length, h, mod, w_qkv, w_proj, qkv, probs, att, branch, d_middle, d_in, small_a, score_sum, normed_low, d_qkv, d_ob),
    )
    scores[...] = score_sum[...].astype(BF16)
    attention_weight_grads(normed_low, d_qkv, att, d_ob, g_qkv, g_proj)
    pack_attention((keep, send), section, g_qkv, g_proj, shard, pieces, 6, 0)
    rows = slice(keep.shape[0], keep.shape[0] + h.shape[0])

    @pl.when(section == 0)
    def _():
        send[rows, :] = layer_out[...]

    @pl.when(section == 1)
    def _():
        send[rows, :] = h[...]


def backward_mlp_kernel(layer, pieces, length, n_weights, n_after, pos, grad, middle, own_line, other_line, act, slope, out_branch, *rest):
    refs, rest = rest[:n_weights], rest[n_weights + n_after :]
    (d_middle, small, keep, send,
     w_qkv, w_proj, w_fc1, w_fc2, line, normed_low, d_pre, d_ob, g_fc1, g_fc2, sems) = rest
    section, shard = pos[0], pos[1]
    for_attention, for_mlp = weight_loads(layer, section, shard, refs, (w_qkv, w_proj, w_fc1, w_fc2), sems)
    set_line(line, layer, section, own_line, other_line)
    mod = Modulation(line, middle.shape[1])
    wait_all(for_mlp)
    each_sample(
        middle.shape[0] // length,
        lambda b: mlp_backward(b, length, grad, middle, mod, w_fc1, w_fc2, act, slope, out_branch, d_middle, small, normed_low, d_pre, d_ob),
    )
    mlp_weight_grads(normed_low, d_pre, act, d_ob, g_fc1, g_fc2)
    pack_mlp((keep, send), section, g_fc1, g_fc2, shard, pieces, 4, 0)
    wait_all(for_attention)


def backward_attention_kernel(layer, pieces, length, n_weights, n_after, pos, h, own_line, other_line, qkv, probs, att, branch, d_middle,
                              index, d_h1, small_m0, small_a1, small_m1, table1, *rest):
    refs, rest = rest[:n_weights], rest[n_weights + n_after :]
    (d_in, keep, send, kept_small,
     w_qkv, w_proj, w_fc1, w_fc2, line, small, table, normed_low, d_qkv, d_br, score_sum, g_qkv, g_proj, sems) = rest
    section, shard = pos[0], pos[1]
    model = h.shape[1]
    samples = h.shape[0] // length
    for_attention, for_mlp = weight_loads(layer, section, shard, refs, (w_qkv, w_proj, w_fc1, w_fc2), sems)
    set_line(line, layer, section, own_line, other_line)
    mod = Modulation(line, model)
    score_sum[...] = jnp.zeros_like(score_sum)
    wait_all(for_attention)
    each_sample(
        samples,
        lambda b: attention_backward(b, length, h, mod, w_qkv, w_proj, qkv, probs, att, branch, d_middle, d_in, small, score_sum, normed_low, d_qkv, d_br),
    )
    attention_weight_grads(normed_low, d_qkv, att, d_br, g_qkv, g_proj)
    pack_attention((keep, send), section, g_qkv, g_proj, shard, pieces, 2, 0)
    add_table(score_sum, index, table)
    at = keep.shape[0]
    rows = slice(at, at + h.shape[0])
    at += h.shape[0]
    size = samples * 8
    smalls = (
        jnp.concatenate([small[...].reshape(size, model), small_m0[...].reshape(size, model), table[...]], axis=0),
        jnp.concatenate([small_a1[...].reshape(size, model), small_m1[...].reshape(size, model), table1[...]], axis=0),
    )

    @pl.when(section == 0)
    def _():
        send[rows, :] = d_h1[...]
        send[at:, :] = smalls[1].astype(BF16)
        kept_small[...] = smalls[0]

    @pl.when(section == 1)
    def _():
        send[rows, :] = d_in[...].astype(BF16)
        send[at:, :] = smalls[0].astype(BF16)
        kept_small[...] = smalls[1]

    wait_all(for_mlp)


def call(kernel, pos, operands, in_hbm, outs, scratch, sems=0):
    specs = [pl.BlockSpec(memory_space=pltpu.SMEM)]
    specs += [pl.BlockSpec(memory_space=pltpu.VMEM) for _ in operands]
    specs += [pl.BlockSpec(memory_space=pl.ANY) for _ in in_hbm]
    shapes = [pltpu.VMEM(shape, dtype) for shape, dtype in scratch]
    if sems:
        shapes.append(pltpu.SemaphoreType.DMA((sems,)))
    return pl.pallas_call(
        kernel,
        out_shape=[jax.ShapeDtypeStruct(shape, dtype) for shape, dtype in outs],
        in_specs=specs,
        out_specs=[pl.BlockSpec(memory_space=pltpu.VMEM) for _ in outs],
        scratch_shapes=shapes,
        compiler_params=pltpu.CompilerParams(vmem_limit_bytes=VMEM_BYTES),
    )(pos, *operands, *in_hbm)


class Sizes:
    def __init__(self, samples, length, model, heads, hidden, pieces):
        self.samples, self.length, self.model = samples, length, model
        self.heads, self.hidden, self.pieces = heads, hidden, pieces
        self.rows = samples * length
        self.line = ((1, (6 * samples + 4 + hidden // model) * model), F32)
        self.weights = [
            ((model, 3 * model), BF16), ((model, model), BF16), ((model, hidden), BF16), ((hidden, model), BF16),
        ]
        self.bias = ((heads, length, length), BF16)
        self.probs = ((samples, heads, length, length), BF16)
        self.low = ((self.rows, model), BF16)
        self.full = ((self.rows, model), F32)
        self.qkv = ((self.rows, 3 * model), BF16)
        self.wide = ((self.rows, hidden), BF16)
        self.small = ((samples, 8, model), F32)

    def pack(self, blocks, more=0):
        return [((blocks * self.model, self.model), BF16), ((blocks * self.model + more, self.model), BF16)]


def forward_layer(layer, z, pos, h, lines, biases, weights, earlier):
    return call(
        functools.partial(forward_kernel, layer, z.length, len(weights), len(earlier)),
        pos, (h, *lines), (*biases, *weights, *earlier),
        [z.qkv, z.probs, z.low, z.full, z.full, z.wide, z.wide, z.full, z.low],
        [*z.weights, z.bias, z.line], weight_count(len(weights)) + 1,
    )


def both_ways(layer, z, pos, h, grad, lines, biases, weights):
    return call(
        functools.partial(both_kernel, layer, z.pieces, z.length, len(weights)),
        pos, (h, grad, *lines), (*biases, *weights),
        [z.low, z.low, z.small, z.small, z.bias, *z.pack(6, z.rows)],
        [*z.weights, z.bias, z.line, z.qkv, z.probs, z.low, z.full, z.full, z.wide, z.wide, z.full,
         z.full, z.low, z.wide, z.low, z.qkv, (z.bias[0], F32), *z.weights],
        weight_count(len(weights)) + 1,
    )


def backward_mlp(layer, z, pos, grad, middle, lines, act, slope, out_branch, weights, earlier):
    return call(
        functools.partial(backward_mlp_kernel, layer, z.pieces, z.length, len(weights), len(earlier)),
        pos, (grad, middle, *lines, act, slope, out_branch), (*weights, *earlier),
        [z.full, z.small, *z.pack(4)],
        [*z.weights, z.line, z.low, z.wide, z.low, *z.weights[2:]],
        weight_count(len(weights)),
    )


def backward_attention(layer, z, pos, h, lines, qkv, probs, att, branch, d_middle, index, others, weights, earlier):
    rows = 2 * 8 * z.samples + HIGH
    return call(
        functools.partial(backward_attention_kernel, layer, z.pieces, z.length, len(weights), len(earlier)),
        pos, (h, *lines, qkv, probs, att, branch, d_middle, index, *others), (*weights, *earlier),
        [z.full, *z.pack(2, z.rows + rows), ((rows, z.model), F32)],
        [*z.weights, z.line, z.small, ((HIGH, z.heads * LOW), F32), z.low, z.qkv, z.low, (z.bias[0], F32), *z.weights[:2]],
        weight_count(len(weights)),
    )


def plane_kernel(samples, n_rows, pos, keep, other, kept_small, cond, own, own_small, *rest):
    messages, work = rest[:3], rest[3]
    section = pos[0]
    size, model = own.shape
    for p in range(4):
        rows = slice(p * size, (p + 1) * size)
        total = keep[rows, :].astype(F32) + other[rows, :].astype(F32)
        if p == 0:
            own[...] = total
        else:
            messages[p - 1][:size, :] = total.astype(BF16)
    at = keep.shape[0] + n_rows
    theirs = other[at:, :].astype(F32)
    mine = kept_small[...]
    each = samples // 2
    work[...] = jnp.zeros_like(work)
    for b in range(each):
        for kind in range(6):
            row = b * 8 + kind if kind < 3 else (each + b) * 8 + kind - 3
            work[pl.ds(kind * samples + section * each + b, 1), :] = mine[row : row + 1, :]
            work[pl.ds(kind * samples + (1 - section) * each + b, 1), :] = theirs[row : row + 1, :]
    work[6 * samples : 7 * samples, :] = cond[...].astype(F32)
    both = mine + theirs
    bias_rows = sum(both[(each + b) * 8 + 3 : (each + b) * 8 + 8, :] for b in range(each))
    more_rows = sum(both[b * 8 + 3 : b * 8 + 6, :] for b in range(each))
    at = 7 * samples
    work[at : at + 5, :] = bias_rows
    work[at + 5 : at + 8, :] = more_rows
    work[at + 8 : at + 8 + HIGH, :] = both[2 * each * 8 :, :]
    small = work[...].astype(BF16)
    own_small[...] = small
    for message in messages:
        message[size:, :] = small


def plane_step(pos, keep, other, kept_small, cond, n_rows):
    samples, model = cond.shape
    size = keep.shape[0] // 4
    small = -(-(7 * samples + 8 + HIGH) // 16) * 16
    outs = [((size, model), F32), ((small, model), BF16)] + [((size + small, model), BF16)] * 3
    return call(
        functools.partial(plane_kernel, samples, n_rows), pos, (keep, other, kept_small, cond), (), outs,
        [((small, model), F32)],
    )


def column_kernel(samples, pos, own, own_small, got_a, got_b, got_c, part, own_out, *rest):
    messages, work = rest[:3], rest[3]
    rank = pos[2]
    size, model = own.shape
    n = size // 4
    got = (got_a, got_b, got_c)
    for j in range(4):
        at = pl.multiple_of((rank ^ j) * n, 16)
        total = own[pl.ds(at, n), :]
        for piece in got:
            total = total + piece[pl.ds(at, n), :].astype(F32)
        if j == 0:
            part[...] = total
        else:
            messages[j - 1][:n, :] = total.astype(BF16)
    smalls = [own_small[...].astype(F32)] + [piece[size:, :].astype(F32) for piece in got]
    work[...] = jnp.zeros_like(work)
    for p in range(4):
        for kind in range(7):
            at = (kind * 4 + p) * samples
            work[at : at + samples, :] = smalls[p][kind * samples : (kind + 1) * samples, :]
    at = 7 * samples
    summed = (smalls[0] + smalls[1]) + (smalls[2] + smalls[3])
    work[4 * at : 4 * at + 8 + HIGH, :] = summed[at : at + 8 + HIGH, :]
    small = work[...].astype(BF16)
    own_out[...] = small
    for message in messages:
        message[n:, :] = small


def column_step(pos, own, own_small, got, samples):
    size, model = own.shape
    small = -(-(28 * samples + 8 + HIGH) // 16) * 16
    outs = [((size // 4, model), F32), ((small, model), BF16)] + [((size // 4 + small, model), BF16)] * 3
    return call(
        functools.partial(column_kernel, samples), pos, (own, own_small, *got), (), outs, [((small, model), F32)]
    )


def finish_kernel(samples, width, pos, own_small, got_a, got_b, got_c, g_ada, g_b_ada, summed, work, whole):
    shard, rank = pos[1], pos[2]
    model = own_small.shape[1]
    each = 4 * samples
    n = got_a.shape[0] - own_small.shape[0]
    pieces = [own_small[...]] + [piece[n:, :] for piece in (got_a, got_b, got_c)]
    for j in range(4):
        for kind in range(7):
            at = pl.multiple_of(kind * 4 * each + (rank ^ j) * each, 16)
            work[pl.ds(at, each), :] = pieces[j][kind * each : (kind + 1) * each, :].astype(F32)
    cond = work[24 * each :, :]
    act = (cond * (1.0 / (1.0 + jnp.exp(-cond)))).astype(BF16)
    for kind in range(6):
        rows = work[kind * 4 * each : (kind + 1) * 4 * each, :]
        whole[...] = dot_cols(act, rows.astype(BF16))
        cols = slice(kind * model, (kind + 1) * model)
        g_ada[:, cols] = whole[pl.ds(pl.multiple_of(shard * width, 16), width), :]
        g_b_ada[:, cols] = col_sum(rows)
    at = 7 * each
    rows = [piece[at : at + 8 + HIGH, :].astype(F32) for piece in pieces]
    summed[...] = (rows[0] + rows[1]) + (rows[2] + rows[3])


def finish_step(pos, own_small, got, samples, width):
    model = own_small.shape[1]
    return call(
        functools.partial(finish_kernel, samples, width), pos, (own_small, *got), (),
        [((width, 6 * model), F32), ((1, 6 * model), F32), ((8 + HIGH, model), F32)],
        [((7 * 16 * samples, model), F32), ((model, model), F32)],
    )


def cond_kernel(samples, pos, small, cond, *rest):
    out, w_ada = rest[-2:]
    model = cond.shape[1]
    for p, piece in enumerate(rest[:-2]):
        q = piece.shape[0]
        off = pl.multiple_of((pos[1] ^ p) * q, 16) if q < model else 0
        w_ada[pl.ds(off, q), :] = piece[...]
    total = None
    for kind in range(6):
        rows = small[...].astype(F32)[kind * samples : (kind + 1) * samples, :].astype(BF16)
        part = dot_rows(rows, w_ada[:, kind * model : (kind + 1) * model])
        total = part if total is None else total + part
    c = cond[...].astype(F32)
    gate = 1.0 / (1.0 + jnp.exp(-c))
    out[...] = total * (gate * (1.0 + c * (1.0 - gate)))


def cond_step(pos, small, w_ada, cond):
    model = cond.shape[1]
    return call(
        functools.partial(cond_kernel, cond.shape[0]), pos, (small, cond, *w_ada), (), [(cond.shape, F32)],
        [((model, w_ada[0].shape[1]), BF16)],
    )[0]


def halve_kernel(pos, own, got_a, got_b, got_c, keep, send):
    bit = pos[2] & 1
    n = own.shape[0] // 4
    for high in range(2):
        for out, low in ((keep, bit), (send, 1 - bit)):
            rows = pl.ds(pl.multiple_of((2 * high + low) * n, 16), n)
            total = own[rows, :]
            for piece in (got_a, got_b, got_c):
                total = total + piece[rows, :].astype(F32)
            out[high * n : (high + 1) * n, :] = total.astype(out.dtype)


def halve_step(pos, own, got):
    shape = (own.shape[0] // 2, own.shape[1])
    return call(halve_kernel, pos, (own, *got), (), [(shape, F32), (shape, BF16)], [])


def quarter_kernel(pos, kept, got, keep, send):
    bit = pos[2] >> 1
    n = kept.shape[0] // 2
    for out, high in ((keep, bit), (send, 1 - bit)):
        rows = pl.ds(pl.multiple_of(high * n, 16), n)
        out[...] = (kept[rows, :] + got[rows, :].astype(F32)).astype(out.dtype)


def quarter_step(pos, kept, got):
    shape = (kept.shape[0] // 2, kept.shape[1])
    return call(quarter_kernel, pos, (kept, got), (), [(shape, F32), (shape, BF16)], [])


def pack_kernel(pos, qkv, proj, fc1, fc2, out):
    q, model = proj.shape
    for c in range(3):
        out[c * q : (c + 1) * q, :] = qkv[:, c * model : (c + 1) * model]
    out[3 * q : 4 * q, :] = proj[...]
    for c in range(4):
        out[(4 + c) * q : (5 + c) * q, :] = fc1[:, c * model : (c + 1) * model]
    out[8 * q : 12 * q, :] = fc2[...]


def pack_shard(pos, own):
    q, model = own[1].shape
    return call(pack_kernel, pos, own, (), [((12 * q, model), BF16)], [])[0]


def after(values, others):
    return pl.pallas_call(
        lambda *refs: None,
        out_shape=[jax.ShapeDtypeStruct(v.shape, v.dtype) for v in values],
        in_specs=[pl.BlockSpec(memory_space=pl.ANY)] * (len(values) + len(others)),
        out_specs=[pl.BlockSpec(memory_space=pl.ANY)] * len(values),
        input_output_aliases={i: i for i in range(len(values))},
    )(*values, *others)


def lookup_kernel(table, index, *rest):
    out, work = rest[-2:]
    heads, length = out.shape[0], out.shape[1]
    high_count = table.shape[0] // 8
    values = table[...]
    low_id = lax.broadcasted_iota(jnp.int32, (LOW, length), 0)

    def step(i, carry):
        block = index[pl.ds(pl.multiple_of(i * 8, 8), 8), :]
        for r in range(8):
            entry = block[r : r + 1, :]
            picks = jnp.where(low_id == (entry & (LOW - 1)), 1.0, 0.0).astype(BF16)
            found = dot(values, picks).reshape(high_count, 8, length)
            high = jnp.broadcast_to(entry >> LOW_BITS, (8, length))
            bit = high_count // 2
            while bit:
                chosen = (high & bit) != 0
                found = jnp.where(chosen[None], found[bit : 2 * bit], found[:bit])
                bit //= 2
            for head in range(heads):
                work[head, pl.ds(i * 8 + r, 1), :] = found[0, head : head + 1, :]
        return carry

    lax.fori_loop(0, length // 8, step, 0)
    out[...] = work[...].astype(BF16)


def lookup(table, index, earlier):
    heads, entries = table.shape
    high_count = HIGH
    padded = jnp.pad(table, ((0, 8 - heads), (0, high_count * LOW - entries)))
    rows = jnp.transpose(padded.reshape(8, high_count, LOW), (1, 0, 2)).reshape(high_count * 8, LOW)
    length = index.shape[0]
    return pl.pallas_call(
        lookup_kernel,
        out_shape=jax.ShapeDtypeStruct((heads, length, length), BF16),
        in_specs=[pl.BlockSpec(memory_space=pltpu.VMEM)] * 2 + [pl.BlockSpec(memory_space=pl.ANY)] * len(earlier),
        out_specs=pl.BlockSpec(memory_space=pltpu.VMEM),
        scratch_shapes=[pltpu.VMEM((heads, length, length), F32)],
        compiler_params=pltpu.CompilerParams(vmem_limit_bytes=VMEM_BYTES),
    )(rows, index, *earlier)


def swap_section(value):
    return lax.ppermute(value, "section", [(0, 1), (1, 0)])


def pairs_of(count, step):
    return [(i, i ^ step) for i in range(count)]


def by_rank(pieces, rank):
    stack = jnp.stack(pieces)
    count = len(pieces)
    bit = 1
    while bit < count:
        moved = jnp.stack([stack[i ^ bit] for i in range(count)])
        stack = jnp.where((rank & bit) != 0, moved, stack)
        bit *= 2
    return stack


def section_sums(keep, other, shards):
    size = keep.shape[0] // shards
    return [
        keep[p * size : (p + 1) * size].astype(F32) + other[p * size : (p + 1) * size].astype(F32)
        for p in range(shards)
    ]


def low_pieces(sums):
    return [x.astype(BF16) for x in sums[1:]]


def to_peers(messages, axis):
    count = lax.axis_size(axis)
    return [lax.ppermute(messages[p - 1], axis, pairs_of(count, p)) for p in range(1, count)]


def add_pieces(own, got):
    total = own
    for piece in got:
        total = total + piece.astype(F32)
    return total


def replica_parts(total, rank):
    replicas = lax.axis_size("rep")
    parts = total if total.ndim == 3 else total.reshape(replicas, total.shape[0] // replicas, -1)
    low = parts.astype(BF16)
    mine = lax.dynamic_index_in_dim(parts, rank, 0, keepdims=False)
    return mine, [lax.dynamic_index_in_dim(low, rank ^ j, 0, keepdims=False) for j in range(1, replicas)]


def unpack_attention(pack):
    q = pack.shape[0] // 4
    return jnp.concatenate([pack[c * q : (c + 1) * q] for c in range(3)], axis=1), pack[3 * q :]


def unpack_mlp(pack):
    q = pack.shape[0] // 8
    return jnp.concatenate([pack[c * q : (c + 1) * q] for c in range(4)], axis=1), pack[4 * q :]


def pad_rows(value):
    return jnp.pad(value, ((0, -value.shape[0] % 16), (0, 0)))


def from_peers(value, axis):
    return [lax.ppermute(value, axis, pairs_of(lax.axis_size(axis), p)) for p in range(1, lax.axis_size(axis))]


def pair_sum(values):
    while len(values) > 1:
        values = [values[i] + values[i + 1] for i in range(0, len(values), 2)]
    return values[0]


def per_device(inputs, conditioning, cotangent, micro_sizes, relative_bias_index,
               w_ada, w_qkv, w_proj, w_fc1, w_fc2, b_ada, b_qv, b_proj, b_fc1, b_fc2, bias_table):
    section = lax.axis_index("section")
    shard = lax.axis_index("fsdp")
    rank = lax.axis_index("rep")
    shards, replicas = lax.axis_size("fsdp"), lax.axis_size("rep")
    direct = shards == 4 and replicas == 4
    is_first = section == 0
    samples, length, model = inputs.shape
    heads, entries = bias_table.shape[1:]
    half = samples // 2
    z = Sizes(half, length, model, heads, 4 * model, shards if direct else 1)
    pos = jnp.stack([section, shard, rank]).astype(jnp.int32)

    def mine(first, second):
        return jnp.where(is_first, first, second)

    def own_samples(array):
        return lax.dynamic_slice_in_dim(array, section * half, half, 0)

    def in_order(own, other):
        return jnp.where(is_first, jnp.concatenate([own, other]), jnp.concatenate([other, own]))

    live = (jnp.arange(half)[:, None, None] < lax.dynamic_index_in_dim(micro_sizes[0], section, 0)).astype(BF16)
    h0 = own_samples(inputs).reshape(half * length, model)
    grad1 = (own_samples(cotangent) * live).reshape(half * length, model)
    own_raw = [w_qkv[0], w_proj[0], w_fc1[0], w_fc2[0]]
    cond_size = conditioning.size
    width = model // shards
    if direct:
        row = jnp.concatenate([conditioning.reshape(1, -1), b_ada, b_qv, b_proj, b_fc1, b_fc2], axis=1)
        rows = [row] + from_peers(row, "fsdp")
        own_pack = pack_shard(pos, own_raw)
        middle_row = own_pack.shape[0] // 2
        got_x = lax.ppermute(own_pack, "fsdp", pairs_of(shards, 1))
        got_y = lax.ppermute(own_pack, "fsdp", pairs_of(shards, 2))
        got_first = lax.ppermute(got_x[:middle_row], "fsdp", pairs_of(shards, 2))
        got_second = lax.ppermute(got_y[middle_row:], "fsdp", pairs_of(shards, 1))
        own_weights = [own_pack, got_x, got_y, got_first, got_second]
        weights = own_weights + [swap_section(w) for w in own_weights]
        cond_pieces = jnp.stack([r[0, :cond_size].reshape(samples, model) for r in rows])
        acts = jax.nn.silu(cond_pieces.astype(F32)).astype(BF16)
        acts = lax.dynamic_slice_in_dim(acts, shard * width, width, 2)
        partial = lax.dot_general(acts, w_ada[0], (((2,), (0,)), ((), ())), preferred_element_type=F32)
        bias_rows = by_rank([r[0, cond_size:] for r in rows], shard)
        bias_own = lookup(bias_table[0], relative_bias_index, [own_pack, partial, h0, grad1])
        parts = after(to_peers(partial[1:], "fsdp"), [got_x, got_y, bias_own])
        modulation = add_pieces(partial[0], parts)
    else:
        row = jnp.concatenate([b_ada, b_qv, b_proj, b_fc1, b_fc2], axis=1)
        bias_rows = lax.all_gather(row[0], "fsdp", axis=0)
        whole = [lax.all_gather(w, "fsdp", axis=0, tiled=True) for w in own_raw]
        own_whole = pack_shard(pos, whole)
        weights = [own_whole, swap_section(own_whole)]
        acts = jax.nn.silu(conditioning.astype(F32)).astype(BF16)
        modulation = dot(acts, lax.all_gather(w_ada[0], "fsdp", axis=0, tiled=True))
        bias_own = lookup(bias_table[0], relative_bias_index, [])
    cuts = [b_ada.shape[1], b_qv.shape[1], b_proj.shape[1], b_fc1.shape[1], b_fc2.shape[1]]
    biases, at = [], 0
    for cut in cuts:
        biases.append(bias_rows[:, at : at + cut].reshape(1, -1).astype(F32))
        at += cut
    modulation = modulation + biases[0]
    other_samples = lax.dynamic_slice_in_dim(modulation, (1 - section) * half, half, 0)
    own_line = jnp.concatenate([own_samples(modulation).reshape(1, -1)] + biases[1:], axis=1)
    other_line = swap_section(jnp.concatenate([other_samples.reshape(1, -1)] + biases[1:], axis=1))
    lines = (own_line, other_line)
    bias_heads = (bias_own, swap_section(bias_own))

    if direct:
        w_ada_later = after([w_ada[0]], weights[3:5])[0]
        w_ada_pieces = [w_ada_later] + from_peers(w_ada_later, "fsdp")
    else:
        w_ada_pieces = [lax.all_gather(w_ada[0], "fsdp", axis=0, tiled=True)]
    qkv, probs, att, branch, middle, act, slope, out_branch, h1 = forward_layer(0, z, pos, h0, lines, bias_heads, weights, w_ada_pieces[:1] if direct else [])
    out1, d_h1, small_a1, small_m1, scores1, keep1, send1 = both_ways(1, z, pos, h1, grad1, lines, bias_heads, weights)
    d_middle, small_m0, keep_m0, send_m0 = backward_mlp(0, z, pos, d_h1, middle, lines, act, slope, out_branch, weights, w_ada_pieces[1:])
    pieces = z.pieces
    rows = half * length
    other1 = swap_section(send1)
    sums1 = section_sums(keep1, other1[: keep1.shape[0]], pieces)
    low1 = low_pieces(sums1)
    table1 = table_gradient(scores1, relative_bias_index, low1)
    other_m0 = after([swap_section(send_m0)], [table1])[0]
    sums_m0 = section_sums(keep_m0, other_m0, pieces)
    low_m0 = low_pieces(sums_m0)
    if direct:
        got1 = after(to_peers(low1, "fsdp"), [table1, *low_m0])
        keep_z1, send_z1 = halve_step(pos, sums1[0], got1)
        earlier = [table1, *low_m0, send_z1]
    else:
        earlier = [table1, *low_m0]
    d_h0, keep_a0, send_a0, kept_small = backward_attention(
        0, z, pos, h0, lines, qkv, probs, att, branch, d_middle, relative_bias_index,
        (d_h1, small_m0, small_a1, small_m1, table1), weights, earlier,
    )
    if direct:
        got_z1, *got_m0 = after([lax.ppermute(send_z1, "rep", pairs_of(replicas, 1)), *to_peers(low_m0, "fsdp")], [d_h0])
        send_a0 = after([send_a0], [got_z1, *got_m0])[0]
    other_a0 = swap_section(send_a0)
    size_a = keep_a0.shape[0]

    def replica(value, step):
        return lax.ppermute(value, "rep", pairs_of(replicas, step))

    def ordered(own, other, bit):
        return jnp.where(bit == 0, jnp.concatenate([own, other]), jnp.concatenate([other, own]))

    if direct:
        own_a0, own_small, *messages = plane_step(pos, keep_a0, other_a0, kept_small, conditioning, rows)
        keep_z1, send_z1 = quarter_step(pos, keep_z1, got_z1)
        keep_zm, send_zm = halve_step(pos, sums_m0[0], got_m0)
        cond_part = cond_step(pos, after([own_small], [send_zm, send_z1])[0], w_ada_pieces, conditioning)
        got = to_peers(messages, "fsdp")
        part0, plane_small, *messages = column_step(pos, own_a0, own_small, got, samples)
        got_z1, got_zm = after([replica(send_z1, 2), replica(send_zm, 1)], [plane_small])
        quarter1 = (keep_z1 + got_z1.astype(F32)).astype(BF16)
        keep_zm, send_zm = quarter_step(pos, keep_zm, got_zm)
        got = to_peers(messages, "rep")
        size = part0.shape[0]
        quarter0 = add_pieces(part0, [x[:size] for x in got]).astype(BF16)
        got_z1, got_zm = after([replica(quarter1, 2), replica(send_zm, 2)], [quarter0])
        high, low = rank >> 1, rank & 1
        pair1 = ordered(quarter1, got_z1, high)
        quarter_m = (keep_zm + got_zm.astype(F32)).astype(BF16)
        pair_m = ordered(quarter_m, replica(quarter_m, 2), high)
        half_a0 = by_rank([quarter0] + from_peers(quarter0, "rep"), rank).reshape(-1, model)

        def by_low(pair):
            n = pair.shape[0] // 2
            both = ordered(pair.reshape(1, 2, n, model), replica(pair, 1).reshape(1, 2, n, model), low)
            return jnp.transpose(both, (1, 0, 2, 3)).reshape(-1, model)

        half1, half_m0 = by_low(pair1), by_low(pair_m)
        g_ada, g_b_ada, summed = finish_step(pos, plane_small, got, samples, width)
        g_b_ada = g_b_ada[0]
    else:
        theirs = other_a0[size_a + rows :].astype(F32)
        both = kept_small + theirs
        cut = half * 8

        def d_mod_of(values):
            a, m = values[:cut].reshape(half, 8, model), values[cut : 2 * cut].reshape(half, 8, model)
            return jnp.concatenate([a[:, :3], m[:, :3]], axis=1)

        low = in_order(d_mod_of(kept_small), d_mod_of(theirs)).astype(BF16)
        bias_rows = jnp.sum(both[: 2 * cut].reshape(2, half, 8, model), axis=1)
        summed = jnp.concatenate([bias_rows[1, 3:8], bias_rows[0, 3:6], both[2 * cut :]])
        cond_part = cond_step(pos, jnp.transpose(low, (1, 0, 2)).reshape(-1, model), w_ada_pieces, conditioning)
        kept = jnp.concatenate([low, conditioning[:, None]], axis=1)
        kept = lax.all_gather(kept, ("fsdp", "rep"), axis=0, tiled=True)
        summed = lax.psum(summed, ("fsdp", "rep"))
        act_all = jax.nn.silu(kept[:, 6].astype(F32)).astype(BF16)
        act_cols = lax.dynamic_slice_in_dim(act_all, shard * width, width, 1)
        g_ada = jnp.concatenate([dot_cols(act_cols, kept[:, i]) for i in range(6)], axis=1)
        g_b_ada = jnp.sum(kept[:, :6].astype(F32), axis=0).reshape(-1)
        sums_a0 = section_sums(keep_a0, other_a0[:size_a], pieces)
        half_a0, half_m0, half1 = sums_a0[0].astype(BF16), sums_m0[0].astype(BF16), sums1[0].astype(BF16)
    cond_grad = cond_part + swap_section(cond_part)
    cut = half_a0.shape[0]
    half_a1, half_m1 = half1[:cut], half1[cut:]
    grads = unpack_mlp(in_order(mine(half_m0, half_m1), swap_section(mine(half_m1, half_m0))))
    grads = unpack_attention(in_order(mine(half_a0, half_a1), swap_section(mine(half_a1, half_a0)))) + grads
    if not direct:
        grads = [lax.psum_scatter(g, "fsdp", scatter_dimension=0, tiled=True) for g in grads]
        grads = lax.psum(tuple(grads), "rep")
    g_qkv, g_proj, g_fc1, g_fc2 = [g.astype(F32) for g in grads]

    activations = in_order(
        mine(h1, out1).reshape(half, length, model), other1[keep1.shape[0] :].reshape(half, length, model)
    )
    input_grads = in_order(
        mine(d_h0, d_h1.astype(F32)).reshape(half, length, model),
        other_a0[size_a : size_a + rows].astype(F32).reshape(half, length, model),
    )

    g_b_fc2, g_b_fc1 = summed[0], summed[1:5].reshape(-1)
    g_b_qv, g_b_proj = summed[5:7].reshape(-1), summed[7]
    g_table = jnp.transpose(summed[8:].reshape(HIGH, heads, LOW), (1, 0, 2)).reshape(heads, HIGH * LOW)[:, :entries]

    def own_part(vector):
        size = vector.shape[0] // shards
        return lax.dynamic_slice_in_dim(vector, shard * size, size, 0)[None]

    return (
        activations[None], input_grads[None], cond_grad,
        g_ada[None], g_qkv[None], g_proj[None], g_fc1[None], g_fc2[None],
        own_part(g_b_ada), own_part(g_b_qv), own_part(g_b_proj), own_part(g_b_fc1), own_part(g_b_fc2),
        g_table[None],
    )


def solution(mesh):
    batch = ("fsdp", "rep")
    matrix = P("section", "fsdp", None)
    vector = P("section", "fsdp")
    return jax.shard_map(
        per_device,
        mesh=mesh,
        in_specs=(
            P(batch, None, None), P(batch, None), P(batch, None, None), P(batch, None), P(),
            matrix, matrix, matrix, matrix, matrix, vector, vector, vector, vector, vector,
            P("section", None, None),
        ),
        out_specs=(
            P("section", batch, None, None), P("section", batch, None, None), P(batch, None),
            matrix, matrix, matrix, matrix, matrix, vector, vector, vector, vector, vector,
            P("section", None, None),
        ),
        check_vma=False,
    )
```

```python
import functools

import jax
import jax.numpy as jnp
from jax import lax
from jax.experimental import pallas as pl
from jax.experimental.pallas import tpu as pltpu
from jax.sharding import PartitionSpec as P

EPSILON = 1e-06
F32 = jnp.float32
BF16 = jnp.bfloat16
VMEM_BYTES = 58 * 1024 * 1024
LOW_BITS = 6
LOW = 1 << LOW_BITS
HIGH = 16


def dot(a, b):
    return jnp.dot(a, b, preferred_element_type=F32)


def dot_rows(a, b):
    return lax.dot_general(a, b, (((1,), (1,)), ((), ())), preferred_element_type=F32)


def dot_cols(a, b):
    return lax.dot_general(a, b, (((0,), (0,)), ((), ())), preferred_element_type=F32)


def norm_parts(v):
    centre = v - jnp.mean(v, axis=-1, keepdims=True)
    inverse = lax.rsqrt(jnp.mean(centre * centre, axis=-1, keepdims=True) + EPSILON)
    return centre * inverse, inverse


def norm_back(d_normed, scale, normed, inverse):
    d = d_normed * (1.0 + scale)
    return inverse * (
        d
        - jnp.mean(d, axis=-1, keepdims=True)
        - normed * jnp.mean(d * normed, axis=-1, keepdims=True)
    )


def col_sum(v):
    return jnp.sum(v, axis=0, keepdims=True)


def half_masks(width):
    lane = lax.broadcasted_iota(jnp.int32, (1, width), 1)
    first = jnp.where(lane < width // 2, 1.0, 0.0)
    return first.astype(BF16), (1.0 - first).astype(BF16)


def block_targets(mats, off, q):
    w_qkv, w_proj, w_fc1, w_fc2 = mats
    model = w_proj.shape[0]
    targets = [w_qkv.at[pl.ds(off, q), pl.ds(c * model, model)] for c in range(3)]
    targets.append(w_proj.at[pl.ds(off, q), :])
    targets += [w_fc1.at[pl.ds(off, q), pl.ds(c * model, model)] for c in range(4)]
    targets.append(w_fc2.at[pl.ds(off * 4, 4 * q), :])
    return targets


def weight_count(refs):
    return 9 if refs == 2 else 36


def weight_loads(layer, section, shard, refs, mats, sems):
    model = mats[1].shape[0]
    plans = []
    if len(refs) == 2:
        for i, target in enumerate(block_targets(mats, 0, model)):
            rows = pl.ds(i * model, 4 * model if i == 8 else model)
            plans.append((refs[0].at[rows, :], refs[1].at[rows, :], target, i < 4))
    else:
        count = len(refs) // 2
        q = refs[0].shape[0] // 12
        for p in range(4):
            targets = block_targets(mats, pl.multiple_of((shard ^ p) * q, 16), q)
            for i, target in enumerate(targets):
                which, at = p, i
                if p == 3 and i >= 6:
                    which, at = 4, i - 6
                rows = pl.ds(at * q, 4 * q if i == 8 else q)
                plans.append((refs[which].at[rows, :], refs[count + which].at[rows, :], target, i < 4))
    ones = [pltpu.make_async_copy(x[0], x[2], sems.at[i]) for i, x in enumerate(plans)]
    twos = [pltpu.make_async_copy(x[1], x[2], sems.at[i]) for i, x in enumerate(plans)]

    @pl.when(section == layer)
    def _():
        for copy in ones:
            copy.start()

    @pl.when(section != layer)
    def _():
        for copy in twos:
            copy.start()

    return (
        [copy for copy, x in zip(ones, plans) if x[3]],
        [copy for copy, x in zip(ones, plans) if not x[3]],
    )


def wait_all(copies):
    for copy in copies:
        copy.wait()


def put_half(refs, section, half, at, value):
    keep, send = refs
    rows = slice(at, at + value.shape[0])

    @pl.when(section == half)
    def _():
        keep[rows, :] = value

    @pl.when(section != half)
    def _():
        send[rows, :] = value


def pack_attention(refs, section, g_qkv, g_proj, shard, pieces, stride, first):
    model = g_proj.shape[0]
    q = model // pieces
    for p in range(pieces):
        off = pl.multiple_of((shard ^ p) * q, 16) if pieces > 1 else 0
        at = (stride * p + first) * q
        for c in range(3):
            value = g_qkv[pl.ds(off, q), c * model : (c + 1) * model]
            put_half(refs, section, c // 2, at + (c % 2) * q, value)
        put_half(refs, section, 1, at + q, g_proj[pl.ds(off, q), :])


def pack_mlp(refs, section, g_fc1, g_fc2, shard, pieces, stride, first):
    model = g_fc1.shape[0]
    q = model // pieces
    for p in range(pieces):
        off = pl.multiple_of((shard ^ p) * q, 16) if pieces > 1 else 0
        at = (stride * p + first) * q
        for c in range(4):
            value = g_fc1[pl.ds(off, q), c * model : (c + 1) * model]
            put_half(refs, section, 0, at + c * q, value)
        put_half(refs, section, 1, at, g_fc2[pl.ds(pl.multiple_of(off * 4, 16), 4 * q), :])


class Modulation:
    def __init__(self, line, model):
        self.line, self.model = line, model

    def __getitem__(self, key):
        b, rows, _ = key
        return self.line[:, pl.ds(pl.multiple_of((6 * b + rows.start) * self.model, 128), self.model)]


def bias_at(line, samples, model, start, size):
    return line[:, (6 * samples + start) * model : (6 * samples + start + size) * model]


def attention_forward(b, length, h, mod, bias, w_qkv, w_proj, b_qkv, b_proj, qkv, probs, att, branch, middle):
    model = w_proj.shape[0]
    heads = bias.shape[0]
    pair = 2 * model // heads
    rows = pl.ds(pl.multiple_of(b * length, length), length)
    masks = half_masks(pair)
    x = h[rows, :].astype(F32)
    normed, _ = norm_parts(x)
    normed_low = (normed * (1.0 + mod[b, 1:2, :]) + mod[b, 0:1, :]).astype(BF16)
    qkv[rows, :] = (dot(normed_low, w_qkv[...]) + b_qkv[...]).astype(BF16)
    for j in range(heads // 2):
        q_pair = qkv[rows, j * pair : (j + 1) * pair] * BF16((pair // 2) ** (-0.5))
        k_pair = qkv[rows, model + j * pair : model + (j + 1) * pair]
        v_pair = qkv[rows, 2 * model + j * pair : 2 * model + (j + 1) * pair]
        total = None
        for e in range(2):
            scores = dot_rows(q_pair * masks[e], k_pair) + bias[2 * j + e].astype(F32)
            raised = jnp.exp(scores - jnp.max(scores, axis=-1, keepdims=True))
            p = (raised * (1.0 / jnp.sum(raised, axis=-1, keepdims=True))).astype(BF16)
            probs[b, 2 * j + e] = p
            part = dot(p, v_pair * masks[e])
            total = part if total is None else total + part
        att[rows, j * pair : (j + 1) * pair] = total.astype(BF16)
    out = dot(att[rows, :], w_proj[...]) + b_proj[...]
    branch[rows, :] = out
    middle[rows, :] = x + mod[b, 2:3, :] * out


def mlp_forward(b, length, middle, mod, w_fc1, w_fc2, b_fc1, b_fc2, act, slope, out_branch, layer_out):
    model = w_fc1.shape[0]
    rows = pl.ds(pl.multiple_of(b * length, length), length)
    mid = middle[rows, :]
    normed, _ = norm_parts(mid)
    normed_low = (normed * (1.0 + mod[b, 4:5, :]) + mod[b, 3:4, :]).astype(BF16)
    total = b_fc2[...]
    for c in range(w_fc1.shape[1] // model):
        cols = slice(c * model, (c + 1) * model)
        v = dot(normed_low, w_fc1[:, cols]) + b_fc1[:, cols]
        square = v * v
        t = jnp.tanh(0.7978845608028654 * v * (1.0 + 0.044715 * square))
        half = 0.5 * (1.0 + t)
        a = (v * half).astype(BF16)
        act[rows, cols] = a
        slope[rows, cols] = (
            half
            + 0.5 * v * (1.0 - t * t) * (0.7978845608028654 + (3 * 0.044715 * 0.7978845608028654) * square)
        ).astype(BF16)
        total = total + dot(a, w_fc2[cols, :])
    out_branch[rows, :] = total
    layer_out[rows, :] = (mid + mod[b, 5:6, :] * total).astype(layer_out.dtype)


def mlp_backward(b, length, grad, middle, mod, w_fc1, w_fc2, act, slope, out_branch, d_middle, small, normed_low, d_pre, d_ob):
    model = w_fc1.shape[0]
    rows = pl.ds(pl.multiple_of(b * length, length), length)
    g = grad[rows, :].astype(F32)
    small[b, 2:3, :] = col_sum(g * out_branch[rows, :])
    d_out = g * mod[b, 5:6, :]
    d_out_low = d_out.astype(BF16)
    d_ob[rows, :] = d_out_low
    small[b, 3:4, :] = col_sum(d_out_low.astype(F32))
    normed, inverse = norm_parts(middle[rows, :])
    normed_low[rows, :] = (normed * (1.0 + mod[b, 4:5, :]) + mod[b, 3:4, :]).astype(BF16)
    d_normed = None
    for c in range(w_fc1.shape[1] // model):
        cols = slice(c * model, (c + 1) * model)
        d_act = dot_rows(d_out_low, w_fc2[cols, :])
        d_low = (d_act * slope[rows, cols].astype(F32)).astype(BF16)
        d_pre[rows, cols] = d_low
        small[b, 4 + c : 5 + c, :] = col_sum(d_low.astype(F32))
        part = dot_rows(d_low, w_fc1[:, cols])
        d_normed = part if d_normed is None else d_normed + part
    small[b, 0:1, :] = col_sum(d_normed)
    small[b, 1:2, :] = col_sum(d_normed * normed)
    d_middle[rows, :] = norm_back(d_normed, mod[b, 4:5, :], normed, inverse) + g


def mlp_weight_grads(normed_low, d_pre, act, d_ob, g_fc1, g_fc2):
    model = g_fc1.shape[0]
    for c in range(g_fc1.shape[1] // model):
        cols = slice(c * model, (c + 1) * model)
        g_fc1[:, cols] = dot_cols(normed_low[...], d_pre[:, cols]).astype(BF16)
        g_fc2[cols, :] = dot_cols(act[:, cols], d_ob[...]).astype(BF16)


def attention_backward(b, length, h, mod, w_qkv, w_proj, qkv, probs, att, branch, d_middle, d_in, small, score_sum, normed_low, d_qkv, d_br):
    model = w_proj.shape[0]
    heads = probs.shape[1]
    pair = 2 * model // heads
    scale = F32((pair // 2) ** (-0.5))
    rows = pl.ds(pl.multiple_of(b * length, length), length)
    masks = half_masks(pair)
    d_mid = d_middle[rows, :]
    small[b, 2:3, :] = col_sum(d_mid * branch[rows, :])
    d_branch = (d_mid * mod[b, 2:3, :]).astype(BF16)
    d_br[rows, :] = d_branch
    small[b, 5:6, :] = col_sum(d_branch.astype(F32))
    d_att = dot_rows(d_branch, w_proj[...]).astype(BF16)
    for j in range(heads // 2):
        q_pair = qkv[rows, j * pair : (j + 1) * pair]
        k_pair = qkv[rows, model + j * pair : model + (j + 1) * pair]
        v_pair = qkv[rows, 2 * model + j * pair : 2 * model + (j + 1) * pair]
        d_pair = d_att[:, j * pair : (j + 1) * pair]
        d_q = d_k = d_v = None
        for e in range(2):
            p_low = probs[b, 2 * j + e]
            p = p_low.astype(F32)
            d_here = d_pair * masks[e]
            d_p = dot_rows(d_here, v_pair)
            d_s = (p * (d_p - jnp.sum(d_p * p, axis=-1, keepdims=True))).astype(BF16)
            score_sum[2 * j + e] += d_s.astype(F32)
            v_part = dot_cols(p_low, d_here)
            q_part = dot(d_s, k_pair * masks[e])
            k_part = dot_cols(d_s, q_pair * masks[e])
            d_v = v_part if d_v is None else d_v + v_part
            d_q = q_part if d_q is None else d_q + q_part
            d_k = k_part if d_k is None else d_k + k_part
        d_qkv[rows, j * pair : (j + 1) * pair] = (d_q * scale).astype(BF16)
        d_qkv[rows, model + j * pair : model + (j + 1) * pair] = (d_k * scale).astype(BF16)
        d_qkv[rows, 2 * model + j * pair : 2 * model + (j + 1) * pair] = d_v.astype(BF16)
    small[b, 3:4, :] = col_sum(d_qkv[rows, :model].astype(F32))
    small[b, 4:5, :] = col_sum(d_qkv[rows, 2 * model :].astype(F32))
    small[b, 6:8, :] = jnp.zeros((2, model), F32)
    d_normed = dot_rows(d_qkv[rows, :], w_qkv[...])
    normed, inverse = norm_parts(h[rows, :].astype(F32))
    normed_low[rows, :] = (normed * (1.0 + mod[b, 1:2, :]) + mod[b, 0:1, :]).astype(BF16)
    small[b, 0:1, :] = col_sum(d_normed)
    small[b, 1:2, :] = col_sum(d_normed * normed)
    d_in[rows, :] = (norm_back(d_normed, mod[b, 1:2, :], normed, inverse) + d_mid).astype(d_in.dtype)


def attention_weight_grads(normed_low, d_qkv, att, d_br, g_qkv, g_proj):
    model = g_proj.shape[0]
    for c in range(3):
        cols = slice(c * model, (c + 1) * model)
        g_qkv[:, cols] = dot_cols(normed_low[...], d_qkv[:, cols]).astype(BF16)
    g_proj[...] = dot_cols(att[...], d_br[...]).astype(BF16)


def each_sample(count, body):
    def step(b, carry):
        body(b)
        return carry

    lax.fori_loop(0, count, step, 0)


def add_table(scores, index, out):
    heads, length = scores.shape[0], scores.shape[1]
    low_ids = lax.broadcasted_iota(jnp.int32, (LOW, length), 0)
    high_ids = lax.broadcasted_iota(jnp.int32, (HIGH, length), 0)

    def step(i, carry):
        rows = pl.ds(pl.multiple_of(i * 16, 16), 16)
        entries = index[rows, :]
        block = [scores[head, rows, :].astype(F32) for head in range(heads)]
        total = carry
        for r in range(16):
            entry = entries[r : r + 1, :]
            low = jnp.where(low_ids == (entry & (LOW - 1)), 1.0, 0.0).astype(BF16)
            high = high_ids == (entry >> LOW_BITS)
            left = jnp.concatenate([jnp.where(high, part[r : r + 1, :], 0.0) for part in block], axis=0).astype(BF16)
            total = total + dot_rows(left, low)
        return total

    total = lax.fori_loop(0, length // 16, step, jnp.zeros((heads * HIGH, LOW), F32))
    out[...] = jnp.concatenate([total[head * HIGH : (head + 1) * HIGH] for head in range(heads)], axis=1)


def table_kernel(scores, index, *rest):
    add_table(scores, index, rest[-1])


def table_gradient(scores, index, earlier):
    heads = scores.shape[0]
    return pl.pallas_call(
        table_kernel,
        out_shape=jax.ShapeDtypeStruct((HIGH, heads * LOW), F32),
        in_specs=[pl.BlockSpec(memory_space=pltpu.VMEM)] * 2 + [pl.BlockSpec(memory_space=pl.ANY)] * len(earlier),
        out_specs=pl.BlockSpec(memory_space=pltpu.VMEM),
        cost_estimate=cost(8),
        compiler_params=pltpu.CompilerParams(vmem_limit_bytes=VMEM_BYTES),
    )(scores, index, *earlier)


def small_kernel(pos, scores, index, small_a0, small_m0, small_a1, small_m1, table1, *rest):
    keep, send, table = rest[-3:]
    size = small_a0.shape[0] * small_a0.shape[1]
    add_table(scores, index, table)
    parts = (
        (small_a0[...], small_m0[...], table[...]),
        (small_a1[...], small_m1[...], table1[...]),
    )
    rows = [
        jnp.concatenate([x[0].reshape(size, -1), x[1].reshape(size, -1), x[2]], axis=0) for x in parts
    ]

    @pl.when(pos[0] == 0)
    def _():
        keep[...] = rows[0]
        send[...] = rows[1].astype(BF16)

    @pl.when(pos[0] == 1)
    def _():
        keep[...] = rows[1]
        send[...] = rows[0].astype(BF16)


def small_step(pos, scores, index, smalls, table1, earlier):
    samples, _, model = smalls[0].shape
    shape = (16 * samples + HIGH, model)
    return call(
        small_kernel, pos, (scores, index, *smalls, table1), earlier, [(shape, F32), (shape, BF16)],
        [((HIGH, model), F32)], work=8,
    )


def set_line(line, layer, section, own_line, other_line):
    line[...] = jnp.where(section == layer, own_line[...], other_line[...])


def start_bias(layer, section, own, other, bias, sem):
    one = pltpu.make_async_copy(own, bias, sem)
    two = pltpu.make_async_copy(other, bias, sem)
    pl.when(section == layer)(one.start)
    pl.when(section != layer)(two.start)
    return one


def line_biases(line, samples, model):
    q_bias = bias_at(line, samples, model, 0, 1)
    v_bias = bias_at(line, samples, model, 1, 1)
    b_qkv = jnp.concatenate([q_bias, jnp.zeros_like(q_bias), v_bias], axis=1)
    return b_qkv, bias_at(line, samples, model, 2, 1), bias_at(line, samples, model, 3, 4), bias_at(line, samples, model, 7, 1)


def forward_kernel(layer, length, n_weights, n_after, pos, h, own_line, other_line, own_bias, other_bias, *rest):
    refs, rest = rest[:n_weights], rest[n_weights + n_after :]
    (qkv, probs, att, branch, middle, act, slope, out_branch, layer_out,
     w_qkv, w_proj, w_fc1, w_fc2, bias, line, sems) = rest
    section, shard = pos[0], pos[1]
    model = h.shape[1]
    samples = h.shape[0] // length
    got_bias = start_bias(layer, section, own_bias, other_bias, bias, sems.at[weight_count(n_weights)])
    for_attention, for_mlp = weight_loads(layer, section, shard, refs, (w_qkv, w_proj, w_fc1, w_fc2), sems)
    set_line(line, layer, section, own_line, other_line)
    mod = Modulation(line, model)
    b_qkv, b_proj, b_fc1, b_fc2 = line_biases(line, samples, model)
    got_bias.wait()
    wait_all(for_attention)
    each_sample(
        samples,
        lambda b: attention_forward(b, length, h, mod, bias, w_qkv, w_proj, b_qkv, b_proj, qkv, probs, att, branch, middle),
    )
    wait_all(for_mlp)
    each_sample(
        samples,
        lambda b: mlp_forward(b, length, middle, mod, w_fc1, w_fc2, b_fc1, b_fc2, act, slope, out_branch, layer_out),
    )


def both_kernel(layer, pieces, length, n_weights, n_after, pos, h, grad, own_line, other_line, own_bias, other_bias, *rest):
    refs, rest = rest[:n_weights], rest[n_weights + n_after :]
    (layer_out, d_in, small_a, small_m, scores, keep, send,
     w_qkv, w_proj, w_fc1, w_fc2, bias, line, qkv, probs, att, branch, middle, act, slope, out_branch,
     d_middle, normed_low, d_pre, d_ob, d_qkv, score_sum, g_qkv, g_proj, g_fc1, g_fc2, sems) = rest
    section, shard = pos[0], pos[1]
    model = h.shape[1]
    samples = h.shape[0] // length
    got_bias = start_bias(layer, section, own_bias, other_bias, bias, sems.at[weight_count(n_weights)])
    for_attention, for_mlp = weight_loads(layer, section, shard, refs, (w_qkv, w_proj, w_fc1, w_fc2), sems)
    set_line(line, layer, section, own_line, other_line)
    mod = Modulation(line, model)
    b_qkv, b_proj, b_fc1, b_fc2 = line_biases(line, samples, model)
    got_bias.wait()
    wait_all(for_attention)
    each_sample(
        samples,
        lambda b: attention_forward(b, length, h, mod, bias, w_qkv, w_proj, b_qkv, b_proj, qkv, probs, att, branch, middle),
    )
    wait_all(for_mlp)

    def mlp(b):
        mlp_forward(b, length, middle, mod, w_fc1, w_fc2, b_fc1, b_fc2, act, slope, out_branch, layer_out)
        mlp_backward(b, length, grad, middle, mod, w_fc1, w_fc2, act, slope, out_branch, d_middle, small_m, normed_low, d_pre, d_ob)

    each_sample(samples, mlp)
    mlp_weight_grads(normed_low, d_pre, act, d_ob, g_fc1, g_fc2)
    pack_mlp((keep, send), section, g_fc1, g_fc2, shard, pieces, 6, 2)
    score_sum[...] = jnp.zeros_like(score_sum)
    each_sample(
        samples,
        lambda b: attention_backward(b, length, h, mod, w_qkv, w_proj, qkv, probs, att, branch, d_middle, d_in, small_a, score_sum, normed_low, d_qkv, d_ob),
    )
    scores[...] = score_sum[...].astype(BF16)
    attention_weight_grads(normed_low, d_qkv, att, d_ob, g_qkv, g_proj)
    pack_attention((keep, send), section, g_qkv, g_proj, shard, pieces, 6, 0)
    rows = slice(keep.shape[0], keep.shape[0] + h.shape[0])

    @pl.when(section == 0)
    def _():
        send[rows, :] = layer_out[...]

    @pl.when(section == 1)
    def _():
        send[rows, :] = h[...]


def backward_mlp_kernel(layer, pieces, length, n_weights, n_after, pos, grad, middle, own_line, other_line, act, slope, out_branch, *rest):
    refs, rest = rest[:n_weights], rest[n_weights + n_after :]
    (d_middle, small, keep, send,
     w_qkv, w_proj, w_fc1, w_fc2, line, normed_low, d_pre, d_ob, g_fc1, g_fc2, sems) = rest
    section, shard = pos[0], pos[1]
    for_attention, for_mlp = weight_loads(layer, section, shard, refs, (w_qkv, w_proj, w_fc1, w_fc2), sems)
    set_line(line, layer, section, own_line, other_line)
    mod = Modulation(line, middle.shape[1])
    wait_all(for_mlp)
    each_sample(
        middle.shape[0] // length,
        lambda b: mlp_backward(b, length, grad, middle, mod, w_fc1, w_fc2, act, slope, out_branch, d_middle, small, normed_low, d_pre, d_ob),
    )
    mlp_weight_grads(normed_low, d_pre, act, d_ob, g_fc1, g_fc2)
    pack_mlp((keep, send), section, g_fc1, g_fc2, shard, pieces, 4, 0)
    wait_all(for_attention)


def backward_attention_kernel(layer, pieces, length, n_weights, n_after, pos, h, own_line, other_line, qkv, probs, att, branch, d_middle, d_h1, *rest):
    refs, rest = rest[:n_weights], rest[n_weights + n_after :]
    (d_in, small, scores, keep, send,
     w_qkv, w_proj, w_fc1, w_fc2, line, normed_low, d_qkv, d_br, score_sum, g_qkv, g_proj, sems) = rest
    section, shard = pos[0], pos[1]
    for_attention, for_mlp = weight_loads(layer, section, shard, refs, (w_qkv, w_proj, w_fc1, w_fc2), sems)
    set_line(line, layer, section, own_line, other_line)
    mod = Modulation(line, h.shape[1])
    score_sum[...] = jnp.zeros_like(score_sum)
    wait_all(for_attention)
    each_sample(
        h.shape[0] // length,
        lambda b: attention_backward(b, length, h, mod, w_qkv, w_proj, qkv, probs, att, branch, d_middle, d_in, small, score_sum, normed_low, d_qkv, d_br),
    )
    scores[...] = score_sum[...].astype(BF16)
    attention_weight_grads(normed_low, d_qkv, att, d_br, g_qkv, g_proj)
    pack_attention((keep, send), section, g_qkv, g_proj, shard, pieces, 2, 0)
    rows = slice(keep.shape[0], keep.shape[0] + h.shape[0])

    @pl.when(section == 0)
    def _():
        send[rows, :] = d_h1[...]

    @pl.when(section == 1)
    def _():
        send[rows, :] = d_in[...].astype(BF16)

    wait_all(for_mlp)


def cost(gigaflop):
    return pl.CostEstimate(flops=int(gigaflop * 1e9), bytes_accessed=0, transcendentals=0)


def call(kernel, pos, operands, in_hbm, outs, scratch, sems=0, work=2):
    specs = [pl.BlockSpec(memory_space=pltpu.SMEM)]
    specs += [pl.BlockSpec(memory_space=pltpu.VMEM) for _ in operands]
    specs += [pl.BlockSpec(memory_space=pl.ANY) for _ in in_hbm]
    shapes = [pltpu.VMEM(shape, dtype) for shape, dtype in scratch]
    if sems:
        shapes.append(pltpu.SemaphoreType.DMA((sems,)))
    return pl.pallas_call(
        kernel,
        out_shape=[jax.ShapeDtypeStruct(shape, dtype) for shape, dtype in outs],
        in_specs=specs,
        out_specs=[pl.BlockSpec(memory_space=pltpu.VMEM) for _ in outs],
        scratch_shapes=shapes,
        cost_estimate=cost(work),
        compiler_params=pltpu.CompilerParams(vmem_limit_bytes=VMEM_BYTES),
    )(pos, *operands, *in_hbm)


class Sizes:
    def __init__(self, samples, length, model, heads, hidden, pieces):
        self.samples, self.length, self.model = samples, length, model
        self.heads, self.hidden, self.pieces = heads, hidden, pieces
        self.rows = samples * length
        self.line = ((1, (6 * samples + 4 + hidden // model) * model), F32)
        self.weights = [
            ((model, 3 * model), BF16), ((model, model), BF16), ((model, hidden), BF16), ((hidden, model), BF16),
        ]
        self.bias = ((heads, length, length), BF16)
        self.probs = ((samples, heads, length, length), BF16)
        self.low = ((self.rows, model), BF16)
        self.full = ((self.rows, model), F32)
        self.qkv = ((self.rows, 3 * model), BF16)
        self.wide = ((self.rows, hidden), BF16)
        self.small = ((samples, 8, model), F32)

    def pack(self, blocks, more=0):
        return [((blocks * self.model, self.model), BF16), ((blocks * self.model + more, self.model), BF16)]


def forward_layer(layer, z, pos, h, lines, biases, weights, earlier):
    return call(
        functools.partial(forward_kernel, layer, z.length, len(weights), len(earlier)),
        pos, (h, *lines), (*biases, *weights, *earlier),
        [z.qkv, z.probs, z.low, z.full, z.full, z.wide, z.wide, z.full, z.low],
        [*z.weights, z.bias, z.line], weight_count(len(weights)) + 1, work=15,
    )


def both_ways(layer, z, pos, h, grad, lines, biases, weights, earlier):
    return call(
        functools.partial(both_kernel, layer, z.pieces, z.length, len(weights), len(earlier)),
        pos, (h, grad, *lines), (*biases, *weights, *earlier),
        [z.low, z.low, z.small, z.small, z.bias, *z.pack(6, z.rows)],
        [*z.weights, z.bias, z.line, z.qkv, z.probs, z.low, z.full, z.full, z.wide, z.wide, z.full,
         z.full, z.low, z.wide, z.low, z.qkv, (z.bias[0], F32), *z.weights],
        weight_count(len(weights)) + 1, work=25,
    )


def backward_mlp(layer, z, pos, grad, middle, lines, act, slope, out_branch, weights, earlier):
    return call(
        functools.partial(backward_mlp_kernel, layer, z.pieces, z.length, len(weights), len(earlier)),
        pos, (grad, middle, *lines, act, slope, out_branch), (*weights, *earlier),
        [z.full, z.small, *z.pack(4)],
        [*z.weights, z.line, z.low, z.wide, z.low, *z.weights[2:]],
        weight_count(len(weights)), work=12,
    )


def backward_attention(layer, z, pos, h, lines, qkv, probs, att, branch, d_middle, d_h1, weights, earlier):
    return call(
        functools.partial(backward_attention_kernel, layer, z.pieces, z.length, len(weights), len(earlier)),
        pos, (h, *lines, qkv, probs, att, branch, d_middle, d_h1), (*weights, *earlier),
        [z.full, z.small, z.bias, *z.pack(2, z.rows)],
        [*z.weights, z.line, z.low, z.qkv, z.low, (z.bias[0], F32), *z.weights[:2]],
        weight_count(len(weights)), work=13,
    )


def partial_kernel(pos, w_ada, cond_a, cond_b, cond_c, cond_d, b_ada, b_qv, b_proj, b_fc1, b_fc2, *rest):
    outs, whole = rest[-5:-1], rest[-1]
    shard = pos[1]
    q, wide = w_ada.shape
    samples, model = cond_a.shape
    whole[...] = jnp.zeros_like(whole)
    whole[pl.ds(pl.multiple_of(shard * q, 16), q), :] = w_ada[...]
    for cond, out in zip((cond_a, cond_b, cond_c, cond_d), outs):
        c = cond[...].astype(F32)
        act = (c * (1.0 / (1.0 + jnp.exp(-c)))).astype(BF16)
        out[:, :wide] = dot(act, whole[...])
        out[:, wide:] = jnp.zeros((samples, 2 * model), F32)
        for f in range(4):
            @pl.when(shard == f)
            def _():
                here = slice(f * b_ada.shape[1], (f + 1) * b_ada.shape[1])
                out[:, here] += b_ada[...].astype(F32)
                for bias, row, at in ((b_qv, 0, 0), (b_proj, 1, 0), (b_fc1, 1, model), (b_fc2, 3, model)):
                    width = bias.shape[1]
                    at += f * width
                    row, at = row + at // (2 * model), wide + at % (2 * model)
                    out[row : row + 1, at : at + width] = bias[...].astype(F32)


def partial_step(pos, w_ada, conds, biases, earlier):
    q, wide = w_ada.shape
    samples, model = conds[0].shape
    return call(
        partial_kernel, pos, (w_ada, *conds, *biases), earlier, [((samples, wide + 2 * model), F32)] * 4,
        [((4 * q, wide), BF16)],
    )


def line_kernel(pos, own, got_a, got_b, got_c, keep, send, total):
    section = pos[0]
    samples = own.shape[0]
    each = samples // 2
    model = own.shape[1] // 8
    total[...] = (own[...] + got_a[...]) + (got_b[...] + got_c[...])
    for out, side in ((keep, section), (send, 1 - section)):
        for b in range(each):
            out[:, b * 6 * model : (b + 1) * 6 * model] = total[pl.ds(side * each + b, 1), : 6 * model]
        for row in range(samples):
            at = (6 * each + 2 * row) * model
            out[:, at : at + 2 * model] = total[row : row + 1, 6 * model :]


def line_step(pos, own, got):
    samples, model = own.shape[0], own.shape[1] // 8
    shape = (1, (3 * samples + 8) * model)
    return call(line_kernel, pos, (own, *got), (), [(shape, F32)] * 2, [(own.shape, F32)])


def plane_kernel(samples, pos, keep, other, kept_small, other_small, cond, own, own_small, *rest):
    messages, work = rest[:3], rest[3]
    section = pos[0]
    size, model = own.shape
    for p in range(4):
        rows = slice(p * size, (p + 1) * size)
        total = keep[rows, :].astype(F32) + other[rows, :].astype(F32)
        if p == 0:
            own[...] = total
        else:
            messages[p - 1][:size, :] = total.astype(BF16)
    theirs = other_small[...].astype(F32)
    mine = kept_small[...]
    each = samples // 2
    work[...] = jnp.zeros_like(work)
    for b in range(each):
        for kind in range(6):
            row = b * 8 + kind if kind < 3 else (each + b) * 8 + kind - 3
            work[pl.ds(kind * samples + section * each + b, 1), :] = mine[row : row + 1, :]
            work[pl.ds(kind * samples + (1 - section) * each + b, 1), :] = theirs[row : row + 1, :]
    work[6 * samples : 7 * samples, :] = cond[...].astype(F32)
    both = mine + theirs
    bias_rows = sum(both[(each + b) * 8 + 3 : (each + b) * 8 + 8, :] for b in range(each))
    more_rows = sum(both[b * 8 + 3 : b * 8 + 6, :] for b in range(each))
    at = 7 * samples
    work[at : at + 5, :] = bias_rows
    work[at + 5 : at + 8, :] = more_rows
    work[at + 8 : at + 8 + HIGH, :] = both[2 * each * 8 :, :]
    small = work[...].astype(BF16)
    own_small[...] = small
    for message in messages:
        message[size:, :] = small


def plane_step(pos, keep, other, kept_small, other_small, cond):
    samples, model = cond.shape
    size = keep.shape[0] // 4
    small = -(-(7 * samples + 8 + HIGH) // 16) * 16
    outs = [((size, model), F32), ((small, model), BF16)] + [((size + small, model), BF16)] * 3
    return call(
        functools.partial(plane_kernel, samples), pos, (keep, other, kept_small, other_small, cond), (), outs,
        [((small, model), F32)],
    )


def column_kernel(samples, pos, own, own_small, got_a, got_b, got_c, part, own_out, *rest):
    messages, work = rest[:3], rest[3]
    rank = pos[2]
    size, model = own.shape
    n = size // 4
    got = (got_a, got_b, got_c)
    for j in range(4):
        at = pl.multiple_of((rank ^ j) * n, 16)
        total = own[pl.ds(at, n), :]
        for piece in got:
            total = total + piece[pl.ds(at, n), :].astype(F32)
        if j == 0:
            part[...] = total
        else:
            messages[j - 1][:n, :] = total.astype(BF16)
    smalls = [own_small[...].astype(F32)] + [piece[size:, :].astype(F32) for piece in got]
    work[...] = jnp.zeros_like(work)
    for p in range(4):
        for kind in range(7):
            at = (kind * 4 + p) * samples
            work[at : at + samples, :] = smalls[p][kind * samples : (kind + 1) * samples, :]
    at = 7 * samples
    summed = (smalls[0] + smalls[1]) + (smalls[2] + smalls[3])
    work[4 * at : 4 * at + 8 + HIGH, :] = summed[at : at + 8 + HIGH, :]
    small = work[...].astype(BF16)
    own_out[...] = small
    for message in messages:
        message[n:, :] = small


def column_step(pos, own, own_small, got, samples):
    size, model = own.shape
    small = -(-(28 * samples + 8 + HIGH) // 16) * 16
    outs = [((size // 4, model), F32), ((small, model), BF16)] + [((size // 4 + small, model), BF16)] * 3
    return call(
        functools.partial(column_kernel, samples), pos, (own, own_small, *got), (), outs, [((small, model), F32)]
    )


def finish_kernel(samples, width, pos, own_small, got_a, got_b, got_c, g_ada, g_b_ada, summed, work, whole):
    shard, rank = pos[1], pos[2]
    model = own_small.shape[1]
    each = 4 * samples
    n = got_a.shape[0] - own_small.shape[0]
    pieces = [own_small[...]] + [piece[n:, :] for piece in (got_a, got_b, got_c)]
    for j in range(4):
        for kind in range(7):
            at = pl.multiple_of(kind * 4 * each + (rank ^ j) * each, 16)
            work[pl.ds(at, each), :] = pieces[j][kind * each : (kind + 1) * each, :].astype(F32)
    cond = work[24 * each :, :]
    act = (cond * (1.0 / (1.0 + jnp.exp(-cond)))).astype(BF16)
    for kind in range(6):
        rows = work[kind * 4 * each : (kind + 1) * 4 * each, :]
        whole[...] = dot_cols(act, rows.astype(BF16))
        cols = slice(kind * model, (kind + 1) * model)
        g_ada[:, cols] = whole[pl.ds(pl.multiple_of(shard * width, 16), width), :]
        g_b_ada[:, cols] = col_sum(rows)
    at = 7 * each
    rows = [piece[at : at + 8 + HIGH, :].astype(F32) for piece in pieces]
    summed[...] = (rows[0] + rows[1]) + (rows[2] + rows[3])


def finish_step(pos, own_small, got, samples, width):
    model = own_small.shape[1]
    return call(
        functools.partial(finish_kernel, samples, width), pos, (own_small, *got), (),
        [((width, 6 * model), F32), ((1, 6 * model), F32), ((8 + HIGH, model), F32)],
        [((7 * 16 * samples, model), F32), ((model, model), F32)],
    )


def cond_kernel(samples, pos, small, cond, *rest):
    out, w_ada = rest[-2:]
    model = cond.shape[1]
    for p, piece in enumerate(rest[:-2]):
        q = piece.shape[0]
        off = pl.multiple_of((pos[1] ^ p) * q, 16) if q < model else 0
        w_ada[pl.ds(off, q), :] = piece[...]
    total = None
    for kind in range(6):
        rows = small[...].astype(F32)[kind * samples : (kind + 1) * samples, :].astype(BF16)
        part = dot_rows(rows, w_ada[:, kind * model : (kind + 1) * model])
        total = part if total is None else total + part
    c = cond[...].astype(F32)
    gate = 1.0 / (1.0 + jnp.exp(-c))
    out[...] = total * (gate * (1.0 + c * (1.0 - gate)))


def cond_step(pos, small, w_ada, cond):
    model = cond.shape[1]
    return call(
        functools.partial(cond_kernel, cond.shape[0]), pos, (small, cond, *w_ada), (), [(cond.shape, F32)],
        [((model, w_ada[0].shape[1]), BF16)],
    )[0]


def final_kernel(pos, own_a, own_m, other, g_qkv, g_proj, g_fc1, g_fc2):
    section = pos[0]
    q, model = g_proj.shape
    cut = own_a.shape[0]

    def write(first_a, first_m, second_a, second_m):
        for c in range(2):
            g_qkv[:, c * model : (c + 1) * model] = first_a[c * q : (c + 1) * q, :].astype(F32)
        g_qkv[:, 2 * model : 3 * model] = second_a[:q, :].astype(F32)
        g_proj[...] = second_a[q : 2 * q, :].astype(F32)
        for c in range(4):
            g_fc1[:, c * model : (c + 1) * model] = first_m[c * q : (c + 1) * q, :].astype(F32)
        g_fc2[...] = second_m[...].astype(F32)

    other_a, other_m = other.at[:cut, :], other.at[cut:, :]

    @pl.when(section == 0)
    def _():
        write(own_a, own_m, other_a, other_m)

    @pl.when(section == 1)
    def _():
        write(other_a, other_m, own_a, own_m)


def final_step(pos, own_a, own_m, other):
    q, model = own_a.shape[0] // 2, own_a.shape[1]
    return call(
        final_kernel, pos, (own_a, own_m, other), (),
        [((q, 3 * model), F32), ((q, model), F32), ((q, 4 * model), F32), ((4 * q, model), F32)], [],
    )


def halve_kernel(pos, own, got_a, got_b, got_c, keep, send):
    bit = pos[2] & 1
    n = own.shape[0] // 4
    for high in range(2):
        for out, low in ((keep, bit), (send, 1 - bit)):
            rows = pl.ds(pl.multiple_of((2 * high + low) * n, 16), n)
            total = own[rows, :]
            for piece in (got_a, got_b, got_c):
                total = total + piece[rows, :].astype(F32)
            out[high * n : (high + 1) * n, :] = total.astype(out.dtype)


def halve_step(pos, own, got):
    shape = (own.shape[0] // 2, own.shape[1])
    return call(halve_kernel, pos, (own, *got), (), [(shape, F32), (shape, BF16)], [])


def quarter_kernel(pos, kept, got, keep, send):
    bit = pos[2] >> 1
    n = kept.shape[0] // 2
    for out, high in ((keep, bit), (send, 1 - bit)):
        rows = pl.ds(pl.multiple_of(high * n, 16), n)
        out[...] = (kept[rows, :] + got[rows, :].astype(F32)).astype(out.dtype)


def quarter_step(pos, kept, got):
    shape = (kept.shape[0] // 2, kept.shape[1])
    return call(quarter_kernel, pos, (kept, got), (), [(shape, F32), (shape, BF16)], [])


def pack_kernel(pos, qkv, proj, fc1, fc2, out):
    q, model = proj.shape
    for c in range(3):
        out[c * q : (c + 1) * q, :] = qkv[:, c * model : (c + 1) * model]
    out[3 * q : 4 * q, :] = proj[...]
    for c in range(4):
        out[(4 + c) * q : (5 + c) * q, :] = fc1[:, c * model : (c + 1) * model]
    out[8 * q : 12 * q, :] = fc2[...]


def pack_shard(pos, own):
    q, model = own[1].shape
    return call(pack_kernel, pos, own, (), [((12 * q, model), BF16)], [])[0]


def after(values, others):
    return pl.pallas_call(
        lambda *refs: None,
        out_shape=[jax.ShapeDtypeStruct(v.shape, v.dtype) for v in values],
        in_specs=[pl.BlockSpec(memory_space=pl.ANY)] * (len(values) + len(others)),
        out_specs=[pl.BlockSpec(memory_space=pl.ANY)] * len(values),
        input_output_aliases={i: i for i in range(len(values))},
    )(*values, *others)


def lookup_kernel(table, index, *rest):
    out, work = rest[-2:]
    heads, length = out.shape[0], out.shape[1]
    high_count = table.shape[0] // 8
    values = table[...]
    low_id = lax.broadcasted_iota(jnp.int32, (LOW, length), 0)

    def step(i, carry):
        block = index[pl.ds(pl.multiple_of(i * 8, 8), 8), :]
        for r in range(8):
            entry = block[r : r + 1, :]
            picks = jnp.where(low_id == (entry & (LOW - 1)), 1.0, 0.0).astype(BF16)
            found = dot(values, picks).reshape(high_count, 8, length)
            high = jnp.broadcast_to(entry >> LOW_BITS, (8, length))
            bit = high_count // 2
            while bit:
                chosen = (high & bit) != 0
                found = jnp.where(chosen[None], found[bit : 2 * bit], found[:bit])
                bit //= 2
            for head in range(heads):
                work[head, pl.ds(i * 8 + r, 1), :] = found[0, head : head + 1, :]
        return carry

    lax.fori_loop(0, length // 8, step, 0)
    out[...] = work[...].astype(BF16)


def lookup(table, index, earlier):
    heads, entries = table.shape
    high_count = HIGH
    padded = jnp.pad(table, ((0, 8 - heads), (0, high_count * LOW - entries)))
    rows = jnp.transpose(padded.reshape(8, high_count, LOW), (1, 0, 2)).reshape(high_count * 8, LOW)
    length = index.shape[0]
    return pl.pallas_call(
        lookup_kernel,
        out_shape=jax.ShapeDtypeStruct((heads, length, length), BF16),
        in_specs=[pl.BlockSpec(memory_space=pltpu.VMEM)] * 2 + [pl.BlockSpec(memory_space=pl.ANY)] * len(earlier),
        out_specs=pl.BlockSpec(memory_space=pltpu.VMEM),
        scratch_shapes=[pltpu.VMEM((heads, length, length), F32)],
        cost_estimate=cost(11),
        compiler_params=pltpu.CompilerParams(vmem_limit_bytes=VMEM_BYTES),
    )(rows, index, *earlier)


def swap_section(value):
    return lax.ppermute(value, "section", [(0, 1), (1, 0)])


def pairs_of(count, step):
    return [(i, i ^ step) for i in range(count)]


def by_rank(pieces, rank):
    stack = jnp.stack(pieces)
    count = len(pieces)
    bit = 1
    while bit < count:
        moved = jnp.stack([stack[i ^ bit] for i in range(count)])
        stack = jnp.where((rank & bit) != 0, moved, stack)
        bit *= 2
    return stack


def section_sums(keep, other, shards):
    size = keep.shape[0] // shards
    return [
        keep[p * size : (p + 1) * size].astype(F32) + other[p * size : (p + 1) * size].astype(F32)
        for p in range(shards)
    ]


def low_pieces(sums):
    return [x.astype(BF16) for x in sums[1:]]


def to_peers(messages, axis):
    count = lax.axis_size(axis)
    return [lax.ppermute(messages[p - 1], axis, pairs_of(count, p)) for p in range(1, count)]


def add_pieces(own, got):
    total = own
    for piece in got:
        total = total + piece.astype(F32)
    return total


def replica_parts(total, rank):
    replicas = lax.axis_size("rep")
    parts = total if total.ndim == 3 else total.reshape(replicas, total.shape[0] // replicas, -1)
    low = parts.astype(BF16)
    mine = lax.dynamic_index_in_dim(parts, rank, 0, keepdims=False)
    return mine, [lax.dynamic_index_in_dim(low, rank ^ j, 0, keepdims=False) for j in range(1, replicas)]


def unpack_attention(pack):
    q = pack.shape[0] // 4
    return jnp.concatenate([pack[c * q : (c + 1) * q] for c in range(3)], axis=1), pack[3 * q :]


def unpack_mlp(pack):
    q = pack.shape[0] // 8
    return jnp.concatenate([pack[c * q : (c + 1) * q] for c in range(4)], axis=1), pack[4 * q :]


def pad_rows(value):
    return jnp.pad(value, ((0, -value.shape[0] % 16), (0, 0)))


def from_peers(value, axis):
    return [lax.ppermute(value, axis, pairs_of(lax.axis_size(axis), p)) for p in range(1, lax.axis_size(axis))]


def pair_sum(values):
    while len(values) > 1:
        values = [values[i] + values[i + 1] for i in range(0, len(values), 2)]
    return values[0]


def per_device(inputs, conditioning, cotangent, micro_sizes, relative_bias_index,
               w_ada, w_qkv, w_proj, w_fc1, w_fc2, b_ada, b_qv, b_proj, b_fc1, b_fc2, bias_table):
    section = lax.axis_index("section")
    shard = lax.axis_index("fsdp")
    rank = lax.axis_index("rep")
    shards, replicas = lax.axis_size("fsdp"), lax.axis_size("rep")
    direct = shards == 4 and replicas == 4
    is_first = section == 0
    samples, length, model = inputs.shape
    heads, entries = bias_table.shape[1:]
    half = samples // 2
    z = Sizes(half, length, model, heads, 4 * model, shards if direct else 1)
    pos = jnp.stack([section, shard, rank]).astype(jnp.int32)

    def mine(first, second):
        return jnp.where(is_first, first, second)

    def own_samples(array):
        return lax.dynamic_slice_in_dim(array, section * half, half, 0)

    def in_order(own, other):
        return jnp.where(is_first, jnp.concatenate([own, other]), jnp.concatenate([other, own]))

    live = (jnp.arange(half)[:, None, None] < lax.dynamic_index_in_dim(micro_sizes[0], section, 0)).astype(BF16)
    h0 = own_samples(inputs).reshape(half * length, model)
    grad1 = (own_samples(cotangent) * live).reshape(half * length, model)
    own_raw = [w_qkv[0], w_proj[0], w_fc1[0], w_fc2[0]]
    width = model // shards
    if direct:
        conds = [conditioning] + from_peers(conditioning, "fsdp")
        own_pack = pack_shard(pos, own_raw)
        middle_row = own_pack.shape[0] // 2
        got_x = lax.ppermute(own_pack, "fsdp", pairs_of(shards, 1))
        got_y = lax.ppermute(own_pack, "fsdp", pairs_of(shards, 2))
        bias_own = lookup(bias_table[0], relative_bias_index, [own_pack, h0, grad1])
        partial = partial_step(pos, w_ada[0], conds, (b_ada, b_qv, b_proj, b_fc1, b_fc2), [bias_own])
        got_first = lax.ppermute(got_x[:middle_row], "fsdp", pairs_of(shards, 2))
        got_second = lax.ppermute(got_y[middle_row:], "fsdp", pairs_of(shards, 1))
        own_weights = [own_pack, got_x, got_y, got_first, got_second]
        weights = own_weights + [swap_section(w) for w in own_weights]
        own_line, send_line = line_step(pos, partial[0], after(to_peers(partial[1:], "fsdp"), [got_x, got_y]))
    else:
        row = jnp.concatenate([b_ada, b_qv, b_proj, b_fc1, b_fc2], axis=1)
        bias_rows = lax.all_gather(row[0], "fsdp", axis=0)
        whole = [lax.all_gather(w, "fsdp", axis=0, tiled=True) for w in own_raw]
        own_whole = pack_shard(pos, whole)
        weights = [own_whole, swap_section(own_whole)]
        acts = jax.nn.silu(conditioning.astype(F32)).astype(BF16)
        modulation = dot(acts, lax.all_gather(w_ada[0], "fsdp", axis=0, tiled=True))
        bias_own = lookup(bias_table[0], relative_bias_index, [])
        cuts = [b_ada.shape[1], b_qv.shape[1], b_proj.shape[1], b_fc1.shape[1], b_fc2.shape[1]]
        biases, at = [], 0
        for cut in cuts:
            biases.append(bias_rows[:, at : at + cut].reshape(1, -1).astype(F32))
            at += cut
        modulation = modulation + biases[0]
        other_samples = lax.dynamic_slice_in_dim(modulation, (1 - section) * half, half, 0)
        own_line = jnp.concatenate([own_samples(modulation).reshape(1, -1)] + biases[1:], axis=1)
        send_line = jnp.concatenate([other_samples.reshape(1, -1)] + biases[1:], axis=1)
    lines = (own_line, swap_section(send_line))
    bias_heads = (bias_own, swap_section(bias_own))

    if direct:
        w_ada_later = after([w_ada[0]], weights[3:5])[0]
        w_ada_pieces = [w_ada_later] + from_peers(w_ada_later, "fsdp")
    else:
        w_ada_pieces = [lax.all_gather(w_ada[0], "fsdp", axis=0, tiled=True)]
    qkv, probs, att, branch, middle, act, slope, out_branch, h1 = forward_layer(0, z, pos, h0, lines, bias_heads, weights, w_ada_pieces[:1] if direct else [])
    out1, d_h1, small_a1, small_m1, scores1, keep1, send1 = both_ways(1, z, pos, h1, grad1, lines, bias_heads, weights, w_ada_pieces[1:])
    d_middle, small_m0, keep_m0, send_m0 = backward_mlp(0, z, pos, d_h1, middle, lines, act, slope, out_branch, weights, [])
    pieces = z.pieces
    rows = half * length
    other1 = swap_section(send1)
    sums1 = section_sums(keep1, other1[: keep1.shape[0]], pieces)
    low1 = low_pieces(sums1)
    table1 = table_gradient(scores1, relative_bias_index, low1)
    other_m0 = after([swap_section(send_m0)], [table1])[0]
    sums_m0 = section_sums(keep_m0, other_m0, pieces)
    low_m0 = low_pieces(sums_m0)
    if direct:
        got1 = after(to_peers(low1, "fsdp"), [table1, *low_m0])
        keep_z1, send_z1 = halve_step(pos, sums1[0], got1)
        earlier = [table1, *low_m0, send_z1]
    else:
        earlier = [table1, *low_m0]
    d_h0, small_a0, scores0, keep_a0, send_a0 = backward_attention(
        0, z, pos, h0, lines, qkv, probs, att, branch, d_middle, d_h1, weights, earlier
    )
    smalls = (small_a0, small_m0, small_a1, small_m1)
    size_a = keep_a0.shape[0]

    def replica(value, step):
        return lax.ppermute(value, "rep", pairs_of(replicas, step))

    def ordered(own, other, bit):
        return jnp.where(bit == 0, jnp.concatenate([own, other]), jnp.concatenate([other, own]))

    if direct:
        got_z1, *got_m0 = after([replica(send_z1, 1), *to_peers(low_m0, "fsdp")], [d_h0])
        other_a0 = swap_section(after([send_a0], [got_z1, *got_m0])[0])
        keep_z1, send_z1 = quarter_step(pos, keep_z1, got_z1)
        keep_zm, send_zm = halve_step(pos, sums_m0[0], got_m0)
        kept_small, send_small = small_step(pos, scores0, relative_bias_index, smalls, table1, [send_z1, send_zm])
        other_small = swap_section(send_small)
        other_a0, got_z1, got_zm = after([other_a0, replica(send_z1, 2), replica(send_zm, 1)], [kept_small])
        own_a0, own_small, *messages = plane_step(pos, keep_a0, other_a0, kept_small, other_small, conditioning)
        got = to_peers(messages, "fsdp")
        got_z1, got_zm = after([got_z1, got_zm], [own_small])
        quarter1 = (keep_z1 + got_z1.astype(F32)).astype(BF16)
        keep_zm, send_zm = quarter_step(pos, keep_zm, got_zm)
        cond_part = cond_step(pos, after([own_small], [send_zm, quarter1])[0], w_ada_pieces, conditioning)
        part0, plane_small, *messages = column_step(pos, own_a0, own_small, got, samples)
        got_z1, got_zm = after([replica(quarter1, 2), replica(send_zm, 2)], [plane_small])
        got = to_peers(messages, "rep")
        size = part0.shape[0]
        high, low = rank >> 1, rank & 1

        def by_low(pair):
            n = pair.shape[0] // 2
            both = ordered(pair.reshape(1, 2, n, model), replica(pair, 1).reshape(1, 2, n, model), low)
            return jnp.transpose(both, (1, 0, 2, 3)).reshape(-1, model)

        half1 = by_low(ordered(quarter1, got_z1, high))
        quarter_m = (keep_zm + got_zm.astype(F32)).astype(BF16)
        pair_m = ordered(quarter_m, replica(quarter_m, 2), high)
        quarter0 = add_pieces(part0, [x[:size] for x in got]).astype(BF16)
        half_m0 = by_low(pair_m)
        half_a0 = by_rank([quarter0] + from_peers(quarter0, "rep"), rank).reshape(-1, model)
        g_ada, g_b_ada, summed = finish_step(pos, plane_small, got, samples, width)
        g_b_ada = g_b_ada[0]
    else:
        other_a0 = swap_section(send_a0)
        kept_small, send_small = small_step(pos, scores0, relative_bias_index, smalls, table1, [])
        theirs = swap_section(send_small).astype(F32)
        both = kept_small + theirs
        cut = half * 8

        def d_mod_of(values):
            a, m = values[:cut].reshape(half, 8, model), values[cut : 2 * cut].reshape(half, 8, model)
            return jnp.concatenate([a[:, :3], m[:, :3]], axis=1)

        low = in_order(d_mod_of(kept_small), d_mod_of(theirs)).astype(BF16)
        bias_rows = jnp.sum(both[: 2 * cut].reshape(2, half, 8, model), axis=1)
        summed = jnp.concatenate([bias_rows[1, 3:8], bias_rows[0, 3:6], both[2 * cut :]])
        cond_part = cond_step(pos, jnp.transpose(low, (1, 0, 2)).reshape(-1, model), w_ada_pieces, conditioning)
        kept = jnp.concatenate([low, conditioning[:, None]], axis=1)
        kept = lax.all_gather(kept, ("fsdp", "rep"), axis=0, tiled=True)
        summed = lax.psum(summed, ("fsdp", "rep"))
        act_all = jax.nn.silu(kept[:, 6].astype(F32)).astype(BF16)
        act_cols = lax.dynamic_slice_in_dim(act_all, shard * width, width, 1)
        g_ada = jnp.concatenate([dot_cols(act_cols, kept[:, i]) for i in range(6)], axis=1)
        g_b_ada = jnp.sum(kept[:, :6].astype(F32), axis=0).reshape(-1)
        sums_a0 = section_sums(keep_a0, other_a0[:size_a], pieces)
        half_a0, half_m0, half1 = sums_a0[0].astype(BF16), sums_m0[0].astype(BF16), sums1[0].astype(BF16)
    cond_grad = cond_part + swap_section(cond_part)
    cut = half_a0.shape[0]
    half_a1, half_m1 = half1[:cut], half1[cut:]
    grads = final_step(
        pos, mine(half_a0, half_a1), mine(half_m0, half_m1),
        swap_section(mine(jnp.concatenate([half_a1, half_m1]), jnp.concatenate([half_a0, half_m0]))),
    )
    if not direct:
        grads = [lax.psum_scatter(g.astype(BF16), "fsdp", scatter_dimension=0, tiled=True) for g in grads]
        grads = [g.astype(F32) for g in lax.psum(tuple(grads), "rep")]
    g_qkv, g_proj, g_fc1, g_fc2 = grads

    activations = in_order(
        mine(h1, out1).reshape(half, length, model), other1[keep1.shape[0] :].reshape(half, length, model)
    )
    input_grads = in_order(
        mine(d_h0, d_h1.astype(F32)).reshape(half, length, model),
        other_a0[size_a : size_a + rows].astype(F32).reshape(half, length, model),
    )

    g_b_fc2, g_b_fc1 = summed[0], summed[1:5].reshape(-1)
    g_b_qv, g_b_proj = summed[5:7].reshape(-1), summed[7]
    g_table = jnp.transpose(summed[8:].reshape(HIGH, heads, LOW), (1, 0, 2)).reshape(heads, HIGH * LOW)[:, :entries]

    def own_part(vector):
        size = vector.shape[0] // shards
        return lax.dynamic_slice_in_dim(vector, shard * size, size, 0)[None]

    return (
        activations[None], input_grads[None], cond_grad,
        g_ada[None], g_qkv[None], g_proj[None], g_fc1[None], g_fc2[None],
        own_part(g_b_ada), own_part(g_b_qv), own_part(g_b_proj), own_part(g_b_fc1), own_part(g_b_fc2),
        g_table[None],
    )


def solution(mesh):
    batch = ("fsdp", "rep")
    matrix = P("section", "fsdp", None)
    vector = P("section", "fsdp")
    return jax.shard_map(
        per_device,
        mesh=mesh,
        in_specs=(
            P(batch, None, None), P(batch, None), P(batch, None, None), P(batch, None), P(),
            matrix, matrix, matrix, matrix, matrix, vector, vector, vector, vector, vector,
            P("section", None, None),
        ),
        out_specs=(
            P("section", batch, None, None), P("section", batch, None, None), P(batch, None),
            matrix, matrix, matrix, matrix, matrix, vector, vector, vector, vector, vector,
            P("section", None, None),
        ),
        check_vma=False,
    )
```

```python
import functools

import jax
import jax.numpy as jnp
from jax import lax
from jax.experimental import pallas as pl
from jax.experimental.pallas import tpu as pltpu
from jax.sharding import PartitionSpec as P

EPSILON = 1e-06
F32 = jnp.float32
BF16 = jnp.bfloat16
VMEM_BYTES = 58 * 1024 * 1024
LOW_BITS = 6
LOW = 1 << LOW_BITS
HIGH = 16


def dot(a, b):
    return jnp.dot(a, b, preferred_element_type=F32)


def dot_rows(a, b):
    return lax.dot_general(a, b, (((1,), (1,)), ((), ())), preferred_element_type=F32)


def dot_cols(a, b):
    return lax.dot_general(a, b, (((0,), (0,)), ((), ())), preferred_element_type=F32)


def norm_parts(v):
    centre = v - jnp.mean(v, axis=-1, keepdims=True)
    inverse = lax.rsqrt(jnp.mean(centre * centre, axis=-1, keepdims=True) + EPSILON)
    return centre * inverse, inverse


def norm_back(d_normed, scale, normed, inverse):
    d = d_normed * (1.0 + scale)
    return inverse * (
        d
        - jnp.mean(d, axis=-1, keepdims=True)
        - normed * jnp.mean(d * normed, axis=-1, keepdims=True)
    )


def col_sum(v):
    return jnp.sum(v, axis=0, keepdims=True)


def half_masks(width):
    lane = lax.broadcasted_iota(jnp.int32, (1, width), 1)
    first = jnp.where(lane < width // 2, 1.0, 0.0)
    return first.astype(BF16), (1.0 - first).astype(BF16)


def block_targets(mats, off, q):
    w_qkv, w_proj, w_fc1, w_fc2 = mats
    model = w_proj.shape[0]
    targets = [w_qkv.at[pl.ds(off, q), pl.ds(c * model, model)] for c in range(3)]
    targets.append(w_proj.at[pl.ds(off, q), :])
    targets += [w_fc1.at[pl.ds(off, q), pl.ds(c * model, model)] for c in range(4)]
    targets.append(w_fc2.at[pl.ds(off * 4, 4 * q), :])
    return targets


def weight_count(refs):
    return 9 if refs == 2 else 36


def weight_loads(layer, section, shard, refs, mats, sems):
    model = mats[1].shape[0]
    plans = []
    if len(refs) == 2:
        for i, target in enumerate(block_targets(mats, 0, model)):
            rows = pl.ds(i * model, 4 * model if i == 8 else model)
            plans.append((refs[0].at[rows, :], refs[1].at[rows, :], target, i < 4))
    else:
        count = len(refs) // 2
        q = refs[0].shape[0] // 12
        for p in range(4):
            targets = block_targets(mats, pl.multiple_of((shard ^ p) * q, 16), q)
            for i, target in enumerate(targets):
                which, at = p, i
                if p == 3 and i >= 6:
                    which, at = 4, i - 6
                rows = pl.ds(at * q, 4 * q if i == 8 else q)
                plans.append((refs[which].at[rows, :], refs[count + which].at[rows, :], target, i < 4))
    ones = [pltpu.make_async_copy(x[0], x[2], sems.at[i]) for i, x in enumerate(plans)]
    twos = [pltpu.make_async_copy(x[1], x[2], sems.at[i]) for i, x in enumerate(plans)]

    @pl.when(section == layer)
    def _():
        for copy in ones:
            copy.start()

    @pl.when(section != layer)
    def _():
        for copy in twos:
            copy.start()

    return (
        [copy for copy, x in zip(ones, plans) if x[3]],
        [copy for copy, x in zip(ones, plans) if not x[3]],
    )


def wait_all(copies):
    for copy in copies:
        copy.wait()


def put_half(refs, section, half, at, value):
    keep, send = refs
    rows = slice(at, at + value.shape[0])

    @pl.when(section == half)
    def _():
        keep[rows, :] = value

    @pl.when(section != half)
    def _():
        send[rows, :] = value


def pack_attention(refs, section, g_qkv, g_proj, shard, pieces, stride, first):
    model = g_proj.shape[0]
    q = model // pieces
    for p in range(pieces):
        off = pl.multiple_of((shard ^ p) * q, 16) if pieces > 1 else 0
        at = (stride * p + first) * q
        for c in range(3):
            value = g_qkv[pl.ds(off, q), c * model : (c + 1) * model]
            put_half(refs, section, c // 2, at + (c % 2) * q, value)
        put_half(refs, section, 1, at + q, g_proj[pl.ds(off, q), :])


def pack_mlp(refs, section, g_fc1, g_fc2, shard, pieces, stride, first):
    model = g_fc1.shape[0]
    q = model // pieces
    for p in range(pieces):
        off = pl.multiple_of((shard ^ p) * q, 16) if pieces > 1 else 0
        at = (stride * p + first) * q
        for c in range(4):
            value = g_fc1[pl.ds(off, q), c * model : (c + 1) * model]
            put_half(refs, section, 0, at + c * q, value)
        put_half(refs, section, 1, at, g_fc2[pl.ds(pl.multiple_of(off * 4, 16), 4 * q), :])


class Modulation:
    def __init__(self, line, model):
        self.line, self.model = line, model

    def __getitem__(self, key):
        b, rows, _ = key
        return self.line[:, pl.ds(pl.multiple_of((6 * b + rows.start) * self.model, 128), self.model)]


def bias_at(line, samples, model, start, size):
    return line[:, (6 * samples + start) * model : (6 * samples + start + size) * model]


def attention_forward(b, length, h, mod, bias, w_qkv, w_proj, b_qkv, b_proj, qkv, probs, att, branch, middle):
    model = w_proj.shape[0]
    heads = bias.shape[0]
    pair = 2 * model // heads
    rows = pl.ds(pl.multiple_of(b * length, length), length)
    masks = half_masks(pair)
    x = h[rows, :].astype(F32)
    normed, _ = norm_parts(x)
    normed_low = (normed * (1.0 + mod[b, 1:2, :]) + mod[b, 0:1, :]).astype(BF16)
    qkv[rows, :] = (dot(normed_low, w_qkv[...]) + b_qkv[...]).astype(BF16)
    for j in range(heads // 2):
        q_pair = qkv[rows, j * pair : (j + 1) * pair] * BF16((pair // 2) ** (-0.5))
        k_pair = qkv[rows, model + j * pair : model + (j + 1) * pair]
        v_pair = qkv[rows, 2 * model + j * pair : 2 * model + (j + 1) * pair]
        total = None
        for e in range(2):
            scores = dot_rows(q_pair * masks[e], k_pair) + bias[2 * j + e].astype(F32)
            raised = jnp.exp(scores - jnp.max(scores, axis=-1, keepdims=True))
            p = (raised * (1.0 / jnp.sum(raised, axis=-1, keepdims=True))).astype(BF16)
            probs[b, 2 * j + e] = p
            part = dot(p, v_pair * masks[e])
            total = part if total is None else total + part
        att[rows, j * pair : (j + 1) * pair] = total.astype(BF16)
    out = dot(att[rows, :], w_proj[...]) + b_proj[...]
    branch[rows, :] = out
    middle[rows, :] = x + mod[b, 2:3, :] * out


def mlp_forward(b, length, middle, mod, w_fc1, w_fc2, b_fc1, b_fc2, act, slope, out_branch, layer_out):
    model = w_fc1.shape[0]
    rows = pl.ds(pl.multiple_of(b * length, length), length)
    mid = middle[rows, :]
    normed, _ = norm_parts(mid)
    normed_low = (normed * (1.0 + mod[b, 4:5, :]) + mod[b, 3:4, :]).astype(BF16)
    total = b_fc2[...]
    for c in range(w_fc1.shape[1] // model):
        cols = slice(c * model, (c + 1) * model)
        v = dot(normed_low, w_fc1[:, cols]) + b_fc1[:, cols]
        square = v * v
        t = jnp.tanh(0.7978845608028654 * v * (1.0 + 0.044715 * square))
        half = 0.5 * (1.0 + t)
        a = (v * half).astype(BF16)
        act[rows, cols] = a
        slope[rows, cols] = (
            half
            + 0.5 * v * (1.0 - t * t) * (0.7978845608028654 + (3 * 0.044715 * 0.7978845608028654) * square)
        ).astype(BF16)
        total = total + dot(a, w_fc2[cols, :])
    out_branch[rows, :] = total
    layer_out[rows, :] = (mid + mod[b, 5:6, :] * total).astype(layer_out.dtype)


def mlp_backward(b, length, grad, middle, mod, w_fc1, w_fc2, act, slope, out_branch, d_middle, small, normed_low, d_pre, d_ob):
    model = w_fc1.shape[0]
    rows = pl.ds(pl.multiple_of(b * length, length), length)
    g = grad[rows, :].astype(F32)
    small[b, 2:3, :] = col_sum(g * out_branch[rows, :])
    d_out = g * mod[b, 5:6, :]
    d_out_low = d_out.astype(BF16)
    d_ob[rows, :] = d_out_low
    small[b, 3:4, :] = col_sum(d_out_low.astype(F32))
    normed, inverse = norm_parts(middle[rows, :])
    normed_low[rows, :] = (normed * (1.0 + mod[b, 4:5, :]) + mod[b, 3:4, :]).astype(BF16)
    d_normed = None
    for c in range(w_fc1.shape[1] // model):
        cols = slice(c * model, (c + 1) * model)
        d_act = dot_rows(d_out_low, w_fc2[cols, :])
        d_low = (d_act * slope[rows, cols].astype(F32)).astype(BF16)
        d_pre[rows, cols] = d_low
        small[b, 4 + c : 5 + c, :] = col_sum(d_low.astype(F32))
        part = dot_rows(d_low, w_fc1[:, cols])
        d_normed = part if d_normed is None else d_normed + part
    small[b, 0:1, :] = col_sum(d_normed)
    small[b, 1:2, :] = col_sum(d_normed * normed)
    d_middle[rows, :] = norm_back(d_normed, mod[b, 4:5, :], normed, inverse) + g


def mlp_weight_grads(normed_low, d_pre, act, d_ob, g_fc1, g_fc2):
    model = g_fc1.shape[0]
    for c in range(g_fc1.shape[1] // model):
        cols = slice(c * model, (c + 1) * model)
        g_fc1[:, cols] = dot_cols(normed_low[...], d_pre[:, cols]).astype(BF16)
        g_fc2[cols, :] = dot_cols(act[:, cols], d_ob[...]).astype(BF16)


def attention_backward(b, length, h, mod, w_qkv, w_proj, qkv, probs, att, branch, d_middle, d_in, small, score_sum, normed_low, d_qkv, d_br):
    model = w_proj.shape[0]
    heads = probs.shape[1]
    pair = 2 * model // heads
    scale = F32((pair // 2) ** (-0.5))
    rows = pl.ds(pl.multiple_of(b * length, length), length)
    masks = half_masks(pair)
    d_mid = d_middle[rows, :]
    small[b, 2:3, :] = col_sum(d_mid * branch[rows, :])
    d_branch = (d_mid * mod[b, 2:3, :]).astype(BF16)
    d_br[rows, :] = d_branch
    small[b, 5:6, :] = col_sum(d_branch.astype(F32))
    d_att = dot_rows(d_branch, w_proj[...]).astype(BF16)
    for j in range(heads // 2):
        q_pair = qkv[rows, j * pair : (j + 1) * pair]
        k_pair = qkv[rows, model + j * pair : model + (j + 1) * pair]
        v_pair = qkv[rows, 2 * model + j * pair : 2 * model + (j + 1) * pair]
        d_pair = d_att[:, j * pair : (j + 1) * pair]
        d_q = d_k = d_v = None
        for e in range(2):
            p_low = probs[b, 2 * j + e]
            p = p_low.astype(F32)
            d_here = d_pair * masks[e]
            d_p = dot_rows(d_here, v_pair)
            d_s = (p * (d_p - jnp.sum(d_p * p, axis=-1, keepdims=True))).astype(BF16)
            score_sum[2 * j + e] += d_s.astype(F32)
            v_part = dot_cols(p_low, d_here)
            q_part = dot(d_s, k_pair * masks[e])
            k_part = dot_cols(d_s, q_pair * masks[e])
            d_v = v_part if d_v is None else d_v + v_part
            d_q = q_part if d_q is None else d_q + q_part
            d_k = k_part if d_k is None else d_k + k_part
        d_qkv[rows, j * pair : (j + 1) * pair] = (d_q * scale).astype(BF16)
        d_qkv[rows, model + j * pair : model + (j + 1) * pair] = (d_k * scale).astype(BF16)
        d_qkv[rows, 2 * model + j * pair : 2 * model + (j + 1) * pair] = d_v.astype(BF16)
    small[b, 3:4, :] = col_sum(d_qkv[rows, :model].astype(F32))
    small[b, 4:5, :] = col_sum(d_qkv[rows, 2 * model :].astype(F32))
    small[b, 6:8, :] = jnp.zeros((2, model), F32)
    d_normed = dot_rows(d_qkv[rows, :], w_qkv[...])
    normed, inverse = norm_parts(h[rows, :].astype(F32))
    normed_low[rows, :] = (normed * (1.0 + mod[b, 1:2, :]) + mod[b, 0:1, :]).astype(BF16)
    small[b, 0:1, :] = col_sum(d_normed)
    small[b, 1:2, :] = col_sum(d_normed * normed)
    d_in[rows, :] = (norm_back(d_normed, mod[b, 1:2, :], normed, inverse) + d_mid).astype(d_in.dtype)


def attention_weight_grads(normed_low, d_qkv, att, d_br, g_qkv, g_proj):
    model = g_proj.shape[0]
    for c in range(3):
        cols = slice(c * model, (c + 1) * model)
        g_qkv[:, cols] = dot_cols(normed_low[...], d_qkv[:, cols]).astype(BF16)
    g_proj[...] = dot_cols(att[...], d_br[...]).astype(BF16)


def each_sample(count, body):
    def step(b, carry):
        body(b)
        return carry

    lax.fori_loop(0, count, step, 0)


def add_tables(all_scores, index, outs):
    heads, length = all_scores[0].shape[0], all_scores[0].shape[1]
    low_ids = lax.broadcasted_iota(jnp.int32, (LOW, length), 0)
    high_ids = lax.broadcasted_iota(jnp.int32, (HIGH, length), 0)
    count = len(all_scores) * heads

    def step(i, carry):
        rows = pl.ds(pl.multiple_of(i * 16, 16), 16)
        entries = index[rows, :]
        block = [scores[head, rows, :].astype(F32) for scores in all_scores for head in range(heads)]
        total = carry
        for r in range(16):
            entry = entries[r : r + 1, :]
            low = jnp.where(low_ids == (entry & (LOW - 1)), 1.0, 0.0).astype(BF16)
            high = high_ids == (entry >> LOW_BITS)
            left = jnp.concatenate([jnp.where(high, part[r : r + 1, :], 0.0) for part in block], axis=0).astype(BF16)
            total = total + dot_rows(left, low)
        return total

    total = lax.fori_loop(0, length // 16, step, jnp.zeros((count * HIGH, LOW), F32))
    parts = [total[i * HIGH : (i + 1) * HIGH] for i in range(count)]
    for layer, out in enumerate(outs):
        out[...] = jnp.concatenate(parts[layer * heads : (layer + 1) * heads], axis=1)


def small_kernel(pos, scores0, scores1, index, small_a0, small_m0, small_a1, small_m1, *rest):
    keep, send, table0, table1 = rest[-4:]
    size = small_a0.shape[0] * small_a0.shape[1]
    add_tables((scores0, scores1), index, (table0, table1))
    parts = (
        (small_a0[...], small_m0[...], table0[...]),
        (small_a1[...], small_m1[...], table1[...]),
    )
    rows = [
        jnp.concatenate([x[0].reshape(size, -1), x[1].reshape(size, -1), x[2]], axis=0) for x in parts
    ]

    @pl.when(pos[0] == 0)
    def _():
        keep[...] = rows[0]
        send[...] = rows[1].astype(BF16)

    @pl.when(pos[0] == 1)
    def _():
        keep[...] = rows[1]
        send[...] = rows[0].astype(BF16)


def small_step(pos, scores0, scores1, index, smalls, earlier):
    samples, _, model = smalls[0].shape
    shape = (16 * samples + HIGH, model)
    return call(
        small_kernel, pos, (scores0, scores1, index, *smalls), earlier, [(shape, F32), (shape, BF16)],
        [((HIGH, model), F32)] * 2, work=12,
    )


def set_line(line, layer, section, own_line, other_line):
    line[...] = jnp.where(section == layer, own_line[...], other_line[...])


def start_bias(layer, section, own, other, bias, sem):
    one = pltpu.make_async_copy(own, bias, sem)
    two = pltpu.make_async_copy(other, bias, sem)
    pl.when(section == layer)(one.start)
    pl.when(section != layer)(two.start)
    return one


def line_biases(line, samples, model):
    q_bias = bias_at(line, samples, model, 0, 1)
    v_bias = bias_at(line, samples, model, 1, 1)
    b_qkv = jnp.concatenate([q_bias, jnp.zeros_like(q_bias), v_bias], axis=1)
    return b_qkv, bias_at(line, samples, model, 2, 1), bias_at(line, samples, model, 3, 4), bias_at(line, samples, model, 7, 1)


def forward_kernel(layer, length, n_weights, n_after, pos, h, own_line, other_line, own_bias, other_bias, *rest):
    refs, rest = rest[:n_weights], rest[n_weights + n_after :]
    (qkv, probs, att, branch, middle, act, slope, out_branch, layer_out,
     w_qkv, w_proj, w_fc1, w_fc2, bias, line, sems) = rest
    section, shard = pos[0], pos[1]
    model = h.shape[1]
    samples = h.shape[0] // length
    got_bias = start_bias(layer, section, own_bias, other_bias, bias, sems.at[weight_count(n_weights)])
    for_attention, for_mlp = weight_loads(layer, section, shard, refs, (w_qkv, w_proj, w_fc1, w_fc2), sems)
    set_line(line, layer, section, own_line, other_line)
    mod = Modulation(line, model)
    b_qkv, b_proj, b_fc1, b_fc2 = line_biases(line, samples, model)
    got_bias.wait()
    wait_all(for_attention)
    each_sample(
        samples,
        lambda b: attention_forward(b, length, h, mod, bias, w_qkv, w_proj, b_qkv, b_proj, qkv, probs, att, branch, middle),
    )
    wait_all(for_mlp)
    each_sample(
        samples,
        lambda b: mlp_forward(b, length, middle, mod, w_fc1, w_fc2, b_fc1, b_fc2, act, slope, out_branch, layer_out),
    )


def both_kernel(layer, pieces, length, n_weights, n_after, pos, h, grad, own_line, other_line, own_bias, other_bias, *rest):
    refs, rest = rest[:n_weights], rest[n_weights + n_after :]
    (layer_out, d_in, small_a, small_m, scores, keep, send,
     w_qkv, w_proj, w_fc1, w_fc2, bias, line, qkv, probs, att, branch, middle, act, slope, out_branch,
     d_middle, normed_low, d_pre, d_ob, d_qkv, score_sum, g_qkv, g_proj, g_fc1, g_fc2, sems) = rest
    section, shard = pos[0], pos[1]
    model = h.shape[1]
    samples = h.shape[0] // length
    got_bias = start_bias(layer, section, own_bias, other_bias, bias, sems.at[weight_count(n_weights)])
    for_attention, for_mlp = weight_loads(layer, section, shard, refs, (w_qkv, w_proj, w_fc1, w_fc2), sems)
    set_line(line, layer, section, own_line, other_line)
    mod = Modulation(line, model)
    b_qkv, b_proj, b_fc1, b_fc2 = line_biases(line, samples, model)
    got_bias.wait()
    wait_all(for_attention)
    each_sample(
        samples,
        lambda b: attention_forward(b, length, h, mod, bias, w_qkv, w_proj, b_qkv, b_proj, qkv, probs, att, branch, middle),
    )
    wait_all(for_mlp)

    def mlp(b):
        mlp_forward(b, length, middle, mod, w_fc1, w_fc2, b_fc1, b_fc2, act, slope, out_branch, layer_out)
        mlp_backward(b, length, grad, middle, mod, w_fc1, w_fc2, act, slope, out_branch, d_middle, small_m, normed_low, d_pre, d_ob)

    each_sample(samples, mlp)
    mlp_weight_grads(normed_low, d_pre, act, d_ob, g_fc1, g_fc2)
    pack_mlp((keep, send), section, g_fc1, g_fc2, shard, pieces, 6, 2)
    score_sum[...] = jnp.zeros_like(score_sum)
    each_sample(
        samples,
        lambda b: attention_backward(b, length, h, mod, w_qkv, w_proj, qkv, probs, att, branch, d_middle, d_in, small_a, score_sum, normed_low, d_qkv, d_ob),
    )
    scores[...] = score_sum[...].astype(BF16)
    attention_weight_grads(normed_low, d_qkv, att, d_ob, g_qkv, g_proj)
    pack_attention((keep, send), section, g_qkv, g_proj, shard, pieces, 6, 0)
    rows = slice(keep.shape[0], keep.shape[0] + h.shape[0])

    @pl.when(section == 0)
    def _():
        send[rows, :] = layer_out[...]

    @pl.when(section == 1)
    def _():
        send[rows, :] = h[...]


def backward_mlp_kernel(layer, pieces, length, n_weights, n_after, pos, grad, middle, own_line, other_line, act, slope, out_branch, *rest):
    refs, rest = rest[:n_weights], rest[n_weights + n_after :]
    (d_middle, small, keep, send,
     w_qkv, w_proj, w_fc1, w_fc2, line, normed_low, d_pre, d_ob, g_fc1, g_fc2, sems) = rest
    section, shard = pos[0], pos[1]
    for_attention, for_mlp = weight_loads(layer, section, shard, refs, (w_qkv, w_proj, w_fc1, w_fc2), sems)
    set_line(line, layer, section, own_line, other_line)
    mod = Modulation(line, middle.shape[1])
    wait_all(for_mlp)
    each_sample(
        middle.shape[0] // length,
        lambda b: mlp_backward(b, length, grad, middle, mod, w_fc1, w_fc2, act, slope, out_branch, d_middle, small, normed_low, d_pre, d_ob),
    )
    mlp_weight_grads(normed_low, d_pre, act, d_ob, g_fc1, g_fc2)
    pack_mlp((keep, send), section, g_fc1, g_fc2, shard, pieces, 4, 0)
    wait_all(for_attention)


def backward_attention_kernel(layer, pieces, length, n_weights, n_after, pos, h, own_line, other_line, qkv, probs, att, branch, d_middle, d_h1, *rest):
    refs, rest = rest[:n_weights], rest[n_weights + n_after :]
    (d_in, small, scores, keep, send,
     w_qkv, w_proj, w_fc1, w_fc2, line, normed_low, d_qkv, d_br, score_sum, g_qkv, g_proj, sems) = rest
    section, shard = pos[0], pos[1]
    for_attention, for_mlp = weight_loads(layer, section, shard, refs, (w_qkv, w_proj, w_fc1, w_fc2), sems)
    set_line(line, layer, section, own_line, other_line)
    mod = Modulation(line, h.shape[1])
    score_sum[...] = jnp.zeros_like(score_sum)
    wait_all(for_attention)
    each_sample(
        h.shape[0] // length,
        lambda b: attention_backward(b, length, h, mod, w_qkv, w_proj, qkv, probs, att, branch, d_middle, d_in, small, score_sum, normed_low, d_qkv, d_br),
    )
    scores[...] = score_sum[...].astype(BF16)
    attention_weight_grads(normed_low, d_qkv, att, d_br, g_qkv, g_proj)
    pack_attention((keep, send), section, g_qkv, g_proj, shard, pieces, 2, 0)
    rows = slice(keep.shape[0], keep.shape[0] + h.shape[0])

    @pl.when(section == 0)
    def _():
        send[rows, :] = d_h1[...]

    @pl.when(section == 1)
    def _():
        send[rows, :] = d_in[...].astype(BF16)

    wait_all(for_mlp)


def cost(gigaflop):
    return pl.CostEstimate(flops=int(gigaflop * 1e9), bytes_accessed=0, transcendentals=0)


def call(kernel, pos, operands, in_hbm, outs, scratch, sems=0, work=2):
    specs = [pl.BlockSpec(memory_space=pltpu.SMEM)]
    specs += [pl.BlockSpec(memory_space=pltpu.VMEM) for _ in operands]
    specs += [pl.BlockSpec(memory_space=pl.ANY) for _ in in_hbm]
    shapes = [pltpu.VMEM(shape, dtype) for shape, dtype in scratch]
    if sems:
        shapes.append(pltpu.SemaphoreType.DMA((sems,)))
    return pl.pallas_call(
        kernel,
        out_shape=[jax.ShapeDtypeStruct(shape, dtype) for shape, dtype in outs],
        in_specs=specs,
        out_specs=[pl.BlockSpec(memory_space=pltpu.VMEM) for _ in outs],
        scratch_shapes=shapes,
        cost_estimate=cost(work),
        compiler_params=pltpu.CompilerParams(vmem_limit_bytes=VMEM_BYTES),
    )(pos, *operands, *in_hbm)


class Sizes:
    def __init__(self, samples, length, model, heads, hidden, pieces):
        self.samples, self.length, self.model = samples, length, model
        self.heads, self.hidden, self.pieces = heads, hidden, pieces
        self.rows = samples * length
        self.line = ((1, (6 * samples + 4 + hidden // model) * model), F32)
        self.weights = [
            ((model, 3 * model), BF16), ((model, model), BF16), ((model, hidden), BF16), ((hidden, model), BF16),
        ]
        self.bias = ((heads, length, length), BF16)
        self.probs = ((samples, heads, length, length), BF16)
        self.low = ((self.rows, model), BF16)
        self.full = ((self.rows, model), F32)
        self.qkv = ((self.rows, 3 * model), BF16)
        self.wide = ((self.rows, hidden), BF16)
        self.small = ((samples, 8, model), F32)

    def pack(self, blocks, more=0):
        return [((blocks * self.model, self.model), BF16), ((blocks * self.model + more, self.model), BF16)]


def forward_layer(layer, z, pos, h, lines, biases, weights, earlier):
    return call(
        functools.partial(forward_kernel, layer, z.length, len(weights), len(earlier)),
        pos, (h, *lines), (*biases, *weights, *earlier),
        [z.qkv, z.probs, z.low, z.full, z.full, z.wide, z.wide, z.full, z.low],
        [*z.weights, z.bias, z.line], weight_count(len(weights)) + 1, work=15,
    )


def both_ways(layer, z, pos, h, grad, lines, biases, weights, earlier):
    return call(
        functools.partial(both_kernel, layer, z.pieces, z.length, len(weights), len(earlier)),
        pos, (h, grad, *lines), (*biases, *weights, *earlier),
        [z.low, z.low, z.small, z.small, z.bias, *z.pack(6, z.rows)],
        [*z.weights, z.bias, z.line, z.qkv, z.probs, z.low, z.full, z.full, z.wide, z.wide, z.full,
         z.full, z.low, z.wide, z.low, z.qkv, (z.bias[0], F32), *z.weights],
        weight_count(len(weights)) + 1, work=25,
    )


def backward_mlp(layer, z, pos, grad, middle, lines, act, slope, out_branch, weights, earlier):
    return call(
        functools.partial(backward_mlp_kernel, layer, z.pieces, z.length, len(weights), len(earlier)),
        pos, (grad, middle, *lines, act, slope, out_branch), (*weights, *earlier),
        [z.full, z.small, *z.pack(4)],
        [*z.weights, z.line, z.low, z.wide, z.low, *z.weights[2:]],
        weight_count(len(weights)), work=12,
    )


def backward_attention(layer, z, pos, h, lines, qkv, probs, att, branch, d_middle, d_h1, weights, earlier):
    return call(
        functools.partial(backward_attention_kernel, layer, z.pieces, z.length, len(weights), len(earlier)),
        pos, (h, *lines, qkv, probs, att, branch, d_middle, d_h1), (*weights, *earlier),
        [z.full, z.small, z.bias, *z.pack(2, z.rows)],
        [*z.weights, z.line, z.low, z.qkv, z.low, (z.bias[0], F32), *z.weights[:2]],
        weight_count(len(weights)), work=13,
    )


def partial_kernel(pos, w_ada, cond_a, cond_b, cond_c, cond_d, b_ada, b_qv, b_proj, b_fc1, b_fc2, *rest):
    outs, whole = rest[-5:-1], rest[-1]
    shard = pos[1]
    q, wide = w_ada.shape
    samples, model = cond_a.shape
    whole[...] = jnp.zeros_like(whole)
    whole[pl.ds(pl.multiple_of(shard * q, 16), q), :] = w_ada[...]
    for cond, out in zip((cond_a, cond_b, cond_c, cond_d), outs):
        c = cond[...].astype(F32)
        act = (c * (1.0 / (1.0 + jnp.exp(-c)))).astype(BF16)
        out[:, :wide] = dot(act, whole[...])
        out[:, wide:] = jnp.zeros((samples, 2 * model), F32)
        for f in range(4):
            @pl.when(shard == f)
            def _():
                here = slice(f * b_ada.shape[1], (f + 1) * b_ada.shape[1])
                out[:, here] += b_ada[...].astype(F32)
                for bias, row, at in ((b_qv, 0, 0), (b_proj, 1, 0), (b_fc1, 1, model), (b_fc2, 3, model)):
                    width = bias.shape[1]
                    at += f * width
                    row, at = row + at // (2 * model), wide + at % (2 * model)
                    out[row : row + 1, at : at + width] = bias[...].astype(F32)


def partial_step(pos, w_ada, conds, biases, earlier):
    q, wide = w_ada.shape
    samples, model = conds[0].shape
    return call(
        partial_kernel, pos, (w_ada, *conds, *biases), earlier, [((samples, wide + 2 * model), F32)] * 4,
        [((4 * q, wide), BF16)],
    )


def line_kernel(pos, own, got_a, got_b, got_c, keep, send, total):
    section = pos[0]
    samples = own.shape[0]
    each = samples // 2
    model = own.shape[1] // 8
    total[...] = (own[...] + got_a[...]) + (got_b[...] + got_c[...])
    for out, side in ((keep, section), (send, 1 - section)):
        for b in range(each):
            out[:, b * 6 * model : (b + 1) * 6 * model] = total[pl.ds(side * each + b, 1), : 6 * model]
        for row in range(samples):
            at = (6 * each + 2 * row) * model
            out[:, at : at + 2 * model] = total[row : row + 1, 6 * model :]


def line_step(pos, own, got):
    samples, model = own.shape[0], own.shape[1] // 8
    shape = (1, (3 * samples + 8) * model)
    return call(line_kernel, pos, (own, *got), (), [(shape, F32)] * 2, [(own.shape, F32)])


def first_kernel(keep1, other1, keep_m, other_m, own, *messages):
    pieces = 4
    size1, size_m = keep1.shape[0] // pieces, keep_m.shape[0] // pieces
    n1, nm = size1 // 4, size_m // 4
    for p in range(pieces):
        for k in range(4):
            at = k * (n1 + nm)
            for keep, other, first, n, to in (
                (keep1, other1, p * size1 + k * n1, n1, at), (keep_m, other_m, p * size_m + k * nm, nm, at + n1)
            ):
                total = keep[first : first + n, :].astype(F32) + other[first : first + n, :].astype(F32)
                if p == 0:
                    own[to : to + n, :] = total
                else:
                    messages[p - 1][to : to + n, :] = total.astype(BF16)


def first_step(keep1, other1, keep_m, other_m):
    shape = ((keep1.shape[0] + keep_m.shape[0]) // 4, keep1.shape[1])
    return pl.pallas_call(
        first_kernel,
        out_shape=[jax.ShapeDtypeStruct(shape, F32)] + [jax.ShapeDtypeStruct(shape, BF16)] * 3,
        compiler_params=pltpu.CompilerParams(vmem_limit_bytes=VMEM_BYTES),
    )(keep1, other1, keep_m, other_m)


def plane_kernel(samples, pos, keep, other, kept_small, other_small, cond, own, own_small, *rest):
    messages, work = rest[:3], rest[3]
    section = pos[0]
    size, model = own.shape
    for p in range(4):
        rows = slice(p * size, (p + 1) * size)
        total = keep[rows, :].astype(F32) + other[rows, :].astype(F32)
        if p == 0:
            own[...] = total
        else:
            messages[p - 1][:size, :] = total.astype(BF16)
    theirs = other_small[...].astype(F32)
    mine = kept_small[...]
    each = samples // 2
    work[...] = jnp.zeros_like(work)
    for b in range(each):
        for kind in range(6):
            row = b * 8 + kind if kind < 3 else (each + b) * 8 + kind - 3
            work[pl.ds(kind * samples + section * each + b, 1), :] = mine[row : row + 1, :]
            work[pl.ds(kind * samples + (1 - section) * each + b, 1), :] = theirs[row : row + 1, :]
    work[6 * samples : 7 * samples, :] = cond[...].astype(F32)
    both = mine + theirs
    bias_rows = sum(both[(each + b) * 8 + 3 : (each + b) * 8 + 8, :] for b in range(each))
    more_rows = sum(both[b * 8 + 3 : b * 8 + 6, :] for b in range(each))
    at = 7 * samples
    work[at : at + 5, :] = bias_rows
    work[at + 5 : at + 8, :] = more_rows
    work[at + 8 : at + 8 + HIGH, :] = both[2 * each * 8 :, :]
    small = work[...].astype(BF16)
    own_small[...] = small
    for message in messages:
        message[size:, :] = small


def plane_step(pos, keep, other, kept_small, other_small, cond):
    samples, model = cond.shape
    size = keep.shape[0] // 4
    small = -(-(7 * samples + 8 + HIGH) // 16) * 16
    outs = [((size, model), F32), ((small, model), BF16)] + [((size + small, model), BF16)] * 3
    return call(
        functools.partial(plane_kernel, samples), pos, (keep, other, kept_small, other_small, cond), (), outs,
        [((small, model), F32)],
    )


def column_kernel(samples, pos, own, own_small, got_a, got_b, got_c, part, own_out, *rest):
    messages, work = rest[:3], rest[3]
    rank = pos[2]
    size, model = own.shape
    n = size // 4
    got = (got_a, got_b, got_c)
    for j in range(4):
        at = pl.multiple_of((rank ^ j) * n, 16)
        total = own[pl.ds(at, n), :]
        for piece in got:
            total = total + piece[pl.ds(at, n), :].astype(F32)
        if j == 0:
            part[...] = total
        else:
            messages[j - 1][:n, :] = total.astype(BF16)
    smalls = [own_small[...].astype(F32)] + [piece[size:, :].astype(F32) for piece in got]
    work[...] = jnp.zeros_like(work)
    for p in range(4):
        for kind in range(7):
            at = (kind * 4 + p) * samples
            work[at : at + samples, :] = smalls[p][kind * samples : (kind + 1) * samples, :]
    at = 7 * samples
    summed = (smalls[0] + smalls[1]) + (smalls[2] + smalls[3])
    work[4 * at : 4 * at + 8 + HIGH, :] = summed[at : at + 8 + HIGH, :]
    small = work[...].astype(BF16)
    own_out[...] = small
    for message in messages:
        message[n:, :] = small


def column_step(pos, own, own_small, got, samples):
    size, model = own.shape
    small = -(-(28 * samples + 8 + HIGH) // 16) * 16
    outs = [((size // 4, model), F32), ((small, model), BF16)] + [((size // 4 + small, model), BF16)] * 3
    return call(
        functools.partial(column_kernel, samples), pos, (own, own_small, *got), (), outs, [((small, model), F32)]
    )


def finish_kernel(samples, width, pos, own_small, got_a, got_b, got_c,
                  g_ada, g_b_ada, g_b_qv, g_b_proj, g_b_fc1, g_b_fc2, g_table, work, whole, row):
    shard, rank = pos[1], pos[2]
    model = own_small.shape[1]
    each = 4 * samples
    n = got_a.shape[0] - own_small.shape[0]
    pieces = [own_small[...]] + [piece[n:, :] for piece in (got_a, got_b, got_c)]
    for j in range(4):
        for kind in range(7):
            at = pl.multiple_of(kind * 4 * each + (rank ^ j) * each, 16)
            work[pl.ds(at, each), :] = pieces[j][kind * each : (kind + 1) * each, :].astype(F32)
    cond = work[24 * each :, :]
    act = (cond * (1.0 / (1.0 + jnp.exp(-cond)))).astype(BF16)
    for kind in range(6):
        rows = work[kind * 4 * each : (kind + 1) * 4 * each, :]
        whole[...] = dot_cols(act, rows.astype(BF16))
        cols = slice(kind * model, (kind + 1) * model)
        g_ada[:, cols] = whole[pl.ds(pl.multiple_of(shard * width, 16), width), :]
        row[:, cols] = col_sum(rows)
    at = 7 * each
    rows = [piece[at : at + 8 + HIGH, :].astype(F32) for piece in pieces]
    summed = (rows[0] + rows[1]) + (rows[2] + rows[3])
    for c in range(4):
        row[:, (6 + c) * model : (7 + c) * model] = summed[1 + c : 2 + c, :]
    row[:, 10 * model : 11 * model] = summed[5:6, :]
    row[:, 11 * model : 12 * model] = summed[6:7, :]
    row[:, 12 * model : 13 * model] = summed[7:8, :]
    row[:, 13 * model : 14 * model] = summed[0:1, :]
    for f in range(4):
        @pl.when(shard == f)
        def _():
            for out, start in ((g_b_ada, 0), (g_b_fc1, 6), (g_b_qv, 10), (g_b_proj, 12), (g_b_fc2, 13)):
                size = out.shape[1]
                out[...] = row[:, start * model + f * size : start * model + (f + 1) * size]
    heads, entries = g_table.shape
    for high in range(-(-entries // LOW)):
        size = min(LOW, entries - high * LOW)
        for head in range(heads):
            g_table[head : head + 1, high * LOW : high * LOW + size] = summed[
                8 + high : 9 + high, head * LOW : head * LOW + size
            ]


def finish_step(pos, own_small, got, samples, width, heads, entries):
    model = own_small.shape[1]
    sizes = [6 * width, 2 * width, width, 4 * width, width]
    return call(
        functools.partial(finish_kernel, samples, width), pos, (own_small, *got), (),
        [((width, 6 * model), F32)] + [((1, size), F32) for size in sizes] + [((heads, entries), F32)],
        [((7 * 16 * samples, model), F32), ((model, model), F32), ((1, 14 * model), F32)],
    )


def cond_kernel(samples, pos, small, cond, *rest):
    out, w_ada = rest[-2:]
    model = cond.shape[1]
    for p, piece in enumerate(rest[:-2]):
        q = piece.shape[0]
        off = pl.multiple_of((pos[1] ^ p) * q, 16) if q < model else 0
        w_ada[pl.ds(off, q), :] = piece[...]
    total = None
    for kind in range(6):
        rows = small[...].astype(F32)[kind * samples : (kind + 1) * samples, :].astype(BF16)
        part = dot_rows(rows, w_ada[:, kind * model : (kind + 1) * model])
        total = part if total is None else total + part
    c = cond[...].astype(F32)
    gate = 1.0 / (1.0 + jnp.exp(-c))
    out[...] = total * (gate * (1.0 + c * (1.0 - gate)))


def cond_step(pos, small, w_ada, cond):
    model = cond.shape[1]
    return call(
        functools.partial(cond_kernel, cond.shape[0]), pos, (small, cond, *w_ada), (), [(cond.shape, F32)],
        [((model, w_ada[0].shape[1]), BF16)],
    )[0]


def final_kernel(pos, own_a, own_m, other, g_qkv, g_proj, g_fc1, g_fc2):
    section = pos[0]
    q, model = g_proj.shape
    cut = own_a.shape[0]

    def write(first_a, first_m, second_a, second_m):
        for c in range(2):
            g_qkv[:, c * model : (c + 1) * model] = first_a[c * q : (c + 1) * q, :].astype(F32)
        g_qkv[:, 2 * model : 3 * model] = second_a[:q, :].astype(F32)
        g_proj[...] = second_a[q : 2 * q, :].astype(F32)
        for c in range(4):
            g_fc1[:, c * model : (c + 1) * model] = first_m[c * q : (c + 1) * q, :].astype(F32)
        g_fc2[...] = second_m[...].astype(F32)

    other_a, other_m = other.at[:cut, :], other.at[cut:, :]

    @pl.when(section == 0)
    def _():
        write(own_a, own_m, other_a, other_m)

    @pl.when(section == 1)
    def _():
        write(other_a, other_m, own_a, own_m)


def final_step(pos, own_a, own_m, other):
    q, model = own_a.shape[0] // 2, own_a.shape[1]
    return call(
        final_kernel, pos, (own_a, own_m, other), (),
        [((q, 3 * model), F32), ((q, model), F32), ((q, 4 * model), F32), ((4 * q, model), F32)], [],
    )


def halve_kernel(pos, own, got_a, got_b, got_c, keep, send):
    bit = pos[2] & 1
    n = own.shape[0] // 4
    for high in range(2):
        for out, low in ((keep, bit), (send, 1 - bit)):
            rows = pl.ds(pl.multiple_of((2 * high + low) * n, 16), n)
            total = own[rows, :]
            for piece in (got_a, got_b, got_c):
                total = total + piece[rows, :].astype(F32)
            out[high * n : (high + 1) * n, :] = total.astype(out.dtype)


def halve_step(pos, own, got):
    shape = (own.shape[0] // 2, own.shape[1])
    return call(halve_kernel, pos, (own, *got), (), [(shape, F32), (shape, BF16)], [])


def quarter_kernel(pos, kept, got, keep, send):
    bit = pos[2] >> 1
    n = kept.shape[0] // 2
    for out, high in ((keep, bit), (send, 1 - bit)):
        rows = pl.ds(pl.multiple_of(high * n, 16), n)
        out[...] = (kept[rows, :] + got[rows, :].astype(F32)).astype(out.dtype)


def quarter_step(pos, kept, got):
    shape = (kept.shape[0] // 2, kept.shape[1])
    return call(quarter_kernel, pos, (kept, got), (), [(shape, F32), (shape, BF16)], [])


def pack_kernel(qkv, proj, fc1, fc2, out):
    q, model = proj.shape
    for c in range(3):
        out[c * q : (c + 1) * q, :] = qkv[:, c * model : (c + 1) * model]
    out[3 * q : 4 * q, :] = proj[...]
    for c in range(4):
        out[(4 + c) * q : (5 + c) * q, :] = fc1[:, c * model : (c + 1) * model]
    out[8 * q : 12 * q, :] = fc2[...]


def pack_shard(own):
    q, model = own[1].shape
    return pl.pallas_call(
        pack_kernel,
        out_shape=jax.ShapeDtypeStruct((12 * q, model), BF16),
        compiler_params=pltpu.CompilerParams(vmem_limit_bytes=VMEM_BYTES),
    )(*own)


def after(values, others):
    return pl.pallas_call(
        lambda *refs: None,
        out_shape=[jax.ShapeDtypeStruct(v.shape, v.dtype) for v in values],
        in_specs=[pl.BlockSpec(memory_space=pl.ANY)] * (len(values) + len(others)),
        out_specs=[pl.BlockSpec(memory_space=pl.ANY)] * len(values),
        input_output_aliases={i: i for i in range(len(values))},
    )(*values, *others)


def lookup_kernel(table, index, *rest):
    out, work = rest[-2:]
    heads, length = out.shape[0], out.shape[1]
    high_count = table.shape[0] // 8
    values = table[...]
    low_id = lax.broadcasted_iota(jnp.int32, (LOW, length), 0)

    def step(i, carry):
        block = index[pl.ds(pl.multiple_of(i * 8, 8), 8), :]
        for r in range(8):
            entry = block[r : r + 1, :]
            picks = jnp.where(low_id == (entry & (LOW - 1)), 1.0, 0.0).astype(BF16)
            found = dot(values, picks).reshape(high_count, 8, length)
            high = jnp.broadcast_to(entry >> LOW_BITS, (8, length))
            bit = high_count // 2
            while bit:
                chosen = (high & bit) != 0
                found = jnp.where(chosen[None], found[bit : 2 * bit], found[:bit])
                bit //= 2
            for head in range(heads):
                work[head, pl.ds(i * 8 + r, 1), :] = found[0, head : head + 1, :]
        return carry

    lax.fori_loop(0, length // 8, step, 0)
    out[...] = work[...].astype(BF16)


def lookup(table, index, earlier):
    heads, entries = table.shape
    high_count = HIGH
    padded = jnp.pad(table, ((0, 8 - heads), (0, high_count * LOW - entries)))
    rows = jnp.transpose(padded.reshape(8, high_count, LOW), (1, 0, 2)).reshape(high_count * 8, LOW)
    length = index.shape[0]
    return pl.pallas_call(
        lookup_kernel,
        out_shape=jax.ShapeDtypeStruct((heads, length, length), BF16),
        in_specs=[pl.BlockSpec(memory_space=pltpu.VMEM)] * 2 + [pl.BlockSpec(memory_space=pl.ANY)] * len(earlier),
        out_specs=pl.BlockSpec(memory_space=pltpu.VMEM),
        scratch_shapes=[pltpu.VMEM((heads, length, length), F32)],
        cost_estimate=cost(11),
        compiler_params=pltpu.CompilerParams(vmem_limit_bytes=VMEM_BYTES),
    )(rows, index, *earlier)


def swap_section(value):
    return lax.ppermute(value, "section", [(0, 1), (1, 0)])


def pairs_of(count, step):
    return [(i, i ^ step) for i in range(count)]


def by_rank(pieces, rank):
    stack = jnp.stack(pieces)
    count = len(pieces)
    bit = 1
    while bit < count:
        moved = jnp.stack([stack[i ^ bit] for i in range(count)])
        stack = jnp.where((rank & bit) != 0, moved, stack)
        bit *= 2
    return stack


def section_sums(keep, other, shards):
    size = keep.shape[0] // shards
    return [
        keep[p * size : (p + 1) * size].astype(F32) + other[p * size : (p + 1) * size].astype(F32)
        for p in range(shards)
    ]


def low_pieces(sums):
    return [x.astype(BF16) for x in sums[1:]]


def to_peers(messages, axis):
    count = lax.axis_size(axis)
    return [lax.ppermute(messages[p - 1], axis, pairs_of(count, p)) for p in range(1, count)]


def add_pieces(own, got):
    total = own
    for piece in got:
        total = total + piece.astype(F32)
    return total


def replica_parts(total, rank):
    replicas = lax.axis_size("rep")
    parts = total if total.ndim == 3 else total.reshape(replicas, total.shape[0] // replicas, -1)
    low = parts.astype(BF16)
    mine = lax.dynamic_index_in_dim(parts, rank, 0, keepdims=False)
    return mine, [lax.dynamic_index_in_dim(low, rank ^ j, 0, keepdims=False) for j in range(1, replicas)]


def unpack_attention(pack):
    q = pack.shape[0] // 4
    return jnp.concatenate([pack[c * q : (c + 1) * q] for c in range(3)], axis=1), pack[3 * q :]


def unpack_mlp(pack):
    q = pack.shape[0] // 8
    return jnp.concatenate([pack[c * q : (c + 1) * q] for c in range(4)], axis=1), pack[4 * q :]


def pad_rows(value):
    return jnp.pad(value, ((0, -value.shape[0] % 16), (0, 0)))


def from_peers(value, axis):
    return [lax.ppermute(value, axis, pairs_of(lax.axis_size(axis), p)) for p in range(1, lax.axis_size(axis))]


def pair_sum(values):
    while len(values) > 1:
        values = [values[i] + values[i + 1] for i in range(0, len(values), 2)]
    return values[0]


def per_device(inputs, conditioning, cotangent, micro_sizes, relative_bias_index,
               w_ada, w_qkv, w_proj, w_fc1, w_fc2, b_ada, b_qv, b_proj, b_fc1, b_fc2, bias_table):
    section = lax.axis_index("section")
    shard = lax.axis_index("fsdp")
    rank = lax.axis_index("rep")
    shards, replicas = lax.axis_size("fsdp"), lax.axis_size("rep")
    direct = shards == 4 and replicas == 4
    is_first = section == 0
    samples, length, model = inputs.shape
    heads, entries = bias_table.shape[1:]
    half = samples // 2
    z = Sizes(half, length, model, heads, 4 * model, shards if direct else 1)
    pos = jnp.stack([section, shard, rank]).astype(jnp.int32)

    def mine(first, second):
        return jnp.where(is_first, first, second)

    def own_samples(array):
        return lax.dynamic_slice_in_dim(array, section * half, half, 0)

    def in_order(own, other):
        return jnp.where(is_first, jnp.concatenate([own, other]), jnp.concatenate([other, own]))

    live = (jnp.arange(half)[:, None, None] < lax.dynamic_index_in_dim(micro_sizes[0], section, 0)).astype(BF16)
    h0 = own_samples(inputs).reshape(half * length, model)
    grad1 = (own_samples(cotangent) * live).reshape(half * length, model)
    own_raw = [w_qkv[0], w_proj[0], w_fc1[0], w_fc2[0]]
    width = model // shards
    if direct:
        conds = [conditioning] + from_peers(conditioning, "fsdp")
        own_pack = pack_shard(own_raw)
        middle_row = own_pack.shape[0] // 2
        got_x = lax.ppermute(own_pack, "fsdp", pairs_of(shards, 1))
        got_y = lax.ppermute(own_pack, "fsdp", pairs_of(shards, 2))
        partial = partial_step(pos, w_ada[0], conds, (b_ada, b_qv, b_proj, b_fc1, b_fc2), [own_pack])
        table = after([bias_table[0]], [own_pack])[0]
        bias_own = lookup(table, relative_bias_index, [h0, grad1, *partial])
        got_first = lax.ppermute(got_x[:middle_row], "fsdp", pairs_of(shards, 2))
        got_second = lax.ppermute(got_y[middle_row:], "fsdp", pairs_of(shards, 1))
        own_weights = [own_pack, got_x, got_y, got_first, got_second]
        weights = own_weights + [swap_section(w) for w in own_weights]
        own_line, send_line = line_step(pos, partial[0], after(to_peers(partial[1:], "fsdp"), [got_x, got_y]))
    else:
        row = jnp.concatenate([b_ada, b_qv, b_proj, b_fc1, b_fc2], axis=1)
        bias_rows = lax.all_gather(row[0], "fsdp", axis=0)
        whole = [lax.all_gather(w, "fsdp", axis=0, tiled=True) for w in own_raw]
        own_whole = pack_shard(whole)
        weights = [own_whole, swap_section(own_whole)]
        acts = jax.nn.silu(conditioning.astype(F32)).astype(BF16)
        modulation = dot(acts, lax.all_gather(w_ada[0], "fsdp", axis=0, tiled=True))
        bias_own = lookup(bias_table[0], relative_bias_index, [])
        cuts = [b_ada.shape[1], b_qv.shape[1], b_proj.shape[1], b_fc1.shape[1], b_fc2.shape[1]]
        biases, at = [], 0
        for cut in cuts:
            biases.append(bias_rows[:, at : at + cut].reshape(1, -1).astype(F32))
            at += cut
        modulation = modulation + biases[0]
        other_samples = lax.dynamic_slice_in_dim(modulation, (1 - section) * half, half, 0)
        own_line = jnp.concatenate([own_samples(modulation).reshape(1, -1)] + biases[1:], axis=1)
        send_line = jnp.concatenate([other_samples.reshape(1, -1)] + biases[1:], axis=1)
    lines = (own_line, swap_section(send_line))
    bias_heads = (bias_own, swap_section(bias_own))

    if direct:
        w_ada_later = after([w_ada[0]], weights[3:5])[0]
        w_ada_pieces = [w_ada_later] + from_peers(w_ada_later, "fsdp")
    else:
        w_ada_pieces = [lax.all_gather(w_ada[0], "fsdp", axis=0, tiled=True)]
    qkv, probs, att, branch, middle, act, slope, out_branch, h1 = forward_layer(0, z, pos, h0, lines, bias_heads, weights, w_ada_pieces[:1] if direct else [])
    out1, d_h1, small_a1, small_m1, scores1, keep1, send1 = both_ways(1, z, pos, h1, grad1, lines, bias_heads, weights, w_ada_pieces[1:])
    d_middle, small_m0, keep_m0, send_m0 = backward_mlp(0, z, pos, d_h1, middle, lines, act, slope, out_branch, weights, [])
    pieces = z.pieces
    rows = half * length
    other1 = swap_section(send1)
    other_m0 = swap_section(send_m0)
    if direct:
        own_first, *first_messages = first_step(keep1, other1, keep_m0, other_m0)
        earlier = first_messages
    else:
        sums1 = section_sums(keep1, other1[: keep1.shape[0]], pieces)
        sums_m0 = section_sums(keep_m0, other_m0, pieces)
        earlier = []
    d_h0, small_a0, scores0, keep_a0, send_a0 = backward_attention(
        0, z, pos, h0, lines, qkv, probs, att, branch, d_middle, d_h1, weights, earlier
    )
    smalls = (small_a0, small_m0, small_a1, small_m1)
    size_a = keep_a0.shape[0]

    def replica(value, step):
        return lax.ppermute(value, "rep", pairs_of(replicas, step))

    def ordered(own, other, bit):
        return jnp.where(bit == 0, jnp.concatenate([own, other]), jnp.concatenate([other, own]))

    if direct:
        kept_small, send_small = small_step(pos, scores0, scores1, relative_bias_index, smalls, [])
        other_small = swap_section(send_small)
        other_a0 = after([swap_section(send_a0)], [kept_small])[0]
        own_a0, own_small, *messages = plane_step(pos, keep_a0, other_a0, kept_small, other_small, conditioning)
        got = to_peers(messages, "fsdp")
        got_first = after(to_peers(first_messages, "fsdp"), [own_small])
        keep_z, send_z = halve_step(pos, own_first, got_first)
        cond_part = cond_step(pos, after([own_small], [send_z])[0], w_ada_pieces, conditioning)
        part0, plane_small, *messages = column_step(pos, own_a0, own_small, got, samples)
        got_z = after([replica(send_z, 1)], [plane_small])[0]
        keep_z, send_z = quarter_step(pos, keep_z, got_z)
        got = to_peers(messages, "rep")
        size = part0.shape[0]
        high, low = rank >> 1, rank & 1
        quarter0 = add_pieces(part0, [x[:size] for x in got]).astype(BF16)
        got_z = after([replica(send_z, 2)], [quarter0])[0]
        quarter = (keep_z + got_z.astype(F32)).astype(BF16)
        pair = ordered(quarter, replica(quarter, 2), high)
        half_a0 = by_rank([quarter0] + from_peers(quarter0, "rep"), rank).reshape(-1, model)
        n = pair.shape[0] // 2
        quarters = ordered(pair.reshape(1, 2, n, model), replica(pair, 1).reshape(1, 2, n, model), low)
        quarters = jnp.transpose(quarters, (1, 0, 2, 3)).reshape(4, n, model)
        n = 3 * n // 5
        half1 = quarters[:, :n].reshape(-1, model)
        half_m0 = quarters[:, n:].reshape(-1, model)
        g_ada, g_b_ada, g_b_qv, g_b_proj, g_b_fc1, g_b_fc2, g_table = finish_step(
            pos, plane_small, got, samples, width, heads, entries
        )
    else:
        other_a0 = swap_section(send_a0)
        kept_small, send_small = small_step(pos, scores0, scores1, relative_bias_index, smalls, [])
        theirs = swap_section(send_small).astype(F32)
        both = kept_small + theirs
        cut = half * 8

        def d_mod_of(values):
            a, m = values[:cut].reshape(half, 8, model), values[cut : 2 * cut].reshape(half, 8, model)
            return jnp.concatenate([a[:, :3], m[:, :3]], axis=1)

        low = in_order(d_mod_of(kept_small), d_mod_of(theirs)).astype(BF16)
        bias_rows = jnp.sum(both[: 2 * cut].reshape(2, half, 8, model), axis=1)
        summed = jnp.concatenate([bias_rows[1, 3:8], bias_rows[0, 3:6], both[2 * cut :]])
        cond_part = cond_step(pos, jnp.transpose(low, (1, 0, 2)).reshape(-1, model), w_ada_pieces, conditioning)
        kept = jnp.concatenate([low, conditioning[:, None]], axis=1)
        kept = lax.all_gather(kept, ("fsdp", "rep"), axis=0, tiled=True)
        summed = lax.psum(summed, ("fsdp", "rep"))
        act_all = jax.nn.silu(kept[:, 6].astype(F32)).astype(BF16)
        act_cols = lax.dynamic_slice_in_dim(act_all, shard * width, width, 1)
        g_ada = jnp.concatenate([dot_cols(act_cols, kept[:, i]) for i in range(6)], axis=1)
        g_b_ada = jnp.sum(kept[:, :6].astype(F32), axis=0).reshape(-1)
        vectors = [g_b_ada, summed[5:7].reshape(-1), summed[7], summed[1:5].reshape(-1), summed[0]]
        g_b_ada, g_b_qv, g_b_proj, g_b_fc1, g_b_fc2 = [
            lax.dynamic_slice_in_dim(v, shard * (v.shape[0] // shards), v.shape[0] // shards, 0)[None] for v in vectors
        ]
        g_table = jnp.transpose(summed[8:].reshape(HIGH, heads, LOW), (1, 0, 2)).reshape(heads, HIGH * LOW)[:, :entries]
        sums_a0 = section_sums(keep_a0, other_a0[:size_a], pieces)
        half_a0, half_m0, half1 = sums_a0[0].astype(BF16), sums_m0[0].astype(BF16), sums1[0].astype(BF16)
    cond_grad = cond_part + swap_section(cond_part)
    cut = half_a0.shape[0]
    half_a1, half_m1 = half1[:cut], half1[cut:]
    grads = final_step(
        pos, mine(half_a0, half_a1), mine(half_m0, half_m1),
        swap_section(mine(jnp.concatenate([half_a1, half_m1]), jnp.concatenate([half_a0, half_m0]))),
    )
    if not direct:
        grads = [lax.psum_scatter(g.astype(BF16), "fsdp", scatter_dimension=0, tiled=True) for g in grads]
        grads = [g.astype(F32) for g in lax.psum(tuple(grads), "rep")]
    g_qkv, g_proj, g_fc1, g_fc2 = grads

    activations = in_order(
        mine(h1, out1).reshape(half, length, model), other1[keep1.shape[0] :].reshape(half, length, model)
    )
    input_grads = in_order(
        mine(d_h0, d_h1.astype(F32)).reshape(half, length, model),
        other_a0[size_a : size_a + rows].astype(F32).reshape(half, length, model),
    )

    return (
        activations[None], input_grads[None], cond_grad,
        g_ada[None], g_qkv[None], g_proj[None], g_fc1[None], g_fc2[None],
        g_b_ada, g_b_qv, g_b_proj, g_b_fc1, g_b_fc2,
        g_table[None],
    )


def solution(mesh):
    batch = ("fsdp", "rep")
    matrix = P("section", "fsdp", None)
    vector = P("section", "fsdp")
    return jax.shard_map(
        per_device,
        mesh=mesh,
        in_specs=(
            P(batch, None, None), P(batch, None), P(batch, None, None), P(batch, None), P(),
            matrix, matrix, matrix, matrix, matrix, vector, vector, vector, vector, vector,
            P("section", None, None),
        ),
        out_specs=(
            P("section", batch, None, None), P("section", batch, None, None), P(batch, None),
            matrix, matrix, matrix, matrix, matrix, vector, vector, vector, vector, vector,
            P("section", None, None),
        ),
        check_vma=False,
    )
```

```python
import functools

import jax
import jax.numpy as jnp
from jax import lax
from jax.experimental import pallas as pl
from jax.experimental.pallas import tpu as pltpu
from jax.sharding import PartitionSpec as P

EPSILON = 1e-06
F32 = jnp.float32
BF16 = jnp.bfloat16
VMEM_BYTES = 58 * 1024 * 1024
LOW_BITS = 6
LOW = 1 << LOW_BITS
HIGH = 16


def dot(a, b):
    return jnp.dot(a, b, preferred_element_type=F32)


def dot_rows(a, b):
    return lax.dot_general(a, b, (((1,), (1,)), ((), ())), preferred_element_type=F32)


def dot_cols(a, b):
    return lax.dot_general(a, b, (((0,), (0,)), ((), ())), preferred_element_type=F32)


def norm_parts(v):
    centre = v - jnp.mean(v, axis=-1, keepdims=True)
    inverse = lax.rsqrt(jnp.mean(centre * centre, axis=-1, keepdims=True) + EPSILON)
    return centre * inverse, inverse


def norm_back(d_normed, scale, normed, inverse):
    d = d_normed * (1.0 + scale)
    return inverse * (
        d
        - jnp.mean(d, axis=-1, keepdims=True)
        - normed * jnp.mean(d * normed, axis=-1, keepdims=True)
    )


def col_sum(v):
    return jnp.sum(v, axis=0, keepdims=True)


def half_masks(width):
    lane = lax.broadcasted_iota(jnp.int32, (1, width), 1)
    first = jnp.where(lane < width // 2, 1.0, 0.0)
    return first.astype(BF16), (1.0 - first).astype(BF16)


def block_targets(mats, off, q):
    w_qkv, w_proj, w_fc1, w_fc2 = mats
    model = w_proj.shape[0]
    targets = [w_qkv.at[pl.ds(off, q), pl.ds(c * model, model)] for c in range(3)]
    targets.append(w_proj.at[pl.ds(off, q), :])
    targets += [w_fc1.at[pl.ds(off, q), pl.ds(c * model, model)] for c in range(4)]
    targets.append(w_fc2.at[pl.ds(off * 4, 4 * q), :])
    return targets


def weight_count(refs):
    return 9 if refs == 2 else 36


def weight_loads(layer, section, shard, refs, mats, sems):
    model = mats[1].shape[0]
    plans = []
    if len(refs) == 2:
        for i, target in enumerate(block_targets(mats, 0, model)):
            rows = pl.ds(i * model, 4 * model if i == 8 else model)
            plans.append((refs[0].at[rows, :], refs[1].at[rows, :], target, i < 4))
    else:
        count = len(refs) // 2
        q = refs[0].shape[0] // 12
        for p in range(4):
            targets = block_targets(mats, pl.multiple_of((shard ^ p) * q, 16), q)
            for i, target in enumerate(targets):
                which, at = p, i
                if p == 3 and i >= 6:
                    which, at = 4, i - 6
                rows = pl.ds(at * q, 4 * q if i == 8 else q)
                plans.append((refs[which].at[rows, :], refs[count + which].at[rows, :], target, i < 4))
    ones = [pltpu.make_async_copy(x[0], x[2], sems.at[i]) for i, x in enumerate(plans)]
    twos = [pltpu.make_async_copy(x[1], x[2], sems.at[i]) for i, x in enumerate(plans)]

    @pl.when(section == layer)
    def _():
        for copy in ones:
            copy.start()

    @pl.when(section != layer)
    def _():
        for copy in twos:
            copy.start()

    return (
        [copy for copy, x in zip(ones, plans) if x[3]],
        [copy for copy, x in zip(ones, plans) if not x[3]],
    )


def wait_all(copies):
    for copy in copies:
        copy.wait()


def put_half(refs, section, half, at, value):
    keep, send = refs
    rows = slice(at, at + value.shape[0])

    @pl.when(section == half)
    def _():
        keep[rows, :] = value

    @pl.when(section != half)
    def _():
        send[rows, :] = value


def pack_attention(refs, section, g_qkv, g_proj, shard, pieces, stride, first):
    model = g_proj.shape[0]
    q = model // pieces
    for p in range(pieces):
        off = pl.multiple_of((shard ^ p) * q, 16) if pieces > 1 else 0
        at = (stride * p + first) * q
        for c in range(3):
            value = g_qkv[pl.ds(off, q), c * model : (c + 1) * model]
            put_half(refs, section, c // 2, at + (c % 2) * q, value)
        put_half(refs, section, 1, at + q, g_proj[pl.ds(off, q), :])


def pack_mlp(refs, section, g_fc1, g_fc2, shard, pieces, stride, first):
    model = g_fc1.shape[0]
    q = model // pieces
    for p in range(pieces):
        off = pl.multiple_of((shard ^ p) * q, 16) if pieces > 1 else 0
        at = (stride * p + first) * q
        for c in range(4):
            value = g_fc1[pl.ds(off, q), c * model : (c + 1) * model]
            put_half(refs, section, 0, at + c * q, value)
        put_half(refs, section, 1, at, g_fc2[pl.ds(pl.multiple_of(off * 4, 16), 4 * q), :])


class Modulation:
    def __init__(self, line, model):
        self.line, self.model = line, model

    def __getitem__(self, key):
        b, rows, _ = key
        return self.line[:, pl.ds(pl.multiple_of((6 * b + rows.start) * self.model, 128), self.model)]


def bias_at(line, samples, model, start, size):
    return line[:, (6 * samples + start) * model : (6 * samples + start + size) * model]


def attention_forward(b, length, h, mod, bias, w_qkv, w_proj, b_qkv, b_proj, qkv, probs, att, branch, middle):
    model = w_proj.shape[0]
    heads = bias.shape[0]
    pair = 2 * model // heads
    rows = pl.ds(pl.multiple_of(b * length, length), length)
    masks = half_masks(pair)
    x = h[rows, :].astype(F32)
    normed, _ = norm_parts(x)
    normed_low = (normed * (1.0 + mod[b, 1:2, :]) + mod[b, 0:1, :]).astype(BF16)
    qkv[rows, :] = (dot(normed_low, w_qkv[...]) + b_qkv[...]).astype(BF16)
    for j in range(heads // 2):
        q_pair = qkv[rows, j * pair : (j + 1) * pair] * BF16((pair // 2) ** (-0.5))
        k_pair = qkv[rows, model + j * pair : model + (j + 1) * pair]
        v_pair = qkv[rows, 2 * model + j * pair : 2 * model + (j + 1) * pair]
        v_turned = v_pair.T
        parts = []
        for e in range(2):
            scores = dot_rows(k_pair * masks[e], q_pair) + bias[2 * j + e].astype(F32)
            raised = jnp.exp(scores - jnp.max(scores, axis=0, keepdims=True))
            p = (raised * (1.0 / jnp.sum(raised, axis=0, keepdims=True))).astype(BF16)
            probs[b, 2 * j + e] = p
            parts.append(dot(v_turned[e * (pair // 2) : (e + 1) * (pair // 2), :], p))
        att[rows, j * pair : (j + 1) * pair] = jnp.concatenate(parts, axis=0).astype(BF16).T
    out = dot(att[rows, :], w_proj[...]) + b_proj[...]
    branch[rows, :] = out
    middle[rows, :] = x + mod[b, 2:3, :] * out


def mlp_forward(b, length, middle, mod, w_fc1, w_fc2, b_fc1, b_fc2, act, slope, out_branch, layer_out):
    model = w_fc1.shape[0]
    rows = pl.ds(pl.multiple_of(b * length, length), length)
    mid = middle[rows, :]
    normed, _ = norm_parts(mid)
    normed_low = (normed * (1.0 + mod[b, 4:5, :]) + mod[b, 3:4, :]).astype(BF16)
    total = b_fc2[...]
    for c in range(w_fc1.shape[1] // model):
        cols = slice(c * model, (c + 1) * model)
        v = dot(normed_low, w_fc1[:, cols]) + b_fc1[:, cols]
        square = v * v
        t = jnp.tanh(0.7978845608028654 * v * (1.0 + 0.044715 * square))
        half = 0.5 * (1.0 + t)
        a = (v * half).astype(BF16)
        act[rows, cols] = a
        slope[rows, cols] = (
            half
            + 0.5 * v * (1.0 - t * t) * (0.7978845608028654 + (3 * 0.044715 * 0.7978845608028654) * square)
        ).astype(BF16)
        total = total + dot(a, w_fc2[cols, :])
    out_branch[rows, :] = total
    layer_out[rows, :] = (mid + mod[b, 5:6, :] * total).astype(layer_out.dtype)


def mlp_backward(b, length, grad, middle, mod, w_fc1, w_fc2, act, slope, out_branch, d_middle, small, normed_low, d_pre, d_ob):
    model = w_fc1.shape[0]
    rows = pl.ds(pl.multiple_of(b * length, length), length)
    g = grad[rows, :].astype(F32)
    small[b, 2:3, :] = col_sum(g * out_branch[rows, :])
    d_out = g * mod[b, 5:6, :]
    d_out_low = d_out.astype(BF16)
    d_ob[rows, :] = d_out_low
    small[b, 3:4, :] = col_sum(d_out_low.astype(F32))
    normed, inverse = norm_parts(middle[rows, :])
    normed_low[rows, :] = (normed * (1.0 + mod[b, 4:5, :]) + mod[b, 3:4, :]).astype(BF16)
    d_normed = None
    for c in range(w_fc1.shape[1] // model):
        cols = slice(c * model, (c + 1) * model)
        d_act = dot_rows(d_out_low, w_fc2[cols, :])
        d_low = (d_act * slope[rows, cols].astype(F32)).astype(BF16)
        d_pre[rows, cols] = d_low
        small[b, 4 + c : 5 + c, :] = col_sum(d_low.astype(F32))
        part = dot_rows(d_low, w_fc1[:, cols])
        d_normed = part if d_normed is None else d_normed + part
    small[b, 0:1, :] = col_sum(d_normed)
    small[b, 1:2, :] = col_sum(d_normed * normed)
    d_middle[rows, :] = norm_back(d_normed, mod[b, 4:5, :], normed, inverse) + g


def mlp_weight_grads(normed_low, d_pre, act, d_ob, g_fc1, g_fc2):
    model = g_fc1.shape[0]
    for c in range(g_fc1.shape[1] // model):
        cols = slice(c * model, (c + 1) * model)
        g_fc1[:, cols] = dot_cols(normed_low[...], d_pre[:, cols]).astype(BF16)
        g_fc2[cols, :] = dot_cols(act[:, cols], d_ob[...]).astype(BF16)


def attention_backward(b, length, h, mod, w_qkv, w_proj, qkv, probs, att, branch, d_middle, d_in, small, score_sum, normed_low, d_qkv, d_br):
    model = w_proj.shape[0]
    heads = probs.shape[1]
    pair = 2 * model // heads
    scale = F32((pair // 2) ** (-0.5))
    rows = pl.ds(pl.multiple_of(b * length, length), length)
    masks = half_masks(pair)
    d_mid = d_middle[rows, :]
    small[b, 2:3, :] = col_sum(d_mid * branch[rows, :])
    d_branch = (d_mid * mod[b, 2:3, :]).astype(BF16)
    d_br[rows, :] = d_branch
    small[b, 5:6, :] = col_sum(d_branch.astype(F32))
    d_att = dot_rows(d_branch, w_proj[...]).astype(BF16)
    for j in range(heads // 2):
        q_pair = qkv[rows, j * pair : (j + 1) * pair]
        k_pair = qkv[rows, model + j * pair : model + (j + 1) * pair]
        v_pair = qkv[rows, 2 * model + j * pair : 2 * model + (j + 1) * pair]
        d_pair = d_att[:, j * pair : (j + 1) * pair]
        k_turned = k_pair.T
        d_k = d_v = None
        q_parts = []
        for e in range(2):
            p_low = probs[b, 2 * j + e]
            p = p_low.astype(F32)
            d_p = dot_rows(v_pair * masks[e], d_pair)
            d_s = (p * (d_p - jnp.sum(d_p * p, axis=0, keepdims=True))).astype(BF16)
            score_sum[2 * j + e] += d_s.astype(F32)
            v_part = dot(p_low, d_pair * masks[e])
            k_part = dot(d_s, q_pair * masks[e])
            q_parts.append(dot(k_turned[e * (pair // 2) : (e + 1) * (pair // 2), :], d_s))
            d_v = v_part if d_v is None else d_v + v_part
            d_k = k_part if d_k is None else d_k + k_part
        d_q = jnp.concatenate(q_parts, axis=0) * scale
        d_qkv[rows, j * pair : (j + 1) * pair] = d_q.astype(BF16).T
        d_qkv[rows, model + j * pair : model + (j + 1) * pair] = (d_k * scale).astype(BF16)
        d_qkv[rows, 2 * model + j * pair : 2 * model + (j + 1) * pair] = d_v.astype(BF16)
    small[b, 3:4, :] = col_sum(d_qkv[rows, :model].astype(F32))
    small[b, 4:5, :] = col_sum(d_qkv[rows, 2 * model :].astype(F32))
    small[b, 6:8, :] = jnp.zeros((2, model), F32)
    d_normed = dot_rows(d_qkv[rows, :], w_qkv[...])
    normed, inverse = norm_parts(h[rows, :].astype(F32))
    normed_low[rows, :] = (normed * (1.0 + mod[b, 1:2, :]) + mod[b, 0:1, :]).astype(BF16)
    small[b, 0:1, :] = col_sum(d_normed)
    small[b, 1:2, :] = col_sum(d_normed * normed)
    d_in[rows, :] = (norm_back(d_normed, mod[b, 1:2, :], normed, inverse) + d_mid).astype(d_in.dtype)


def attention_weight_grads(normed_low, d_qkv, att, d_br, g_qkv, g_proj):
    model = g_proj.shape[0]
    for c in range(3):
        cols = slice(c * model, (c + 1) * model)
        g_qkv[:, cols] = dot_cols(normed_low[...], d_qkv[:, cols]).astype(BF16)
    g_proj[...] = dot_cols(att[...], d_br[...]).astype(BF16)


def each_sample(count, body):
    def step(b, carry):
        body(b)
        return carry

    lax.fori_loop(0, count, step, 0)


def add_tables(all_scores, index, outs):
    heads, length = all_scores[0].shape[0], all_scores[0].shape[1]
    low_ids = lax.broadcasted_iota(jnp.int32, (LOW, length), 0)
    high_ids = lax.broadcasted_iota(jnp.int32, (HIGH, length), 0)
    count = len(all_scores) * heads

    def step(i, carry):
        rows = pl.ds(pl.multiple_of(i * 16, 16), 16)
        entries = index[rows, :]
        block = [scores[head, rows, :].astype(F32) for scores in all_scores for head in range(heads)]
        total = carry
        for r in range(16):
            entry = entries[r : r + 1, :]
            low = jnp.where(low_ids == (entry & (LOW - 1)), 1.0, 0.0).astype(BF16)
            high = high_ids == (entry >> LOW_BITS)
            left = jnp.concatenate([jnp.where(high, part[r : r + 1, :], 0.0) for part in block], axis=0).astype(BF16)
            total = total + dot_rows(left, low)
        return total

    total = lax.fori_loop(0, length // 16, step, jnp.zeros((count * HIGH, LOW), F32))
    parts = [total[i * HIGH : (i + 1) * HIGH] for i in range(count)]
    for layer, out in enumerate(outs):
        out[...] = jnp.concatenate(parts[layer * heads : (layer + 1) * heads], axis=1)


def small_kernel(pos, scores0, scores1, index, small_a0, small_m0, small_a1, small_m1, *rest):
    keep, send, table0, table1 = rest[-4:]
    size = small_a0.shape[0] * small_a0.shape[1]
    add_tables((scores0, scores1), index, (table0, table1))
    parts = (
        (small_a0[...], small_m0[...], table0[...]),
        (small_a1[...], small_m1[...], table1[...]),
    )
    rows = [
        jnp.concatenate([x[0].reshape(size, -1), x[1].reshape(size, -1), x[2]], axis=0) for x in parts
    ]

    @pl.when(pos[0] == 0)
    def _():
        keep[...] = rows[0]
        send[...] = rows[1].astype(BF16)

    @pl.when(pos[0] == 1)
    def _():
        keep[...] = rows[1]
        send[...] = rows[0].astype(BF16)


def small_step(pos, scores0, scores1, index, smalls, earlier):
    samples, _, model = smalls[0].shape
    shape = (16 * samples + HIGH, model)
    return call(
        small_kernel, pos, (scores0, scores1, index, *smalls), earlier, [(shape, F32), (shape, BF16)],
        [((HIGH, model), F32)] * 2, work=12,
    )


def set_line(line, layer, section, own_line, other_line):
    line[...] = jnp.where(section == layer, own_line[...], other_line[...])


def start_bias(layer, section, own, other, bias, sem):
    one = pltpu.make_async_copy(own, bias, sem)
    two = pltpu.make_async_copy(other, bias, sem)
    pl.when(section == layer)(one.start)
    pl.when(section != layer)(two.start)
    return one


def line_biases(line, samples, model):
    q_bias = bias_at(line, samples, model, 0, 1)
    v_bias = bias_at(line, samples, model, 1, 1)
    b_qkv = jnp.concatenate([q_bias, jnp.zeros_like(q_bias), v_bias], axis=1)
    return b_qkv, bias_at(line, samples, model, 2, 1), bias_at(line, samples, model, 3, 4), bias_at(line, samples, model, 7, 1)


def forward_kernel(layer, length, n_weights, n_after, pos, h, own_line, other_line, own_bias, other_bias, *rest):
    refs, rest = rest[:n_weights], rest[n_weights + n_after :]
    (qkv, probs, att, branch, middle, act, slope, out_branch, layer_out,
     w_qkv, w_proj, w_fc1, w_fc2, bias, line, sems) = rest
    section, shard = pos[0], pos[1]
    model = h.shape[1]
    samples = h.shape[0] // length
    got_bias = start_bias(layer, section, own_bias, other_bias, bias, sems.at[weight_count(n_weights)])
    for_attention, for_mlp = weight_loads(layer, section, shard, refs, (w_qkv, w_proj, w_fc1, w_fc2), sems)
    set_line(line, layer, section, own_line, other_line)
    mod = Modulation(line, model)
    b_qkv, b_proj, b_fc1, b_fc2 = line_biases(line, samples, model)
    got_bias.wait()
    wait_all(for_attention)
    each_sample(
        samples,
        lambda b: attention_forward(b, length, h, mod, bias, w_qkv, w_proj, b_qkv, b_proj, qkv, probs, att, branch, middle),
    )
    wait_all(for_mlp)
    each_sample(
        samples,
        lambda b: mlp_forward(b, length, middle, mod, w_fc1, w_fc2, b_fc1, b_fc2, act, slope, out_branch, layer_out),
    )


def both_kernel(layer, pieces, length, n_weights, n_after, pos, h, grad, own_line, other_line, own_bias, other_bias, *rest):
    refs, rest = rest[:n_weights], rest[n_weights + n_after :]
    (layer_out, d_in, small_a, small_m, scores, keep, send,
     w_qkv, w_proj, w_fc1, w_fc2, bias, line, qkv, probs, att, branch, middle, act, slope, out_branch,
     d_middle, normed_low, d_pre, d_ob, d_qkv, score_sum, g_qkv, g_proj, g_fc1, g_fc2, sems) = rest
    section, shard = pos[0], pos[1]
    model = h.shape[1]
    samples = h.shape[0] // length
    got_bias = start_bias(layer, section, own_bias, other_bias, bias, sems.at[weight_count(n_weights)])
    for_attention, for_mlp = weight_loads(layer, section, shard, refs, (w_qkv, w_proj, w_fc1, w_fc2), sems)
    set_line(line, layer, section, own_line, other_line)
    mod = Modulation(line, model)
    b_qkv, b_proj, b_fc1, b_fc2 = line_biases(line, samples, model)
    got_bias.wait()
    wait_all(for_attention)
    each_sample(
        samples,
        lambda b: attention_forward(b, length, h, mod, bias, w_qkv, w_proj, b_qkv, b_proj, qkv, probs, att, branch, middle),
    )
    wait_all(for_mlp)

    def mlp(b):
        mlp_forward(b, length, middle, mod, w_fc1, w_fc2, b_fc1, b_fc2, act, slope, out_branch, layer_out)
        mlp_backward(b, length, grad, middle, mod, w_fc1, w_fc2, act, slope, out_branch, d_middle, small_m, normed_low, d_pre, d_ob)

    each_sample(samples, mlp)
    mlp_weight_grads(normed_low, d_pre, act, d_ob, g_fc1, g_fc2)
    pack_mlp((keep, send), section, g_fc1, g_fc2, shard, pieces, 6, 2)
    score_sum[...] = jnp.zeros_like(score_sum)
    each_sample(
        samples,
        lambda b: attention_backward(b, length, h, mod, w_qkv, w_proj, qkv, probs, att, branch, d_middle, d_in, small_a, score_sum, normed_low, d_qkv, d_ob),
    )
    scores[...] = score_sum[...].astype(BF16)
    attention_weight_grads(normed_low, d_qkv, att, d_ob, g_qkv, g_proj)
    pack_attention((keep, send), section, g_qkv, g_proj, shard, pieces, 6, 0)
    rows = slice(keep.shape[0], keep.shape[0] + h.shape[0])

    @pl.when(section == 0)
    def _():
        send[rows, :] = layer_out[...]

    @pl.when(section == 1)
    def _():
        send[rows, :] = h[...]


def backward_mlp_kernel(layer, pieces, length, n_weights, n_after, pos, grad, middle, own_line, other_line, act, slope, out_branch, *rest):
    refs, rest = rest[:n_weights], rest[n_weights + n_after :]
    (d_middle, small, keep, send,
     w_qkv, w_proj, w_fc1, w_fc2, line, normed_low, d_pre, d_ob, g_fc1, g_fc2, sems) = rest
    section, shard = pos[0], pos[1]
    for_attention, for_mlp = weight_loads(layer, section, shard, refs, (w_qkv, w_proj, w_fc1, w_fc2), sems)
    set_line(line, layer, section, own_line, other_line)
    mod = Modulation(line, middle.shape[1])
    wait_all(for_mlp)
    each_sample(
        middle.shape[0] // length,
        lambda b: mlp_backward(b, length, grad, middle, mod, w_fc1, w_fc2, act, slope, out_branch, d_middle, small, normed_low, d_pre, d_ob),
    )
    mlp_weight_grads(normed_low, d_pre, act, d_ob, g_fc1, g_fc2)
    pack_mlp((keep, send), section, g_fc1, g_fc2, shard, pieces, 4, 0)
    wait_all(for_attention)


def backward_attention_kernel(layer, pieces, length, n_weights, n_after, pos, h, own_line, other_line, qkv, probs, att, branch, d_middle, d_h1, *rest):
    refs, rest = rest[:n_weights], rest[n_weights + n_after :]
    (d_in, small, scores, keep, send,
     w_qkv, w_proj, w_fc1, w_fc2, line, normed_low, d_qkv, d_br, score_sum, g_qkv, g_proj, sems) = rest
    section, shard = pos[0], pos[1]
    for_attention, for_mlp = weight_loads(layer, section, shard, refs, (w_qkv, w_proj, w_fc1, w_fc2), sems)
    set_line(line, layer, section, own_line, other_line)
    mod = Modulation(line, h.shape[1])
    score_sum[...] = jnp.zeros_like(score_sum)
    wait_all(for_attention)
    each_sample(
        h.shape[0] // length,
        lambda b: attention_backward(b, length, h, mod, w_qkv, w_proj, qkv, probs, att, branch, d_middle, d_in, small, score_sum, normed_low, d_qkv, d_br),
    )
    scores[...] = score_sum[...].astype(BF16)
    attention_weight_grads(normed_low, d_qkv, att, d_br, g_qkv, g_proj)
    pack_attention((keep, send), section, g_qkv, g_proj, shard, pieces, 2, 0)
    rows = slice(keep.shape[0], keep.shape[0] + h.shape[0])

    @pl.when(section == 0)
    def _():
        send[rows, :] = d_h1[...]

    @pl.when(section == 1)
    def _():
        send[rows, :] = d_in[...].astype(BF16)

    wait_all(for_mlp)


def cost(gigaflop):
    return pl.CostEstimate(flops=int(gigaflop * 1e9), bytes_accessed=0, transcendentals=0)


def call(kernel, pos, operands, in_hbm, outs, scratch, sems=0, work=2):
    specs = [pl.BlockSpec(memory_space=pltpu.SMEM)]
    specs += [pl.BlockSpec(memory_space=pltpu.VMEM) for _ in operands]
    specs += [pl.BlockSpec(memory_space=pl.ANY) for _ in in_hbm]
    shapes = [pltpu.VMEM(shape, dtype) for shape, dtype in scratch]
    if sems:
        shapes.append(pltpu.SemaphoreType.DMA((sems,)))
    return pl.pallas_call(
        kernel,
        out_shape=[jax.ShapeDtypeStruct(shape, dtype) for shape, dtype in outs],
        in_specs=specs,
        out_specs=[pl.BlockSpec(memory_space=pltpu.VMEM) for _ in outs],
        scratch_shapes=shapes,
        cost_estimate=cost(work),
        compiler_params=pltpu.CompilerParams(vmem_limit_bytes=VMEM_BYTES, fuse_transposed_lhs_in_matmul=True),
    )(pos, *operands, *in_hbm)


class Sizes:
    def __init__(self, samples, length, model, heads, hidden, pieces):
        self.samples, self.length, self.model = samples, length, model
        self.heads, self.hidden, self.pieces = heads, hidden, pieces
        self.rows = samples * length
        self.line = ((1, (6 * samples + 4 + hidden // model) * model), F32)
        self.weights = [
            ((model, 3 * model), BF16), ((model, model), BF16), ((model, hidden), BF16), ((hidden, model), BF16),
        ]
        self.bias = ((heads, length, length), BF16)
        self.probs = ((samples, heads, length, length), BF16)
        self.low = ((self.rows, model), BF16)
        self.full = ((self.rows, model), F32)
        self.qkv = ((self.rows, 3 * model), BF16)
        self.wide = ((self.rows, hidden), BF16)
        self.small = ((samples, 8, model), F32)

    def pack(self, blocks, more=0):
        return [((blocks * self.model, self.model), BF16), ((blocks * self.model + more, self.model), BF16)]


def forward_layer(layer, z, pos, h, lines, biases, weights, earlier):
    return call(
        functools.partial(forward_kernel, layer, z.length, len(weights), len(earlier)),
        pos, (h, *lines), (*biases, *weights, *earlier),
        [z.qkv, z.probs, z.low, z.full, z.full, z.wide, z.wide, z.full, z.low],
        [*z.weights, z.bias, z.line], weight_count(len(weights)) + 1, work=15,
    )


def both_ways(layer, z, pos, h, grad, lines, biases, weights, earlier):
    return call(
        functools.partial(both_kernel, layer, z.pieces, z.length, len(weights), len(earlier)),
        pos, (h, grad, *lines), (*biases, *weights, *earlier),
        [z.low, z.low, z.small, z.small, z.bias, *z.pack(6, z.rows)],
        [*z.weights, z.bias, z.line, z.qkv, z.probs, z.low, z.full, z.full, z.wide, z.wide, z.full,
         z.full, z.low, z.wide, z.low, z.qkv, (z.bias[0], F32), *z.weights],
        weight_count(len(weights)) + 1, work=25,
    )


def backward_mlp(layer, z, pos, grad, middle, lines, act, slope, out_branch, weights, earlier):
    return call(
        functools.partial(backward_mlp_kernel, layer, z.pieces, z.length, len(weights), len(earlier)),
        pos, (grad, middle, *lines, act, slope, out_branch), (*weights, *earlier),
        [z.full, z.small, *z.pack(4)],
        [*z.weights, z.line, z.low, z.wide, z.low, *z.weights[2:]],
        weight_count(len(weights)), work=12,
    )


def backward_attention(layer, z, pos, h, lines, qkv, probs, att, branch, d_middle, d_h1, weights, earlier):
    return call(
        functools.partial(backward_attention_kernel, layer, z.pieces, z.length, len(weights), len(earlier)),
        pos, (h, *lines, qkv, probs, att, branch, d_middle, d_h1), (*weights, *earlier),
        [z.full, z.small, z.bias, *z.pack(2, z.rows)],
        [*z.weights, z.line, z.low, z.qkv, z.low, (z.bias[0], F32), *z.weights[:2]],
        weight_count(len(weights)), work=13,
    )


def partial_kernel(pos, w_ada, cond_a, cond_b, cond_c, cond_d, b_ada, b_qv, b_proj, b_fc1, b_fc2, *rest):
    copied, outs, whole = rest[-6], rest[-5:-1], rest[-1]
    copied[...] = w_ada[...]
    shard = pos[1]
    q, wide = w_ada.shape
    samples, model = cond_a.shape
    whole[...] = jnp.zeros_like(whole)
    whole[pl.ds(pl.multiple_of(shard * q, 16), q), :] = w_ada[...]
    for cond, out in zip((cond_a, cond_b, cond_c, cond_d), outs):
        c = cond[...].astype(F32)
        act = (c * (1.0 / (1.0 + jnp.exp(-c)))).astype(BF16)
        out[:, :wide] = dot(act, whole[...])
        out[:, wide:] = jnp.zeros((samples, 2 * model), F32)
        for f in range(4):
            @pl.when(shard == f)
            def _():
                here = slice(f * b_ada.shape[1], (f + 1) * b_ada.shape[1])
                out[:, here] += b_ada[...].astype(F32)
                for bias, row, at in ((b_qv, 0, 0), (b_proj, 1, 0), (b_fc1, 1, model), (b_fc2, 3, model)):
                    width = bias.shape[1]
                    at += f * width
                    row, at = row + at // (2 * model), wide + at % (2 * model)
                    out[row : row + 1, at : at + width] = bias[...].astype(F32)


def partial_step(pos, w_ada, conds, biases, earlier):
    q, wide = w_ada.shape
    samples, model = conds[0].shape
    return call(
        partial_kernel, pos, (w_ada, *conds, *biases), earlier, [(w_ada.shape, BF16)] + [((samples, wide + 2 * model), F32)] * 4,
        [((4 * q, wide), BF16)],
    )


def line_kernel(pos, own, got_a, got_b, got_c, *rest):
    keep, send, total = rest[-3:]
    section = pos[0]
    samples = own.shape[0]
    each = samples // 2
    model = own.shape[1] // 8
    total[...] = (own[...] + got_a[...]) + (got_b[...] + got_c[...])
    for out, side in ((keep, section), (send, 1 - section)):
        for b in range(each):
            out[:, b * 6 * model : (b + 1) * 6 * model] = total[pl.ds(side * each + b, 1), : 6 * model]
        for row in range(samples):
            at = (6 * each + 2 * row) * model
            out[:, at : at + 2 * model] = total[row : row + 1, 6 * model :]


def line_step(pos, own, got, earlier):
    samples, model = own.shape[0], own.shape[1] // 8
    shape = (1, (3 * samples + 8) * model)
    return call(line_kernel, pos, (own, *got), earlier, [(shape, F32)] * 2, [(own.shape, F32)])


def first_kernel(keep1, other1, keep_m, other_m, own, *messages):
    pieces = 4
    size1, size_m = keep1.shape[0] // pieces, keep_m.shape[0] // pieces
    n1, nm = size1 // 4, size_m // 4
    for p in range(pieces):
        for k in range(4):
            at = k * (n1 + nm)
            for keep, other, first, n, to in (
                (keep1, other1, p * size1 + k * n1, n1, at), (keep_m, other_m, p * size_m + k * nm, nm, at + n1)
            ):
                total = keep[first : first + n, :].astype(F32) + other[first : first + n, :].astype(F32)
                if p == 0:
                    own[to : to + n, :] = total
                else:
                    messages[p - 1][to : to + n, :] = total.astype(BF16)


def first_step(keep1, other1, keep_m, other_m):
    shape = ((keep1.shape[0] + keep_m.shape[0]) // 4, keep1.shape[1])
    return pl.pallas_call(
        first_kernel,
        out_shape=[jax.ShapeDtypeStruct(shape, F32)] + [jax.ShapeDtypeStruct(shape, BF16)] * 3,
        compiler_params=pltpu.CompilerParams(vmem_limit_bytes=VMEM_BYTES),
    )(keep1, other1, keep_m, other_m)


def plane_kernel(samples, pos, keep, other, kept_small, other_small, cond, own, own_small, *rest):
    messages, work = rest[:3], rest[3]
    section = pos[0]
    size, model = own.shape
    for p in range(4):
        rows = slice(p * size, (p + 1) * size)
        total = keep[rows, :].astype(F32) + other[rows, :].astype(F32)
        if p == 0:
            own[...] = total
        else:
            messages[p - 1][:size, :] = total.astype(BF16)
    theirs = other_small[...].astype(F32)
    mine = kept_small[...]
    each = samples // 2
    work[...] = jnp.zeros_like(work)
    for b in range(each):
        for kind in range(6):
            row = b * 8 + kind if kind < 3 else (each + b) * 8 + kind - 3
            work[pl.ds(kind * samples + section * each + b, 1), :] = mine[row : row + 1, :]
            work[pl.ds(kind * samples + (1 - section) * each + b, 1), :] = theirs[row : row + 1, :]
    work[6 * samples : 7 * samples, :] = cond[...].astype(F32)
    both = mine + theirs
    bias_rows = sum(both[(each + b) * 8 + 3 : (each + b) * 8 + 8, :] for b in range(each))
    more_rows = sum(both[b * 8 + 3 : b * 8 + 6, :] for b in range(each))
    at = 7 * samples
    work[at : at + 5, :] = bias_rows
    work[at + 5 : at + 8, :] = more_rows
    work[at + 8 : at + 8 + HIGH, :] = both[2 * each * 8 :, :]
    small = work[...].astype(BF16)
    own_small[...] = small
    for message in messages:
        message[size:, :] = small


def plane_step(pos, keep, other, kept_small, other_small, cond):
    samples, model = cond.shape
    size = keep.shape[0] // 4
    small = -(-(7 * samples + 8 + HIGH) // 16) * 16
    outs = [((size, model), F32), ((small, model), BF16)] + [((size + small, model), BF16)] * 3
    return call(
        functools.partial(plane_kernel, samples), pos, (keep, other, kept_small, other_small, cond), (), outs,
        [((small, model), F32)],
    )


def column_kernel(samples, pos, own, own_small, got_a, got_b, got_c, part, own_out, *rest):
    messages, work = rest[:3], rest[3]
    rank = pos[2]
    size, model = own.shape
    n = size // 4
    got = (got_a, got_b, got_c)
    for j in range(4):
        at = pl.multiple_of((rank ^ j) * n, 16)
        total = own[pl.ds(at, n), :]
        for piece in got:
            total = total + piece[pl.ds(at, n), :].astype(F32)
        if j == 0:
            part[...] = total
        else:
            messages[j - 1][:n, :] = total.astype(BF16)
    smalls = [own_small[...].astype(F32)] + [piece[size:, :].astype(F32) for piece in got]
    work[...] = jnp.zeros_like(work)
    for p in range(4):
        for kind in range(7):
            at = (kind * 4 + p) * samples
            work[at : at + samples, :] = smalls[p][kind * samples : (kind + 1) * samples, :]
    at = 7 * samples
    summed = (smalls[0] + smalls[1]) + (smalls[2] + smalls[3])
    work[4 * at : 4 * at + 8 + HIGH, :] = summed[at : at + 8 + HIGH, :]
    small = work[...].astype(BF16)
    own_out[...] = small
    for message in messages:
        message[n:, :] = small


def column_step(pos, own, own_small, got, samples):
    size, model = own.shape
    small = -(-(28 * samples + 8 + HIGH) // 16) * 16
    outs = [((size // 4, model), F32), ((small, model), BF16)] + [((size // 4 + small, model), BF16)] * 3
    return call(
        functools.partial(column_kernel, samples), pos, (own, own_small, *got), (), outs, [((small, model), F32)]
    )


def finish_kernel(samples, width, pos, own_small, got_a, got_b, got_c,
                  g_ada, g_b_ada, g_b_qv, g_b_proj, g_b_fc1, g_b_fc2, g_table, work, whole, row):
    shard, rank = pos[1], pos[2]
    model = own_small.shape[1]
    each = 4 * samples
    n = got_a.shape[0] - own_small.shape[0]
    pieces = [own_small[...]] + [piece[n:, :] for piece in (got_a, got_b, got_c)]
    for j in range(4):
        for kind in range(7):
            at = pl.multiple_of(kind * 4 * each + (rank ^ j) * each, 16)
            work[pl.ds(at, each), :] = pieces[j][kind * each : (kind + 1) * each, :].astype(F32)
    cond = work[24 * each :, :]
    act = (cond * (1.0 / (1.0 + jnp.exp(-cond)))).astype(BF16)
    for kind in range(6):
        rows = work[kind * 4 * each : (kind + 1) * 4 * each, :]
        whole[...] = dot_cols(act, rows.astype(BF16))
        cols = slice(kind * model, (kind + 1) * model)
        g_ada[:, cols] = whole[pl.ds(pl.multiple_of(shard * width, 16), width), :]
        row[:, cols] = col_sum(rows)
    at = 7 * each
    rows = [piece[at : at + 8 + HIGH, :].astype(F32) for piece in pieces]
    summed = (rows[0] + rows[1]) + (rows[2] + rows[3])
    for c in range(4):
        row[:, (6 + c) * model : (7 + c) * model] = summed[1 + c : 2 + c, :]
    row[:, 10 * model : 11 * model] = summed[5:6, :]
    row[:, 11 * model : 12 * model] = summed[6:7, :]
    row[:, 12 * model : 13 * model] = summed[7:8, :]
    row[:, 13 * model : 14 * model] = summed[0:1, :]
    for f in range(4):
        @pl.when(shard == f)
        def _():
            for out, start in ((g_b_ada, 0), (g_b_fc1, 6), (g_b_qv, 10), (g_b_proj, 12), (g_b_fc2, 13)):
                size = out.shape[1]
                out[...] = row[:, start * model + f * size : start * model + (f + 1) * size]
    heads, entries = g_table.shape
    for high in range(-(-entries // LOW)):
        size = min(LOW, entries - high * LOW)
        for head in range(heads):
            g_table[head : head + 1, high * LOW : high * LOW + size] = summed[
                8 + high : 9 + high, head * LOW : head * LOW + size
            ]


def finish_step(pos, own_small, got, samples, width, heads, entries):
    model = own_small.shape[1]
    sizes = [6 * width, 2 * width, width, 4 * width, width]
    return call(
        functools.partial(finish_kernel, samples, width), pos, (own_small, *got), (),
        [((width, 6 * model), F32)] + [((1, size), F32) for size in sizes] + [((heads, entries), F32)],
        [((7 * 16 * samples, model), F32), ((model, model), F32), ((1, 14 * model), F32)],
    )


def cond_kernel(samples, pos, small, cond, *rest):
    out, w_ada = rest[-2:]
    model = cond.shape[1]
    for p, piece in enumerate(rest[:-2]):
        q = piece.shape[0]
        off = pl.multiple_of((pos[1] ^ p) * q, 16) if q < model else 0
        w_ada[pl.ds(off, q), :] = piece[...]
    total = None
    for kind in range(6):
        rows = small[...].astype(F32)[kind * samples : (kind + 1) * samples, :].astype(BF16)
        part = dot_rows(rows, w_ada[:, kind * model : (kind + 1) * model])
        total = part if total is None else total + part
    c = cond[...].astype(F32)
    gate = 1.0 / (1.0 + jnp.exp(-c))
    out[...] = total * (gate * (1.0 + c * (1.0 - gate)))


def cond_step(pos, small, w_ada, cond):
    model = cond.shape[1]
    return call(
        functools.partial(cond_kernel, cond.shape[0]), pos, (small, cond, *w_ada), (), [(cond.shape, F32)],
        [((model, w_ada[0].shape[1]), BF16)],
    )[0]


def final_kernel(pos, own_a, own_m, other, g_qkv, g_proj, g_fc1, g_fc2):
    section = pos[0]
    q, model = g_proj.shape
    cut = own_a.shape[0]

    def write(first_a, first_m, second_a, second_m):
        for c in range(2):
            g_qkv[:, c * model : (c + 1) * model] = first_a[c * q : (c + 1) * q, :].astype(F32)
        g_qkv[:, 2 * model : 3 * model] = second_a[:q, :].astype(F32)
        g_proj[...] = second_a[q : 2 * q, :].astype(F32)
        for c in range(4):
            g_fc1[:, c * model : (c + 1) * model] = first_m[c * q : (c + 1) * q, :].astype(F32)
        g_fc2[...] = second_m[...].astype(F32)

    other_a, other_m = other.at[:cut, :], other.at[cut:, :]

    @pl.when(section == 0)
    def _():
        write(own_a, own_m, other_a, other_m)

    @pl.when(section == 1)
    def _():
        write(other_a, other_m, own_a, own_m)


def final_step(pos, own_a, own_m, other):
    q, model = own_a.shape[0] // 2, own_a.shape[1]
    return call(
        final_kernel, pos, (own_a, own_m, other), (),
        [((q, 3 * model), F32), ((q, model), F32), ((q, 4 * model), F32), ((4 * q, model), F32)], [],
    )


def halve_kernel(pos, own, got_a, got_b, got_c, keep, send):
    bit = pos[2] & 1
    n = own.shape[0] // 4
    for high in range(2):
        for out, low in ((keep, bit), (send, 1 - bit)):
            rows = pl.ds(pl.multiple_of((2 * high + low) * n, 16), n)
            total = own[rows, :]
            for piece in (got_a, got_b, got_c):
                total = total + piece[rows, :].astype(F32)
            out[high * n : (high + 1) * n, :] = total.astype(out.dtype)


def halve_step(pos, own, got):
    shape = (own.shape[0] // 2, own.shape[1])
    return call(halve_kernel, pos, (own, *got), (), [(shape, F32), (shape, BF16)], [])


def quarter_kernel(pos, kept, got, keep, send):
    bit = pos[2] >> 1
    n = kept.shape[0] // 2
    for out, high in ((keep, bit), (send, 1 - bit)):
        rows = pl.ds(pl.multiple_of(high * n, 16), n)
        out[...] = (kept[rows, :] + got[rows, :].astype(F32)).astype(out.dtype)


def quarter_step(pos, kept, got):
    shape = (kept.shape[0] // 2, kept.shape[1])
    return call(quarter_kernel, pos, (kept, got), (), [(shape, F32), (shape, BF16)], [])


def pack_kernel(qkv, proj, fc1, fc2, out):
    q, model = proj.shape
    for c in range(3):
        out[c * q : (c + 1) * q, :] = qkv[:, c * model : (c + 1) * model]
    out[3 * q : 4 * q, :] = proj[...]
    for c in range(4):
        out[(4 + c) * q : (5 + c) * q, :] = fc1[:, c * model : (c + 1) * model]
    out[8 * q : 12 * q, :] = fc2[...]


def pack_shard(own):
    q, model = own[1].shape
    return pl.pallas_call(
        pack_kernel,
        out_shape=jax.ShapeDtypeStruct((12 * q, model), BF16),
        compiler_params=pltpu.CompilerParams(vmem_limit_bytes=VMEM_BYTES),
    )(*own)


def after(values, others):
    return pl.pallas_call(
        lambda *refs: None,
        out_shape=[jax.ShapeDtypeStruct(v.shape, v.dtype) for v in values],
        in_specs=[pl.BlockSpec(memory_space=pl.ANY)] * (len(values) + len(others)),
        out_specs=[pl.BlockSpec(memory_space=pl.ANY)] * len(values),
        input_output_aliases={i: i for i in range(len(values))},
    )(*values, *others)


def lookup_kernel(table, index, *rest):
    out, work = rest[-2:]
    heads, length = out.shape[0], out.shape[1]
    high_count = table.shape[0] // 8
    values = table[...]
    low_id = lax.broadcasted_iota(jnp.int32, (LOW, length), 0)

    def step(i, carry):
        block = index[pl.ds(pl.multiple_of(i * 8, 8), 8), :]
        for r in range(8):
            entry = block[r : r + 1, :]
            picks = jnp.where(low_id == (entry & (LOW - 1)), 1.0, 0.0).astype(BF16)
            found = dot(values, picks).reshape(high_count, 8, length)
            high = jnp.broadcast_to(entry >> LOW_BITS, (8, length))
            bit = high_count // 2
            while bit:
                chosen = (high & bit) != 0
                found = jnp.where(chosen[None], found[bit : 2 * bit], found[:bit])
                bit //= 2
            for head in range(heads):
                work[head, pl.ds(i * 8 + r, 1), :] = found[0, head : head + 1, :]
        return carry

    lax.fori_loop(0, length // 8, step, 0)
    out[...] = work[...].astype(BF16)


def lookup(table, index, earlier):
    heads, entries = table.shape
    high_count = HIGH
    padded = jnp.pad(table, ((0, 8 - heads), (0, high_count * LOW - entries)))
    rows = jnp.transpose(padded.reshape(8, high_count, LOW), (1, 0, 2)).reshape(high_count * 8, LOW)
    length = index.shape[0]
    return pl.pallas_call(
        lookup_kernel,
        out_shape=jax.ShapeDtypeStruct((heads, length, length), BF16),
        in_specs=[pl.BlockSpec(memory_space=pltpu.VMEM)] * 2 + [pl.BlockSpec(memory_space=pl.ANY)] * len(earlier),
        out_specs=pl.BlockSpec(memory_space=pltpu.VMEM),
        scratch_shapes=[pltpu.VMEM((heads, length, length), F32)],
        cost_estimate=cost(11),
        compiler_params=pltpu.CompilerParams(vmem_limit_bytes=VMEM_BYTES),
    )(rows, index, *earlier)


def swap_section(value):
    return lax.ppermute(value, "section", [(0, 1), (1, 0)])


def pairs_of(count, step):
    return [(i, i ^ step) for i in range(count)]


def by_rank(pieces, rank):
    stack = jnp.stack(pieces)
    count = len(pieces)
    bit = 1
    while bit < count:
        moved = jnp.stack([stack[i ^ bit] for i in range(count)])
        stack = jnp.where((rank & bit) != 0, moved, stack)
        bit *= 2
    return stack


def section_sums(keep, other, shards):
    size = keep.shape[0] // shards
    return [
        keep[p * size : (p + 1) * size].astype(F32) + other[p * size : (p + 1) * size].astype(F32)
        for p in range(shards)
    ]


def low_pieces(sums):
    return [x.astype(BF16) for x in sums[1:]]


def to_peers(messages, axis):
    count = lax.axis_size(axis)
    return [lax.ppermute(messages[p - 1], axis, pairs_of(count, p)) for p in range(1, count)]


def add_pieces(own, got):
    total = own
    for piece in got:
        total = total + piece.astype(F32)
    return total


def replica_parts(total, rank):
    replicas = lax.axis_size("rep")
    parts = total if total.ndim == 3 else total.reshape(replicas, total.shape[0] // replicas, -1)
    low = parts.astype(BF16)
    mine = lax.dynamic_index_in_dim(parts, rank, 0, keepdims=False)
    return mine, [lax.dynamic_index_in_dim(low, rank ^ j, 0, keepdims=False) for j in range(1, replicas)]


def unpack_attention(pack):
    q = pack.shape[0] // 4
    return jnp.concatenate([pack[c * q : (c + 1) * q] for c in range(3)], axis=1), pack[3 * q :]


def unpack_mlp(pack):
    q = pack.shape[0] // 8
    return jnp.concatenate([pack[c * q : (c + 1) * q] for c in range(4)], axis=1), pack[4 * q :]


def pad_rows(value):
    return jnp.pad(value, ((0, -value.shape[0] % 16), (0, 0)))


def from_peers(value, axis):
    return [lax.ppermute(value, axis, pairs_of(lax.axis_size(axis), p)) for p in range(1, lax.axis_size(axis))]


def pair_sum(values):
    while len(values) > 1:
        values = [values[i] + values[i + 1] for i in range(0, len(values), 2)]
    return values[0]


def per_device(inputs, conditioning, cotangent, micro_sizes, relative_bias_index,
               w_ada, w_qkv, w_proj, w_fc1, w_fc2, b_ada, b_qv, b_proj, b_fc1, b_fc2, bias_table):
    section = lax.axis_index("section")
    shard = lax.axis_index("fsdp")
    rank = lax.axis_index("rep")
    shards, replicas = lax.axis_size("fsdp"), lax.axis_size("rep")
    direct = shards == 4 and replicas == 4
    is_first = section == 0
    samples, length, model = inputs.shape
    heads, entries = bias_table.shape[1:]
    half = samples // 2
    z = Sizes(half, length, model, heads, 4 * model, shards if direct else 1)
    pos = jnp.stack([section, shard, rank]).astype(jnp.int32)

    def mine(first, second):
        return jnp.where(is_first, first, second)

    def own_samples(array):
        return lax.dynamic_slice_in_dim(array, section * half, half, 0)

    def in_order(own, other):
        return jnp.where(is_first, jnp.concatenate([own, other]), jnp.concatenate([other, own]))

    live = (jnp.arange(half)[:, None, None] < lax.dynamic_index_in_dim(micro_sizes[0], section, 0)).astype(BF16)
    h0 = own_samples(inputs).reshape(half * length, model)
    grad1 = (own_samples(cotangent) * live).reshape(half * length, model)
    index = relative_bias_index.T
    own_raw = [w_qkv[0], w_proj[0], w_fc1[0], w_fc2[0]]
    width = model // shards
    if direct:
        conds = [conditioning] + from_peers(conditioning, "fsdp")
        own_pack = pack_shard(own_raw)
        middle_row = own_pack.shape[0] // 2
        got_x = lax.ppermute(own_pack, "fsdp", pairs_of(shards, 1))
        got_y = lax.ppermute(own_pack, "fsdp", pairs_of(shards, 2))
        bias_own = lookup(bias_table[0], index, [own_pack, *conds[1:]])
        w_ada_copy, *partial = partial_step(pos, w_ada[0], conds, (b_ada, b_qv, b_proj, b_fc1, b_fc2), [bias_own])
        got_first = lax.ppermute(got_x[:middle_row], "fsdp", pairs_of(shards, 2))
        got_second = lax.ppermute(got_y[middle_row:], "fsdp", pairs_of(shards, 1))
        own_weights = [own_pack, got_x, got_y, got_first, got_second]
        weights = own_weights + [swap_section(w) for w in own_weights]
        own_line, send_line = line_step(pos, partial[0], after(to_peers(partial[1:], "fsdp"), [got_x, got_y]), [h0, grad1])
    else:
        row = jnp.concatenate([b_ada, b_qv, b_proj, b_fc1, b_fc2], axis=1)
        bias_rows = lax.all_gather(row[0], "fsdp", axis=0)
        whole = [lax.all_gather(w, "fsdp", axis=0, tiled=True) for w in own_raw]
        own_whole = pack_shard(whole)
        weights = [own_whole, swap_section(own_whole)]
        acts = jax.nn.silu(conditioning.astype(F32)).astype(BF16)
        modulation = dot(acts, lax.all_gather(w_ada[0], "fsdp", axis=0, tiled=True))
        bias_own = lookup(bias_table[0], index, [])
        cuts = [b_ada.shape[1], b_qv.shape[1], b_proj.shape[1], b_fc1.shape[1], b_fc2.shape[1]]
        biases, at = [], 0
        for cut in cuts:
            biases.append(bias_rows[:, at : at + cut].reshape(1, -1).astype(F32))
            at += cut
        modulation = modulation + biases[0]
        other_samples = lax.dynamic_slice_in_dim(modulation, (1 - section) * half, half, 0)
        own_line = jnp.concatenate([own_samples(modulation).reshape(1, -1)] + biases[1:], axis=1)
        send_line = jnp.concatenate([other_samples.reshape(1, -1)] + biases[1:], axis=1)
    lines = (own_line, swap_section(send_line))
    bias_heads = (bias_own, swap_section(bias_own))

    if direct:
        w_ada_later = after([w_ada_copy], weights[3:5])[0]
        w_ada_pieces = [w_ada_later] + from_peers(w_ada_later, "fsdp")
    else:
        w_ada_pieces = [lax.all_gather(w_ada[0], "fsdp", axis=0, tiled=True)]
    qkv, probs, att, branch, middle, act, slope, out_branch, h1 = forward_layer(0, z, pos, h0, lines, bias_heads, weights, w_ada_pieces[:1] if direct else [])
    out1, d_h1, small_a1, small_m1, scores1, keep1, send1 = both_ways(1, z, pos, h1, grad1, lines, bias_heads, weights, w_ada_pieces[1:])
    d_middle, small_m0, keep_m0, send_m0 = backward_mlp(0, z, pos, d_h1, middle, lines, act, slope, out_branch, weights, [])
    pieces = z.pieces
    rows = half * length
    other1 = swap_section(send1)
    other_m0 = swap_section(send_m0)
    if direct:
        own_first, *first_messages = first_step(keep1, other1, keep_m0, other_m0)
        earlier = first_messages
    else:
        sums1 = section_sums(keep1, other1[: keep1.shape[0]], pieces)
        sums_m0 = section_sums(keep_m0, other_m0, pieces)
        earlier = []
    d_h0, small_a0, scores0, keep_a0, send_a0 = backward_attention(
        0, z, pos, h0, lines, qkv, probs, att, branch, d_middle, d_h1, weights, earlier
    )
    smalls = (small_a0, small_m0, small_a1, small_m1)
    size_a = keep_a0.shape[0]

    def replica(value, step):
        return lax.ppermute(value, "rep", pairs_of(replicas, step))

    def ordered(own, other, bit):
        return jnp.where(bit == 0, jnp.concatenate([own, other]), jnp.concatenate([other, own]))

    if direct:
        kept_small, send_small = small_step(pos, scores0, scores1, index, smalls, [])
        other_small = swap_section(send_small)
        other_a0 = after([swap_section(send_a0)], [kept_small])[0]
        own_a0, own_small, *messages = plane_step(pos, keep_a0, other_a0, kept_small, other_small, conditioning)
        got = to_peers(messages, "fsdp")
        got_first = after(to_peers(first_messages, "fsdp"), [own_small])
        keep_z, send_z = halve_step(pos, own_first, got_first)
        cond_part = cond_step(pos, after([own_small], [send_z])[0], w_ada_pieces, conditioning)
        part0, plane_small, *messages = column_step(pos, own_a0, own_small, got, samples)
        got_z = after([replica(send_z, 1)], [plane_small])[0]
        keep_z, send_z = quarter_step(pos, keep_z, got_z)
        got = to_peers(messages, "rep")
        size = part0.shape[0]
        high, low = rank >> 1, rank & 1
        quarter0 = add_pieces(part0, [x[:size] for x in got]).astype(BF16)
        got_z = after([replica(send_z, 2)], [quarter0])[0]
        quarter = (keep_z + got_z.astype(F32)).astype(BF16)
        pair = ordered(quarter, replica(quarter, 2), high)
        half_a0 = by_rank([quarter0] + from_peers(quarter0, "rep"), rank).reshape(-1, model)
        n = pair.shape[0] // 2
        quarters = ordered(pair.reshape(1, 2, n, model), replica(pair, 1).reshape(1, 2, n, model), low)
        quarters = jnp.transpose(quarters, (1, 0, 2, 3)).reshape(4, n, model)
        n = 3 * n // 5
        half1 = quarters[:, :n].reshape(-1, model)
        half_m0 = quarters[:, n:].reshape(-1, model)
        g_ada, g_b_ada, g_b_qv, g_b_proj, g_b_fc1, g_b_fc2, g_table = finish_step(
            pos, plane_small, got, samples, width, heads, entries
        )
    else:
        other_a0 = swap_section(send_a0)
        kept_small, send_small = small_step(pos, scores0, scores1, index, smalls, [])
        theirs = swap_section(send_small).astype(F32)
        both = kept_small + theirs
        cut = half * 8

        def d_mod_of(values):
            a, m = values[:cut].reshape(half, 8, model), values[cut : 2 * cut].reshape(half, 8, model)
            return jnp.concatenate([a[:, :3], m[:, :3]], axis=1)

        low = in_order(d_mod_of(kept_small), d_mod_of(theirs)).astype(BF16)
        bias_rows = jnp.sum(both[: 2 * cut].reshape(2, half, 8, model), axis=1)
        summed = jnp.concatenate([bias_rows[1, 3:8], bias_rows[0, 3:6], both[2 * cut :]])
        cond_part = cond_step(pos, jnp.transpose(low, (1, 0, 2)).reshape(-1, model), w_ada_pieces, conditioning)
        kept = jnp.concatenate([low, conditioning[:, None]], axis=1)
        kept = lax.all_gather(kept, ("fsdp", "rep"), axis=0, tiled=True)
        summed = lax.psum(summed, ("fsdp", "rep"))
        act_all = jax.nn.silu(kept[:, 6].astype(F32)).astype(BF16)
        act_cols = lax.dynamic_slice_in_dim(act_all, shard * width, width, 1)
        g_ada = jnp.concatenate([dot_cols(act_cols, kept[:, i]) for i in range(6)], axis=1)
        g_b_ada = jnp.sum(kept[:, :6].astype(F32), axis=0).reshape(-1)
        vectors = [g_b_ada, summed[5:7].reshape(-1), summed[7], summed[1:5].reshape(-1), summed[0]]
        g_b_ada, g_b_qv, g_b_proj, g_b_fc1, g_b_fc2 = [
            lax.dynamic_slice_in_dim(v, shard * (v.shape[0] // shards), v.shape[0] // shards, 0)[None] for v in vectors
        ]
        g_table = jnp.transpose(summed[8:].reshape(HIGH, heads, LOW), (1, 0, 2)).reshape(heads, HIGH * LOW)[:, :entries]
        sums_a0 = section_sums(keep_a0, other_a0[:size_a], pieces)
        half_a0, half_m0, half1 = sums_a0[0].astype(BF16), sums_m0[0].astype(BF16), sums1[0].astype(BF16)
    cond_grad = cond_part + swap_section(cond_part)
    cut = half_a0.shape[0]
    half_a1, half_m1 = half1[:cut], half1[cut:]
    grads = final_step(
        pos, mine(half_a0, half_a1), mine(half_m0, half_m1),
        swap_section(mine(jnp.concatenate([half_a1, half_m1]), jnp.concatenate([half_a0, half_m0]))),
    )
    if not direct:
        grads = [lax.psum_scatter(g.astype(BF16), "fsdp", scatter_dimension=0, tiled=True) for g in grads]
        grads = [g.astype(F32) for g in lax.psum(tuple(grads), "rep")]
    g_qkv, g_proj, g_fc1, g_fc2 = grads

    activations = in_order(
        mine(h1, out1).reshape(half, length, model), other1[keep1.shape[0] :].reshape(half, length, model)
    )
    input_grads = in_order(
        mine(d_h0, d_h1.astype(F32)).reshape(half, length, model),
        other_a0[size_a : size_a + rows].astype(F32).reshape(half, length, model),
    )

    return (
        activations[None], input_grads[None], cond_grad,
        g_ada[None], g_qkv[None], g_proj[None], g_fc1[None], g_fc2[None],
        g_b_ada, g_b_qv, g_b_proj, g_b_fc1, g_b_fc2,
        g_table[None],
    )


def solution(mesh):
    batch = ("fsdp", "rep")
    matrix = P("section", "fsdp", None)
    vector = P("section", "fsdp")
    return jax.shard_map(
        per_device,
        mesh=mesh,
        in_specs=(
            P(batch, None, None), P(batch, None), P(batch, None, None), P(batch, None), P(),
            matrix, matrix, matrix, matrix, matrix, vector, vector, vector, vector, vector,
            P("section", None, None),
        ),
        out_specs=(
            P("section", batch, None, None), P("section", batch, None, None), P(batch, None),
            matrix, matrix, matrix, matrix, matrix, vector, vector, vector, vector, vector,
            P("section", None, None),
        ),
        check_vma=False,
    )
```

```python
import functools

import jax
import jax.numpy as jnp
from jax import lax
from jax.experimental import pallas as pl
from jax.experimental.pallas import tpu as pltpu
from jax.sharding import PartitionSpec as P

EPSILON = 1e-06
F32 = jnp.float32
BF16 = jnp.bfloat16
VMEM_BYTES = 58 * 1024 * 1024
LOW_BITS = 6
LOW = 1 << LOW_BITS
HIGH = 16


def dot(a, b):
    return jnp.dot(a, b, preferred_element_type=F32)


def dot_rows(a, b):
    return lax.dot_general(a, b, (((1,), (1,)), ((), ())), preferred_element_type=F32)


def dot_cols(a, b):
    return lax.dot_general(a, b, (((0,), (0,)), ((), ())), preferred_element_type=F32)


def norm_parts(v):
    centre = v - jnp.mean(v, axis=-1, keepdims=True)
    inverse = lax.rsqrt(jnp.mean(centre * centre, axis=-1, keepdims=True) + EPSILON)
    return centre * inverse, inverse


def norm_back(d_normed, scale, normed, inverse):
    d = d_normed * (1.0 + scale)
    return inverse * (
        d
        - jnp.mean(d, axis=-1, keepdims=True)
        - normed * jnp.mean(d * normed, axis=-1, keepdims=True)
    )


def col_sum(v):
    return jnp.sum(v, axis=0, keepdims=True)


def half_masks(width):
    lane = lax.broadcasted_iota(jnp.int32, (1, width), 1)
    first = jnp.where(lane < width // 2, 1.0, 0.0)
    return first.astype(BF16), (1.0 - first).astype(BF16)


def block_targets(mats, off, q):
    w_qkv, w_proj, w_fc1, w_fc2 = mats
    model = w_proj.shape[0]
    targets = [w_qkv.at[pl.ds(off, q), pl.ds(c * model, model)] for c in range(3)]
    targets.append(w_proj.at[pl.ds(off, q), :])
    targets += [w_fc1.at[pl.ds(off, q), pl.ds(c * model, model)] for c in range(4)]
    targets.append(w_fc2.at[pl.ds(off * 4, 4 * q), :])
    return targets


def weight_count(refs):
    return 9 if refs == 2 else 36


def weight_loads(layer, section, shard, refs, mats, sems):
    model = mats[1].shape[0]
    plans = []
    if len(refs) == 2:
        for i, target in enumerate(block_targets(mats, 0, model)):
            rows = pl.ds(i * model, 4 * model if i == 8 else model)
            plans.append((refs[0].at[rows, :], refs[1].at[rows, :], target, i < 4))
    else:
        count = len(refs) // 2
        q = refs[0].shape[0] // 12
        for p in range(4):
            targets = block_targets(mats, pl.multiple_of((shard ^ p) * q, 16), q)
            for i, target in enumerate(targets):
                which, at = p, i
                if p == 3 and i >= 6:
                    which, at = 4, i - 6
                rows = pl.ds(at * q, 4 * q if i == 8 else q)
                plans.append((refs[which].at[rows, :], refs[count + which].at[rows, :], target, i < 4))
    ones = [pltpu.make_async_copy(x[0], x[2], sems.at[i]) for i, x in enumerate(plans)]
    twos = [pltpu.make_async_copy(x[1], x[2], sems.at[i]) for i, x in enumerate(plans)]

    @pl.when(section == layer)
    def _():
        for copy in ones:
            copy.start()

    @pl.when(section != layer)
    def _():
        for copy in twos:
            copy.start()

    return (
        [copy for copy, x in zip(ones, plans) if x[3]],
        [copy for copy, x in zip(ones, plans) if not x[3]],
    )


def wait_all(copies):
    for copy in copies:
        copy.wait()


def put_half(refs, section, half, at, value):
    keep, send = refs
    rows = slice(at, at + value.shape[0])

    @pl.when(section == half)
    def _():
        keep[rows, :] = value

    @pl.when(section != half)
    def _():
        send[rows, :] = value


def pack_attention(refs, section, g_qkv, g_proj, shard, pieces, stride, first):
    model = g_proj.shape[0]
    q = model // pieces
    for p in range(pieces):
        off = pl.multiple_of((shard ^ p) * q, 16) if pieces > 1 else 0
        at = (stride * p + first) * q
        for c in range(3):
            value = g_qkv[pl.ds(off, q), c * model : (c + 1) * model]
            put_half(refs, section, c // 2, at + (c % 2) * q, value)
        put_half(refs, section, 1, at + q, g_proj[pl.ds(off, q), :])


def pack_mlp(refs, section, g_fc1, g_fc2, shard, pieces, stride, first):
    model = g_fc1.shape[0]
    q = model // pieces
    for p in range(pieces):
        off = pl.multiple_of((shard ^ p) * q, 16) if pieces > 1 else 0
        at = (stride * p + first) * q
        for c in range(4):
            value = g_fc1[pl.ds(off, q), c * model : (c + 1) * model]
            put_half(refs, section, 0, at + c * q, value)
        put_half(refs, section, 1, at, g_fc2[pl.ds(pl.multiple_of(off * 4, 16), 4 * q), :])


class Modulation:
    def __init__(self, line, model):
        self.line, self.model = line, model

    def __getitem__(self, key):
        b, rows, _ = key
        return self.line[:, pl.ds(pl.multiple_of((6 * b + rows.start) * self.model, 128), self.model)]


def bias_at(line, samples, model, start, size):
    return line[:, (6 * samples + start) * model : (6 * samples + start + size) * model]


def attention_forward(b, length, h, mod, bias, w_qkv, w_proj, b_qkv, b_proj, qkv, probs, att, branch, middle):
    model = w_proj.shape[0]
    heads = bias.shape[0]
    pair = 2 * model // heads
    rows = pl.ds(pl.multiple_of(b * length, length), length)
    masks = half_masks(pair)
    x = h[rows, :].astype(F32)
    normed, _ = norm_parts(x)
    normed_low = (normed * (1.0 + mod[b, 1:2, :]) + mod[b, 0:1, :]).astype(BF16)
    qkv[rows, :] = (dot(normed_low, w_qkv[...]) + b_qkv[...]).astype(BF16)
    for j in range(heads // 2):
        q_pair = qkv[rows, j * pair : (j + 1) * pair] * BF16((pair // 2) ** (-0.5))
        k_pair = qkv[rows, model + j * pair : model + (j + 1) * pair]
        v_pair = qkv[rows, 2 * model + j * pair : 2 * model + (j + 1) * pair]
        total = None
        for e in range(2):
            scores = dot_rows(q_pair * masks[e], k_pair) + bias[2 * j + e].astype(F32)
            raised = jnp.exp(scores - jnp.max(scores, axis=-1, keepdims=True))
            p = (raised * (1.0 / jnp.sum(raised, axis=-1, keepdims=True))).astype(BF16)
            probs[b, 2 * j + e] = p
            part = dot(p, v_pair * masks[e])
            total = part if total is None else total + part
        att[rows, j * pair : (j + 1) * pair] = total.astype(BF16)
    out = dot(att[rows, :], w_proj[...]) + b_proj[...]
    branch[rows, :] = out
    middle[rows, :] = x + mod[b, 2:3, :] * out


def mlp_forward(b, length, middle, mod, w_fc1, w_fc2, b_fc1, b_fc2, act, slope, out_branch, layer_out):
    model = w_fc1.shape[0]
    rows = pl.ds(pl.multiple_of(b * length, length), length)
    mid = middle[rows, :]
    normed, _ = norm_parts(mid)
    normed_low = (normed * (1.0 + mod[b, 4:5, :]) + mod[b, 3:4, :]).astype(BF16)
    total = b_fc2[...]
    for c in range(w_fc1.shape[1] // model):
        cols = slice(c * model, (c + 1) * model)
        v = dot(normed_low, w_fc1[:, cols]) + b_fc1[:, cols]
        square = v * v
        t = jnp.tanh(0.7978845608028654 * v * (1.0 + 0.044715 * square))
        half = 0.5 * (1.0 + t)
        a = (v * half).astype(BF16)
        act[rows, cols] = a
        slope[rows, cols] = (
            half
            + 0.5 * v * (1.0 - t * t) * (0.7978845608028654 + (3 * 0.044715 * 0.7978845608028654) * square)
        ).astype(BF16)
        total = total + dot(a, w_fc2[cols, :])
    out_branch[rows, :] = total
    layer_out[rows, :] = (mid + mod[b, 5:6, :] * total).astype(layer_out.dtype)


def mlp_backward(b, length, grad, middle, mod, w_fc1, w_fc2, act, slope, out_branch, d_middle, small, normed_low, d_pre, d_ob):
    model = w_fc1.shape[0]
    rows = pl.ds(pl.multiple_of(b * length, length), length)
    g = grad[rows, :].astype(F32)
    small[b, 2:3, :] = col_sum(g * out_branch[rows, :])
    d_out = g * mod[b, 5:6, :]
    d_out_low = d_out.astype(BF16)
    d_ob[rows, :] = d_out_low
    small[b, 3:4, :] = col_sum(d_out_low.astype(F32))
    normed, inverse = norm_parts(middle[rows, :])
    normed_low[rows, :] = (normed * (1.0 + mod[b, 4:5, :]) + mod[b, 3:4, :]).astype(BF16)
    d_normed = None
    for c in range(w_fc1.shape[1] // model):
        cols = slice(c * model, (c + 1) * model)
        d_act = dot_rows(d_out_low, w_fc2[cols, :])
        d_low = (d_act * slope[rows, cols].astype(F32)).astype(BF16)
        d_pre[rows, cols] = d_low
        small[b, 4 + c : 5 + c, :] = col_sum(d_low.astype(F32))
        part = dot_rows(d_low, w_fc1[:, cols])
        d_normed = part if d_normed is None else d_normed + part
    small[b, 0:1, :] = col_sum(d_normed)
    small[b, 1:2, :] = col_sum(d_normed * normed)
    d_middle[rows, :] = norm_back(d_normed, mod[b, 4:5, :], normed, inverse) + g


def mlp_weight_grads(normed_low, d_pre, act, d_ob, g_fc1, g_fc2):
    model = g_fc1.shape[0]
    for c in range(g_fc1.shape[1] // model):
        cols = slice(c * model, (c + 1) * model)
        g_fc1[:, cols] = dot_cols(normed_low[...], d_pre[:, cols]).astype(BF16)
        g_fc2[cols, :] = dot_cols(act[:, cols], d_ob[...]).astype(BF16)


def attention_backward(b, length, h, mod, w_qkv, w_proj, qkv, probs, att, branch, d_middle, d_in, small, score_sum, normed_low, d_qkv, d_br):
    model = w_proj.shape[0]
    heads = probs.shape[1]
    pair = 2 * model // heads
    scale = F32((pair // 2) ** (-0.5))
    rows = pl.ds(pl.multiple_of(b * length, length), length)
    masks = half_masks(pair)
    d_mid = d_middle[rows, :]
    small[b, 2:3, :] = col_sum(d_mid * branch[rows, :])
    d_branch = (d_mid * mod[b, 2:3, :]).astype(BF16)
    d_br[rows, :] = d_branch
    small[b, 5:6, :] = col_sum(d_branch.astype(F32))
    d_att = dot_rows(d_branch, w_proj[...]).astype(BF16)
    for j in range(heads // 2):
        q_pair = qkv[rows, j * pair : (j + 1) * pair]
        k_pair = qkv[rows, model + j * pair : model + (j + 1) * pair]
        v_pair = qkv[rows, 2 * model + j * pair : 2 * model + (j + 1) * pair]
        d_pair = d_att[:, j * pair : (j + 1) * pair]
        d_q = d_k = d_v = None
        for e in range(2):
            p_low = probs[b, 2 * j + e]
            p = p_low.astype(F32)
            d_here = d_pair * masks[e]
            d_p = dot_rows(d_here, v_pair)
            d_s = (p * (d_p - jnp.sum(d_p * p, axis=-1, keepdims=True))).astype(BF16)
            score_sum[2 * j + e] += d_s.astype(F32)
            v_part = dot_cols(p_low, d_here)
            q_part = dot(d_s, k_pair * masks[e])
            k_part = dot_cols(d_s, q_pair * masks[e])
            d_v = v_part if d_v is None else d_v + v_part
            d_q = q_part if d_q is None else d_q + q_part
            d_k = k_part if d_k is None else d_k + k_part
        d_qkv[rows, j * pair : (j + 1) * pair] = (d_q * scale).astype(BF16)
        d_qkv[rows, model + j * pair : model + (j + 1) * pair] = (d_k * scale).astype(BF16)
        d_qkv[rows, 2 * model + j * pair : 2 * model + (j + 1) * pair] = d_v.astype(BF16)
    small[b, 3:4, :] = col_sum(d_qkv[rows, :model].astype(F32))
    small[b, 4:5, :] = col_sum(d_qkv[rows, 2 * model :].astype(F32))
    small[b, 6:8, :] = jnp.zeros((2, model), F32)
    d_normed = dot_rows(d_qkv[rows, :], w_qkv[...])
    normed, inverse = norm_parts(h[rows, :].astype(F32))
    normed_low[rows, :] = (normed * (1.0 + mod[b, 1:2, :]) + mod[b, 0:1, :]).astype(BF16)
    small[b, 0:1, :] = col_sum(d_normed)
    small[b, 1:2, :] = col_sum(d_normed * normed)
    d_in[rows, :] = (norm_back(d_normed, mod[b, 1:2, :], normed, inverse) + d_mid).astype(d_in.dtype)


def attention_weight_grads(normed_low, d_qkv, att, d_br, g_qkv, g_proj):
    model = g_proj.shape[0]
    for c in range(3):
        cols = slice(c * model, (c + 1) * model)
        g_qkv[:, cols] = dot_cols(normed_low[...], d_qkv[:, cols]).astype(BF16)
    g_proj[...] = dot_cols(att[...], d_br[...]).astype(BF16)


def each_sample(count, body):
    def step(b, carry):
        body(b)
        return carry

    lax.fori_loop(0, count, step, 0)


def add_tables(all_scores, index, outs):
    heads, length = all_scores[0].shape[0], all_scores[0].shape[1]
    low_ids = lax.broadcasted_iota(jnp.int32, (LOW, length), 0)
    high_ids = lax.broadcasted_iota(jnp.int32, (HIGH, length), 0)
    count = len(all_scores) * heads

    def step(i, carry):
        rows = pl.ds(pl.multiple_of(i * 16, 16), 16)
        entries = index[rows, :]
        block = [scores[head, rows, :].astype(F32) for scores in all_scores for head in range(heads)]
        total = carry
        for r in range(16):
            entry = entries[r : r + 1, :]
            low = jnp.where(low_ids == (entry & (LOW - 1)), 1.0, 0.0).astype(BF16)
            high = high_ids == (entry >> LOW_BITS)
            left = jnp.concatenate([jnp.where(high, part[r : r + 1, :], 0.0) for part in block], axis=0).astype(BF16)
            total = total + dot_rows(left, low)
        return total

    total = lax.fori_loop(0, length // 16, step, jnp.zeros((count * HIGH, LOW), F32))
    parts = [total[i * HIGH : (i + 1) * HIGH] for i in range(count)]
    for layer, out in enumerate(outs):
        out[...] = jnp.concatenate(parts[layer * heads : (layer + 1) * heads], axis=1)


def table_kernel(scores, index, out):
    add_tables((scores,), index, (out,))


def table_step(scores, index):
    return pl.pallas_call(
        table_kernel,
        out_shape=jax.ShapeDtypeStruct((HIGH, scores.shape[0] * LOW), F32),
        cost_estimate=cost(8),
        compiler_params=pltpu.CompilerParams(vmem_limit_bytes=VMEM_BYTES),
    )(scores, index)


def small_kernel(pos, scores, index, small_a0, small_m0, small_a1, small_m1, table1, *rest):
    keep, send, table0 = rest[-3:]
    size = small_a0.shape[0] * small_a0.shape[1]
    add_tables((scores,), index, (table0,))
    parts = (
        (small_a0[...], small_m0[...], table0[...]),
        (small_a1[...], small_m1[...], table1[...]),
    )
    rows = [
        jnp.concatenate([x[0].reshape(size, -1), x[1].reshape(size, -1), x[2]], axis=0) for x in parts
    ]

    @pl.when(pos[0] == 0)
    def _():
        keep[...] = rows[0]
        send[...] = rows[1].astype(BF16)

    @pl.when(pos[0] == 1)
    def _():
        keep[...] = rows[1]
        send[...] = rows[0].astype(BF16)


def small_step(pos, scores, index, smalls, table1, earlier):
    samples, _, model = smalls[0].shape
    shape = (16 * samples + HIGH, model)
    return call(
        small_kernel, pos, (scores, index, *smalls, table1), earlier, [(shape, F32), (shape, BF16)],
        [((HIGH, model), F32)], work=8,
    )


def set_line(line, layer, section, own_line, other_line):
    line[...] = jnp.where(section == layer, own_line[...], other_line[...])


def start_bias(layer, section, own, other, bias, sem):
    one = pltpu.make_async_copy(own, bias, sem)
    two = pltpu.make_async_copy(other, bias, sem)
    pl.when(section == layer)(one.start)
    pl.when(section != layer)(two.start)
    return one


def line_biases(line, samples, model):
    q_bias = bias_at(line, samples, model, 0, 1)
    v_bias = bias_at(line, samples, model, 1, 1)
    b_qkv = jnp.concatenate([q_bias, jnp.zeros_like(q_bias), v_bias], axis=1)
    return b_qkv, bias_at(line, samples, model, 2, 1), bias_at(line, samples, model, 3, 4), bias_at(line, samples, model, 7, 1)


def forward_kernel(layer, length, n_weights, n_after, pos, h, own_line, other_line, own_bias, other_bias, *rest):
    refs, rest = rest[:n_weights], rest[n_weights + n_after :]
    (qkv, probs, att, branch, middle, act, slope, out_branch, layer_out,
     w_qkv, w_proj, w_fc1, w_fc2, bias, line, sems) = rest
    section, shard = pos[0], pos[1]
    model = h.shape[1]
    samples = h.shape[0] // length
    got_bias = start_bias(layer, section, own_bias, other_bias, bias, sems.at[weight_count(n_weights)])
    for_attention, for_mlp = weight_loads(layer, section, shard, refs, (w_qkv, w_proj, w_fc1, w_fc2), sems)
    set_line(line, layer, section, own_line, other_line)
    mod = Modulation(line, model)
    b_qkv, b_proj, b_fc1, b_fc2 = line_biases(line, samples, model)
    got_bias.wait()
    wait_all(for_attention)
    each_sample(
        samples,
        lambda b: attention_forward(b, length, h, mod, bias, w_qkv, w_proj, b_qkv, b_proj, qkv, probs, att, branch, middle),
    )
    wait_all(for_mlp)
    each_sample(
        samples,
        lambda b: mlp_forward(b, length, middle, mod, w_fc1, w_fc2, b_fc1, b_fc2, act, slope, out_branch, layer_out),
    )


def both_kernel(layer, pieces, length, n_weights, n_after, pos, h, grad, own_line, other_line, own_bias, other_bias, *rest):
    refs, rest = rest[:n_weights], rest[n_weights + n_after :]
    (layer_out, d_in, small_a, small_m, scores, keep, send,
     w_qkv, w_proj, w_fc1, w_fc2, bias, line, qkv, probs, att, branch, middle, act, slope, out_branch,
     d_middle, normed_low, d_pre, d_ob, d_qkv, score_sum, g_qkv, g_proj, g_fc1, g_fc2, sems) = rest
    section, shard = pos[0], pos[1]
    model = h.shape[1]
    samples = h.shape[0] // length
    got_bias = start_bias(layer, section, own_bias, other_bias, bias, sems.at[weight_count(n_weights)])
    for_attention, for_mlp = weight_loads(layer, section, shard, refs, (w_qkv, w_proj, w_fc1, w_fc2), sems)
    set_line(line, layer, section, own_line, other_line)
    mod = Modulation(line, model)
    b_qkv, b_proj, b_fc1, b_fc2 = line_biases(line, samples, model)
    got_bias.wait()
    wait_all(for_attention)
    each_sample(
        samples,
        lambda b: attention_forward(b, length, h, mod, bias, w_qkv, w_proj, b_qkv, b_proj, qkv, probs, att, branch, middle),
    )
    wait_all(for_mlp)

    def mlp(b):
        mlp_forward(b, length, middle, mod, w_fc1, w_fc2, b_fc1, b_fc2, act, slope, out_branch, layer_out)
        mlp_backward(b, length, grad, middle, mod, w_fc1, w_fc2, act, slope, out_branch, d_middle, small_m, normed_low, d_pre, d_ob)

    each_sample(samples, mlp)
    mlp_weight_grads(normed_low, d_pre, act, d_ob, g_fc1, g_fc2)
    pack_mlp((keep, send), section, g_fc1, g_fc2, shard, pieces, 6, 2)
    score_sum[...] = jnp.zeros_like(score_sum)
    each_sample(
        samples,
        lambda b: attention_backward(b, length, h, mod, w_qkv, w_proj, qkv, probs, att, branch, d_middle, d_in, small_a, score_sum, normed_low, d_qkv, d_ob),
    )
    scores[...] = score_sum[...].astype(BF16)
    attention_weight_grads(normed_low, d_qkv, att, d_ob, g_qkv, g_proj)
    pack_attention((keep, send), section, g_qkv, g_proj, shard, pieces, 6, 0)
    rows = slice(keep.shape[0], keep.shape[0] + h.shape[0])

    @pl.when(section == 0)
    def _():
        send[rows, :] = layer_out[...]

    @pl.when(section == 1)
    def _():
        send[rows, :] = h[...]


def backward_mlp_kernel(layer, pieces, length, n_weights, n_after, pos, grad, middle, own_line, other_line, act, slope, out_branch, *rest):
    refs, rest = rest[:n_weights], rest[n_weights + n_after :]
    (d_middle, small, keep, send,
     w_qkv, w_proj, w_fc1, w_fc2, line, normed_low, d_pre, d_ob, g_fc1, g_fc2, sems) = rest
    section, shard = pos[0], pos[1]
    for_attention, for_mlp = weight_loads(layer, section, shard, refs, (w_qkv, w_proj, w_fc1, w_fc2), sems)
    set_line(line, layer, section, own_line, other_line)
    mod = Modulation(line, middle.shape[1])
    wait_all(for_mlp)
    each_sample(
        middle.shape[0] // length,
        lambda b: mlp_backward(b, length, grad, middle, mod, w_fc1, w_fc2, act, slope, out_branch, d_middle, small, normed_low, d_pre, d_ob),
    )
    mlp_weight_grads(normed_low, d_pre, act, d_ob, g_fc1, g_fc2)
    pack_mlp((keep, send), section, g_fc1, g_fc2, shard, pieces, 4, 0)
    wait_all(for_attention)


def backward_attention_kernel(layer, pieces, length, n_weights, n_after, pos, h, own_line, other_line, qkv, probs, att, branch, d_middle, d_h1, *rest):
    refs, rest = rest[:n_weights], rest[n_weights + n_after :]
    (d_in, small, scores, keep, send,
     w_qkv, w_proj, w_fc1, w_fc2, line, normed_low, d_qkv, d_br, score_sum, g_qkv, g_proj, sems) = rest
    section, shard = pos[0], pos[1]
    for_attention, for_mlp = weight_loads(layer, section, shard, refs, (w_qkv, w_proj, w_fc1, w_fc2), sems)
    set_line(line, layer, section, own_line, other_line)
    mod = Modulation(line, h.shape[1])
    score_sum[...] = jnp.zeros_like(score_sum)
    wait_all(for_attention)
    each_sample(
        h.shape[0] // length,
        lambda b: attention_backward(b, length, h, mod, w_qkv, w_proj, qkv, probs, att, branch, d_middle, d_in, small, score_sum, normed_low, d_qkv, d_br),
    )
    scores[...] = score_sum[...].astype(BF16)
    attention_weight_grads(normed_low, d_qkv, att, d_br, g_qkv, g_proj)
    pack_attention((keep, send), section, g_qkv, g_proj, shard, pieces, 2, 0)
    rows = slice(keep.shape[0], keep.shape[0] + h.shape[0])

    @pl.when(section == 0)
    def _():
        send[rows, :] = d_h1[...]

    @pl.when(section == 1)
    def _():
        send[rows, :] = d_in[...].astype(BF16)

    wait_all(for_mlp)


def cost(gigaflop):
    return pl.CostEstimate(flops=int(gigaflop * 1e9), bytes_accessed=0, transcendentals=0)


def call(kernel, pos, operands, in_hbm, outs, scratch, sems=0, work=2):
    specs = [pl.BlockSpec(memory_space=pltpu.SMEM)]
    specs += [pl.BlockSpec(memory_space=pltpu.VMEM) for _ in operands]
    specs += [pl.BlockSpec(memory_space=pl.ANY) for _ in in_hbm]
    shapes = [pltpu.VMEM(shape, dtype) for shape, dtype in scratch]
    if sems:
        shapes.append(pltpu.SemaphoreType.DMA((sems,)))
    return pl.pallas_call(
        kernel,
        out_shape=[jax.ShapeDtypeStruct(shape, dtype) for shape, dtype in outs],
        in_specs=specs,
        out_specs=[pl.BlockSpec(memory_space=pltpu.VMEM) for _ in outs],
        scratch_shapes=shapes,
        cost_estimate=cost(work),
        compiler_params=pltpu.CompilerParams(vmem_limit_bytes=VMEM_BYTES),
    )(pos, *operands, *in_hbm)


class Sizes:
    def __init__(self, samples, length, model, heads, hidden, pieces):
        self.samples, self.length, self.model = samples, length, model
        self.heads, self.hidden, self.pieces = heads, hidden, pieces
        self.rows = samples * length
        self.line = ((1, (6 * samples + 4 + hidden // model) * model), F32)
        self.weights = [
            ((model, 3 * model), BF16), ((model, model), BF16), ((model, hidden), BF16), ((hidden, model), BF16),
        ]
        self.bias = ((heads, length, length), BF16)
        self.probs = ((samples, heads, length, length), BF16)
        self.low = ((self.rows, model), BF16)
        self.full = ((self.rows, model), F32)
        self.qkv = ((self.rows, 3 * model), BF16)
        self.wide = ((self.rows, hidden), BF16)
        self.small = ((samples, 8, model), F32)

    def pack(self, blocks, more=0):
        return [((blocks * self.model, self.model), BF16), ((blocks * self.model + more, self.model), BF16)]


def forward_layer(layer, z, pos, h, lines, biases, weights, earlier):
    return call(
        functools.partial(forward_kernel, layer, z.length, len(weights), len(earlier)),
        pos, (h, *lines), (*biases, *weights, *earlier),
        [z.qkv, z.probs, z.low, z.full, z.full, z.wide, z.wide, z.full, z.low],
        [*z.weights, z.bias, z.line], weight_count(len(weights)) + 1, work=15,
    )


def both_ways(layer, z, pos, h, grad, lines, biases, weights, earlier):
    return call(
        functools.partial(both_kernel, layer, z.pieces, z.length, len(weights), len(earlier)),
        pos, (h, grad, *lines), (*biases, *weights, *earlier),
        [z.low, z.low, z.small, z.small, z.bias, *z.pack(6, z.rows)],
        [*z.weights, z.bias, z.line, z.qkv, z.probs, z.low, z.full, z.full, z.wide, z.wide, z.full,
         z.full, z.low, z.wide, z.low, z.qkv, (z.bias[0], F32), *z.weights],
        weight_count(len(weights)) + 1, work=25,
    )


def backward_mlp(layer, z, pos, grad, middle, lines, act, slope, out_branch, weights, earlier):
    return call(
        functools.partial(backward_mlp_kernel, layer, z.pieces, z.length, len(weights), len(earlier)),
        pos, (grad, middle, *lines, act, slope, out_branch), (*weights, *earlier),
        [z.full, z.small, *z.pack(4)],
        [*z.weights, z.line, z.low, z.wide, z.low, *z.weights[2:]],
        weight_count(len(weights)), work=12,
    )


def backward_attention(layer, z, pos, h, lines, qkv, probs, att, branch, d_middle, d_h1, weights, earlier):
    return call(
        functools.partial(backward_attention_kernel, layer, z.pieces, z.length, len(weights), len(earlier)),
        pos, (h, *lines, qkv, probs, att, branch, d_middle, d_h1), (*weights, *earlier),
        [z.full, z.small, z.bias, *z.pack(2, z.rows)],
        [*z.weights, z.line, z.low, z.qkv, z.low, (z.bias[0], F32), *z.weights[:2]],
        weight_count(len(weights)), work=13,
    )


def partial_kernel(pos, w_ada, cond_a, cond_b, cond_c, cond_d, b_ada, b_qv, b_proj, b_fc1, b_fc2, *rest):
    copied, outs, whole = rest[-6], rest[-5:-1], rest[-1]
    copied[...] = w_ada[...]
    shard = pos[1]
    q, wide = w_ada.shape
    samples, model = cond_a.shape
    whole[...] = jnp.zeros_like(whole)
    whole[pl.ds(pl.multiple_of(shard * q, 16), q), :] = w_ada[...]
    for cond, out in zip((cond_a, cond_b, cond_c, cond_d), outs):
        c = cond[...].astype(F32)
        act = (c * (1.0 / (1.0 + jnp.exp(-c)))).astype(BF16)
        out[:, :wide] = dot(act, whole[...])
        out[:, wide:] = jnp.zeros((samples, 2 * model), F32)
        for f in range(4):
            @pl.when(shard == f)
            def _():
                here = slice(f * b_ada.shape[1], (f + 1) * b_ada.shape[1])
                out[:, here] += b_ada[...].astype(F32)
                for bias, row, at in ((b_qv, 0, 0), (b_proj, 1, 0), (b_fc1, 1, model), (b_fc2, 3, model)):
                    width = bias.shape[1]
                    at += f * width
                    row, at = row + at // (2 * model), wide + at % (2 * model)
                    out[row : row + 1, at : at + width] = bias[...].astype(F32)


def partial_step(pos, w_ada, conds, biases, earlier):
    q, wide = w_ada.shape
    samples, model = conds[0].shape
    return call(
        partial_kernel, pos, (w_ada, *conds, *biases), earlier, [(w_ada.shape, BF16)] + [((samples, wide + 2 * model), F32)] * 4,
        [((4 * q, wide), BF16)],
    )


def line_kernel(pos, own, got_a, got_b, got_c, *rest):
    keep, send, total = rest[-3:]
    section = pos[0]
    samples = own.shape[0]
    each = samples // 2
    model = own.shape[1] // 8
    total[...] = (own[...] + got_a[...]) + (got_b[...] + got_c[...])
    for out, side in ((keep, section), (send, 1 - section)):
        for b in range(each):
            out[:, b * 6 * model : (b + 1) * 6 * model] = total[pl.ds(side * each + b, 1), : 6 * model]
        for row in range(samples):
            at = (6 * each + 2 * row) * model
            out[:, at : at + 2 * model] = total[row : row + 1, 6 * model :]


def line_step(pos, own, got, earlier):
    samples, model = own.shape[0], own.shape[1] // 8
    shape = (1, (3 * samples + 8) * model)
    return call(line_kernel, pos, (own, *got), earlier, [(shape, F32)] * 2, [(own.shape, F32)])


def sum_kernel(keep, other, own, *messages):
    size = own.shape[0]
    for p in range(4):
        total = keep[p * size : (p + 1) * size, :].astype(F32) + other[p * size : (p + 1) * size, :].astype(F32)
        if p == 0:
            own[...] = total
        else:
            messages[p - 1][...] = total.astype(BF16)


def sum_step(keep, other):
    shape = (keep.shape[0] // 4, keep.shape[1])
    return pl.pallas_call(
        sum_kernel,
        out_shape=[jax.ShapeDtypeStruct(shape, F32)] + [jax.ShapeDtypeStruct(shape, BF16)] * 3,
        compiler_params=pltpu.CompilerParams(vmem_limit_bytes=VMEM_BYTES),
    )(keep, other)


def halve(bit, own, got, keep, send):
    n = own.shape[0] // 4
    for high in range(2):
        for out, low in ((keep, bit), (send, 1 - bit)):
            rows = pl.ds(pl.multiple_of((2 * high + low) * n, 16), n)
            total = own[rows, :]
            for piece in got:
                total = total + piece[rows, :].astype(F32)
            out[high * n : (high + 1) * n, :] = total.astype(out.dtype)


def quarter(bit, kept, got, keep, send):
    n = kept.shape[0] // 2
    for out, high in ((keep, bit), (send, 1 - bit)):
        rows = pl.ds(pl.multiple_of(high * n, 16), n)
        out[...] = (kept[rows, :] + got[rows, :].astype(F32)).astype(out.dtype)


def pair_up(bit, own, got, out):
    n = own.shape[0]
    out[pl.ds(pl.multiple_of(bit * n, 16), n), :] = own[...]
    out[pl.ds(pl.multiple_of((1 - bit) * n, 16), n), :] = got[...]


def whole_from(bit, pair, got, out, at=0):
    n = pair.shape[0] // 2
    for high in range(2):
        rows = slice(high * n, (high + 1) * n)
        out[pl.ds(pl.multiple_of(at + (2 * high + bit) * n, 16), n), :] = pair[rows, :]
        out[pl.ds(pl.multiple_of(at + (2 * high + 1 - bit) * n, 16), n), :] = got[rows, :]


def a_kernel(pos, own1, got_a, got_b, got_c, keep_m, other_m, keep1, send1, own_m, *messages):
    halve(pos[2] & 1, own1, (got_a, got_b, got_c), keep1, send1)
    sum_kernel(keep_m, other_m, own_m, *messages)


def a_step(pos, own1, got1, keep_m, other_m):
    two = (own1.shape[0] // 2, own1.shape[1])
    one = (keep_m.shape[0] // 4, keep_m.shape[1])
    return call(a_kernel, pos, (own1, *got1, keep_m, other_m), (), [(two, F32), (two, BF16), (one, F32)] + [(one, BF16)] * 3, [])


def b_kernel(pos, kept1, got1, own_m, got_a, got_b, got_c, keep1, send1, keep_m, send_m):
    quarter(pos[2] >> 1, kept1, got1, keep1, send1)
    halve(pos[2] & 1, own_m, (got_a, got_b, got_c), keep_m, send_m)


def b_step(pos, kept1, got1, own_m, got_m):
    one, two = (kept1.shape[0] // 2, kept1.shape[1]), (own_m.shape[0] // 2, own_m.shape[1])
    return call(b_kernel, pos, (kept1, got1, own_m, *got_m), (), [(one, F32), (one, BF16), (two, F32), (two, BF16)], [])


def c_kernel(pos, kept1, got1, kept_m, got_m, quarter1, keep_m, send_m):
    quarter1[...] = (kept1[...] + got1[...].astype(F32)).astype(BF16)
    quarter(pos[2] >> 1, kept_m, got_m, keep_m, send_m)


def c_step(pos, kept1, got1, kept_m, got_m):
    one = (kept_m.shape[0] // 2, kept_m.shape[1])
    return call(c_kernel, pos, (kept1, got1, kept_m, got_m), (), [(kept1.shape, BF16), (one, F32), (one, BF16)], [])


def d_kernel(pos, quarter1, got1, kept_m, got_m, pair1, quarter_m):
    pair_up(pos[2] >> 1, quarter1, got1, pair1)
    quarter_m[...] = (kept_m[...] + got_m[...].astype(F32)).astype(BF16)


def d_step(pos, quarter1, got1, kept_m, got_m):
    two = (2 * quarter1.shape[0], quarter1.shape[1])
    return call(d_kernel, pos, (quarter1, got1, kept_m, got_m), (), [(two, BF16), (kept_m.shape, BF16)], [])


def e_kernel(pos, pair1, got1, quarter_m, got_m, half1, pair_m):
    whole_from(pos[2] & 1, pair1, got1, half1)
    pair_up(pos[2] >> 1, quarter_m, got_m, pair_m)


def e_step(pos, pair1, got1, quarter_m, got_m):
    two = (2 * quarter_m.shape[0], quarter_m.shape[1])
    return call(e_kernel, pos, (pair1, got1, quarter_m, got_m), (), [((2 * pair1.shape[0], pair1.shape[1]), BF16), (two, BF16)], [])


def g_kernel(pos, quarter_a, got_a, got_b, got_c, pair_m, got_m, half1, *rest):
    own, send = rest[-2:]
    n = quarter_a.shape[0]

    def layer0(out):
        for j, piece in enumerate((quarter_a, got_a, got_b, got_c)):
            out[pl.ds(pl.multiple_of((pos[2] ^ j) * n, 16), n), :] = piece[...]
        whole_from(pos[2] & 1, pair_m, got_m, out, 4 * n)

    @pl.when(pos[0] == 0)
    def _():
        layer0(own)
        send[...] = half1[...]

    @pl.when(pos[0] == 1)
    def _():
        layer0(send)
        own[...] = half1[...]


def g_step(pos, quarter_a, got_a, pair_m, got_m, half1, earlier):
    return call(g_kernel, pos, (quarter_a, *got_a, pair_m, got_m, half1), earlier, [(half1.shape, BF16)] * 2, [])


def plane_kernel(samples, pos, keep, other, kept_small, other_small, cond, own, own_small, *rest):
    messages, work = rest[:3], rest[3]
    section = pos[0]
    size, model = own.shape
    for p in range(4):
        rows = slice(p * size, (p + 1) * size)
        total = keep[rows, :].astype(F32) + other[rows, :].astype(F32)
        if p == 0:
            own[...] = total
        else:
            messages[p - 1][:size, :] = total.astype(BF16)
    theirs = other_small[...].astype(F32)
    mine = kept_small[...]
    each = samples // 2
    work[...] = jnp.zeros_like(work)
    for b in range(each):
        for kind in range(6):
            row = b * 8 + kind if kind < 3 else (each + b) * 8 + kind - 3
            work[pl.ds(kind * samples + section * each + b, 1), :] = mine[row : row + 1, :]
            work[pl.ds(kind * samples + (1 - section) * each + b, 1), :] = theirs[row : row + 1, :]
    work[6 * samples : 7 * samples, :] = cond[...].astype(F32)
    both = mine + theirs
    bias_rows = sum(both[(each + b) * 8 + 3 : (each + b) * 8 + 8, :] for b in range(each))
    more_rows = sum(both[b * 8 + 3 : b * 8 + 6, :] for b in range(each))
    at = 7 * samples
    work[at : at + 5, :] = bias_rows
    work[at + 5 : at + 8, :] = more_rows
    work[at + 8 : at + 8 + HIGH, :] = both[2 * each * 8 :, :]
    small = work[...].astype(BF16)
    own_small[...] = small
    for message in messages:
        message[size:, :] = small


def plane_step(pos, keep, other, kept_small, other_small, cond):
    samples, model = cond.shape
    size = keep.shape[0] // 4
    small = -(-(7 * samples + 8 + HIGH) // 16) * 16
    outs = [((size, model), F32), ((small, model), BF16)] + [((size + small, model), BF16)] * 3
    return call(
        functools.partial(plane_kernel, samples), pos, (keep, other, kept_small, other_small, cond), (), outs,
        [((small, model), F32)],
    )


def column_kernel(samples, pos, own, own_small, got_a, got_b, got_c, part, own_out, *rest):
    messages, work = rest[:3], rest[3]
    rank = pos[2]
    size, model = own.shape
    n = size // 4
    got = (got_a, got_b, got_c)
    for j in range(4):
        at = pl.multiple_of((rank ^ j) * n, 16)
        total = own[pl.ds(at, n), :]
        for piece in got:
            total = total + piece[pl.ds(at, n), :].astype(F32)
        if j == 0:
            part[...] = total
        else:
            messages[j - 1][:n, :] = total.astype(BF16)
    smalls = [own_small[...].astype(F32)] + [piece[size:, :].astype(F32) for piece in got]
    work[...] = jnp.zeros_like(work)
    for p in range(4):
        for kind in range(7):
            at = (kind * 4 + p) * samples
            work[at : at + samples, :] = smalls[p][kind * samples : (kind + 1) * samples, :]
    at = 7 * samples
    summed = (smalls[0] + smalls[1]) + (smalls[2] + smalls[3])
    work[4 * at : 4 * at + 8 + HIGH, :] = summed[at : at + 8 + HIGH, :]
    small = work[...].astype(BF16)
    own_out[...] = small
    for message in messages:
        message[n:, :] = small


def column_step(pos, own, own_small, got, samples):
    size, model = own.shape
    small = -(-(28 * samples + 8 + HIGH) // 16) * 16
    outs = [((size // 4, model), F32), ((small, model), BF16)] + [((size // 4 + small, model), BF16)] * 3
    return call(
        functools.partial(column_kernel, samples), pos, (own, own_small, *got), (), outs, [((small, model), F32)]
    )


def finish_kernel(samples, width, pos, own_small, got_a, got_b, got_c,
                  g_ada, g_b_ada, g_b_qv, g_b_proj, g_b_fc1, g_b_fc2, g_table, work, whole, row):
    shard, rank = pos[1], pos[2]
    model = own_small.shape[1]
    each = 4 * samples
    n = got_a.shape[0] - own_small.shape[0]
    pieces = [own_small[...]] + [piece[n:, :] for piece in (got_a, got_b, got_c)]
    for j in range(4):
        for kind in range(7):
            at = pl.multiple_of(kind * 4 * each + (rank ^ j) * each, 16)
            work[pl.ds(at, each), :] = pieces[j][kind * each : (kind + 1) * each, :].astype(F32)
    cond = work[24 * each :, :]
    act = (cond * (1.0 / (1.0 + jnp.exp(-cond)))).astype(BF16)
    for kind in range(6):
        rows = work[kind * 4 * each : (kind + 1) * 4 * each, :]
        whole[...] = dot_cols(act, rows.astype(BF16))
        cols = slice(kind * model, (kind + 1) * model)
        g_ada[:, cols] = whole[pl.ds(pl.multiple_of(shard * width, 16), width), :]
        row[:, cols] = col_sum(rows)
    at = 7 * each
    rows = [piece[at : at + 8 + HIGH, :].astype(F32) for piece in pieces]
    summed = (rows[0] + rows[1]) + (rows[2] + rows[3])
    for c in range(4):
        row[:, (6 + c) * model : (7 + c) * model] = summed[1 + c : 2 + c, :]
    row[:, 10 * model : 11 * model] = summed[5:6, :]
    row[:, 11 * model : 12 * model] = summed[6:7, :]
    row[:, 12 * model : 13 * model] = summed[7:8, :]
    row[:, 13 * model : 14 * model] = summed[0:1, :]
    for f in range(4):
        @pl.when(shard == f)
        def _():
            for out, start in ((g_b_ada, 0), (g_b_fc1, 6), (g_b_qv, 10), (g_b_proj, 12), (g_b_fc2, 13)):
                size = out.shape[1]
                out[...] = row[:, start * model + f * size : start * model + (f + 1) * size]
    heads, entries = g_table.shape
    for high in range(-(-entries // LOW)):
        size = min(LOW, entries - high * LOW)
        for head in range(heads):
            g_table[head : head + 1, high * LOW : high * LOW + size] = summed[
                8 + high : 9 + high, head * LOW : head * LOW + size
            ]


def finish_step(pos, own_small, got, samples, width, heads, entries):
    model = own_small.shape[1]
    sizes = [6 * width, 2 * width, width, 4 * width, width]
    return call(
        functools.partial(finish_kernel, samples, width), pos, (own_small, *got), (),
        [((width, 6 * model), F32)] + [((1, size), F32) for size in sizes] + [((heads, entries), F32)],
        [((7 * 16 * samples, model), F32), ((model, model), F32), ((1, 14 * model), F32)],
    )


def cond_kernel(samples, pos, small, cond, *rest):
    out, w_ada = rest[-2:]
    model = cond.shape[1]
    for p, piece in enumerate(rest[:-2]):
        q = piece.shape[0]
        off = pl.multiple_of((pos[1] ^ p) * q, 16) if q < model else 0
        w_ada[pl.ds(off, q), :] = piece[...]
    total = None
    for kind in range(6):
        rows = small[...].astype(F32)[kind * samples : (kind + 1) * samples, :].astype(BF16)
        part = dot_rows(rows, w_ada[:, kind * model : (kind + 1) * model])
        total = part if total is None else total + part
    c = cond[...].astype(F32)
    gate = 1.0 / (1.0 + jnp.exp(-c))
    out[...] = total * (gate * (1.0 + c * (1.0 - gate)))


def cond_step(pos, small, w_ada, cond):
    model = cond.shape[1]
    return call(
        functools.partial(cond_kernel, cond.shape[0]), pos, (small, cond, *w_ada), (), [(cond.shape, F32)],
        [((model, w_ada[0].shape[1]), BF16)],
    )[0]


def final_kernel(pos, own, other, g_qkv, g_proj, g_fc1, g_fc2):
    q, model = g_proj.shape

    def write(first, second):
        for c in range(2):
            g_qkv[:, c * model : (c + 1) * model] = first[c * q : (c + 1) * q, :].astype(F32)
        g_qkv[:, 2 * model : 3 * model] = second[:q, :].astype(F32)
        g_proj[...] = second[q : 2 * q, :].astype(F32)
        for c in range(4):
            g_fc1[:, c * model : (c + 1) * model] = first[(2 + c) * q : (3 + c) * q, :].astype(F32)
        g_fc2[...] = second[2 * q : 6 * q, :].astype(F32)

    @pl.when(pos[0] == 0)
    def _():
        write(own, other)

    @pl.when(pos[0] == 1)
    def _():
        write(other, own)


def final_step(pos, own, other):
    q, model = own.shape[0] // 6, own.shape[1]
    return call(
        final_kernel, pos, (own, other), (),
        [((q, 3 * model), F32), ((q, model), F32), ((q, 4 * model), F32), ((4 * q, model), F32)], [],
    )


def pack_kernel(qkv, proj, fc1, fc2, out):
    q, model = proj.shape
    for c in range(3):
        out[c * q : (c + 1) * q, :] = qkv[:, c * model : (c + 1) * model]
    out[3 * q : 4 * q, :] = proj[...]
    for c in range(4):
        out[(4 + c) * q : (5 + c) * q, :] = fc1[:, c * model : (c + 1) * model]
    out[8 * q : 12 * q, :] = fc2[...]


def pack_shard(own):
    q, model = own[1].shape
    return pl.pallas_call(
        pack_kernel,
        out_shape=jax.ShapeDtypeStruct((12 * q, model), BF16),
        compiler_params=pltpu.CompilerParams(vmem_limit_bytes=VMEM_BYTES),
    )(*own)


def after(values, others):
    return pl.pallas_call(
        lambda *refs: None,
        out_shape=[jax.ShapeDtypeStruct(v.shape, v.dtype) for v in values],
        in_specs=[pl.BlockSpec(memory_space=pl.ANY)] * (len(values) + len(others)),
        out_specs=[pl.BlockSpec(memory_space=pl.ANY)] * len(values),
        input_output_aliases={i: i for i in range(len(values))},
    )(*values, *others)


def lookup_kernel(table, index, *rest):
    out, work = rest[-2:]
    heads, length = out.shape[0], out.shape[1]
    high_count = table.shape[0] // 8
    values = table[...]
    low_id = lax.broadcasted_iota(jnp.int32, (LOW, length), 0)

    def step(i, carry):
        block = index[pl.ds(pl.multiple_of(i * 8, 8), 8), :]
        for r in range(8):
            entry = block[r : r + 1, :]
            picks = jnp.where(low_id == (entry & (LOW - 1)), 1.0, 0.0).astype(BF16)
            found = dot(values, picks).reshape(high_count, 8, length)
            high = jnp.broadcast_to(entry >> LOW_BITS, (8, length))
            bit = high_count // 2
            while bit:
                chosen = (high & bit) != 0
                found = jnp.where(chosen[None], found[bit : 2 * bit], found[:bit])
                bit //= 2
            for head in range(heads):
                work[head, pl.ds(i * 8 + r, 1), :] = found[0, head : head + 1, :]
        return carry

    lax.fori_loop(0, length // 8, step, 0)
    out[...] = work[...].astype(BF16)


def lookup(table, index, earlier):
    heads, entries = table.shape
    high_count = HIGH
    padded = jnp.pad(table, ((0, 8 - heads), (0, high_count * LOW - entries)))
    rows = jnp.transpose(padded.reshape(8, high_count, LOW), (1, 0, 2)).reshape(high_count * 8, LOW)
    length = index.shape[0]
    return pl.pallas_call(
        lookup_kernel,
        out_shape=jax.ShapeDtypeStruct((heads, length, length), BF16),
        in_specs=[pl.BlockSpec(memory_space=pltpu.VMEM)] * 2 + [pl.BlockSpec(memory_space=pl.ANY)] * len(earlier),
        out_specs=pl.BlockSpec(memory_space=pltpu.VMEM),
        scratch_shapes=[pltpu.VMEM((heads, length, length), F32)],
        cost_estimate=cost(11),
        compiler_params=pltpu.CompilerParams(vmem_limit_bytes=VMEM_BYTES),
    )(rows, index, *earlier)


def swap_section(value):
    return lax.ppermute(value, "section", [(0, 1), (1, 0)])


def pairs_of(count, step):
    return [(i, i ^ step) for i in range(count)]


def by_rank(pieces, rank):
    stack = jnp.stack(pieces)
    count = len(pieces)
    bit = 1
    while bit < count:
        moved = jnp.stack([stack[i ^ bit] for i in range(count)])
        stack = jnp.where((rank & bit) != 0, moved, stack)
        bit *= 2
    return stack


def section_sums(keep, other, shards):
    size = keep.shape[0] // shards
    return [
        keep[p * size : (p + 1) * size].astype(F32) + other[p * size : (p + 1) * size].astype(F32)
        for p in range(shards)
    ]


def low_pieces(sums):
    return [x.astype(BF16) for x in sums[1:]]


def to_peers(messages, axis):
    count = lax.axis_size(axis)
    return [lax.ppermute(messages[p - 1], axis, pairs_of(count, p)) for p in range(1, count)]


def add_pieces(own, got):
    total = own
    for piece in got:
        total = total + piece.astype(F32)
    return total


def replica_parts(total, rank):
    replicas = lax.axis_size("rep")
    parts = total if total.ndim == 3 else total.reshape(replicas, total.shape[0] // replicas, -1)
    low = parts.astype(BF16)
    mine = lax.dynamic_index_in_dim(parts, rank, 0, keepdims=False)
    return mine, [lax.dynamic_index_in_dim(low, rank ^ j, 0, keepdims=False) for j in range(1, replicas)]


def unpack_attention(pack):
    q = pack.shape[0] // 4
    return jnp.concatenate([pack[c * q : (c + 1) * q] for c in range(3)], axis=1), pack[3 * q :]


def unpack_mlp(pack):
    q = pack.shape[0] // 8
    return jnp.concatenate([pack[c * q : (c + 1) * q] for c in range(4)], axis=1), pack[4 * q :]


def pad_rows(value):
    return jnp.pad(value, ((0, -value.shape[0] % 16), (0, 0)))


def from_peers(value, axis):
    return [lax.ppermute(value, axis, pairs_of(lax.axis_size(axis), p)) for p in range(1, lax.axis_size(axis))]


def pair_sum(values):
    while len(values) > 1:
        values = [values[i] + values[i + 1] for i in range(0, len(values), 2)]
    return values[0]


def per_device(inputs, conditioning, cotangent, micro_sizes, relative_bias_index,
               w_ada, w_qkv, w_proj, w_fc1, w_fc2, b_ada, b_qv, b_proj, b_fc1, b_fc2, bias_table):
    section = lax.axis_index("section")
    shard = lax.axis_index("fsdp")
    rank = lax.axis_index("rep")
    shards, replicas = lax.axis_size("fsdp"), lax.axis_size("rep")
    direct = shards == 4 and replicas == 4
    is_first = section == 0
    samples, length, model = inputs.shape
    heads, entries = bias_table.shape[1:]
    half = samples // 2
    z = Sizes(half, length, model, heads, 4 * model, shards if direct else 1)
    pos = jnp.stack([section, shard, rank]).astype(jnp.int32)

    def mine(first, second):
        return jnp.where(is_first, first, second)

    def own_samples(array):
        return lax.dynamic_slice_in_dim(array, section * half, half, 0)

    def in_order(own, other):
        return jnp.where(is_first, jnp.concatenate([own, other]), jnp.concatenate([other, own]))

    live = (jnp.arange(half)[:, None, None] < lax.dynamic_index_in_dim(micro_sizes[0], section, 0)).astype(BF16)
    h0 = own_samples(inputs).reshape(half * length, model)
    grad1 = (own_samples(cotangent) * live).reshape(half * length, model)
    index = relative_bias_index
    own_raw = [w_qkv[0], w_proj[0], w_fc1[0], w_fc2[0]]
    width = model // shards
    if direct:
        conds = [conditioning] + from_peers(conditioning, "fsdp")
        own_pack = pack_shard(own_raw)
        middle_row = own_pack.shape[0] // 2
        got_x = lax.ppermute(own_pack, "fsdp", pairs_of(shards, 1))
        got_y = lax.ppermute(own_pack, "fsdp", pairs_of(shards, 2))
        bias_own = lookup(bias_table[0], index, [own_pack, *conds[1:]])
        w_ada_copy, *partial = partial_step(pos, w_ada[0], conds, (b_ada, b_qv, b_proj, b_fc1, b_fc2), [bias_own])
        got_first = lax.ppermute(got_x[:middle_row], "fsdp", pairs_of(shards, 2))
        got_second = lax.ppermute(got_y[middle_row:], "fsdp", pairs_of(shards, 1))
        own_weights = [own_pack, got_x, got_y, got_first, got_second]
        weights = own_weights + [swap_section(w) for w in own_weights]
        own_line, send_line = line_step(pos, partial[0], after(to_peers(partial[1:], "fsdp"), [got_x, got_y]), [h0, grad1])
    else:
        row = jnp.concatenate([b_ada, b_qv, b_proj, b_fc1, b_fc2], axis=1)
        bias_rows = lax.all_gather(row[0], "fsdp", axis=0)
        whole = [lax.all_gather(w, "fsdp", axis=0, tiled=True) for w in own_raw]
        own_whole = pack_shard(whole)
        weights = [own_whole, swap_section(own_whole)]
        acts = jax.nn.silu(conditioning.astype(F32)).astype(BF16)
        modulation = dot(acts, lax.all_gather(w_ada[0], "fsdp", axis=0, tiled=True))
        bias_own = lookup(bias_table[0], index, [])
        cuts = [b_ada.shape[1], b_qv.shape[1], b_proj.shape[1], b_fc1.shape[1], b_fc2.shape[1]]
        biases, at = [], 0
        for cut in cuts:
            biases.append(bias_rows[:, at : at + cut].reshape(1, -1).astype(F32))
            at += cut
        modulation = modulation + biases[0]
        other_samples = lax.dynamic_slice_in_dim(modulation, (1 - section) * half, half, 0)
        own_line = jnp.concatenate([own_samples(modulation).reshape(1, -1)] + biases[1:], axis=1)
        send_line = jnp.concatenate([other_samples.reshape(1, -1)] + biases[1:], axis=1)
    lines = (own_line, swap_section(send_line))
    bias_heads = (bias_own, swap_section(bias_own))

    if direct:
        w_ada_later = after([w_ada_copy], weights[3:5])[0]
        w_ada_pieces = [w_ada_later] + from_peers(w_ada_later, "fsdp")
    else:
        w_ada_pieces = [lax.all_gather(w_ada[0], "fsdp", axis=0, tiled=True)]
    qkv, probs, att, branch, middle, act, slope, out_branch, h1 = forward_layer(0, z, pos, h0, lines, bias_heads, weights, w_ada_pieces[:1] if direct else [])
    out1, d_h1, small_a1, small_m1, scores1, keep1, send1 = both_ways(1, z, pos, h1, grad1, lines, bias_heads, weights, w_ada_pieces[1:])
    rows = half * length
    table1 = table_step(scores1, index)
    other1 = after([swap_section(send1)], [table1])[0]
    if direct:
        own1, *messages = sum_step(keep1, other1)
        earlier = messages
    else:
        earlier = []
    d_middle, small_m0, keep_m0, send_m0 = backward_mlp(0, z, pos, d_h1, middle, lines, act, slope, out_branch, weights, earlier)
    if direct:
        got1 = after(to_peers(messages, "fsdp"), [d_middle])
        send_m0 = after([send_m0], got1)[0]
    other_m0 = swap_section(send_m0)
    if direct:
        keep_z1, send_z1, own_m, *messages = a_step(pos, own1, got1, keep_m0, other_m0)
        earlier = [send_z1, *messages]
    else:
        sums1 = section_sums(keep1, other1[: keep1.shape[0]], z.pieces)
        sums_m0 = section_sums(keep_m0, other_m0, z.pieces)
    d_h0, small_a0, scores0, keep_a0, send_a0 = backward_attention(
        0, z, pos, h0, lines, qkv, probs, att, branch, d_middle, d_h1, weights, earlier
    )
    smalls = (small_a0, small_m0, small_a1, small_m1)
    size_a = keep_a0.shape[0]

    def replica(value, step):
        return lax.ppermute(value, "rep", pairs_of(replicas, step))

    if direct:
        got_z1, *got_m = after([replica(send_z1, 1), *to_peers(messages, "fsdp")], [d_h0])
        other_a0 = swap_section(after([send_a0], [got_z1, *got_m])[0])
        keep_z1, send_z1, keep_zm, send_zm = b_step(pos, keep_z1, got_z1, own_m, got_m)
        kept_small, send_small = small_step(pos, scores0, index, smalls, table1, [send_z1, send_zm])
        other_small = swap_section(send_small)
        other_a0, got_z1, got_zm = after([other_a0, replica(send_z1, 2), replica(send_zm, 1)], [kept_small])
        own_a0, own_small, *messages = plane_step(pos, keep_a0, other_a0, kept_small, other_small, conditioning)
        got = to_peers(messages, "fsdp")
        got_z1, got_zm = after([got_z1, got_zm], [own_small])
        quarter1, keep_zm, send_zm = c_step(pos, keep_z1, got_z1, keep_zm, got_zm)
        part0, plane_small, *messages = column_step(pos, own_a0, own_small, got, samples)
        got_z1, got_zm = after([replica(quarter1, 2), replica(send_zm, 2)], [plane_small])
        got = to_peers(messages, "rep")
        pair1, quarter_m = d_step(pos, quarter1, got_z1, keep_zm, got_zm)
        cond_part = cond_step(pos, after([own_small], [pair1])[0], w_ada_pieces, conditioning)
        size = part0.shape[0]
        quarter0 = add_pieces(part0, [x[:size] for x in got]).astype(BF16)
        got_z1, got_zm, cond_part = after([replica(pair1, 1), replica(quarter_m, 2), cond_part], [quarter0])
        half1, pair_m = e_step(pos, pair1, got_z1, quarter_m, got_zm)
        g_ada, g_b_ada, g_b_qv, g_b_proj, g_b_fc1, g_b_fc2, g_table = finish_step(
            pos, plane_small, got, samples, width, heads, entries
        )
        cond_grad = cond_part + swap_section(cond_part)
        own_half, send_half = g_step(
            pos, quarter0, from_peers(quarter0, "rep"), pair_m, replica(pair_m, 1), half1, [g_ada, cond_grad]
        )
    else:
        other_a0 = swap_section(send_a0)
        kept_small, send_small = small_step(pos, scores0, index, smalls, table1, [])
        theirs = swap_section(send_small).astype(F32)
        both = kept_small + theirs
        cut = half * 8

        def d_mod_of(values):
            a, m = values[:cut].reshape(half, 8, model), values[cut : 2 * cut].reshape(half, 8, model)
            return jnp.concatenate([a[:, :3], m[:, :3]], axis=1)

        low = in_order(d_mod_of(kept_small), d_mod_of(theirs)).astype(BF16)
        bias_rows = jnp.sum(both[: 2 * cut].reshape(2, half, 8, model), axis=1)
        summed = jnp.concatenate([bias_rows[1, 3:8], bias_rows[0, 3:6], both[2 * cut :]])
        cond_part = cond_step(pos, jnp.transpose(low, (1, 0, 2)).reshape(-1, model), w_ada_pieces, conditioning)
        kept = jnp.concatenate([low, conditioning[:, None]], axis=1)
        kept = lax.all_gather(kept, ("fsdp", "rep"), axis=0, tiled=True)
        summed = lax.psum(summed, ("fsdp", "rep"))
        act_all = jax.nn.silu(kept[:, 6].astype(F32)).astype(BF16)
        act_cols = lax.dynamic_slice_in_dim(act_all, shard * width, width, 1)
        g_ada = jnp.concatenate([dot_cols(act_cols, kept[:, i]) for i in range(6)], axis=1)
        g_b_ada = jnp.sum(kept[:, :6].astype(F32), axis=0).reshape(-1)
        vectors = [g_b_ada, summed[5:7].reshape(-1), summed[7], summed[1:5].reshape(-1), summed[0]]
        g_b_ada, g_b_qv, g_b_proj, g_b_fc1, g_b_fc2 = [
            lax.dynamic_slice_in_dim(v, shard * (v.shape[0] // shards), v.shape[0] // shards, 0)[None] for v in vectors
        ]
        g_table = jnp.transpose(summed[8:].reshape(HIGH, heads, LOW), (1, 0, 2)).reshape(heads, HIGH * LOW)[:, :entries]
        sums_a0 = section_sums(keep_a0, other_a0[:size_a], z.pieces)
        cond_grad = cond_part + swap_section(cond_part)
        half0 = jnp.concatenate([sums_a0[0], sums_m0[0]]).astype(BF16)
        half1 = sums1[0].astype(BF16)
        own_half, send_half = mine(half0, half1), mine(half1, half0)
    grads = final_step(pos, own_half, swap_section(send_half))
    if not direct:
        grads = [lax.psum_scatter(g.astype(BF16), "fsdp", scatter_dimension=0, tiled=True) for g in grads]
        grads = [g.astype(F32) for g in lax.psum(tuple(grads), "rep")]
    g_qkv, g_proj, g_fc1, g_fc2 = grads

    activations = in_order(
        mine(h1, out1).reshape(half, length, model), other1[keep1.shape[0] :].reshape(half, length, model)
    )
    input_grads = in_order(
        mine(d_h0, d_h1.astype(F32)).reshape(half, length, model),
        other_a0[size_a : size_a + rows].astype(F32).reshape(half, length, model),
    )

    return (
        activations[None], input_grads[None], cond_grad,
        g_ada[None], g_qkv[None], g_proj[None], g_fc1[None], g_fc2[None],
        g_b_ada, g_b_qv, g_b_proj, g_b_fc1, g_b_fc2,
        g_table[None],
    )


def solution(mesh):
    batch = ("fsdp", "rep")
    matrix = P("section", "fsdp", None)
    vector = P("section", "fsdp")
    return jax.shard_map(
        per_device,
        mesh=mesh,
        in_specs=(
            P(batch, None, None), P(batch, None), P(batch, None, None), P(batch, None), P(),
            matrix, matrix, matrix, matrix, matrix, vector, vector, vector, vector, vector,
            P("section", None, None),
        ),
        out_specs=(
            P("section", batch, None, None), P("section", batch, None, None), P(batch, None),
            matrix, matrix, matrix, matrix, matrix, vector, vector, vector, vector, vector,
            P("section", None, None),
        ),
        check_vma=False,
    )
```

```python
import functools

import jax
import jax.numpy as jnp
from jax import lax
from jax.experimental import pallas as pl
from jax.experimental.pallas import tpu as pltpu
from jax.sharding import PartitionSpec as P

EPSILON = 1e-06
F32 = jnp.float32
BF16 = jnp.bfloat16
VMEM_BYTES = 58 * 1024 * 1024
LOW_BITS = 6
LOW = 1 << LOW_BITS
HIGH = 16


def dot(a, b):
    return jnp.dot(a, b, preferred_element_type=F32)


def dot_rows(a, b):
    return lax.dot_general(a, b, (((1,), (1,)), ((), ())), preferred_element_type=F32)


def dot_cols(a, b):
    return lax.dot_general(a, b, (((0,), (0,)), ((), ())), preferred_element_type=F32)


def norm_parts(v):
    centre = v - jnp.mean(v, axis=-1, keepdims=True)
    inverse = lax.rsqrt(jnp.mean(centre * centre, axis=-1, keepdims=True) + EPSILON)
    return centre * inverse, inverse


def norm_back(d_normed, scale, normed, inverse):
    d = d_normed * (1.0 + scale)
    return inverse * (
        d
        - jnp.mean(d, axis=-1, keepdims=True)
        - normed * jnp.mean(d * normed, axis=-1, keepdims=True)
    )


def col_sum(v):
    return jnp.sum(v, axis=0, keepdims=True)


def half_masks(width):
    lane = lax.broadcasted_iota(jnp.int32, (1, width), 1)
    first = jnp.where(lane < width // 2, 1.0, 0.0)
    return first.astype(BF16), (1.0 - first).astype(BF16)


def block_targets(mats, off, q):
    w_qkv, w_proj, w_fc1, w_fc2 = mats
    model = w_proj.shape[0]
    targets = [w_qkv.at[pl.ds(off, q), pl.ds(c * model, model)] for c in range(3)]
    targets.append(w_proj.at[pl.ds(off, q), :])
    targets += [w_fc1.at[pl.ds(off, q), pl.ds(c * model, model)] for c in range(4)]
    targets.append(w_fc2.at[pl.ds(off * 4, 4 * q), :])
    return targets


def weight_count(refs):
    return 9 if refs == 2 else 36


def weight_loads(layer, section, shard, refs, mats, sems):
    model = mats[1].shape[0]
    plans = []
    if len(refs) == 2:
        for i, target in enumerate(block_targets(mats, 0, model)):
            rows = pl.ds(i * model, 4 * model if i == 8 else model)
            plans.append((refs[0].at[rows, :], refs[1].at[rows, :], target, i < 4))
    else:
        count = len(refs) // 2
        q = refs[0].shape[0] // 12
        for p in range(4):
            targets = block_targets(mats, pl.multiple_of((shard ^ p) * q, 16), q)
            for i, target in enumerate(targets):
                which, at = p, i
                if p == 3 and i >= 6:
                    which, at = 4, i - 6
                rows = pl.ds(at * q, 4 * q if i == 8 else q)
                plans.append((refs[which].at[rows, :], refs[count + which].at[rows, :], target, i < 4))
    ones = [pltpu.make_async_copy(x[0], x[2], sems.at[i]) for i, x in enumerate(plans)]
    twos = [pltpu.make_async_copy(x[1], x[2], sems.at[i]) for i, x in enumerate(plans)]

    @pl.when(section == layer)
    def _():
        for copy in ones:
            copy.start()

    @pl.when(section != layer)
    def _():
        for copy in twos:
            copy.start()

    return (
        [copy for copy, x in zip(ones, plans) if x[3]],
        [copy for copy, x in zip(ones, plans) if not x[3]],
    )


def wait_all(copies):
    for copy in copies:
        copy.wait()


def put_half(refs, section, half, at, value):
    keep, send = refs
    rows = slice(at, at + value.shape[0])

    @pl.when(section == half)
    def _():
        keep[rows, :] = value

    @pl.when(section != half)
    def _():
        send[rows, :] = value


def pack_attention(refs, section, g_qkv, g_proj, shard, pieces, stride, first):
    model = g_proj.shape[0]
    q = model // pieces
    for p in range(pieces):
        off = pl.multiple_of((shard ^ p) * q, 16) if pieces > 1 else 0
        at = (stride * p + first) * q
        for c in range(3):
            value = g_qkv[pl.ds(off, q), c * model : (c + 1) * model]
            put_half(refs, section, c // 2, at + (c % 2) * q, value)
        put_half(refs, section, 1, at + q, g_proj[pl.ds(off, q), :])


def pack_mlp(refs, section, g_fc1, g_fc2, shard, pieces, stride, first):
    model = g_fc1.shape[0]
    q = model // pieces
    for p in range(pieces):
        off = pl.multiple_of((shard ^ p) * q, 16) if pieces > 1 else 0
        at = (stride * p + first) * q
        for c in range(4):
            value = g_fc1[pl.ds(off, q), c * model : (c + 1) * model]
            put_half(refs, section, 0, at + c * q, value)
        put_half(refs, section, 1, at, g_fc2[pl.ds(pl.multiple_of(off * 4, 16), 4 * q), :])


class Modulation:
    def __init__(self, line, model):
        self.line, self.model = line, model

    def __getitem__(self, key):
        b, rows, _ = key
        return self.line[:, pl.ds(pl.multiple_of((6 * b + rows.start) * self.model, 128), self.model)]


def bias_at(line, samples, model, start, size):
    return line[:, (6 * samples + start) * model : (6 * samples + start + size) * model]


def attention_forward(b, length, h, mod, bias, w_qkv, w_proj, b_qkv, b_proj, qkv, probs, att, branch, middle):
    model = w_proj.shape[0]
    heads = bias.shape[0]
    pair = 2 * model // heads
    rows = pl.ds(pl.multiple_of(b * length, length), length)
    masks = half_masks(pair)
    x = h[rows, :].astype(F32)
    normed, _ = norm_parts(x)
    normed_low = (normed * (1.0 + mod[b, 1:2, :]) + mod[b, 0:1, :]).astype(BF16)
    qkv[rows, :] = (dot(normed_low, w_qkv[...]) + b_qkv[...]).astype(BF16)
    for j in range(heads // 2):
        q_pair = qkv[rows, j * pair : (j + 1) * pair] * BF16((pair // 2) ** (-0.5))
        k_pair = qkv[rows, model + j * pair : model + (j + 1) * pair]
        v_pair = qkv[rows, 2 * model + j * pair : 2 * model + (j + 1) * pair]
        total = None
        for e in range(2):
            scores = dot_rows(q_pair * masks[e], k_pair) + bias[2 * j + e].astype(F32)
            raised = jnp.exp(scores - jnp.max(scores, axis=-1, keepdims=True))
            p = (raised * (1.0 / jnp.sum(raised, axis=-1, keepdims=True))).astype(BF16)
            probs[b, 2 * j + e] = p
            part = dot(p, v_pair * masks[e])
            total = part if total is None else total + part
        att[rows, j * pair : (j + 1) * pair] = total.astype(BF16)
    out = dot(att[rows, :], w_proj[...]) + b_proj[...]
    branch[rows, :] = out
    middle[rows, :] = x + mod[b, 2:3, :] * out


def mlp_forward(b, length, middle, mod, w_fc1, w_fc2, b_fc1, b_fc2, act, slope, out_branch, layer_out):
    model = w_fc1.shape[0]
    rows = pl.ds(pl.multiple_of(b * length, length), length)
    mid = middle[rows, :]
    normed, _ = norm_parts(mid)
    normed_low = (normed * (1.0 + mod[b, 4:5, :]) + mod[b, 3:4, :]).astype(BF16)
    total = b_fc2[...]
    for c in range(w_fc1.shape[1] // model):
        cols = slice(c * model, (c + 1) * model)
        v = dot(normed_low, w_fc1[:, cols]) + b_fc1[:, cols]
        square = v * v
        t = jnp.tanh(0.7978845608028654 * v * (1.0 + 0.044715 * square))
        half = 0.5 * (1.0 + t)
        a = (v * half).astype(BF16)
        act[rows, cols] = a
        slope[rows, cols] = (
            half
            + 0.5 * v * (1.0 - t * t) * (0.7978845608028654 + (3 * 0.044715 * 0.7978845608028654) * square)
        ).astype(BF16)
        total = total + dot(a, w_fc2[cols, :])
    out_branch[rows, :] = total
    layer_out[rows, :] = (mid + mod[b, 5:6, :] * total).astype(layer_out.dtype)


def mlp_backward(b, length, grad, middle, mod, w_fc1, w_fc2, act, slope, out_branch, d_middle, small, normed_low, d_pre, d_ob):
    model = w_fc1.shape[0]
    rows = pl.ds(pl.multiple_of(b * length, length), length)
    g = grad[rows, :].astype(F32)
    small[b, 2:3, :] = col_sum(g * out_branch[rows, :])
    d_out = g * mod[b, 5:6, :]
    d_out_low = d_out.astype(BF16)
    d_ob[rows, :] = d_out_low
    small[b, 3:4, :] = col_sum(d_out_low.astype(F32))
    normed, inverse = norm_parts(middle[rows, :])
    normed_low[rows, :] = (normed * (1.0 + mod[b, 4:5, :]) + mod[b, 3:4, :]).astype(BF16)
    d_normed = None
    for c in range(w_fc1.shape[1] // model):
        cols = slice(c * model, (c + 1) * model)
        d_act = dot_rows(d_out_low, w_fc2[cols, :])
        d_low = (d_act * slope[rows, cols].astype(F32)).astype(BF16)
        d_pre[rows, cols] = d_low
        small[b, 4 + c : 5 + c, :] = col_sum(d_low.astype(F32))
        part = dot_rows(d_low, w_fc1[:, cols])
        d_normed = part if d_normed is None else d_normed + part
    small[b, 0:1, :] = col_sum(d_normed)
    small[b, 1:2, :] = col_sum(d_normed * normed)
    d_middle[rows, :] = norm_back(d_normed, mod[b, 4:5, :], normed, inverse) + g


def mlp_weight_grads(normed_low, d_pre, act, d_ob, g_fc1, g_fc2):
    model = g_fc1.shape[0]
    for c in range(g_fc1.shape[1] // model):
        cols = slice(c * model, (c + 1) * model)
        g_fc1[:, cols] = dot_cols(normed_low[...], d_pre[:, cols]).astype(BF16)
        g_fc2[cols, :] = dot_cols(act[:, cols], d_ob[...]).astype(BF16)


def attention_backward(b, length, h, mod, w_qkv, w_proj, qkv, probs, att, branch, d_middle, d_in, small, score_sum, normed_low, d_qkv, d_br):
    model = w_proj.shape[0]
    heads = probs.shape[1]
    pair = 2 * model // heads
    scale = F32((pair // 2) ** (-0.5))
    rows = pl.ds(pl.multiple_of(b * length, length), length)
    masks = half_masks(pair)
    d_mid = d_middle[rows, :]
    small[b, 2:3, :] = col_sum(d_mid * branch[rows, :])
    d_branch = (d_mid * mod[b, 2:3, :]).astype(BF16)
    d_br[rows, :] = d_branch
    small[b, 5:6, :] = col_sum(d_branch.astype(F32))
    d_att = dot_rows(d_branch, w_proj[...]).astype(BF16)
    for j in range(heads // 2):
        q_pair = qkv[rows, j * pair : (j + 1) * pair]
        k_pair = qkv[rows, model + j * pair : model + (j + 1) * pair]
        v_pair = qkv[rows, 2 * model + j * pair : 2 * model + (j + 1) * pair]
        d_pair = d_att[:, j * pair : (j + 1) * pair]
        d_q = d_k = d_v = None
        for e in range(2):
            p_low = probs[b, 2 * j + e]
            p = p_low.astype(F32)
            d_here = d_pair * masks[e]
            d_p = dot_rows(d_here, v_pair)
            d_s = (p * (d_p - jnp.sum(d_p * p, axis=-1, keepdims=True))).astype(BF16)
            score_sum[2 * j + e] += d_s.astype(F32)
            v_part = dot_cols(p_low, d_here)
            q_part = dot(d_s, k_pair * masks[e])
            k_part = dot_cols(d_s, q_pair * masks[e])
            d_v = v_part if d_v is None else d_v + v_part
            d_q = q_part if d_q is None else d_q + q_part
            d_k = k_part if d_k is None else d_k + k_part
        d_qkv[rows, j * pair : (j + 1) * pair] = (d_q * scale).astype(BF16)
        d_qkv[rows, model + j * pair : model + (j + 1) * pair] = (d_k * scale).astype(BF16)
        d_qkv[rows, 2 * model + j * pair : 2 * model + (j + 1) * pair] = d_v.astype(BF16)
    small[b, 3:4, :] = col_sum(d_qkv[rows, :model].astype(F32))
    small[b, 4:5, :] = col_sum(d_qkv[rows, 2 * model :].astype(F32))
    small[b, 6:8, :] = jnp.zeros((2, model), F32)
    d_normed = dot_rows(d_qkv[rows, :], w_qkv[...])
    normed, inverse = norm_parts(h[rows, :].astype(F32))
    normed_low[rows, :] = (normed * (1.0 + mod[b, 1:2, :]) + mod[b, 0:1, :]).astype(BF16)
    small[b, 0:1, :] = col_sum(d_normed)
    small[b, 1:2, :] = col_sum(d_normed * normed)
    d_in[rows, :] = (norm_back(d_normed, mod[b, 1:2, :], normed, inverse) + d_mid).astype(d_in.dtype)


def attention_weight_grads(normed_low, d_qkv, att, d_br, g_qkv, g_proj):
    model = g_proj.shape[0]
    for c in range(3):
        cols = slice(c * model, (c + 1) * model)
        g_qkv[:, cols] = dot_cols(normed_low[...], d_qkv[:, cols]).astype(BF16)
    g_proj[...] = dot_cols(att[...], d_br[...]).astype(BF16)


def each_sample(count, body):
    def step(b, carry):
        body(b)
        return carry

    lax.fori_loop(0, count, step, 0)


def add_tables(all_scores, index, outs):
    heads, length = all_scores[0].shape[0], all_scores[0].shape[1]
    low_ids = lax.broadcasted_iota(jnp.int32, (LOW, length), 0)
    high_ids = lax.broadcasted_iota(jnp.int32, (HIGH, length), 0)
    count = len(all_scores) * heads

    def step(i, carry):
        rows = pl.ds(pl.multiple_of(i * 16, 16), 16)
        entries = index[rows, :]
        block = [scores[head, rows, :].astype(F32) for scores in all_scores for head in range(heads)]
        total = carry
        for r in range(16):
            entry = entries[r : r + 1, :]
            low = jnp.where(low_ids == (entry & (LOW - 1)), 1.0, 0.0).astype(BF16)
            high = high_ids == (entry >> LOW_BITS)
            left = jnp.concatenate([jnp.where(high, part[r : r + 1, :], 0.0) for part in block], axis=0).astype(BF16)
            total = total + dot_rows(left, low)
        return total

    total = lax.fori_loop(0, length // 16, step, jnp.zeros((count * HIGH, LOW), F32))
    parts = [total[i * HIGH : (i + 1) * HIGH] for i in range(count)]
    for layer, out in enumerate(outs):
        out[...] = jnp.concatenate(parts[layer * heads : (layer + 1) * heads], axis=1)


def small_kernel(pos, scores0, scores1, index, small_a0, small_m0, small_a1, small_m1, *rest):
    keep, send, table0, table1 = rest[-4:]
    size = small_a0.shape[0] * small_a0.shape[1]
    add_tables((scores0, scores1), index, (table0, table1))
    parts = (
        (small_a0[...], small_m0[...], table0[...]),
        (small_a1[...], small_m1[...], table1[...]),
    )
    rows = [
        jnp.concatenate([x[0].reshape(size, -1), x[1].reshape(size, -1), x[2]], axis=0) for x in parts
    ]

    @pl.when(pos[0] == 0)
    def _():
        keep[...] = rows[0]
        send[...] = rows[1].astype(BF16)

    @pl.when(pos[0] == 1)
    def _():
        keep[...] = rows[1]
        send[...] = rows[0].astype(BF16)


def small_step(pos, scores0, scores1, index, smalls, earlier):
    samples, _, model = smalls[0].shape
    shape = (16 * samples + HIGH, model)
    return call(
        small_kernel, pos, (scores0, scores1, index, *smalls), earlier, [(shape, F32), (shape, BF16)],
        [((HIGH, model), F32)] * 2, work=12,
    )


def set_line(line, layer, section, own_line, other_line):
    line[...] = jnp.where(section == layer, own_line[...], other_line[...])


def start_bias(layer, section, own, other, bias, sem):
    one = pltpu.make_async_copy(own, bias, sem)
    two = pltpu.make_async_copy(other, bias, sem)
    pl.when(section == layer)(one.start)
    pl.when(section != layer)(two.start)
    return one


def line_biases(line, samples, model):
    q_bias = bias_at(line, samples, model, 0, 1)
    v_bias = bias_at(line, samples, model, 1, 1)
    b_qkv = jnp.concatenate([q_bias, jnp.zeros_like(q_bias), v_bias], axis=1)
    return b_qkv, bias_at(line, samples, model, 2, 1), bias_at(line, samples, model, 3, 4), bias_at(line, samples, model, 7, 1)


def forward_kernel(layer, length, n_weights, n_after, pos, h, own_line, other_line, own_bias, other_bias, *rest):
    refs, rest = rest[:n_weights], rest[n_weights + n_after :]
    (qkv, probs, att, branch, middle, act, slope, out_branch, layer_out,
     w_qkv, w_proj, w_fc1, w_fc2, bias, line, sems) = rest
    section, shard = pos[0], pos[1]
    model = h.shape[1]
    samples = h.shape[0] // length
    got_bias = start_bias(layer, section, own_bias, other_bias, bias, sems.at[weight_count(n_weights)])
    for_attention, for_mlp = weight_loads(layer, section, shard, refs, (w_qkv, w_proj, w_fc1, w_fc2), sems)
    set_line(line, layer, section, own_line, other_line)
    mod = Modulation(line, model)
    b_qkv, b_proj, b_fc1, b_fc2 = line_biases(line, samples, model)
    got_bias.wait()
    wait_all(for_attention)
    each_sample(
        samples,
        lambda b: attention_forward(b, length, h, mod, bias, w_qkv, w_proj, b_qkv, b_proj, qkv, probs, att, branch, middle),
    )
    wait_all(for_mlp)
    each_sample(
        samples,
        lambda b: mlp_forward(b, length, middle, mod, w_fc1, w_fc2, b_fc1, b_fc2, act, slope, out_branch, layer_out),
    )


def both_kernel(layer, pieces, length, n_weights, n_after, pos, h, grad, own_line, other_line, own_bias, other_bias, *rest):
    refs, rest = rest[:n_weights], rest[n_weights + n_after :]
    (layer_out, d_in, small_a, small_m, scores, keep, send,
     w_qkv, w_proj, w_fc1, w_fc2, bias, line, qkv, probs, att, branch, middle, act, slope, out_branch,
     d_middle, normed_low, d_pre, d_ob, d_qkv, score_sum, g_qkv, g_proj, g_fc1, g_fc2, sems) = rest
    section, shard = pos[0], pos[1]
    model = h.shape[1]
    samples = h.shape[0] // length
    got_bias = start_bias(layer, section, own_bias, other_bias, bias, sems.at[weight_count(n_weights)])
    for_attention, for_mlp = weight_loads(layer, section, shard, refs, (w_qkv, w_proj, w_fc1, w_fc2), sems)
    set_line(line, layer, section, own_line, other_line)
    mod = Modulation(line, model)
    b_qkv, b_proj, b_fc1, b_fc2 = line_biases(line, samples, model)
    got_bias.wait()
    wait_all(for_attention)
    each_sample(
        samples,
        lambda b: attention_forward(b, length, h, mod, bias, w_qkv, w_proj, b_qkv, b_proj, qkv, probs, att, branch, middle),
    )
    wait_all(for_mlp)

    def mlp(b):
        mlp_forward(b, length, middle, mod, w_fc1, w_fc2, b_fc1, b_fc2, act, slope, out_branch, layer_out)
        mlp_backward(b, length, grad, middle, mod, w_fc1, w_fc2, act, slope, out_branch, d_middle, small_m, normed_low, d_pre, d_ob)

    each_sample(samples, mlp)
    mlp_weight_grads(normed_low, d_pre, act, d_ob, g_fc1, g_fc2)
    pack_mlp((keep, send), section, g_fc1, g_fc2, shard, pieces, 6, 2)
    score_sum[...] = jnp.zeros_like(score_sum)
    each_sample(
        samples,
        lambda b: attention_backward(b, length, h, mod, w_qkv, w_proj, qkv, probs, att, branch, d_middle, d_in, small_a, score_sum, normed_low, d_qkv, d_ob),
    )
    scores[...] = score_sum[...].astype(BF16)
    attention_weight_grads(normed_low, d_qkv, att, d_ob, g_qkv, g_proj)
    pack_attention((keep, send), section, g_qkv, g_proj, shard, pieces, 6, 0)
    rows = slice(keep.shape[0], keep.shape[0] + h.shape[0])

    @pl.when(section == 0)
    def _():
        send[rows, :] = layer_out[...]

    @pl.when(section == 1)
    def _():
        send[rows, :] = h[...]


def backward_mlp_kernel(layer, pieces, length, n_weights, n_after, pos, grad, middle, own_line, other_line, act, slope, out_branch, *rest):
    refs, rest = rest[:n_weights], rest[n_weights + n_after :]
    (d_middle, small, keep, send,
     w_qkv, w_proj, w_fc1, w_fc2, line, normed_low, d_pre, d_ob, g_fc1, g_fc2, sems) = rest
    section, shard = pos[0], pos[1]
    for_attention, for_mlp = weight_loads(layer, section, shard, refs, (w_qkv, w_proj, w_fc1, w_fc2), sems)
    set_line(line, layer, section, own_line, other_line)
    mod = Modulation(line, middle.shape[1])
    wait_all(for_mlp)
    each_sample(
        middle.shape[0] // length,
        lambda b: mlp_backward(b, length, grad, middle, mod, w_fc1, w_fc2, act, slope, out_branch, d_middle, small, normed_low, d_pre, d_ob),
    )
    mlp_weight_grads(normed_low, d_pre, act, d_ob, g_fc1, g_fc2)
    pack_mlp((keep, send), section, g_fc1, g_fc2, shard, pieces, 4, 0)
    wait_all(for_attention)


def backward_attention_kernel(layer, pieces, length, n_weights, n_after, pos, h, own_line, other_line, qkv, probs, att, branch, d_middle, d_h1, *rest):
    refs, rest = rest[:n_weights], rest[n_weights + n_after :]
    (d_in, small, scores, keep, send,
     w_qkv, w_proj, w_fc1, w_fc2, line, normed_low, d_qkv, d_br, score_sum, g_qkv, g_proj, sems) = rest
    section, shard = pos[0], pos[1]
    for_attention, for_mlp = weight_loads(layer, section, shard, refs, (w_qkv, w_proj, w_fc1, w_fc2), sems)
    set_line(line, layer, section, own_line, other_line)
    mod = Modulation(line, h.shape[1])
    score_sum[...] = jnp.zeros_like(score_sum)
    wait_all(for_attention)
    each_sample(
        h.shape[0] // length,
        lambda b: attention_backward(b, length, h, mod, w_qkv, w_proj, qkv, probs, att, branch, d_middle, d_in, small, score_sum, normed_low, d_qkv, d_br),
    )
    scores[...] = score_sum[...].astype(BF16)
    attention_weight_grads(normed_low, d_qkv, att, d_br, g_qkv, g_proj)
    pack_attention((keep, send), section, g_qkv, g_proj, shard, pieces, 2, 0)
    rows = slice(keep.shape[0], keep.shape[0] + h.shape[0])

    @pl.when(section == 0)
    def _():
        send[rows, :] = d_h1[...]

    @pl.when(section == 1)
    def _():
        send[rows, :] = d_in[...].astype(BF16)

    wait_all(for_mlp)


def cost(gigaflop):
    return pl.CostEstimate(flops=int(gigaflop * 1e9), bytes_accessed=0, transcendentals=0)


def call(kernel, pos, operands, in_hbm, outs, scratch, sems=0, work=2):
    specs = [pl.BlockSpec(memory_space=pltpu.SMEM)]
    specs += [pl.BlockSpec(memory_space=pltpu.VMEM) for _ in operands]
    specs += [pl.BlockSpec(memory_space=pl.ANY) for _ in in_hbm]
    shapes = [pltpu.VMEM(shape, dtype) for shape, dtype in scratch]
    if sems:
        shapes.append(pltpu.SemaphoreType.DMA((sems,)))
    return pl.pallas_call(
        kernel,
        out_shape=[jax.ShapeDtypeStruct(shape, dtype) for shape, dtype in outs],
        in_specs=specs,
        out_specs=[pl.BlockSpec(memory_space=pltpu.VMEM) for _ in outs],
        scratch_shapes=shapes,
        cost_estimate=cost(work),
        compiler_params=pltpu.CompilerParams(vmem_limit_bytes=VMEM_BYTES),
    )(pos, *operands, *in_hbm)


class Sizes:
    def __init__(self, samples, length, model, heads, hidden, pieces):
        self.samples, self.length, self.model = samples, length, model
        self.heads, self.hidden, self.pieces = heads, hidden, pieces
        self.rows = samples * length
        self.line = ((1, (6 * samples + 4 + hidden // model) * model), F32)
        self.weights = [
            ((model, 3 * model), BF16), ((model, model), BF16), ((model, hidden), BF16), ((hidden, model), BF16),
        ]
        self.bias = ((heads, length, length), BF16)
        self.probs = ((samples, heads, length, length), BF16)
        self.low = ((self.rows, model), BF16)
        self.full = ((self.rows, model), F32)
        self.qkv = ((self.rows, 3 * model), BF16)
        self.wide = ((self.rows, hidden), BF16)
        self.small = ((samples, 8, model), F32)

    def pack(self, blocks, more=0):
        return [((blocks * self.model, self.model), BF16), ((blocks * self.model + more, self.model), BF16)]


def forward_layer(layer, z, pos, h, lines, biases, weights, earlier):
    return call(
        functools.partial(forward_kernel, layer, z.length, len(weights), len(earlier)),
        pos, (h, *lines), (*biases, *weights, *earlier),
        [z.qkv, z.probs, z.low, z.full, z.full, z.wide, z.wide, z.full, z.low],
        [*z.weights, z.bias, z.line], weight_count(len(weights)) + 1, work=15,
    )


def both_ways(layer, z, pos, h, grad, lines, biases, weights, earlier):
    return call(
        functools.partial(both_kernel, layer, z.pieces, z.length, len(weights), len(earlier)),
        pos, (h, grad, *lines), (*biases, *weights, *earlier),
        [z.low, z.low, z.small, z.small, z.bias, *z.pack(6, z.rows)],
        [*z.weights, z.bias, z.line, z.qkv, z.probs, z.low, z.full, z.full, z.wide, z.wide, z.full,
         z.full, z.low, z.wide, z.low, z.qkv, (z.bias[0], F32), *z.weights],
        weight_count(len(weights)) + 1, work=25,
    )


def backward_mlp(layer, z, pos, grad, middle, lines, act, slope, out_branch, weights, earlier):
    return call(
        functools.partial(backward_mlp_kernel, layer, z.pieces, z.length, len(weights), len(earlier)),
        pos, (grad, middle, *lines, act, slope, out_branch), (*weights, *earlier),
        [z.full, z.small, *z.pack(4)],
        [*z.weights, z.line, z.low, z.wide, z.low, *z.weights[2:]],
        weight_count(len(weights)), work=12,
    )


def backward_attention(layer, z, pos, h, lines, qkv, probs, att, branch, d_middle, d_h1, weights, earlier):
    return call(
        functools.partial(backward_attention_kernel, layer, z.pieces, z.length, len(weights), len(earlier)),
        pos, (h, *lines, qkv, probs, att, branch, d_middle, d_h1), (*weights, *earlier),
        [z.full, z.small, z.bias, *z.pack(2, z.rows)],
        [*z.weights, z.line, z.low, z.qkv, z.low, (z.bias[0], F32), *z.weights[:2]],
        weight_count(len(weights)), work=13,
    )


def partial_kernel(pos, w_ada, cond_a, cond_b, cond_c, cond_d, b_ada, b_qv, b_proj, b_fc1, b_fc2, *rest):
    copied, outs, whole = rest[-6], rest[-5:-1], rest[-1]
    copied[...] = w_ada[...]
    shard = pos[1]
    q, wide = w_ada.shape
    samples, model = cond_a.shape
    whole[...] = jnp.zeros_like(whole)
    whole[pl.ds(pl.multiple_of(shard * q, 16), q), :] = w_ada[...]
    for cond, out in zip((cond_a, cond_b, cond_c, cond_d), outs):
        c = cond[...].astype(F32)
        act = (c * (1.0 / (1.0 + jnp.exp(-c)))).astype(BF16)
        out[:, :wide] = dot(act, whole[...])
        out[:, wide:] = jnp.zeros((samples, 2 * model), F32)
        for f in range(4):
            @pl.when(shard == f)
            def _():
                here = slice(f * b_ada.shape[1], (f + 1) * b_ada.shape[1])
                out[:, here] += b_ada[...].astype(F32)
                for bias, row, at in ((b_qv, 0, 0), (b_proj, 1, 0), (b_fc1, 1, model), (b_fc2, 3, model)):
                    width = bias.shape[1]
                    at += f * width
                    row, at = row + at // (2 * model), wide + at % (2 * model)
                    out[row : row + 1, at : at + width] = bias[...].astype(F32)


def partial_step(pos, w_ada, conds, biases, earlier):
    q, wide = w_ada.shape
    samples, model = conds[0].shape
    return call(
        partial_kernel, pos, (w_ada, *conds, *biases), earlier, [(w_ada.shape, BF16)] + [((samples, wide + 2 * model), F32)] * 4,
        [((4 * q, wide), BF16)],
    )


def line_kernel(pos, own, got_a, got_b, got_c, *rest):
    keep, send, total = rest[-3:]
    section = pos[0]
    samples = own.shape[0]
    each = samples // 2
    model = own.shape[1] // 8
    total[...] = (own[...] + got_a[...]) + (got_b[...] + got_c[...])
    for out, side in ((keep, section), (send, 1 - section)):
        for b in range(each):
            out[:, b * 6 * model : (b + 1) * 6 * model] = total[pl.ds(side * each + b, 1), : 6 * model]
        for row in range(samples):
            at = (6 * each + 2 * row) * model
            out[:, at : at + 2 * model] = total[row : row + 1, 6 * model :]


def line_step(pos, own, got, earlier):
    samples, model = own.shape[0], own.shape[1] // 8
    shape = (1, (3 * samples + 8) * model)
    return call(line_kernel, pos, (own, *got), earlier, [(shape, F32)] * 2, [(own.shape, F32)])


def first_kernel(keep1, other1, keep_m, other_m, own1, own_m, *messages):
    at = 0
    for keep, other, own in ((keep1, other1, own1), (keep_m, other_m, own_m)):
        size = own.shape[0]
        for p in range(4):
            total = keep[p * size : (p + 1) * size, :].astype(F32) + other[p * size : (p + 1) * size, :].astype(F32)
            if p == 0:
                own[...] = total
            else:
                messages[p - 1][at : at + size, :] = total.astype(BF16)
        at += size


def first_step(keep1, other1, keep_m, other_m):
    model = keep1.shape[1]
    one, two = keep1.shape[0] // 4, keep_m.shape[0] // 4
    return pl.pallas_call(
        first_kernel,
        out_shape=[jax.ShapeDtypeStruct((one, model), F32), jax.ShapeDtypeStruct((two, model), F32)]
        + [jax.ShapeDtypeStruct((one + two, model), BF16)] * 3,
        compiler_params=pltpu.CompilerParams(vmem_limit_bytes=VMEM_BYTES),
    )(keep1, other1, keep_m, other_m)


def halve(bit, own, got, keep, send):
    n = own.shape[0] // 4
    for high in range(2):
        for out, low in ((keep, bit), (send, 1 - bit)):
            rows = pl.ds(pl.multiple_of((2 * high + low) * n, 16), n)
            total = own[rows, :]
            for piece in got:
                total = total + piece[rows, :].astype(F32)
            out[high * n : (high + 1) * n, :] = total.astype(out.dtype)


def quarter(bit, kept, got, keep, send):
    n = kept.shape[0] // 2
    for out, high in ((keep, bit), (send, 1 - bit)):
        rows = pl.ds(pl.multiple_of(high * n, 16), n)
        out[...] = (kept[rows, :] + got[rows, :].astype(F32)).astype(out.dtype)


def pair_up(bit, own, got, out):
    n = own.shape[0]
    out[pl.ds(pl.multiple_of(bit * n, 16), n), :] = own[...]
    out[pl.ds(pl.multiple_of((1 - bit) * n, 16), n), :] = got[...]


def whole_from(bit, pair, got, out, at=0):
    n = pair.shape[0] // 2
    for high in range(2):
        rows = slice(high * n, (high + 1) * n)
        out[pl.ds(pl.multiple_of(at + (2 * high + bit) * n, 16), n), :] = pair[rows, :]
        out[pl.ds(pl.multiple_of(at + (2 * high + 1 - bit) * n, 16), n), :] = got[rows, :]


def halve_kernel(pos, own, got_a, got_b, got_c, keep, send):
    halve(pos[2] & 1, own, (got_a, got_b, got_c), keep, send)


def halve_step(pos, own, got):
    shape = (own.shape[0] // 2, own.shape[1])
    return call(halve_kernel, pos, (own, *got), (), [(shape, F32), (shape, BF16)], [])


def quarter_kernel(pos, kept, got, keep, send):
    quarter(pos[2] >> 1, kept, got, keep, send)


def quarter_step(pos, kept, got):
    shape = (kept.shape[0] // 2, kept.shape[1])
    return call(quarter_kernel, pos, (kept, got), (), [(shape, F32), (shape, BF16)], [])


def pair_kernel(pos, own, got, out):
    pair_up(pos[2] >> 1, own, got, out)


def pair_step(pos, own, got):
    return call(pair_kernel, pos, (own, got), (), [((2 * own.shape[0], own.shape[1]), BF16)], [])[0]


def g_kernel(cut, pos, quarter_a, got_a, got_b, got_c, pair1, got1, *rest):
    own, send = rest[-2:]
    n = quarter_a.shape[0]

    def layer0(out):
        for j, piece in enumerate((quarter_a, got_a, got_b, got_c)):
            out[pl.ds(pl.multiple_of((pos[2] ^ j) * cut, 16), cut), :] = piece[:cut, :]
            out[pl.ds(pl.multiple_of(4 * cut + (pos[2] ^ j) * (n - cut), 16), n - cut), :] = piece[cut:, :]

    @pl.when(pos[0] == 0)
    def _():
        layer0(own)
        whole_from(pos[2] & 1, pair1, got1, send)

    @pl.when(pos[0] == 1)
    def _():
        layer0(send)
        whole_from(pos[2] & 1, pair1, got1, own)


def g_step(pos, cut, quarter_a, got_a, pair1, got1, earlier):
    shape = (2 * pair1.shape[0], pair1.shape[1])
    return call(functools.partial(g_kernel, cut), pos, (quarter_a, *got_a, pair1, got1), earlier, [(shape, BF16)] * 2, [])


def plane_kernel(samples, pos, keep, other, kept_small, other_small, cond, own, own_small, *rest):
    messages, work = rest[:3], rest[3]
    section = pos[0]
    size, model = own.shape
    for p in range(4):
        rows = slice(p * size, (p + 1) * size)
        total = keep[rows, :].astype(F32) + other[rows, :].astype(F32)
        if p == 0:
            own[...] = total
        else:
            messages[p - 1][:size, :] = total.astype(BF16)
    theirs = other_small[...].astype(F32)
    mine = kept_small[...]
    each = samples // 2
    work[...] = jnp.zeros_like(work)
    for b in range(each):
        for kind in range(6):
            row = b * 8 + kind if kind < 3 else (each + b) * 8 + kind - 3
            work[pl.ds(kind * samples + section * each + b, 1), :] = mine[row : row + 1, :]
            work[pl.ds(kind * samples + (1 - section) * each + b, 1), :] = theirs[row : row + 1, :]
    work[6 * samples : 7 * samples, :] = cond[...].astype(F32)
    both = mine + theirs
    bias_rows = sum(both[(each + b) * 8 + 3 : (each + b) * 8 + 8, :] for b in range(each))
    more_rows = sum(both[b * 8 + 3 : b * 8 + 6, :] for b in range(each))
    at = 7 * samples
    work[at : at + 5, :] = bias_rows
    work[at + 5 : at + 8, :] = more_rows
    work[at + 8 : at + 8 + HIGH, :] = both[2 * each * 8 :, :]
    small = work[...].astype(BF16)
    own_small[...] = small
    for message in messages:
        message[size:, :] = small


def plane_step(pos, keep, other, kept_small, other_small, cond):
    samples, model = cond.shape
    size = keep.shape[0] // 4
    small = -(-(7 * samples + 8 + HIGH) // 16) * 16
    outs = [((size, model), F32), ((small, model), BF16)] + [((size + small, model), BF16)] * 3
    return call(
        functools.partial(plane_kernel, samples), pos, (keep, other, kept_small, other_small, cond), (), outs,
        [((small, model), F32)],
    )


def column_kernel(samples, pos, own, own_small, got_a, got_b, got_c, own_m, first_a, first_b, first_c, part, own_out, *rest):
    messages, work = rest[:3], rest[3]
    rank = pos[2]
    size, size_m = own.shape[0], own_m.shape[0]
    n, nm = size // 4, size_m // 4
    skip = first_a.shape[0] - size_m
    got = (got_a, got_b, got_c)
    for j in range(4):
        at = pl.multiple_of((rank ^ j) * n, 16)
        total = own[pl.ds(at, n), :]
        for piece in got:
            total = total + piece[pl.ds(at, n), :].astype(F32)
        at = pl.multiple_of((rank ^ j) * nm, 16)
        total_m = own_m[pl.ds(at, nm), :]
        for piece in (first_a, first_b, first_c):
            total_m = total_m + piece[pl.ds(skip + at, nm), :].astype(F32)
        out = part if j == 0 else messages[j - 1]
        out[:n, :] = total.astype(out.dtype)
        out[n : n + nm, :] = total_m.astype(out.dtype)
    smalls = [own_small[...].astype(F32)] + [piece[size:, :].astype(F32) for piece in got]
    work[...] = jnp.zeros_like(work)
    for p in range(4):
        for kind in range(7):
            at = (kind * 4 + p) * samples
            work[at : at + samples, :] = smalls[p][kind * samples : (kind + 1) * samples, :]
    at = 7 * samples
    summed = (smalls[0] + smalls[1]) + (smalls[2] + smalls[3])
    work[4 * at : 4 * at + 8 + HIGH, :] = summed[at : at + 8 + HIGH, :]
    small = work[...].astype(BF16)
    own_out[...] = small
    for message in messages:
        message[n + nm :, :] = small


def column_step(pos, own, own_small, got, own_m, first, samples):
    model = own.shape[1]
    n = (own.shape[0] + own_m.shape[0]) // 4
    small = -(-(28 * samples + 8 + HIGH) // 16) * 16
    outs = [((n, model), F32), ((small, model), BF16)] + [((n + small, model), BF16)] * 3
    return call(
        functools.partial(column_kernel, samples), pos, (own, own_small, *got, own_m, *first), (), outs, [((small, model), F32)]
    )


def finish_kernel(samples, width, pos, own_small, got_a, got_b, got_c,
                  g_ada, g_b_ada, g_b_qv, g_b_proj, g_b_fc1, g_b_fc2, g_table, work, whole, row):
    shard, rank = pos[1], pos[2]
    model = own_small.shape[1]
    each = 4 * samples
    n = got_a.shape[0] - own_small.shape[0]
    pieces = [own_small[...]] + [piece[n:, :] for piece in (got_a, got_b, got_c)]
    for j in range(4):
        for kind in range(7):
            at = pl.multiple_of(kind * 4 * each + (rank ^ j) * each, 16)
            work[pl.ds(at, each), :] = pieces[j][kind * each : (kind + 1) * each, :].astype(F32)
    cond = work[24 * each :, :]
    act = (cond * (1.0 / (1.0 + jnp.exp(-cond)))).astype(BF16)
    for kind in range(6):
        rows = work[kind * 4 * each : (kind + 1) * 4 * each, :]
        whole[...] = dot_cols(act, rows.astype(BF16))
        cols = slice(kind * model, (kind + 1) * model)
        g_ada[:, cols] = whole[pl.ds(pl.multiple_of(shard * width, 16), width), :]
        row[:, cols] = col_sum(rows)
    at = 7 * each
    rows = [piece[at : at + 8 + HIGH, :].astype(F32) for piece in pieces]
    summed = (rows[0] + rows[1]) + (rows[2] + rows[3])
    for c in range(4):
        row[:, (6 + c) * model : (7 + c) * model] = summed[1 + c : 2 + c, :]
    row[:, 10 * model : 11 * model] = summed[5:6, :]
    row[:, 11 * model : 12 * model] = summed[6:7, :]
    row[:, 12 * model : 13 * model] = summed[7:8, :]
    row[:, 13 * model : 14 * model] = summed[0:1, :]
    for f in range(4):
        @pl.when(shard == f)
        def _():
            for out, start in ((g_b_ada, 0), (g_b_fc1, 6), (g_b_qv, 10), (g_b_proj, 12), (g_b_fc2, 13)):
                size = out.shape[1]
                out[...] = row[:, start * model + f * size : start * model + (f + 1) * size]
    heads, entries = g_table.shape
    for high in range(-(-entries // LOW)):
        size = min(LOW, entries - high * LOW)
        for head in range(heads):
            g_table[head : head + 1, high * LOW : high * LOW + size] = summed[
                8 + high : 9 + high, head * LOW : head * LOW + size
            ]


def finish_step(pos, own_small, got, samples, width, heads, entries):
    model = own_small.shape[1]
    sizes = [6 * width, 2 * width, width, 4 * width, width]
    return call(
        functools.partial(finish_kernel, samples, width), pos, (own_small, *got), (),
        [((width, 6 * model), F32)] + [((1, size), F32) for size in sizes] + [((heads, entries), F32)],
        [((7 * 16 * samples, model), F32), ((model, model), F32), ((1, 14 * model), F32)],
    )


def plane_kernel(samples, pos, keep, other, kept_small, other_small, cond, own, own_small, *rest):
    messages, work = rest[:3], rest[3]
    section = pos[0]
    size, model = own.shape
    for p in range(4):
        rows = slice(p * size, (p + 1) * size)
        total = keep[rows, :].astype(F32) + other[rows, :].astype(F32)
        if p == 0:
            own[...] = total
        else:
            messages[p - 1][:size, :] = total.astype(BF16)
    theirs = other_small[...].astype(F32)
    mine = kept_small[...]
    each = samples // 2
    work[...] = jnp.zeros_like(work)
    for b in range(each):
        for kind in range(6):
            row = b * 8 + kind if kind < 3 else (each + b) * 8 + kind - 3
            work[pl.ds(kind * samples + section * each + b, 1), :] = mine[row : row + 1, :]
            work[pl.ds(kind * samples + (1 - section) * each + b, 1), :] = theirs[row : row + 1, :]
    work[6 * samples : 7 * samples, :] = cond[...].astype(F32)
    both = mine + theirs
    bias_rows = sum(both[(each + b) * 8 + 3 : (each + b) * 8 + 8, :] for b in range(each))
    more_rows = sum(both[b * 8 + 3 : b * 8 + 6, :] for b in range(each))
    at = 7 * samples
    work[at : at + 5, :] = bias_rows
    work[at + 5 : at + 8, :] = more_rows
    work[at + 8 : at + 8 + HIGH, :] = both[2 * each * 8 :, :]
    small = work[...].astype(BF16)
    own_small[...] = small
    for message in messages:
        message[size:, :] = small


def plane_step(pos, keep, other, kept_small, other_small, cond):
    samples, model = cond.shape
    size = keep.shape[0] // 4
    small = -(-(7 * samples + 8 + HIGH) // 16) * 16
    outs = [((size, model), F32), ((small, model), BF16)] + [((size + small, model), BF16)] * 3
    return call(
        functools.partial(plane_kernel, samples), pos, (keep, other, kept_small, other_small, cond), (), outs,
        [((small, model), F32)],
    )


def cond_kernel(samples, pos, small, cond, *rest):
    out, w_ada = rest[-2:]
    model = cond.shape[1]
    for p, piece in enumerate(rest[:-2]):
        q = piece.shape[0]
        off = pl.multiple_of((pos[1] ^ p) * q, 16) if q < model else 0
        w_ada[pl.ds(off, q), :] = piece[...]
    total = None
    for kind in range(6):
        rows = small[...].astype(F32)[kind * samples : (kind + 1) * samples, :].astype(BF16)
        part = dot_rows(rows, w_ada[:, kind * model : (kind + 1) * model])
        total = part if total is None else total + part
    c = cond[...].astype(F32)
    gate = 1.0 / (1.0 + jnp.exp(-c))
    out[...] = total * (gate * (1.0 + c * (1.0 - gate)))


def cond_step(pos, small, w_ada, cond):
    model = cond.shape[1]
    return call(
        functools.partial(cond_kernel, cond.shape[0]), pos, (small, cond, *w_ada), (), [(cond.shape, F32)],
        [((model, w_ada[0].shape[1]), BF16)],
    )[0]


def final_kernel(pos, own, other, g_qkv, g_proj, g_fc1, g_fc2):
    q, model = g_proj.shape

    def write(first, second):
        for c in range(2):
            g_qkv[:, c * model : (c + 1) * model] = first[c * q : (c + 1) * q, :].astype(F32)
        g_qkv[:, 2 * model : 3 * model] = second[:q, :].astype(F32)
        g_proj[...] = second[q : 2 * q, :].astype(F32)
        for c in range(4):
            g_fc1[:, c * model : (c + 1) * model] = first[(2 + c) * q : (3 + c) * q, :].astype(F32)
        g_fc2[...] = second[2 * q : 6 * q, :].astype(F32)

    @pl.when(pos[0] == 0)
    def _():
        write(own, other)

    @pl.when(pos[0] == 1)
    def _():
        write(other, own)


def final_step(pos, own, other):
    q, model = own.shape[0] // 6, own.shape[1]
    return call(
        final_kernel, pos, (own, other), (),
        [((q, 3 * model), F32), ((q, model), F32), ((q, 4 * model), F32), ((4 * q, model), F32)], [],
    )


def pack_kernel(qkv, proj, fc1, fc2, out):
    q, model = proj.shape
    for c in range(3):
        out[c * q : (c + 1) * q, :] = qkv[:, c * model : (c + 1) * model]
    out[3 * q : 4 * q, :] = proj[...]
    for c in range(4):
        out[(4 + c) * q : (5 + c) * q, :] = fc1[:, c * model : (c + 1) * model]
    out[8 * q : 12 * q, :] = fc2[...]


def pack_shard(own):
    q, model = own[1].shape
    return pl.pallas_call(
        pack_kernel,
        out_shape=jax.ShapeDtypeStruct((12 * q, model), BF16),
        compiler_params=pltpu.CompilerParams(vmem_limit_bytes=VMEM_BYTES),
    )(*own)


def after(values, others):
    return pl.pallas_call(
        lambda *refs: None,
        out_shape=[jax.ShapeDtypeStruct(v.shape, v.dtype) for v in values],
        in_specs=[pl.BlockSpec(memory_space=pl.ANY)] * (len(values) + len(others)),
        out_specs=[pl.BlockSpec(memory_space=pl.ANY)] * len(values),
        input_output_aliases={i: i for i in range(len(values))},
    )(*values, *others)


def lookup_kernel(table, index, *rest):
    out, work = rest[-2:]
    heads, length = out.shape[0], out.shape[1]
    high_count = table.shape[0] // 8
    values = table[...]
    low_id = lax.broadcasted_iota(jnp.int32, (LOW, length), 0)

    def step(i, carry):
        block = index[pl.ds(pl.multiple_of(i * 8, 8), 8), :]
        for r in range(8):
            entry = block[r : r + 1, :]
            picks = jnp.where(low_id == (entry & (LOW - 1)), 1.0, 0.0).astype(BF16)
            found = dot(values, picks).reshape(high_count, 8, length)
            high = jnp.broadcast_to(entry >> LOW_BITS, (8, length))
            bit = high_count // 2
            while bit:
                chosen = (high & bit) != 0
                found = jnp.where(chosen[None], found[bit : 2 * bit], found[:bit])
                bit //= 2
            for head in range(heads):
                work[head, pl.ds(i * 8 + r, 1), :] = found[0, head : head + 1, :]
        return carry

    lax.fori_loop(0, length // 8, step, 0)
    out[...] = work[...].astype(BF16)


def lookup(table, index, earlier):
    heads, entries = table.shape
    high_count = HIGH
    padded = jnp.pad(table, ((0, 8 - heads), (0, high_count * LOW - entries)))
    rows = jnp.transpose(padded.reshape(8, high_count, LOW), (1, 0, 2)).reshape(high_count * 8, LOW)
    length = index.shape[0]
    return pl.pallas_call(
        lookup_kernel,
        out_shape=jax.ShapeDtypeStruct((heads, length, length), BF16),
        in_specs=[pl.BlockSpec(memory_space=pltpu.VMEM)] * 2 + [pl.BlockSpec(memory_space=pl.ANY)] * len(earlier),
        out_specs=pl.BlockSpec(memory_space=pltpu.VMEM),
        scratch_shapes=[pltpu.VMEM((heads, length, length), F32)],
        cost_estimate=cost(11),
        compiler_params=pltpu.CompilerParams(vmem_limit_bytes=VMEM_BYTES),
    )(rows, index, *earlier)


def swap_section(value):
    return lax.ppermute(value, "section", [(0, 1), (1, 0)])


def pairs_of(count, step):
    return [(i, i ^ step) for i in range(count)]


def by_rank(pieces, rank):
    stack = jnp.stack(pieces)
    count = len(pieces)
    bit = 1
    while bit < count:
        moved = jnp.stack([stack[i ^ bit] for i in range(count)])
        stack = jnp.where((rank & bit) != 0, moved, stack)
        bit *= 2
    return stack


def section_sums(keep, other, shards):
    size = keep.shape[0] // shards
    return [
        keep[p * size : (p + 1) * size].astype(F32) + other[p * size : (p + 1) * size].astype(F32)
        for p in range(shards)
    ]


def low_pieces(sums):
    return [x.astype(BF16) for x in sums[1:]]


def to_peers(messages, axis):
    count = lax.axis_size(axis)
    return [lax.ppermute(messages[p - 1], axis, pairs_of(count, p)) for p in range(1, count)]


def add_pieces(own, got):
    total = own
    for piece in got:
        total = total + piece.astype(F32)
    return total


def replica_parts(total, rank):
    replicas = lax.axis_size("rep")
    parts = total if total.ndim == 3 else total.reshape(replicas, total.shape[0] // replicas, -1)
    low = parts.astype(BF16)
    mine = lax.dynamic_index_in_dim(parts, rank, 0, keepdims=False)
    return mine, [lax.dynamic_index_in_dim(low, rank ^ j, 0, keepdims=False) for j in range(1, replicas)]


def unpack_attention(pack):
    q = pack.shape[0] // 4
    return jnp.concatenate([pack[c * q : (c + 1) * q] for c in range(3)], axis=1), pack[3 * q :]


def unpack_mlp(pack):
    q = pack.shape[0] // 8
    return jnp.concatenate([pack[c * q : (c + 1) * q] for c in range(4)], axis=1), pack[4 * q :]


def pad_rows(value):
    return jnp.pad(value, ((0, -value.shape[0] % 16), (0, 0)))


def from_peers(value, axis):
    return [lax.ppermute(value, axis, pairs_of(lax.axis_size(axis), p)) for p in range(1, lax.axis_size(axis))]


def pair_sum(values):
    while len(values) > 1:
        values = [values[i] + values[i + 1] for i in range(0, len(values), 2)]
    return values[0]


def per_device(inputs, conditioning, cotangent, micro_sizes, relative_bias_index,
               w_ada, w_qkv, w_proj, w_fc1, w_fc2, b_ada, b_qv, b_proj, b_fc1, b_fc2, bias_table):
    section = lax.axis_index("section")
    shard = lax.axis_index("fsdp")
    rank = lax.axis_index("rep")
    shards, replicas = lax.axis_size("fsdp"), lax.axis_size("rep")
    direct = shards == 4 and replicas == 4
    is_first = section == 0
    samples, length, model = inputs.shape
    heads, entries = bias_table.shape[1:]
    half = samples // 2
    z = Sizes(half, length, model, heads, 4 * model, shards if direct else 1)
    pos = jnp.stack([section, shard, rank]).astype(jnp.int32)

    def mine(first, second):
        return jnp.where(is_first, first, second)

    def own_samples(array):
        return lax.dynamic_slice_in_dim(array, section * half, half, 0)

    def in_order(own, other):
        return jnp.where(is_first, jnp.concatenate([own, other]), jnp.concatenate([other, own]))

    live = (jnp.arange(half)[:, None, None] < lax.dynamic_index_in_dim(micro_sizes[0], section, 0)).astype(BF16)
    h0 = own_samples(inputs).reshape(half * length, model)
    grad1 = (own_samples(cotangent) * live).reshape(half * length, model)
    index = relative_bias_index
    own_raw = [w_qkv[0], w_proj[0], w_fc1[0], w_fc2[0]]
    width = model // shards
    if direct:
        conds = [conditioning] + from_peers(conditioning, "fsdp")
        own_pack = pack_shard(own_raw)
        middle_row = own_pack.shape[0] // 2
        got_x = lax.ppermute(own_pack, "fsdp", pairs_of(shards, 1))
        got_y = lax.ppermute(own_pack, "fsdp", pairs_of(shards, 2))
        bias_own = lookup(bias_table[0], index, [own_pack, *conds[1:]])
        w_ada_copy, *partial = partial_step(pos, w_ada[0], conds, (b_ada, b_qv, b_proj, b_fc1, b_fc2), [bias_own])
        got_first = lax.ppermute(got_x[:middle_row], "fsdp", pairs_of(shards, 2))
        got_second = lax.ppermute(got_y[middle_row:], "fsdp", pairs_of(shards, 1))
        own_weights = [own_pack, got_x, got_y, got_first, got_second]
        weights = own_weights + [swap_section(w) for w in own_weights]
        own_line, send_line = line_step(pos, partial[0], after(to_peers(partial[1:], "fsdp"), [got_x, got_y]), [h0, grad1])
    else:
        row = jnp.concatenate([b_ada, b_qv, b_proj, b_fc1, b_fc2], axis=1)
        bias_rows = lax.all_gather(row[0], "fsdp", axis=0)
        whole = [lax.all_gather(w, "fsdp", axis=0, tiled=True) for w in own_raw]
        own_whole = pack_shard(whole)
        weights = [own_whole, swap_section(own_whole)]
        acts = jax.nn.silu(conditioning.astype(F32)).astype(BF16)
        modulation = dot(acts, lax.all_gather(w_ada[0], "fsdp", axis=0, tiled=True))
        bias_own = lookup(bias_table[0], index, [])
        cuts = [b_ada.shape[1], b_qv.shape[1], b_proj.shape[1], b_fc1.shape[1], b_fc2.shape[1]]
        biases, at = [], 0
        for cut in cuts:
            biases.append(bias_rows[:, at : at + cut].reshape(1, -1).astype(F32))
            at += cut
        modulation = modulation + biases[0]
        other_samples = lax.dynamic_slice_in_dim(modulation, (1 - section) * half, half, 0)
        own_line = jnp.concatenate([own_samples(modulation).reshape(1, -1)] + biases[1:], axis=1)
        send_line = jnp.concatenate([other_samples.reshape(1, -1)] + biases[1:], axis=1)
    lines = (own_line, swap_section(send_line))
    bias_heads = (bias_own, swap_section(bias_own))

    if direct:
        w_ada_later = after([w_ada_copy], weights[3:5])[0]
        w_ada_pieces = [w_ada_later] + from_peers(w_ada_later, "fsdp")
    else:
        w_ada_pieces = [lax.all_gather(w_ada[0], "fsdp", axis=0, tiled=True)]
    qkv, probs, att, branch, middle, act, slope, out_branch, h1 = forward_layer(0, z, pos, h0, lines, bias_heads, weights, w_ada_pieces[:1] if direct else [])
    out1, d_h1, small_a1, small_m1, scores1, keep1, send1 = both_ways(1, z, pos, h1, grad1, lines, bias_heads, weights, w_ada_pieces[1:])
    d_middle, small_m0, keep_m0, send_m0 = backward_mlp(0, z, pos, d_h1, middle, lines, act, slope, out_branch, weights, [])
    pieces = z.pieces
    rows = half * length
    other1 = swap_section(send1)
    other_m0 = swap_section(send_m0)
    if direct:
        own1, own_m, *first_messages = first_step(keep1, other1, keep_m0, other_m0)
        earlier = first_messages
    else:
        sums1 = section_sums(keep1, other1[: keep1.shape[0]], pieces)
        sums_m0 = section_sums(keep_m0, other_m0, pieces)
        earlier = []
    d_h0, small_a0, scores0, keep_a0, send_a0 = backward_attention(
        0, z, pos, h0, lines, qkv, probs, att, branch, d_middle, d_h1, weights, earlier
    )
    smalls = (small_a0, small_m0, small_a1, small_m1)
    size_a = keep_a0.shape[0]

    def replica(value, step):
        return lax.ppermute(value, "rep", pairs_of(replicas, step))

    if direct:
        kept_small, send_small = small_step(pos, scores0, scores1, index, smalls, [])
        other_small = swap_section(send_small)
        other_a0 = after([swap_section(send_a0)], [kept_small])[0]
        own_a0, own_small, *messages = plane_step(pos, keep_a0, other_a0, kept_small, other_small, conditioning)
        got = to_peers(messages, "fsdp")
        got_first = after(to_peers(first_messages, "fsdp"), [own_small])
        keep_z, send_z = halve_step(pos, own1, got_first)
        part0, plane_small, *messages = column_step(pos, own_a0, own_small, got, own_m, got_first, samples)
        got_z = after([replica(send_z, 1)], [plane_small])[0]
        keep_z, send_z = quarter_step(pos, keep_z, got_z)
        cond_part = cond_step(pos, after([own_small], [send_z])[0], w_ada_pieces, conditioning)
        got_z = after([replica(send_z, 2)], [cond_part])[0]
        quarter1 = (keep_z + got_z.astype(F32)).astype(BF16)
        got = after(to_peers(messages, "rep"), [quarter1])
        size = part0.shape[0]
        quarter0 = add_pieces(part0, [x[:size] for x in got]).astype(BF16)
        g_ada, g_b_ada, g_b_qv, g_b_proj, g_b_fc1, g_b_fc2, g_table = finish_step(
            pos, plane_small, got, samples, width, heads, entries
        )
        got_z, cond_part = after([replica(quarter1, 2), cond_part], [quarter0, g_ada])
        pair1 = pair_step(pos, quarter1, got_z)
        cond_grad = cond_part + swap_section(cond_part)
        own_half, send_half = g_step(
            pos, own_a0.shape[0] // 4, quarter0, from_peers(quarter0, "rep"), pair1, replica(pair1, 1), [g_ada, cond_grad]
        )
    else:
        other_a0 = swap_section(send_a0)
        kept_small, send_small = small_step(pos, scores0, scores1, index, smalls, [])
        theirs = swap_section(send_small).astype(F32)
        both = kept_small + theirs
        cut = half * 8

        def d_mod_of(values):
            a, m = values[:cut].reshape(half, 8, model), values[cut : 2 * cut].reshape(half, 8, model)
            return jnp.concatenate([a[:, :3], m[:, :3]], axis=1)

        low = in_order(d_mod_of(kept_small), d_mod_of(theirs)).astype(BF16)
        bias_rows = jnp.sum(both[: 2 * cut].reshape(2, half, 8, model), axis=1)
        summed = jnp.concatenate([bias_rows[1, 3:8], bias_rows[0, 3:6], both[2 * cut :]])
        cond_part = cond_step(pos, jnp.transpose(low, (1, 0, 2)).reshape(-1, model), w_ada_pieces, conditioning)
        kept = jnp.concatenate([low, conditioning[:, None]], axis=1)
        kept = lax.all_gather(kept, ("fsdp", "rep"), axis=0, tiled=True)
        summed = lax.psum(summed, ("fsdp", "rep"))
        act_all = jax.nn.silu(kept[:, 6].astype(F32)).astype(BF16)
        act_cols = lax.dynamic_slice_in_dim(act_all, shard * width, width, 1)
        g_ada = jnp.concatenate([dot_cols(act_cols, kept[:, i]) for i in range(6)], axis=1)
        g_b_ada = jnp.sum(kept[:, :6].astype(F32), axis=0).reshape(-1)
        vectors = [g_b_ada, summed[5:7].reshape(-1), summed[7], summed[1:5].reshape(-1), summed[0]]
        g_b_ada, g_b_qv, g_b_proj, g_b_fc1, g_b_fc2 = [
            lax.dynamic_slice_in_dim(v, shard * (v.shape[0] // shards), v.shape[0] // shards, 0)[None] for v in vectors
        ]
        g_table = jnp.transpose(summed[8:].reshape(HIGH, heads, LOW), (1, 0, 2)).reshape(heads, HIGH * LOW)[:, :entries]
        sums_a0 = section_sums(keep_a0, other_a0[:size_a], z.pieces)
        cond_grad = cond_part + swap_section(cond_part)
        half0 = jnp.concatenate([sums_a0[0], sums_m0[0]]).astype(BF16)
        half1 = sums1[0].astype(BF16)
        own_half, send_half = mine(half0, half1), mine(half1, half0)
    grads = final_step(pos, own_half, swap_section(send_half))
    if not direct:
        grads = [lax.psum_scatter(g.astype(BF16), "fsdp", scatter_dimension=0, tiled=True) for g in grads]
        grads = [g.astype(F32) for g in lax.psum(tuple(grads), "rep")]
    g_qkv, g_proj, g_fc1, g_fc2 = grads

    activations = in_order(
        mine(h1, out1).reshape(half, length, model), other1[keep1.shape[0] :].reshape(half, length, model)
    )
    input_grads = in_order(
        mine(d_h0, d_h1.astype(F32)).reshape(half, length, model),
        other_a0[size_a : size_a + rows].astype(F32).reshape(half, length, model),
    )

    return (
        activations[None], input_grads[None], cond_grad,
        g_ada[None], g_qkv[None], g_proj[None], g_fc1[None], g_fc2[None],
        g_b_ada, g_b_qv, g_b_proj, g_b_fc1, g_b_fc2,
        g_table[None],
    )


def solution(mesh):
    batch = ("fsdp", "rep")
    matrix = P("section", "fsdp", None)
    vector = P("section", "fsdp")
    return jax.shard_map(
        per_device,
        mesh=mesh,
        in_specs=(
            P(batch, None, None), P(batch, None), P(batch, None, None), P(batch, None), P(),
            matrix, matrix, matrix, matrix, matrix, vector, vector, vector, vector, vector,
            P("section", None, None),
        ),
        out_specs=(
            P("section", batch, None, None), P("section", batch, None, None), P(batch, None),
            matrix, matrix, matrix, matrix, matrix, vector, vector, vector, vector, vector,
            P("section", None, None),
        ),
        check_vma=False,
    )
```

```python
import functools

import jax
import jax.numpy as jnp
from jax import lax
from jax.experimental import pallas as pl
from jax.experimental.pallas import tpu as pltpu
from jax.sharding import PartitionSpec as P

EPSILON = 1e-06
F32 = jnp.float32
BF16 = jnp.bfloat16
VMEM_BYTES = 58 * 1024 * 1024
LOW_BITS = 6
LOW = 1 << LOW_BITS
HIGH = 16


def dot(a, b):
    return jnp.dot(a, b, preferred_element_type=F32)


def dot_rows(a, b):
    return lax.dot_general(a, b, (((1,), (1,)), ((), ())), preferred_element_type=F32)


def dot_cols(a, b):
    return lax.dot_general(a, b, (((0,), (0,)), ((), ())), preferred_element_type=F32)


def norm_parts(v):
    centre = v - jnp.mean(v, axis=-1, keepdims=True)
    inverse = lax.rsqrt(jnp.mean(centre * centre, axis=-1, keepdims=True) + EPSILON)
    return centre * inverse, inverse


def norm_back(d_normed, scale, normed, inverse):
    d = d_normed * (1.0 + scale)
    return inverse * (
        d
        - jnp.mean(d, axis=-1, keepdims=True)
        - normed * jnp.mean(d * normed, axis=-1, keepdims=True)
    )


def col_sum(v):
    return jnp.sum(v, axis=0, keepdims=True)


def half_masks(width):
    lane = lax.broadcasted_iota(jnp.int32, (1, width), 1)
    first = jnp.where(lane < width // 2, 1.0, 0.0)
    return first.astype(BF16), (1.0 - first).astype(BF16)


def block_targets(mats, off, q):
    w_qkv, w_proj, w_fc1, w_fc2 = mats
    model = w_proj.shape[0]
    targets = [w_qkv.at[pl.ds(off, q), pl.ds(c * model, model)] for c in range(3)]
    targets.append(w_proj.at[pl.ds(off, q), :])
    targets += [w_fc1.at[pl.ds(off, q), pl.ds(c * model, model)] for c in range(4)]
    targets.append(w_fc2.at[pl.ds(off * 4, 4 * q), :])
    return targets


def weight_count(refs):
    return 9 if refs == 2 else 36


def weight_loads(layer, section, shard, refs, mats, sems):
    model = mats[1].shape[0]
    plans = []
    if len(refs) == 2:
        for i, target in enumerate(block_targets(mats, 0, model)):
            rows = pl.ds(i * model, 4 * model if i == 8 else model)
            plans.append((refs[0].at[rows, :], refs[1].at[rows, :], target, i < 4))
    else:
        count = len(refs) // 2
        q = refs[0].shape[0] // 12
        for p in range(4):
            targets = block_targets(mats, pl.multiple_of((shard ^ p) * q, 16), q)
            for i, target in enumerate(targets):
                which, at = p, i
                if p == 3 and i >= 6:
                    which, at = 4, i - 6
                rows = pl.ds(at * q, 4 * q if i == 8 else q)
                plans.append((refs[which].at[rows, :], refs[count + which].at[rows, :], target, i < 4))
    ones = [pltpu.make_async_copy(x[0], x[2], sems.at[i]) for i, x in enumerate(plans)]
    twos = [pltpu.make_async_copy(x[1], x[2], sems.at[i]) for i, x in enumerate(plans)]

    @pl.when(section == layer)
    def _():
        for copy in ones:
            copy.start()

    @pl.when(section != layer)
    def _():
        for copy in twos:
            copy.start()

    return (
        [copy for copy, x in zip(ones, plans) if x[3]],
        [copy for copy, x in zip(ones, plans) if not x[3]],
    )


def wait_all(copies):
    for copy in copies:
        copy.wait()


def put_half(refs, section, half, at, value):
    keep, send = refs
    rows = slice(at, at + value.shape[0])

    @pl.when(section == half)
    def _():
        keep[rows, :] = value

    @pl.when(section != half)
    def _():
        send[rows, :] = value


def pack_attention(refs, section, g_qkv, g_proj, shard, pieces, stride, first):
    model = g_proj.shape[0]
    q = model // pieces
    for p in range(pieces):
        off = pl.multiple_of((shard ^ p) * q, 16) if pieces > 1 else 0
        at = (stride * p + first) * q
        for c in range(3):
            value = g_qkv[pl.ds(off, q), c * model : (c + 1) * model]
            put_half(refs, section, c // 2, at + (c % 2) * q, value)
        put_half(refs, section, 1, at + q, g_proj[pl.ds(off, q), :])


def pack_mlp(refs, section, g_fc1, g_fc2, shard, pieces, stride, first):
    model = g_fc1.shape[0]
    q = model // pieces
    for p in range(pieces):
        off = pl.multiple_of((shard ^ p) * q, 16) if pieces > 1 else 0
        at = (stride * p + first) * q
        for c in range(4):
            value = g_fc1[pl.ds(off, q), c * model : (c + 1) * model]
            put_half(refs, section, 0, at + c * q, value)
        put_half(refs, section, 1, at, g_fc2[pl.ds(pl.multiple_of(off * 4, 16), 4 * q), :])


class Modulation:
    def __init__(self, line, model):
        self.line, self.model = line, model

    def __getitem__(self, key):
        b, rows, _ = key
        return self.line[:, pl.ds(pl.multiple_of((6 * b + rows.start) * self.model, 128), self.model)]


def bias_at(line, samples, model, start, size):
    return line[:, (6 * samples + start) * model : (6 * samples + start + size) * model]


def attention_forward(b, length, h, mod, bias, w_qkv, w_proj, b_qkv, b_proj, qkv, probs, att, branch, middle):
    model = w_proj.shape[0]
    heads = bias.shape[0]
    pair = 2 * model // heads
    rows = pl.ds(pl.multiple_of(b * length, length), length)
    masks = half_masks(pair)
    x = h[rows, :].astype(F32)
    normed, _ = norm_parts(x)
    normed_low = (normed * (1.0 + mod[b, 1:2, :]) + mod[b, 0:1, :]).astype(BF16)
    qkv[rows, :] = (dot(normed_low, w_qkv[...]) + b_qkv[...]).astype(BF16)
    for j in range(heads // 2):
        q_pair = qkv[rows, j * pair : (j + 1) * pair] * BF16((pair // 2) ** (-0.5))
        k_pair = qkv[rows, model + j * pair : model + (j + 1) * pair]
        v_pair = qkv[rows, 2 * model + j * pair : 2 * model + (j + 1) * pair]
        total = None
        for e in range(2):
            scores = dot_rows(q_pair * masks[e], k_pair) + bias[2 * j + e].astype(F32)
            raised = jnp.exp(scores - jnp.max(scores, axis=-1, keepdims=True))
            p = (raised * (1.0 / jnp.sum(raised, axis=-1, keepdims=True))).astype(BF16)
            probs[b, 2 * j + e] = p
            part = dot(p, v_pair * masks[e])
            total = part if total is None else total + part
        att[rows, j * pair : (j + 1) * pair] = total.astype(BF16)
    out = dot(att[rows, :], w_proj[...]) + b_proj[...]
    branch[rows, :] = out
    middle[rows, :] = x + mod[b, 2:3, :] * out


def mlp_forward(b, length, middle, mod, w_fc1, w_fc2, b_fc1, b_fc2, act, slope, out_branch, layer_out):
    model = w_fc1.shape[0]
    rows = pl.ds(pl.multiple_of(b * length, length), length)
    mid = middle[rows, :]
    normed, _ = norm_parts(mid)
    normed_low = (normed * (1.0 + mod[b, 4:5, :]) + mod[b, 3:4, :]).astype(BF16)
    total = b_fc2[...]
    for c in range(w_fc1.shape[1] // model):
        cols = slice(c * model, (c + 1) * model)
        v = dot(normed_low, w_fc1[:, cols]) + b_fc1[:, cols]
        square = v * v
        t = jnp.tanh(0.7978845608028654 * v * (1.0 + 0.044715 * square))
        half = 0.5 * (1.0 + t)
        a = (v * half).astype(BF16)
        act[rows, cols] = a
        slope[rows, cols] = (
            half
            + 0.5 * v * (1.0 - t * t) * (0.7978845608028654 + (3 * 0.044715 * 0.7978845608028654) * square)
        ).astype(BF16)
        total = total + dot(a, w_fc2[cols, :])
    out_branch[rows, :] = total
    layer_out[rows, :] = (mid + mod[b, 5:6, :] * total).astype(layer_out.dtype)


def mlp_backward(b, length, grad, middle, mod, w_fc1, w_fc2, act, slope, out_branch, d_middle, small, normed_low, d_pre, d_ob):
    model = w_fc1.shape[0]
    rows = pl.ds(pl.multiple_of(b * length, length), length)
    g = grad[rows, :].astype(F32)
    small[b, 2:3, :] = col_sum(g * out_branch[rows, :])
    d_out = g * mod[b, 5:6, :]
    d_out_low = d_out.astype(BF16)
    d_ob[rows, :] = d_out_low
    small[b, 3:4, :] = col_sum(d_out_low.astype(F32))
    normed, inverse = norm_parts(middle[rows, :])
    normed_low[rows, :] = (normed * (1.0 + mod[b, 4:5, :]) + mod[b, 3:4, :]).astype(BF16)
    d_normed = None
    for c in range(w_fc1.shape[1] // model):
        cols = slice(c * model, (c + 1) * model)
        d_act = dot_rows(d_out_low, w_fc2[cols, :])
        d_low = (d_act * slope[rows, cols].astype(F32)).astype(BF16)
        d_pre[rows, cols] = d_low
        small[b, 4 + c : 5 + c, :] = col_sum(d_low.astype(F32))
        part = dot_rows(d_low, w_fc1[:, cols])
        d_normed = part if d_normed is None else d_normed + part
    small[b, 0:1, :] = col_sum(d_normed)
    small[b, 1:2, :] = col_sum(d_normed * normed)
    d_middle[rows, :] = norm_back(d_normed, mod[b, 4:5, :], normed, inverse) + g


def mlp_weight_grads(normed_low, d_pre, act, d_ob, g_fc1, g_fc2):
    model = g_fc1.shape[0]
    for c in range(g_fc1.shape[1] // model):
        cols = slice(c * model, (c + 1) * model)
        g_fc1[:, cols] = dot_cols(normed_low[...], d_pre[:, cols]).astype(BF16)
        g_fc2[cols, :] = dot_cols(act[:, cols], d_ob[...]).astype(BF16)


def attention_backward(b, length, h, mod, w_qkv, w_proj, qkv, probs, att, branch, d_middle, d_in, small, score_sum, normed_low, d_qkv, d_br):
    model = w_proj.shape[0]
    heads = probs.shape[1]
    pair = 2 * model // heads
    scale = F32((pair // 2) ** (-0.5))
    rows = pl.ds(pl.multiple_of(b * length, length), length)
    masks = half_masks(pair)
    d_mid = d_middle[rows, :]
    small[b, 2:3, :] = col_sum(d_mid * branch[rows, :])
    d_branch = (d_mid * mod[b, 2:3, :]).astype(BF16)
    d_br[rows, :] = d_branch
    small[b, 5:6, :] = col_sum(d_branch.astype(F32))
    d_att = dot_rows(d_branch, w_proj[...]).astype(BF16)
    for j in range(heads // 2):
        q_pair = qkv[rows, j * pair : (j + 1) * pair]
        k_pair = qkv[rows, model + j * pair : model + (j + 1) * pair]
        v_pair = qkv[rows, 2 * model + j * pair : 2 * model + (j + 1) * pair]
        d_pair = d_att[:, j * pair : (j + 1) * pair]
        d_q = d_k = d_v = None
        for e in range(2):
            p_low = probs[b, 2 * j + e]
            p = p_low.astype(F32)
            d_here = d_pair * masks[e]
            d_p = dot_rows(d_here, v_pair)
            d_s = (p * (d_p - jnp.sum(d_p * p, axis=-1, keepdims=True))).astype(BF16)
            score_sum[2 * j + e] += d_s.astype(F32)
            v_part = dot_cols(p_low, d_here)
            q_part = dot(d_s, k_pair * masks[e])
            k_part = dot_cols(d_s, q_pair * masks[e])
            d_v = v_part if d_v is None else d_v + v_part
            d_q = q_part if d_q is None else d_q + q_part
            d_k = k_part if d_k is None else d_k + k_part
        d_qkv[rows, j * pair : (j + 1) * pair] = (d_q * scale).astype(BF16)
        d_qkv[rows, model + j * pair : model + (j + 1) * pair] = (d_k * scale).astype(BF16)
        d_qkv[rows, 2 * model + j * pair : 2 * model + (j + 1) * pair] = d_v.astype(BF16)
    small[b, 3:4, :] = col_sum(d_qkv[rows, :model].astype(F32))
    small[b, 4:5, :] = col_sum(d_qkv[rows, 2 * model :].astype(F32))
    small[b, 6:8, :] = jnp.zeros((2, model), F32)
    d_normed = dot_rows(d_qkv[rows, :], w_qkv[...])
    normed, inverse = norm_parts(h[rows, :].astype(F32))
    normed_low[rows, :] = (normed * (1.0 + mod[b, 1:2, :]) + mod[b, 0:1, :]).astype(BF16)
    small[b, 0:1, :] = col_sum(d_normed)
    small[b, 1:2, :] = col_sum(d_normed * normed)
    d_in[rows, :] = (norm_back(d_normed, mod[b, 1:2, :], normed, inverse) + d_mid).astype(d_in.dtype)


def attention_weight_grads(normed_low, d_qkv, att, d_br, g_qkv, g_proj):
    model = g_proj.shape[0]
    for c in range(3):
        cols = slice(c * model, (c + 1) * model)
        g_qkv[:, cols] = dot_cols(normed_low[...], d_qkv[:, cols]).astype(BF16)
    g_proj[...] = dot_cols(att[...], d_br[...]).astype(BF16)


def each_sample(count, body):
    def step(b, carry):
        body(b)
        return carry

    lax.fori_loop(0, count, step, 0)


def add_tables(all_scores, index, outs):
    heads, length = all_scores[0].shape[0], all_scores[0].shape[1]
    low_ids = lax.broadcasted_iota(jnp.int32, (LOW, length), 0)
    high_ids = lax.broadcasted_iota(jnp.int32, (HIGH, length), 0)
    count = len(all_scores) * heads

    def step(i, carry):
        rows = pl.ds(pl.multiple_of(i * 16, 16), 16)
        entries = index[rows, :]
        block = [scores[head, rows, :].astype(F32) for scores in all_scores for head in range(heads)]
        total = carry
        for r in range(16):
            entry = entries[r : r + 1, :]
            low = jnp.where(low_ids == (entry & (LOW - 1)), 1.0, 0.0).astype(BF16)
            high = high_ids == (entry >> LOW_BITS)
            left = jnp.concatenate([jnp.where(high, part[r : r + 1, :], 0.0) for part in block], axis=0).astype(BF16)
            total = total + dot_rows(left, low)
        return total

    total = lax.fori_loop(0, length // 16, step, jnp.zeros((count * HIGH, LOW), F32))
    parts = [total[i * HIGH : (i + 1) * HIGH] for i in range(count)]
    for layer, out in enumerate(outs):
        out[...] = jnp.concatenate(parts[layer * heads : (layer + 1) * heads], axis=1)


def small_kernel(pos, scores0, scores1, index, small_a0, small_m0, small_a1, small_m1, *rest):
    keep, send, table0, table1 = rest[-4:]
    size = small_a0.shape[0] * small_a0.shape[1]
    add_tables((scores0, scores1), index, (table0, table1))
    parts = (
        (small_a0[...], small_m0[...], table0[...]),
        (small_a1[...], small_m1[...], table1[...]),
    )
    rows = [
        jnp.concatenate([x[0].reshape(size, -1), x[1].reshape(size, -1), x[2]], axis=0) for x in parts
    ]

    @pl.when(pos[0] == 0)
    def _():
        keep[...] = rows[0]
        send[...] = rows[1].astype(BF16)

    @pl.when(pos[0] == 1)
    def _():
        keep[...] = rows[1]
        send[...] = rows[0].astype(BF16)


def small_step(pos, scores0, scores1, index, smalls, earlier):
    samples, _, model = smalls[0].shape
    shape = (16 * samples + HIGH, model)
    return call(
        small_kernel, pos, (scores0, scores1, index, *smalls), earlier, [(shape, F32), (shape, BF16)],
        [((HIGH, model), F32)] * 2, work=12,
    )


def set_line(line, layer, section, own_line, other_line):
    line[...] = jnp.where(section == layer, own_line[...], other_line[...])


def start_bias(layer, section, own, other, bias, sem):
    one = pltpu.make_async_copy(own, bias, sem)
    two = pltpu.make_async_copy(other, bias, sem)
    pl.when(section == layer)(one.start)
    pl.when(section != layer)(two.start)
    return one


def line_biases(line, samples, model):
    q_bias = bias_at(line, samples, model, 0, 1)
    v_bias = bias_at(line, samples, model, 1, 1)
    b_qkv = jnp.concatenate([q_bias, jnp.zeros_like(q_bias), v_bias], axis=1)
    return b_qkv, bias_at(line, samples, model, 2, 1), bias_at(line, samples, model, 3, 4), bias_at(line, samples, model, 7, 1)


def forward_kernel(layer, length, n_weights, n_after, pos, h, own_line, other_line, own_bias, other_bias, *rest):
    refs, rest = rest[:n_weights], rest[n_weights + n_after :]
    (qkv, probs, att, branch, middle, act, slope, out_branch, layer_out,
     w_qkv, w_proj, w_fc1, w_fc2, bias, line, sems) = rest
    section, shard = pos[0], pos[1]
    model = h.shape[1]
    samples = h.shape[0] // length
    got_bias = start_bias(layer, section, own_bias, other_bias, bias, sems.at[weight_count(n_weights)])
    for_attention, for_mlp = weight_loads(layer, section, shard, refs, (w_qkv, w_proj, w_fc1, w_fc2), sems)
    set_line(line, layer, section, own_line, other_line)
    mod = Modulation(line, model)
    b_qkv, b_proj, b_fc1, b_fc2 = line_biases(line, samples, model)
    got_bias.wait()
    wait_all(for_attention)
    each_sample(
        samples,
        lambda b: attention_forward(b, length, h, mod, bias, w_qkv, w_proj, b_qkv, b_proj, qkv, probs, att, branch, middle),
    )
    wait_all(for_mlp)
    each_sample(
        samples,
        lambda b: mlp_forward(b, length, middle, mod, w_fc1, w_fc2, b_fc1, b_fc2, act, slope, out_branch, layer_out),
    )


def both_kernel(layer, pieces, length, n_weights, n_after, pos, h, grad, own_line, other_line, own_bias, other_bias, *rest):
    refs, rest = rest[:n_weights], rest[n_weights + n_after :]
    (layer_out, d_in, small_a, small_m, scores, keep, send,
     w_qkv, w_proj, w_fc1, w_fc2, bias, line, qkv, probs, att, branch, middle, act, slope, out_branch,
     d_middle, normed_low, d_pre, d_ob, d_qkv, score_sum, g_qkv, g_proj, g_fc1, g_fc2, sems) = rest
    section, shard = pos[0], pos[1]
    model = h.shape[1]
    samples = h.shape[0] // length
    got_bias = start_bias(layer, section, own_bias, other_bias, bias, sems.at[weight_count(n_weights)])
    for_attention, for_mlp = weight_loads(layer, section, shard, refs, (w_qkv, w_proj, w_fc1, w_fc2), sems)
    set_line(line, layer, section, own_line, other_line)
    mod = Modulation(line, model)
    b_qkv, b_proj, b_fc1, b_fc2 = line_biases(line, samples, model)
    got_bias.wait()
    wait_all(for_attention)
    each_sample(
        samples,
        lambda b: attention_forward(b, length, h, mod, bias, w_qkv, w_proj, b_qkv, b_proj, qkv, probs, att, branch, middle),
    )
    wait_all(for_mlp)

    def mlp(b):
        mlp_forward(b, length, middle, mod, w_fc1, w_fc2, b_fc1, b_fc2, act, slope, out_branch, layer_out)
        mlp_backward(b, length, grad, middle, mod, w_fc1, w_fc2, act, slope, out_branch, d_middle, small_m, normed_low, d_pre, d_ob)

    each_sample(samples, mlp)
    mlp_weight_grads(normed_low, d_pre, act, d_ob, g_fc1, g_fc2)
    pack_mlp((keep, send), section, g_fc1, g_fc2, shard, pieces, 6, 2)
    score_sum[...] = jnp.zeros_like(score_sum)
    each_sample(
        samples,
        lambda b: attention_backward(b, length, h, mod, w_qkv, w_proj, qkv, probs, att, branch, d_middle, d_in, small_a, score_sum, normed_low, d_qkv, d_ob),
    )
    scores[...] = score_sum[...].astype(BF16)
    attention_weight_grads(normed_low, d_qkv, att, d_ob, g_qkv, g_proj)
    pack_attention((keep, send), section, g_qkv, g_proj, shard, pieces, 6, 0)
    rows = slice(keep.shape[0], keep.shape[0] + h.shape[0])

    @pl.when(section == 0)
    def _():
        send[rows, :] = layer_out[...]

    @pl.when(section == 1)
    def _():
        send[rows, :] = h[...]


def backward_mlp_kernel(layer, pieces, length, n_weights, n_after, pos, grad, middle, own_line, other_line, act, slope, out_branch, *rest):
    refs, rest = rest[:n_weights], rest[n_weights + n_after :]
    (d_middle, small, keep, send,
     w_qkv, w_proj, w_fc1, w_fc2, line, normed_low, d_pre, d_ob, g_fc1, g_fc2, sems) = rest
    section, shard = pos[0], pos[1]
    for_attention, for_mlp = weight_loads(layer, section, shard, refs, (w_qkv, w_proj, w_fc1, w_fc2), sems)
    set_line(line, layer, section, own_line, other_line)
    mod = Modulation(line, middle.shape[1])
    wait_all(for_mlp)
    each_sample(
        middle.shape[0] // length,
        lambda b: mlp_backward(b, length, grad, middle, mod, w_fc1, w_fc2, act, slope, out_branch, d_middle, small, normed_low, d_pre, d_ob),
    )
    mlp_weight_grads(normed_low, d_pre, act, d_ob, g_fc1, g_fc2)
    pack_mlp((keep, send), section, g_fc1, g_fc2, shard, pieces, 4, 0)
    wait_all(for_attention)


def backward_attention_kernel(layer, pieces, length, n_weights, n_after, pos, h, own_line, other_line, qkv, probs, att, branch, d_middle, d_h1, *rest):
    refs, rest = rest[:n_weights], rest[n_weights + n_after :]
    (d_in, small, scores, keep, send,
     w_qkv, w_proj, w_fc1, w_fc2, line, normed_low, d_qkv, d_br, score_sum, g_qkv, g_proj, sems) = rest
    section, shard = pos[0], pos[1]
    for_attention, for_mlp = weight_loads(layer, section, shard, refs, (w_qkv, w_proj, w_fc1, w_fc2), sems)
    set_line(line, layer, section, own_line, other_line)
    mod = Modulation(line, h.shape[1])
    score_sum[...] = jnp.zeros_like(score_sum)
    wait_all(for_attention)
    each_sample(
        h.shape[0] // length,
        lambda b: attention_backward(b, length, h, mod, w_qkv, w_proj, qkv, probs, att, branch, d_middle, d_in, small, score_sum, normed_low, d_qkv, d_br),
    )
    scores[...] = score_sum[...].astype(BF16)
    attention_weight_grads(normed_low, d_qkv, att, d_br, g_qkv, g_proj)
    pack_attention((keep, send), section, g_qkv, g_proj, shard, pieces, 2, 0)
    rows = slice(keep.shape[0], keep.shape[0] + h.shape[0])

    @pl.when(section == 0)
    def _():
        send[rows, :] = d_h1[...]

    @pl.when(section == 1)
    def _():
        send[rows, :] = d_in[...].astype(BF16)

    wait_all(for_mlp)


def cost(gigaflop):
    return pl.CostEstimate(flops=int(gigaflop * 1e9), bytes_accessed=0, transcendentals=0)


def call(kernel, pos, operands, in_hbm, outs, scratch, sems=0, work=2):
    specs = [pl.BlockSpec(memory_space=pltpu.SMEM)]
    specs += [pl.BlockSpec(memory_space=pltpu.VMEM) for _ in operands]
    specs += [pl.BlockSpec(memory_space=pl.ANY) for _ in in_hbm]
    shapes = [pltpu.VMEM(shape, dtype) for shape, dtype in scratch]
    if sems:
        shapes.append(pltpu.SemaphoreType.DMA((sems,)))
    return pl.pallas_call(
        kernel,
        out_shape=[jax.ShapeDtypeStruct(shape, dtype) for shape, dtype in outs],
        in_specs=specs,
        out_specs=[pl.BlockSpec(memory_space=pltpu.VMEM) for _ in outs],
        scratch_shapes=shapes,
        cost_estimate=cost(work),
        compiler_params=pltpu.CompilerParams(vmem_limit_bytes=VMEM_BYTES),
    )(pos, *operands, *in_hbm)


class Sizes:
    def __init__(self, samples, length, model, heads, hidden, pieces):
        self.samples, self.length, self.model = samples, length, model
        self.heads, self.hidden, self.pieces = heads, hidden, pieces
        self.rows = samples * length
        self.line = ((1, (6 * samples + 4 + hidden // model) * model), F32)
        self.weights = [
            ((model, 3 * model), BF16), ((model, model), BF16), ((model, hidden), BF16), ((hidden, model), BF16),
        ]
        self.bias = ((heads, length, length), BF16)
        self.probs = ((samples, heads, length, length), BF16)
        self.low = ((self.rows, model), BF16)
        self.full = ((self.rows, model), F32)
        self.qkv = ((self.rows, 3 * model), BF16)
        self.wide = ((self.rows, hidden), BF16)
        self.small = ((samples, 8, model), F32)

    def pack(self, blocks, more=0):
        return [((blocks * self.model, self.model), BF16), ((blocks * self.model + more, self.model), BF16)]


def forward_layer(layer, z, pos, h, lines, biases, weights, earlier):
    return call(
        functools.partial(forward_kernel, layer, z.length, len(weights), len(earlier)),
        pos, (h, *lines), (*biases, *weights, *earlier),
        [z.qkv, z.probs, z.low, z.full, z.full, z.wide, z.wide, z.full, z.low],
        [*z.weights, z.bias, z.line], weight_count(len(weights)) + 1, work=15,
    )


def both_ways(layer, z, pos, h, grad, lines, biases, weights, earlier):
    return call(
        functools.partial(both_kernel, layer, z.pieces, z.length, len(weights), len(earlier)),
        pos, (h, grad, *lines), (*biases, *weights, *earlier),
        [z.low, z.low, z.small, z.small, z.bias, *z.pack(6, z.rows)],
        [*z.weights, z.bias, z.line, z.qkv, z.probs, z.low, z.full, z.full, z.wide, z.wide, z.full,
         z.full, z.low, z.wide, z.low, z.qkv, (z.bias[0], F32), *z.weights],
        weight_count(len(weights)) + 1, work=25,
    )


def backward_mlp(layer, z, pos, grad, middle, lines, act, slope, out_branch, weights, earlier):
    return call(
        functools.partial(backward_mlp_kernel, layer, z.pieces, z.length, len(weights), len(earlier)),
        pos, (grad, middle, *lines, act, slope, out_branch), (*weights, *earlier),
        [z.full, z.small, *z.pack(4)],
        [*z.weights, z.line, z.low, z.wide, z.low, *z.weights[2:]],
        weight_count(len(weights)), work=12,
    )


def backward_attention(layer, z, pos, h, lines, qkv, probs, att, branch, d_middle, d_h1, weights, earlier):
    return call(
        functools.partial(backward_attention_kernel, layer, z.pieces, z.length, len(weights), len(earlier)),
        pos, (h, *lines, qkv, probs, att, branch, d_middle, d_h1), (*weights, *earlier),
        [z.full, z.small, z.bias, *z.pack(2, z.rows)],
        [*z.weights, z.line, z.low, z.qkv, z.low, (z.bias[0], F32), *z.weights[:2]],
        weight_count(len(weights)), work=13,
    )


def partial_kernel(pos, w_ada, cond_a, cond_b, cond_c, cond_d, b_ada, b_qv, b_proj, b_fc1, b_fc2, *rest):
    copied, outs, whole = rest[-6], rest[-5:-1], rest[-1]
    copied[...] = w_ada[...]
    shard = pos[1]
    q, wide = w_ada.shape
    samples, model = cond_a.shape
    whole[...] = jnp.zeros_like(whole)
    whole[pl.ds(pl.multiple_of(shard * q, 16), q), :] = w_ada[...]
    for cond, out in zip((cond_a, cond_b, cond_c, cond_d), outs):
        c = cond[...].astype(F32)
        act = (c * (1.0 / (1.0 + jnp.exp(-c)))).astype(BF16)
        out[:, :wide] = dot(act, whole[...])
        out[:, wide:] = jnp.zeros((samples, 2 * model), F32)
        for f in range(4):
            @pl.when(shard == f)
            def _():
                here = slice(f * b_ada.shape[1], (f + 1) * b_ada.shape[1])
                out[:, here] += b_ada[...].astype(F32)
                for bias, row, at in ((b_qv, 0, 0), (b_proj, 1, 0), (b_fc1, 1, model), (b_fc2, 3, model)):
                    width = bias.shape[1]
                    at += f * width
                    row, at = row + at // (2 * model), wide + at % (2 * model)
                    out[row : row + 1, at : at + width] = bias[...].astype(F32)


def partial_step(pos, w_ada, conds, biases, earlier):
    q, wide = w_ada.shape
    samples, model = conds[0].shape
    return call(
        partial_kernel, pos, (w_ada, *conds, *biases), earlier, [(w_ada.shape, BF16)] + [((samples, wide + 2 * model), F32)] * 4,
        [((4 * q, wide), BF16)],
    )


def line_kernel(pos, own, got_a, got_b, got_c, *rest):
    keep, send, total = rest[-3:]
    section = pos[0]
    samples = own.shape[0]
    each = samples // 2
    model = own.shape[1] // 8
    total[...] = (own[...] + got_a[...]) + (got_b[...] + got_c[...])
    for out, side in ((keep, section), (send, 1 - section)):
        for b in range(each):
            out[:, b * 6 * model : (b + 1) * 6 * model] = total[pl.ds(side * each + b, 1), : 6 * model]
        for row in range(samples):
            at = (6 * each + 2 * row) * model
            out[:, at : at + 2 * model] = total[row : row + 1, 6 * model :]


def line_step(pos, own, got, earlier):
    samples, model = own.shape[0], own.shape[1] // 8
    shape = (1, (3 * samples + 8) * model)
    return call(line_kernel, pos, (own, *got), earlier, [(shape, F32)] * 2, [(own.shape, F32)])


def first_kernel(keep1, other1, keep_m, other_m, own, *messages):
    pieces = 4
    size1, size_m = keep1.shape[0] // pieces, keep_m.shape[0] // pieces
    n1, nm = size1 // 4, size_m // 4
    for p in range(pieces):
        for k in range(4):
            at = k * (n1 + nm)
            for keep, other, first, n, to in (
                (keep1, other1, p * size1 + k * n1, n1, at), (keep_m, other_m, p * size_m + k * nm, nm, at + n1)
            ):
                total = keep[first : first + n, :].astype(F32) + other[first : first + n, :].astype(F32)
                if p == 0:
                    own[to : to + n, :] = total
                else:
                    messages[p - 1][to : to + n, :] = total.astype(BF16)


def first_step(keep1, other1, keep_m, other_m):
    shape = ((keep1.shape[0] + keep_m.shape[0]) // 4, keep1.shape[1])
    return pl.pallas_call(
        first_kernel,
        out_shape=[jax.ShapeDtypeStruct(shape, F32)] + [jax.ShapeDtypeStruct(shape, BF16)] * 3,
        compiler_params=pltpu.CompilerParams(vmem_limit_bytes=VMEM_BYTES),
    )(keep1, other1, keep_m, other_m)


def plane_kernel(samples, pos, keep, other, kept_small, other_small, cond, own, own_small, *rest):
    messages, work = rest[:3], rest[3]
    section = pos[0]
    size, model = own.shape
    for p in range(4):
        rows = slice(p * size, (p + 1) * size)
        total = keep[rows, :].astype(F32) + other[rows, :].astype(F32)
        if p == 0:
            own[...] = total
        else:
            messages[p - 1][:size, :] = total.astype(BF16)
    theirs = other_small[...].astype(F32)
    mine = kept_small[...]
    each = samples // 2
    work[...] = jnp.zeros_like(work)
    for b in range(each):
        for kind in range(6):
            row = b * 8 + kind if kind < 3 else (each + b) * 8 + kind - 3
            work[pl.ds(kind * samples + section * each + b, 1), :] = mine[row : row + 1, :]
            work[pl.ds(kind * samples + (1 - section) * each + b, 1), :] = theirs[row : row + 1, :]
    work[6 * samples : 7 * samples, :] = cond[...].astype(F32)
    both = mine + theirs
    bias_rows = sum(both[(each + b) * 8 + 3 : (each + b) * 8 + 8, :] for b in range(each))
    more_rows = sum(both[b * 8 + 3 : b * 8 + 6, :] for b in range(each))
    at = 7 * samples
    work[at : at + 5, :] = bias_rows
    work[at + 5 : at + 8, :] = more_rows
    work[at + 8 : at + 8 + HIGH, :] = both[2 * each * 8 :, :]
    small = work[...].astype(BF16)
    own_small[...] = small
    for message in messages:
        message[size:, :] = small


def plane_step(pos, keep, other, kept_small, other_small, cond):
    samples, model = cond.shape
    size = keep.shape[0] // 4
    small = -(-(7 * samples + 8 + HIGH) // 16) * 16
    outs = [((size, model), F32), ((small, model), BF16)] + [((size + small, model), BF16)] * 3
    return call(
        functools.partial(plane_kernel, samples), pos, (keep, other, kept_small, other_small, cond), (), outs,
        [((small, model), F32)],
    )


def column_kernel(samples, pos, own, own_small, got_a, got_b, got_c, part, own_out, *rest):
    messages, work = rest[:3], rest[3]
    rank = pos[2]
    size, model = own.shape
    n = size // 4
    got = (got_a, got_b, got_c)
    for j in range(4):
        at = pl.multiple_of((rank ^ j) * n, 16)
        total = own[pl.ds(at, n), :]
        for piece in got:
            total = total + piece[pl.ds(at, n), :].astype(F32)
        if j == 0:
            part[...] = total
        else:
            messages[j - 1][:n, :] = total.astype(BF16)
    smalls = [own_small[...].astype(F32)] + [piece[size:, :].astype(F32) for piece in got]
    work[...] = jnp.zeros_like(work)
    for p in range(4):
        for kind in range(7):
            at = (kind * 4 + p) * samples
            work[at : at + samples, :] = smalls[p][kind * samples : (kind + 1) * samples, :]
    at = 7 * samples
    summed = (smalls[0] + smalls[1]) + (smalls[2] + smalls[3])
    work[4 * at : 4 * at + 8 + HIGH, :] = summed[at : at + 8 + HIGH, :]
    small = work[...].astype(BF16)
    own_out[...] = small
    for message in messages:
        message[n:, :] = small


def column_step(pos, own, own_small, got, samples):
    size, model = own.shape
    small = -(-(28 * samples + 8 + HIGH) // 16) * 16
    outs = [((size // 4, model), F32), ((small, model), BF16)] + [((size // 4 + small, model), BF16)] * 3
    return call(
        functools.partial(column_kernel, samples), pos, (own, own_small, *got), (), outs, [((small, model), F32)]
    )


def finish_kernel(samples, width, pos, own_small, got_a, got_b, got_c,
                  g_ada, g_b_ada, g_b_qv, g_b_proj, g_b_fc1, g_b_fc2, g_table, work, whole, row):
    shard, rank = pos[1], pos[2]
    model = own_small.shape[1]
    each = 4 * samples
    n = got_a.shape[0] - own_small.shape[0]
    pieces = [own_small[...]] + [piece[n:, :] for piece in (got_a, got_b, got_c)]
    for j in range(4):
        for kind in range(7):
            at = pl.multiple_of(kind * 4 * each + (rank ^ j) * each, 16)
            work[pl.ds(at, each), :] = pieces[j][kind * each : (kind + 1) * each, :].astype(F32)
    cond = work[24 * each :, :]
    act = (cond * (1.0 / (1.0 + jnp.exp(-cond)))).astype(BF16)
    for kind in range(6):
        rows = work[kind * 4 * each : (kind + 1) * 4 * each, :]
        whole[...] = dot_cols(act, rows.astype(BF16))
        cols = slice(kind * model, (kind + 1) * model)
        g_ada[:, cols] = whole[pl.ds(pl.multiple_of(shard * width, 16), width), :]
        row[:, cols] = col_sum(rows)
    at = 7 * each
    rows = [piece[at : at + 8 + HIGH, :].astype(F32) for piece in pieces]
    summed = (rows[0] + rows[1]) + (rows[2] + rows[3])
    for c in range(4):
        row[:, (6 + c) * model : (7 + c) * model] = summed[1 + c : 2 + c, :]
    row[:, 10 * model : 11 * model] = summed[5:6, :]
    row[:, 11 * model : 12 * model] = summed[6:7, :]
    row[:, 12 * model : 13 * model] = summed[7:8, :]
    row[:, 13 * model : 14 * model] = summed[0:1, :]
    for f in range(4):
        @pl.when(shard == f)
        def _():
            for out, start in ((g_b_ada, 0), (g_b_fc1, 6), (g_b_qv, 10), (g_b_proj, 12), (g_b_fc2, 13)):
                size = out.shape[1]
                out[...] = row[:, start * model + f * size : start * model + (f + 1) * size]
    heads, entries = g_table.shape
    for high in range(-(-entries // LOW)):
        size = min(LOW, entries - high * LOW)
        for head in range(heads):
            g_table[head : head + 1, high * LOW : high * LOW + size] = summed[
                8 + high : 9 + high, head * LOW : head * LOW + size
            ]


def finish_step(pos, own_small, got, samples, width, heads, entries):
    model = own_small.shape[1]
    sizes = [6 * width, 2 * width, width, 4 * width, width]
    return call(
        functools.partial(finish_kernel, samples, width), pos, (own_small, *got), (),
        [((width, 6 * model), F32)] + [((1, size), F32) for size in sizes] + [((heads, entries), F32)],
        [((7 * 16 * samples, model), F32), ((model, model), F32), ((1, 14 * model), F32)],
    )


def cond_kernel(samples, pos, small, cond, *rest):
    out, w_ada = rest[-2:]
    model = cond.shape[1]
    for p, piece in enumerate(rest[:-2]):
        q = piece.shape[0]
        off = pl.multiple_of((pos[1] ^ p) * q, 16) if q < model else 0
        w_ada[pl.ds(off, q), :] = piece[...]
    total = None
    for kind in range(6):
        rows = small[...].astype(F32)[kind * samples : (kind + 1) * samples, :].astype(BF16)
        part = dot_rows(rows, w_ada[:, kind * model : (kind + 1) * model])
        total = part if total is None else total + part
    c = cond[...].astype(F32)
    gate = 1.0 / (1.0 + jnp.exp(-c))
    out[...] = total * (gate * (1.0 + c * (1.0 - gate)))


def cond_step(pos, small, w_ada, cond):
    model = cond.shape[1]
    return call(
        functools.partial(cond_kernel, cond.shape[0]), pos, (small, cond, *w_ada), (), [(cond.shape, F32)],
        [((model, w_ada[0].shape[1]), BF16)],
    )[0]


def final_kernel(pos, own_a, own_m, other, g_qkv, g_proj, g_fc1, g_fc2):
    section = pos[0]
    q, model = g_proj.shape
    cut = own_a.shape[0]

    def write(first_a, first_m, second_a, second_m):
        for c in range(2):
            g_qkv[:, c * model : (c + 1) * model] = first_a[c * q : (c + 1) * q, :].astype(F32)
        g_qkv[:, 2 * model : 3 * model] = second_a[:q, :].astype(F32)
        g_proj[...] = second_a[q : 2 * q, :].astype(F32)
        for c in range(4):
            g_fc1[:, c * model : (c + 1) * model] = first_m[c * q : (c + 1) * q, :].astype(F32)
        g_fc2[...] = second_m[...].astype(F32)

    other_a, other_m = other.at[:cut, :], other.at[cut:, :]

    @pl.when(section == 0)
    def _():
        write(own_a, own_m, other_a, other_m)

    @pl.when(section == 1)
    def _():
        write(other_a, other_m, own_a, own_m)


def final_step(pos, own_a, own_m, other):
    q, model = own_a.shape[0] // 2, own_a.shape[1]
    return call(
        final_kernel, pos, (own_a, own_m, other), (),
        [((q, 3 * model), F32), ((q, model), F32), ((q, 4 * model), F32), ((4 * q, model), F32)], [],
    )


def halve_kernel(pos, own, got_a, got_b, got_c, keep, send):
    bit = pos[2] & 1
    n = own.shape[0] // 4
    for high in range(2):
        for out, low in ((keep, bit), (send, 1 - bit)):
            rows = pl.ds(pl.multiple_of((2 * high + low) * n, 16), n)
            total = own[rows, :]
            for piece in (got_a, got_b, got_c):
                total = total + piece[rows, :].astype(F32)
            out[high * n : (high + 1) * n, :] = total.astype(out.dtype)


def halve_step(pos, own, got):
    shape = (own.shape[0] // 2, own.shape[1])
    return call(halve_kernel, pos, (own, *got), (), [(shape, F32), (shape, BF16)], [])


def quarter_kernel(pos, kept, got, keep, send):
    bit = pos[2] >> 1
    n = kept.shape[0] // 2
    for out, high in ((keep, bit), (send, 1 - bit)):
        rows = pl.ds(pl.multiple_of(high * n, 16), n)
        out[...] = (kept[rows, :] + got[rows, :].astype(F32)).astype(out.dtype)


def quarter_step(pos, kept, got):
    shape = (kept.shape[0] // 2, kept.shape[1])
    return call(quarter_kernel, pos, (kept, got), (), [(shape, F32), (shape, BF16)], [])


def pack_kernel(qkv, proj, fc1, fc2, out):
    q, model = proj.shape
    for c in range(3):
        out[c * q : (c + 1) * q, :] = qkv[:, c * model : (c + 1) * model]
    out[3 * q : 4 * q, :] = proj[...]
    for c in range(4):
        out[(4 + c) * q : (5 + c) * q, :] = fc1[:, c * model : (c + 1) * model]
    out[8 * q : 12 * q, :] = fc2[...]


def pack_shard(own):
    q, model = own[1].shape
    return pl.pallas_call(
        pack_kernel,
        out_shape=jax.ShapeDtypeStruct((12 * q, model), BF16),
        compiler_params=pltpu.CompilerParams(vmem_limit_bytes=VMEM_BYTES),
    )(*own)


def after(values, others):
    return pl.pallas_call(
        lambda *refs: None,
        out_shape=[jax.ShapeDtypeStruct(v.shape, v.dtype) for v in values],
        in_specs=[pl.BlockSpec(memory_space=pl.ANY)] * (len(values) + len(others)),
        out_specs=[pl.BlockSpec(memory_space=pl.ANY)] * len(values),
        input_output_aliases={i: i for i in range(len(values))},
    )(*values, *others)


def lookup_kernel(table, index, *rest):
    out, work = rest[-2:]
    heads, length = out.shape[0], out.shape[1]
    high_count = table.shape[0] // 8
    values = table[...]
    low_id = lax.broadcasted_iota(jnp.int32, (LOW, length), 0)

    def step(i, carry):
        block = index[pl.ds(pl.multiple_of(i * 8, 8), 8), :]
        for r in range(8):
            entry = block[r : r + 1, :]
            picks = jnp.where(low_id == (entry & (LOW - 1)), 1.0, 0.0).astype(BF16)
            found = dot(values, picks).reshape(high_count, 8, length)
            high = jnp.broadcast_to(entry >> LOW_BITS, (8, length))
            bit = high_count // 2
            while bit:
                chosen = (high & bit) != 0
                found = jnp.where(chosen[None], found[bit : 2 * bit], found[:bit])
                bit //= 2
            for head in range(heads):
                work[head, pl.ds(i * 8 + r, 1), :] = found[0, head : head + 1, :]
        return carry

    lax.fori_loop(0, length // 8, step, 0)
    out[...] = work[...].astype(BF16)


def lookup(table, index, earlier):
    heads, entries = table.shape
    high_count = HIGH
    padded = jnp.pad(table, ((0, 8 - heads), (0, high_count * LOW - entries)))
    rows = jnp.transpose(padded.reshape(8, high_count, LOW), (1, 0, 2)).reshape(high_count * 8, LOW)
    length = index.shape[0]
    return pl.pallas_call(
        lookup_kernel,
        out_shape=jax.ShapeDtypeStruct((heads, length, length), BF16),
        in_specs=[pl.BlockSpec(memory_space=pltpu.VMEM)] * 2 + [pl.BlockSpec(memory_space=pl.ANY)] * len(earlier),
        out_specs=pl.BlockSpec(memory_space=pltpu.VMEM),
        scratch_shapes=[pltpu.VMEM((heads, length, length), F32)],
        cost_estimate=cost(11),
        compiler_params=pltpu.CompilerParams(vmem_limit_bytes=VMEM_BYTES),
    )(rows, index, *earlier)


def swap_section(value):
    return lax.ppermute(value, "section", [(0, 1), (1, 0)])


def pairs_of(count, step):
    return [(i, i ^ step) for i in range(count)]


def by_rank(pieces, rank):
    stack = jnp.stack(pieces)
    count = len(pieces)
    bit = 1
    while bit < count:
        moved = jnp.stack([stack[i ^ bit] for i in range(count)])
        stack = jnp.where((rank & bit) != 0, moved, stack)
        bit *= 2
    return stack


def section_sums(keep, other, shards):
    size = keep.shape[0] // shards
    return [
        keep[p * size : (p + 1) * size].astype(F32) + other[p * size : (p + 1) * size].astype(F32)
        for p in range(shards)
    ]


def low_pieces(sums):
    return [x.astype(BF16) for x in sums[1:]]


def to_peers(messages, axis):
    count = lax.axis_size(axis)
    return [lax.ppermute(messages[p - 1], axis, pairs_of(count, p)) for p in range(1, count)]


def add_pieces(own, got):
    total = own
    for piece in got:
        total = total + piece.astype(F32)
    return total


def replica_parts(total, rank):
    replicas = lax.axis_size("rep")
    parts = total if total.ndim == 3 else total.reshape(replicas, total.shape[0] // replicas, -1)
    low = parts.astype(BF16)
    mine = lax.dynamic_index_in_dim(parts, rank, 0, keepdims=False)
    return mine, [lax.dynamic_index_in_dim(low, rank ^ j, 0, keepdims=False) for j in range(1, replicas)]


def unpack_attention(pack):
    q = pack.shape[0] // 4
    return jnp.concatenate([pack[c * q : (c + 1) * q] for c in range(3)], axis=1), pack[3 * q :]


def unpack_mlp(pack):
    q = pack.shape[0] // 8
    return jnp.concatenate([pack[c * q : (c + 1) * q] for c in range(4)], axis=1), pack[4 * q :]


def pad_rows(value):
    return jnp.pad(value, ((0, -value.shape[0] % 16), (0, 0)))


def from_peers(value, axis):
    return [lax.ppermute(value, axis, pairs_of(lax.axis_size(axis), p)) for p in range(1, lax.axis_size(axis))]


def pair_sum(values):
    while len(values) > 1:
        values = [values[i] + values[i + 1] for i in range(0, len(values), 2)]
    return values[0]


def per_device(inputs, conditioning, cotangent, micro_sizes, relative_bias_index,
               w_ada, w_qkv, w_proj, w_fc1, w_fc2, b_ada, b_qv, b_proj, b_fc1, b_fc2, bias_table):
    section = lax.axis_index("section")
    shard = lax.axis_index("fsdp")
    rank = lax.axis_index("rep")
    shards, replicas = lax.axis_size("fsdp"), lax.axis_size("rep")
    direct = shards == 4 and replicas == 4
    is_first = section == 0
    samples, length, model = inputs.shape
    heads, entries = bias_table.shape[1:]
    half = samples // 2
    z = Sizes(half, length, model, heads, 4 * model, shards if direct else 1)
    pos = jnp.stack([section, shard, rank]).astype(jnp.int32)

    def mine(first, second):
        return jnp.where(is_first, first, second)

    def own_samples(array):
        return lax.dynamic_slice_in_dim(array, section * half, half, 0)

    def in_order(own, other):
        return jnp.where(is_first, jnp.concatenate([own, other]), jnp.concatenate([other, own]))

    live = (jnp.arange(half)[:, None, None] < lax.dynamic_index_in_dim(micro_sizes[0], section, 0)).astype(BF16)
    h0 = own_samples(inputs).reshape(half * length, model)
    grad1 = (own_samples(cotangent) * live).reshape(half * length, model)
    index = relative_bias_index
    own_raw = [w_qkv[0], w_proj[0], w_fc1[0], w_fc2[0]]
    width = model // shards
    if direct:
        conds = [conditioning] + from_peers(conditioning, "fsdp")
        own_pack = pack_shard(own_raw)
        middle_row = own_pack.shape[0] // 2
        got_x = lax.ppermute(own_pack, "fsdp", pairs_of(shards, 1))
        got_y = lax.ppermute(own_pack, "fsdp", pairs_of(shards, 2))
        bias_own = lookup(bias_table[0], index, [own_pack, *conds[1:]])
        got_x, got_y = after([got_x, got_y], [bias_own])
        forward_x, forward_y = got_x[:middle_row], got_y[middle_row:]
        w_ada_copy, *partial = partial_step(
            pos, w_ada[0], conds, (b_ada, b_qv, b_proj, b_fc1, b_fc2), [bias_own]
        )
        got_first = lax.ppermute(forward_x, "fsdp", pairs_of(shards, 2))
        got_second = lax.ppermute(forward_y, "fsdp", pairs_of(shards, 1))
        got_first, got_second = after([got_first, got_second], [partial[0]])
        own_weights = [own_pack, got_x, got_y, got_first, got_second]
        weights = own_weights + [swap_section(w) for w in own_weights]
        own_line, send_line = line_step(pos, partial[0], to_peers(after(partial[1:], [got_first, got_second]), "fsdp"), [h0, grad1])
    else:
        row = jnp.concatenate([b_ada, b_qv, b_proj, b_fc1, b_fc2], axis=1)
        bias_rows = lax.all_gather(row[0], "fsdp", axis=0)
        whole = [lax.all_gather(w, "fsdp", axis=0, tiled=True) for w in own_raw]
        own_whole = pack_shard(whole)
        weights = [own_whole, swap_section(own_whole)]
        acts = jax.nn.silu(conditioning.astype(F32)).astype(BF16)
        modulation = dot(acts, lax.all_gather(w_ada[0], "fsdp", axis=0, tiled=True))
        bias_own = lookup(bias_table[0], index, [])
        cuts = [b_ada.shape[1], b_qv.shape[1], b_proj.shape[1], b_fc1.shape[1], b_fc2.shape[1]]
        biases, at = [], 0
        for cut in cuts:
            biases.append(bias_rows[:, at : at + cut].reshape(1, -1).astype(F32))
            at += cut
        modulation = modulation + biases[0]
        other_samples = lax.dynamic_slice_in_dim(modulation, (1 - section) * half, half, 0)
        own_line = jnp.concatenate([own_samples(modulation).reshape(1, -1)] + biases[1:], axis=1)
        send_line = jnp.concatenate([other_samples.reshape(1, -1)] + biases[1:], axis=1)
    lines = (own_line, swap_section(send_line))
    bias_heads = (bias_own, swap_section(bias_own))

    if direct:
        w_ada_later = after([w_ada_copy], weights[3:5])[0]
        w_ada_pieces = [w_ada_later] + from_peers(w_ada_later, "fsdp")
    else:
        w_ada_pieces = [lax.all_gather(w_ada[0], "fsdp", axis=0, tiled=True)]
    qkv, probs, att, branch, middle, act, slope, out_branch, h1 = forward_layer(0, z, pos, h0, lines, bias_heads, weights, w_ada_pieces[:1] if direct else [])
    out1, d_h1, small_a1, small_m1, scores1, keep1, send1 = both_ways(1, z, pos, h1, grad1, lines, bias_heads, weights, w_ada_pieces[1:])
    d_middle, small_m0, keep_m0, send_m0 = backward_mlp(0, z, pos, d_h1, middle, lines, act, slope, out_branch, weights, [])
    pieces = z.pieces
    rows = half * length
    other1 = swap_section(send1)
    other_m0 = swap_section(send_m0)
    if direct:
        own_first, *first_messages = first_step(keep1, other1, keep_m0, other_m0)
        earlier = first_messages
    else:
        sums1 = section_sums(keep1, other1[: keep1.shape[0]], pieces)
        sums_m0 = section_sums(keep_m0, other_m0, pieces)
        earlier = []
    d_h0, small_a0, scores0, keep_a0, send_a0 = backward_attention(
        0, z, pos, h0, lines, qkv, probs, att, branch, d_middle, d_h1, weights, earlier
    )
    smalls = (small_a0, small_m0, small_a1, small_m1)
    size_a = keep_a0.shape[0]

    def replica(value, step):
        return lax.ppermute(value, "rep", pairs_of(replicas, step))

    def ordered(own, other, bit):
        return jnp.where(bit == 0, jnp.concatenate([own, other]), jnp.concatenate([other, own]))

    if direct:
        kept_small, send_small = small_step(pos, scores0, scores1, index, smalls, [])
        other_small = swap_section(send_small)
        other_a0 = after([swap_section(send_a0)], [kept_small])[0]
        own_a0, own_small, *messages = plane_step(pos, keep_a0, other_a0, kept_small, other_small, conditioning)
        got = to_peers(messages, "fsdp")
        got_first = after(to_peers(first_messages, "fsdp"), [own_small])
        keep_z, send_z = halve_step(pos, own_first, got_first)
        part0, plane_small, *messages = column_step(pos, own_a0, own_small, got, samples)
        got_z = after([replica(send_z, 1)], [plane_small])[0]
        keep_z, send_z = quarter_step(pos, keep_z, got_z)
        cond_part = cond_step(pos, after([own_small], [send_z])[0], w_ada_pieces, conditioning)
        got = after(to_peers(messages, "rep"), [cond_part])
        size = part0.shape[0]
        high, low = rank >> 1, rank & 1
        quarter0 = add_pieces(part0, [x[:size] for x in got]).astype(BF16)
        got_z, cond_part = after([replica(send_z, 2), cond_part], [quarter0])
        quarter = (keep_z + got_z.astype(F32)).astype(BF16)
        pair = ordered(quarter, replica(quarter, 2), high)
        half_a0 = by_rank([quarter0] + from_peers(quarter0, "rep"), rank).reshape(-1, model)
        n = pair.shape[0] // 2
        quarters = ordered(pair.reshape(1, 2, n, model), replica(pair, 1).reshape(1, 2, n, model), low)
        quarters = jnp.transpose(quarters, (1, 0, 2, 3)).reshape(4, n, model)
        n = 3 * n // 5
        half1 = quarters[:, :n].reshape(-1, model)
        half_m0 = quarters[:, n:].reshape(-1, model)
        g_ada, g_b_ada, g_b_qv, g_b_proj, g_b_fc1, g_b_fc2, g_table = finish_step(
            pos, plane_small, got, samples, width, heads, entries
        )
    else:
        other_a0 = swap_section(send_a0)
        kept_small, send_small = small_step(pos, scores0, scores1, index, smalls, [])
        theirs = swap_section(send_small).astype(F32)
        both = kept_small + theirs
        cut = half * 8

        def d_mod_of(values):
            a, m = values[:cut].reshape(half, 8, model), values[cut : 2 * cut].reshape(half, 8, model)
            return jnp.concatenate([a[:, :3], m[:, :3]], axis=1)

        low = in_order(d_mod_of(kept_small), d_mod_of(theirs)).astype(BF16)
        bias_rows = jnp.sum(both[: 2 * cut].reshape(2, half, 8, model), axis=1)
        summed = jnp.concatenate([bias_rows[1, 3:8], bias_rows[0, 3:6], both[2 * cut :]])
        cond_part = cond_step(pos, jnp.transpose(low, (1, 0, 2)).reshape(-1, model), w_ada_pieces, conditioning)
        kept = jnp.concatenate([low, conditioning[:, None]], axis=1)
        kept = lax.all_gather(kept, ("fsdp", "rep"), axis=0, tiled=True)
        summed = lax.psum(summed, ("fsdp", "rep"))
        act_all = jax.nn.silu(kept[:, 6].astype(F32)).astype(BF16)
        act_cols = lax.dynamic_slice_in_dim(act_all, shard * width, width, 1)
        g_ada = jnp.concatenate([dot_cols(act_cols, kept[:, i]) for i in range(6)], axis=1)
        g_b_ada = jnp.sum(kept[:, :6].astype(F32), axis=0).reshape(-1)
        vectors = [g_b_ada, summed[5:7].reshape(-1), summed[7], summed[1:5].reshape(-1), summed[0]]
        g_b_ada, g_b_qv, g_b_proj, g_b_fc1, g_b_fc2 = [
            lax.dynamic_slice_in_dim(v, shard * (v.shape[0] // shards), v.shape[0] // shards, 0)[None] for v in vectors
        ]
        g_table = jnp.transpose(summed[8:].reshape(HIGH, heads, LOW), (1, 0, 2)).reshape(heads, HIGH * LOW)[:, :entries]
        sums_a0 = section_sums(keep_a0, other_a0[:size_a], z.pieces)
        half_a0, half_m0, half1 = sums_a0[0].astype(BF16), sums_m0[0].astype(BF16), sums1[0].astype(BF16)
    cond_grad = cond_part + swap_section(cond_part)
    cut = half_a0.shape[0]
    half_a1, half_m1 = half1[:cut], half1[cut:]
    grads = final_step(
        pos, mine(half_a0, half_a1), mine(half_m0, half_m1),
        swap_section(mine(jnp.concatenate([half_a1, half_m1]), jnp.concatenate([half_a0, half_m0]))),
    )
    if not direct:
        grads = [lax.psum_scatter(g.astype(BF16), "fsdp", scatter_dimension=0, tiled=True) for g in grads]
        grads = [g.astype(F32) for g in lax.psum(tuple(grads), "rep")]
    g_qkv, g_proj, g_fc1, g_fc2 = grads

    activations = in_order(
        mine(h1, out1).reshape(half, length, model), other1[keep1.shape[0] :].reshape(half, length, model)
    )
    input_grads = in_order(
        mine(d_h0, d_h1.astype(F32)).reshape(half, length, model),
        other_a0[size_a : size_a + rows].astype(F32).reshape(half, length, model),
    )

    return (
        activations[None], input_grads[None], cond_grad,
        g_ada[None], g_qkv[None], g_proj[None], g_fc1[None], g_fc2[None],
        g_b_ada, g_b_qv, g_b_proj, g_b_fc1, g_b_fc2,
        g_table[None],
    )


def solution(mesh):
    batch = ("fsdp", "rep")
    matrix = P("section", "fsdp", None)
    vector = P("section", "fsdp")
    return jax.shard_map(
        per_device,
        mesh=mesh,
        in_specs=(
            P(batch, None, None), P(batch, None), P(batch, None, None), P(batch, None), P(),
            matrix, matrix, matrix, matrix, matrix, vector, vector, vector, vector, vector,
            P("section", None, None),
        ),
        out_specs=(
            P("section", batch, None, None), P("section", batch, None, None), P(batch, None),
            matrix, matrix, matrix, matrix, matrix, vector, vector, vector, vector, vector,
            P("section", None, None),
        ),
        check_vma=False,
    )
```

```python
import functools

import jax
import jax.numpy as jnp
from jax import lax
from jax.experimental import pallas as pl
from jax.experimental.pallas import tpu as pltpu
from jax.sharding import PartitionSpec as P

EPSILON = 1e-06
F32 = jnp.float32
BF16 = jnp.bfloat16
VMEM_BYTES = 58 * 1024 * 1024
LOW_BITS = 6
LOW = 1 << LOW_BITS
HIGH = 16


def dot(a, b):
    return jnp.dot(a, b, preferred_element_type=F32)


def dot_rows(a, b):
    return lax.dot_general(a, b, (((1,), (1,)), ((), ())), preferred_element_type=F32)


def dot_cols(a, b):
    return lax.dot_general(a, b, (((0,), (0,)), ((), ())), preferred_element_type=F32)


def norm_parts(v):
    centre = v - jnp.mean(v, axis=-1, keepdims=True)
    inverse = lax.rsqrt(jnp.mean(centre * centre, axis=-1, keepdims=True) + EPSILON)
    return centre * inverse, inverse


def norm_back(d_normed, scale, normed, inverse):
    d = d_normed * (1.0 + scale)
    return inverse * (
        d
        - jnp.mean(d, axis=-1, keepdims=True)
        - normed * jnp.mean(d * normed, axis=-1, keepdims=True)
    )


def col_sum(v):
    return jnp.sum(v, axis=0, keepdims=True)


def half_masks(width):
    lane = lax.broadcasted_iota(jnp.int32, (1, width), 1)
    first = jnp.where(lane < width // 2, 1.0, 0.0)
    return first.astype(BF16), (1.0 - first).astype(BF16)


def block_targets(mats, off, q):
    w_qkv, w_proj, w_fc1, w_fc2 = mats
    model = w_proj.shape[0]
    targets = [w_qkv.at[pl.ds(off, q), pl.ds(c * model, model)] for c in range(3)]
    targets.append(w_proj.at[pl.ds(off, q), :])
    targets += [w_fc1.at[pl.ds(off, q), pl.ds(c * model, model)] for c in range(4)]
    targets.append(w_fc2.at[pl.ds(off * 4, 4 * q), :])
    return targets


def weight_count(refs):
    return 9 if refs == 2 else 36


def weight_loads(layer, section, shard, refs, mats, sems):
    model = mats[1].shape[0]
    plans = []
    if len(refs) == 2:
        for i, target in enumerate(block_targets(mats, 0, model)):
            rows = pl.ds(i * model, 4 * model if i == 8 else model)
            plans.append((refs[0].at[rows, :], refs[1].at[rows, :], target, i < 4))
    else:
        count = len(refs) // 2
        q = refs[0].shape[0] // 12
        for p in range(4):
            targets = block_targets(mats, pl.multiple_of((shard ^ p) * q, 16), q)
            for i, target in enumerate(targets):
                which, at = p, i
                if p == 3 and i >= 6:
                    which, at = 4, i - 6
                rows = pl.ds(at * q, 4 * q if i == 8 else q)
                plans.append((refs[which].at[rows, :], refs[count + which].at[rows, :], target, i < 4))
    ones = [pltpu.make_async_copy(x[0], x[2], sems.at[i]) for i, x in enumerate(plans)]
    twos = [pltpu.make_async_copy(x[1], x[2], sems.at[i]) for i, x in enumerate(plans)]

    @pl.when(section == layer)
    def _():
        for copy in ones:
            copy.start()

    @pl.when(section != layer)
    def _():
        for copy in twos:
            copy.start()

    return (
        [copy for copy, x in zip(ones, plans) if x[3]],
        [copy for copy, x in zip(ones, plans) if not x[3]],
    )


def wait_all(copies):
    for copy in copies:
        copy.wait()


def put_half(refs, section, half, at, value):
    keep, send = refs
    rows = slice(at, at + value.shape[0])

    @pl.when(section == half)
    def _():
        keep[rows, :] = value

    @pl.when(section != half)
    def _():
        send[rows, :] = value


def pack_attention(refs, section, g_qkv, g_proj, shard, pieces, stride, first):
    model = g_proj.shape[0]
    q = model // pieces
    for p in range(pieces):
        off = pl.multiple_of((shard ^ p) * q, 16) if pieces > 1 else 0
        at = (stride * p + first) * q
        for c in range(3):
            value = g_qkv[pl.ds(off, q), c * model : (c + 1) * model]
            put_half(refs, section, c // 2, at + (c % 2) * q, value)
        put_half(refs, section, 1, at + q, g_proj[pl.ds(off, q), :])


def pack_mlp(refs, section, g_fc1, g_fc2, shard, pieces, stride, first):
    model = g_fc1.shape[0]
    q = model // pieces
    for p in range(pieces):
        off = pl.multiple_of((shard ^ p) * q, 16) if pieces > 1 else 0
        at = (stride * p + first) * q
        for c in range(4):
            value = g_fc1[pl.ds(off, q), c * model : (c + 1) * model]
            put_half(refs, section, 0, at + c * q, value)
        put_half(refs, section, 1, at, g_fc2[pl.ds(pl.multiple_of(off * 4, 16), 4 * q), :])


class Modulation:
    def __init__(self, line, model):
        self.line, self.model = line, model

    def __getitem__(self, key):
        b, rows, _ = key
        return self.line[:, pl.ds(pl.multiple_of((6 * b + rows.start) * self.model, 128), self.model)]


def bias_at(line, samples, model, start, size):
    return line[:, (6 * samples + start) * model : (6 * samples + start + size) * model]


def attention_forward(b, length, h, mod, bias, w_qkv, w_proj, b_qkv, b_proj, qkv, probs, att, branch, middle):
    model = w_proj.shape[0]
    heads = bias.shape[0]
    pair = 2 * model // heads
    rows = pl.ds(pl.multiple_of(b * length, length), length)
    masks = half_masks(pair)
    x = h[rows, :].astype(F32)
    normed, _ = norm_parts(x)
    normed_low = (normed * (1.0 + mod[b, 1:2, :]) + mod[b, 0:1, :]).astype(BF16)
    qkv[rows, :] = (dot(normed_low, w_qkv[...]) + b_qkv[...]).astype(BF16)
    for j in range(heads // 2):
        q_pair = qkv[rows, j * pair : (j + 1) * pair] * BF16((pair // 2) ** (-0.5))
        k_pair = qkv[rows, model + j * pair : model + (j + 1) * pair]
        v_pair = qkv[rows, 2 * model + j * pair : 2 * model + (j + 1) * pair]
        total = None
        for e in range(2):
            scores = dot_rows(q_pair * masks[e], k_pair) + bias[2 * j + e].astype(F32)
            raised = jnp.exp(scores - jnp.max(scores, axis=-1, keepdims=True))
            p = (raised * (1.0 / jnp.sum(raised, axis=-1, keepdims=True))).astype(BF16)
            probs[b, 2 * j + e] = p
            part = dot(p, v_pair * masks[e])
            total = part if total is None else total + part
        att[rows, j * pair : (j + 1) * pair] = total.astype(BF16)
    out = dot(att[rows, :], w_proj[...]) + b_proj[...]
    branch[rows, :] = out
    middle[rows, :] = x + mod[b, 2:3, :] * out


def mlp_forward(b, length, middle, mod, w_fc1, w_fc2, b_fc1, b_fc2, act, slope, out_branch, layer_out):
    model = w_fc1.shape[0]
    rows = pl.ds(pl.multiple_of(b * length, length), length)
    mid = middle[rows, :]
    normed, _ = norm_parts(mid)
    normed_low = (normed * (1.0 + mod[b, 4:5, :]) + mod[b, 3:4, :]).astype(BF16)
    total = b_fc2[...]
    for c in range(w_fc1.shape[1] // model):
        cols = slice(c * model, (c + 1) * model)
        v = dot(normed_low, w_fc1[:, cols]) + b_fc1[:, cols]
        square = v * v
        t = jnp.tanh(0.7978845608028654 * v * (1.0 + 0.044715 * square))
        half = 0.5 * (1.0 + t)
        a = (v * half).astype(BF16)
        act[rows, cols] = a
        slope[rows, cols] = (
            half
            + 0.5 * v * (1.0 - t * t) * (0.7978845608028654 + (3 * 0.044715 * 0.7978845608028654) * square)
        ).astype(BF16)
        total = total + dot(a, w_fc2[cols, :])
    out_branch[rows, :] = total
    layer_out[rows, :] = (mid + mod[b, 5:6, :] * total).astype(layer_out.dtype)


def mlp_backward(b, length, grad, middle, mod, w_fc1, w_fc2, act, slope, out_branch, d_middle, small, normed_low, d_pre, d_ob):
    model = w_fc1.shape[0]
    rows = pl.ds(pl.multiple_of(b * length, length), length)
    g = grad[rows, :].astype(F32)
    small[b, 2:3, :] = col_sum(g * out_branch[rows, :])
    d_out = g * mod[b, 5:6, :]
    d_out_low = d_out.astype(BF16)
    d_ob[rows, :] = d_out_low
    small[b, 3:4, :] = col_sum(d_out_low.astype(F32))
    normed, inverse = norm_parts(middle[rows, :])
    normed_low[rows, :] = (normed * (1.0 + mod[b, 4:5, :]) + mod[b, 3:4, :]).astype(BF16)
    d_normed = None
    for c in range(w_fc1.shape[1] // model):
        cols = slice(c * model, (c + 1) * model)
        d_act = dot_rows(d_out_low, w_fc2[cols, :])
        d_low = (d_act * slope[rows, cols].astype(F32)).astype(BF16)
        d_pre[rows, cols] = d_low
        small[b, 4 + c : 5 + c, :] = col_sum(d_low.astype(F32))
        part = dot_rows(d_low, w_fc1[:, cols])
        d_normed = part if d_normed is None else d_normed + part
    small[b, 0:1, :] = col_sum(d_normed)
    small[b, 1:2, :] = col_sum(d_normed * normed)
    d_middle[rows, :] = norm_back(d_normed, mod[b, 4:5, :], normed, inverse) + g


def mlp_weight_grads(normed_low, d_pre, act, d_ob, g_fc1, g_fc2):
    model = g_fc1.shape[0]
    for c in range(g_fc1.shape[1] // model):
        cols = slice(c * model, (c + 1) * model)
        g_fc1[:, cols] = dot_cols(normed_low[...], d_pre[:, cols]).astype(BF16)
        g_fc2[cols, :] = dot_cols(act[:, cols], d_ob[...]).astype(BF16)


def attention_backward(b, length, h, mod, w_qkv, w_proj, qkv, probs, att, branch, d_middle, d_in, small, score_sum, normed_low, d_qkv, d_br):
    model = w_proj.shape[0]
    heads = probs.shape[1]
    pair = 2 * model // heads
    scale = F32((pair // 2) ** (-0.5))
    rows = pl.ds(pl.multiple_of(b * length, length), length)
    masks = half_masks(pair)
    d_mid = d_middle[rows, :]
    small[b, 2:3, :] = col_sum(d_mid * branch[rows, :])
    d_branch = (d_mid * mod[b, 2:3, :]).astype(BF16)
    d_br[rows, :] = d_branch
    small[b, 5:6, :] = col_sum(d_branch.astype(F32))
    d_att = dot_rows(d_branch, w_proj[...]).astype(BF16)
    for j in range(heads // 2):
        q_pair = qkv[rows, j * pair : (j + 1) * pair]
        k_pair = qkv[rows, model + j * pair : model + (j + 1) * pair]
        v_pair = qkv[rows, 2 * model + j * pair : 2 * model + (j + 1) * pair]
        d_pair = d_att[:, j * pair : (j + 1) * pair]
        d_q = d_k = d_v = None
        for e in range(2):
            p_low = probs[b, 2 * j + e]
            p = p_low.astype(F32)
            d_here = d_pair * masks[e]
            d_p = dot_rows(d_here, v_pair)
            d_s = (p * (d_p - jnp.sum(d_p * p, axis=-1, keepdims=True))).astype(BF16)
            score_sum[2 * j + e] += d_s.astype(F32)
            v_part = dot_cols(p_low, d_here)
            q_part = dot(d_s, k_pair * masks[e])
            k_part = dot_cols(d_s, q_pair * masks[e])
            d_v = v_part if d_v is None else d_v + v_part
            d_q = q_part if d_q is None else d_q + q_part
            d_k = k_part if d_k is None else d_k + k_part
        d_qkv[rows, j * pair : (j + 1) * pair] = (d_q * scale).astype(BF16)
        d_qkv[rows, model + j * pair : model + (j + 1) * pair] = (d_k * scale).astype(BF16)
        d_qkv[rows, 2 * model + j * pair : 2 * model + (j + 1) * pair] = d_v.astype(BF16)
    small[b, 3:4, :] = col_sum(d_qkv[rows, :model].astype(F32))
    small[b, 4:5, :] = col_sum(d_qkv[rows, 2 * model :].astype(F32))
    small[b, 6:8, :] = jnp.zeros((2, model), F32)
    d_normed = dot_rows(d_qkv[rows, :], w_qkv[...])
    normed, inverse = norm_parts(h[rows, :].astype(F32))
    normed_low[rows, :] = (normed * (1.0 + mod[b, 1:2, :]) + mod[b, 0:1, :]).astype(BF16)
    small[b, 0:1, :] = col_sum(d_normed)
    small[b, 1:2, :] = col_sum(d_normed * normed)
    d_in[rows, :] = (norm_back(d_normed, mod[b, 1:2, :], normed, inverse) + d_mid).astype(d_in.dtype)


def attention_weight_grads(normed_low, d_qkv, att, d_br, g_qkv, g_proj):
    model = g_proj.shape[0]
    for c in range(3):
        cols = slice(c * model, (c + 1) * model)
        g_qkv[:, cols] = dot_cols(normed_low[...], d_qkv[:, cols]).astype(BF16)
    g_proj[...] = dot_cols(att[...], d_br[...]).astype(BF16)


def each_sample(count, body):
    def step(b, carry):
        body(b)
        return carry

    lax.fori_loop(0, count, step, 0)


def add_tables(all_scores, index, outs):
    heads, length = all_scores[0].shape[0], all_scores[0].shape[1]
    low_ids = lax.broadcasted_iota(jnp.int32, (LOW, length), 0)
    high_ids = lax.broadcasted_iota(jnp.int32, (HIGH, length), 0)
    count = len(all_scores) * heads

    def step(i, carry):
        rows = pl.ds(pl.multiple_of(i * 16, 16), 16)
        entries = index[rows, :]
        block = [scores[head, rows, :].astype(F32) for scores in all_scores for head in range(heads)]
        total = carry
        for r in range(16):
            entry = entries[r : r + 1, :]
            low = jnp.where(low_ids == (entry & (LOW - 1)), 1.0, 0.0).astype(BF16)
            high = high_ids == (entry >> LOW_BITS)
            left = jnp.concatenate([jnp.where(high, part[r : r + 1, :], 0.0) for part in block], axis=0).astype(BF16)
            total = total + dot_rows(left, low)
        return total

    total = lax.fori_loop(0, length // 16, step, jnp.zeros((count * HIGH, LOW), F32))
    parts = [total[i * HIGH : (i + 1) * HIGH] for i in range(count)]
    for layer, out in enumerate(outs):
        out[...] = jnp.concatenate(parts[layer * heads : (layer + 1) * heads], axis=1)


def small_kernel(pos, scores0, scores1, index, small_a0, small_m0, small_a1, small_m1, *rest):
    keep, send, table0, table1 = rest[-4:]
    size = small_a0.shape[0] * small_a0.shape[1]
    add_tables((scores0, scores1), index, (table0, table1))
    parts = (
        (small_a0[...], small_m0[...], table0[...]),
        (small_a1[...], small_m1[...], table1[...]),
    )
    rows = [
        jnp.concatenate([x[0].reshape(size, -1), x[1].reshape(size, -1), x[2]], axis=0) for x in parts
    ]

    @pl.when(pos[0] == 0)
    def _():
        keep[...] = rows[0]
        send[...] = rows[1].astype(BF16)

    @pl.when(pos[0] == 1)
    def _():
        keep[...] = rows[1]
        send[...] = rows[0].astype(BF16)


def small_step(pos, scores0, scores1, index, smalls, earlier):
    samples, _, model = smalls[0].shape
    shape = (16 * samples + HIGH, model)
    return call(
        small_kernel, pos, (scores0, scores1, index, *smalls), earlier, [(shape, F32), (shape, BF16)],
        [((HIGH, model), F32)] * 2, work=12,
    )


def set_line(line, layer, section, own_line, other_line):
    line[...] = jnp.where(section == layer, own_line[...], other_line[...])


def start_bias(layer, section, own, other, bias, sem):
    one = pltpu.make_async_copy(own, bias, sem)
    two = pltpu.make_async_copy(other, bias, sem)
    pl.when(section == layer)(one.start)
    pl.when(section != layer)(two.start)
    return one


def line_biases(line, samples, model):
    q_bias = bias_at(line, samples, model, 0, 1)
    v_bias = bias_at(line, samples, model, 1, 1)
    b_qkv = jnp.concatenate([q_bias, jnp.zeros_like(q_bias), v_bias], axis=1)
    return b_qkv, bias_at(line, samples, model, 2, 1), bias_at(line, samples, model, 3, 4), bias_at(line, samples, model, 7, 1)


def forward_kernel(layer, length, n_weights, n_after, pos, h, own_line, other_line, own_bias, other_bias, *rest):
    refs, rest = rest[:n_weights], rest[n_weights + n_after :]
    (qkv, probs, att, branch, middle, act, slope, out_branch, layer_out,
     w_qkv, w_proj, w_fc1, w_fc2, bias, line, sems) = rest
    section, shard = pos[0], pos[1]
    model = h.shape[1]
    samples = h.shape[0] // length
    got_bias = start_bias(layer, section, own_bias, other_bias, bias, sems.at[weight_count(n_weights)])
    for_attention, for_mlp = weight_loads(layer, section, shard, refs, (w_qkv, w_proj, w_fc1, w_fc2), sems)
    set_line(line, layer, section, own_line, other_line)
    mod = Modulation(line, model)
    b_qkv, b_proj, b_fc1, b_fc2 = line_biases(line, samples, model)
    got_bias.wait()
    wait_all(for_attention)
    each_sample(
        samples,
        lambda b: attention_forward(b, length, h, mod, bias, w_qkv, w_proj, b_qkv, b_proj, qkv, probs, att, branch, middle),
    )
    wait_all(for_mlp)
    each_sample(
        samples,
        lambda b: mlp_forward(b, length, middle, mod, w_fc1, w_fc2, b_fc1, b_fc2, act, slope, out_branch, layer_out),
    )


def both_kernel(layer, pieces, length, n_weights, n_after, pos, h, grad, own_line, other_line, own_bias, other_bias, *rest):
    refs, rest = rest[:n_weights], rest[n_weights + n_after :]
    (layer_out, d_in, small_a, small_m, scores, keep, send,
     w_qkv, w_proj, w_fc1, w_fc2, bias, line, qkv, probs, att, branch, middle, act, slope, out_branch,
     d_middle, normed_low, d_pre, d_ob, d_qkv, score_sum, g_qkv, g_proj, g_fc1, g_fc2, sems) = rest
    section, shard = pos[0], pos[1]
    model = h.shape[1]
    samples = h.shape[0] // length
    got_bias = start_bias(layer, section, own_bias, other_bias, bias, sems.at[weight_count(n_weights)])
    for_attention, for_mlp = weight_loads(layer, section, shard, refs, (w_qkv, w_proj, w_fc1, w_fc2), sems)
    set_line(line, layer, section, own_line, other_line)
    mod = Modulation(line, model)
    b_qkv, b_proj, b_fc1, b_fc2 = line_biases(line, samples, model)
    got_bias.wait()
    wait_all(for_attention)
    each_sample(
        samples,
        lambda b: attention_forward(b, length, h, mod, bias, w_qkv, w_proj, b_qkv, b_proj, qkv, probs, att, branch, middle),
    )
    wait_all(for_mlp)

    def mlp(b):
        mlp_forward(b, length, middle, mod, w_fc1, w_fc2, b_fc1, b_fc2, act, slope, out_branch, layer_out)
        mlp_backward(b, length, grad, middle, mod, w_fc1, w_fc2, act, slope, out_branch, d_middle, small_m, normed_low, d_pre, d_ob)

    each_sample(samples, mlp)
    mlp_weight_grads(normed_low, d_pre, act, d_ob, g_fc1, g_fc2)
    pack_mlp((keep, send), section, g_fc1, g_fc2, shard, pieces, 6, 2)
    score_sum[...] = jnp.zeros_like(score_sum)
    each_sample(
        samples,
        lambda b: attention_backward(b, length, h, mod, w_qkv, w_proj, qkv, probs, att, branch, d_middle, d_in, small_a, score_sum, normed_low, d_qkv, d_ob),
    )
    scores[...] = score_sum[...].astype(BF16)
    attention_weight_grads(normed_low, d_qkv, att, d_ob, g_qkv, g_proj)
    pack_attention((keep, send), section, g_qkv, g_proj, shard, pieces, 6, 0)
    rows = slice(keep.shape[0], keep.shape[0] + h.shape[0])

    @pl.when(section == 0)
    def _():
        send[rows, :] = layer_out[...]

    @pl.when(section == 1)
    def _():
        send[rows, :] = h[...]


def backward_mlp_kernel(layer, pieces, length, n_weights, n_after, pos, grad, middle, own_line, other_line, act, slope, out_branch, *rest):
    refs, rest = rest[:n_weights], rest[n_weights + n_after :]
    (d_middle, small, keep, send,
     w_qkv, w_proj, w_fc1, w_fc2, line, normed_low, d_pre, d_ob, g_fc1, g_fc2, sems) = rest
    section, shard = pos[0], pos[1]
    for_attention, for_mlp = weight_loads(layer, section, shard, refs, (w_qkv, w_proj, w_fc1, w_fc2), sems)
    set_line(line, layer, section, own_line, other_line)
    mod = Modulation(line, middle.shape[1])
    wait_all(for_mlp)
    each_sample(
        middle.shape[0] // length,
        lambda b: mlp_backward(b, length, grad, middle, mod, w_fc1, w_fc2, act, slope, out_branch, d_middle, small, normed_low, d_pre, d_ob),
    )
    mlp_weight_grads(normed_low, d_pre, act, d_ob, g_fc1, g_fc2)
    pack_mlp((keep, send), section, g_fc1, g_fc2, shard, pieces, 4, 0)
    wait_all(for_attention)


def backward_attention_kernel(layer, pieces, length, n_weights, n_after, pos, h, own_line, other_line, qkv, probs, att, branch, d_middle, d_h1, *rest):
    refs, rest = rest[:n_weights], rest[n_weights + n_after :]
    (d_in, small, scores, keep, send,
     w_qkv, w_proj, w_fc1, w_fc2, line, normed_low, d_qkv, d_br, score_sum, g_qkv, g_proj, sems) = rest
    section, shard = pos[0], pos[1]
    for_attention, for_mlp = weight_loads(layer, section, shard, refs, (w_qkv, w_proj, w_fc1, w_fc2), sems)
    set_line(line, layer, section, own_line, other_line)
    mod = Modulation(line, h.shape[1])
    score_sum[...] = jnp.zeros_like(score_sum)
    wait_all(for_attention)
    each_sample(
        h.shape[0] // length,
        lambda b: attention_backward(b, length, h, mod, w_qkv, w_proj, qkv, probs, att, branch, d_middle, d_in, small, score_sum, normed_low, d_qkv, d_br),
    )
    scores[...] = score_sum[...].astype(BF16)
    attention_weight_grads(normed_low, d_qkv, att, d_br, g_qkv, g_proj)
    pack_attention((keep, send), section, g_qkv, g_proj, shard, pieces, 2, 0)
    rows = slice(keep.shape[0], keep.shape[0] + h.shape[0])

    @pl.when(section == 0)
    def _():
        send[rows, :] = d_h1[...]

    @pl.when(section == 1)
    def _():
        send[rows, :] = d_in[...].astype(BF16)

    wait_all(for_mlp)


def cost(gigaflop):
    return pl.CostEstimate(flops=int(gigaflop * 1e9), bytes_accessed=0, transcendentals=0)


def call(kernel, pos, operands, in_hbm, outs, scratch, sems=0, work=2):
    specs = [pl.BlockSpec(memory_space=pltpu.SMEM)]
    specs += [pl.BlockSpec(memory_space=pltpu.VMEM) for _ in operands]
    specs += [pl.BlockSpec(memory_space=pl.ANY) for _ in in_hbm]
    shapes = [pltpu.VMEM(shape, dtype) for shape, dtype in scratch]
    if sems:
        shapes.append(pltpu.SemaphoreType.DMA((sems,)))
    return pl.pallas_call(
        kernel,
        out_shape=[jax.ShapeDtypeStruct(shape, dtype) for shape, dtype in outs],
        in_specs=specs,
        out_specs=[pl.BlockSpec(memory_space=pltpu.VMEM) for _ in outs],
        scratch_shapes=shapes,
        cost_estimate=cost(work),
        compiler_params=pltpu.CompilerParams(vmem_limit_bytes=VMEM_BYTES),
    )(pos, *operands, *in_hbm)


class Sizes:
    def __init__(self, samples, length, model, heads, hidden, pieces):
        self.samples, self.length, self.model = samples, length, model
        self.heads, self.hidden, self.pieces = heads, hidden, pieces
        self.rows = samples * length
        self.line = ((1, (6 * samples + 4 + hidden // model) * model), F32)
        self.weights = [
            ((model, 3 * model), BF16), ((model, model), BF16), ((model, hidden), BF16), ((hidden, model), BF16),
        ]
        self.bias = ((heads, length, length), BF16)
        self.probs = ((samples, heads, length, length), BF16)
        self.low = ((self.rows, model), BF16)
        self.full = ((self.rows, model), F32)
        self.qkv = ((self.rows, 3 * model), BF16)
        self.wide = ((self.rows, hidden), BF16)
        self.small = ((samples, 8, model), F32)

    def pack(self, blocks, more=0):
        return [((blocks * self.model, self.model), BF16), ((blocks * self.model + more, self.model), BF16)]


def forward_layer(layer, z, pos, h, lines, biases, weights, earlier):
    return call(
        functools.partial(forward_kernel, layer, z.length, len(weights), len(earlier)),
        pos, (h, *lines), (*biases, *weights, *earlier),
        [z.qkv, z.probs, z.low, z.full, z.full, z.wide, z.wide, z.full, z.low],
        [*z.weights, z.bias, z.line], weight_count(len(weights)) + 1, work=15,
    )


def both_ways(layer, z, pos, h, grad, lines, biases, weights, earlier):
    return call(
        functools.partial(both_kernel, layer, z.pieces, z.length, len(weights), len(earlier)),
        pos, (h, grad, *lines), (*biases, *weights, *earlier),
        [z.low, z.low, z.small, z.small, z.bias, *z.pack(6, z.rows)],
        [*z.weights, z.bias, z.line, z.qkv, z.probs, z.low, z.full, z.full, z.wide, z.wide, z.full,
         z.full, z.low, z.wide, z.low, z.qkv, (z.bias[0], F32), *z.weights],
        weight_count(len(weights)) + 1, work=25,
    )


def backward_mlp(layer, z, pos, grad, middle, lines, act, slope, out_branch, weights, earlier):
    return call(
        functools.partial(backward_mlp_kernel, layer, z.pieces, z.length, len(weights), len(earlier)),
        pos, (grad, middle, *lines, act, slope, out_branch), (*weights, *earlier),
        [z.full, z.small, *z.pack(4)],
        [*z.weights, z.line, z.low, z.wide, z.low, *z.weights[2:]],
        weight_count(len(weights)), work=12,
    )


def backward_attention(layer, z, pos, h, lines, qkv, probs, att, branch, d_middle, d_h1, weights, earlier):
    return call(
        functools.partial(backward_attention_kernel, layer, z.pieces, z.length, len(weights), len(earlier)),
        pos, (h, *lines, qkv, probs, att, branch, d_middle, d_h1), (*weights, *earlier),
        [z.full, z.small, z.bias, *z.pack(2, z.rows)],
        [*z.weights, z.line, z.low, z.qkv, z.low, (z.bias[0], F32), *z.weights[:2]],
        weight_count(len(weights)), work=13,
    )


def partial_kernel(pos, w_ada, cond_a, cond_b, cond_c, cond_d, b_ada, b_qv, b_proj, b_fc1, b_fc2, *rest):
    copied, outs, whole = rest[-6], rest[-5:-1], rest[-1]
    copied[...] = w_ada[...]
    shard = pos[1]
    q, wide = w_ada.shape
    samples, model = cond_a.shape
    whole[...] = jnp.zeros_like(whole)
    whole[pl.ds(pl.multiple_of(shard * q, 16), q), :] = w_ada[...]
    for cond, out in zip((cond_a, cond_b, cond_c, cond_d), outs):
        c = cond[...].astype(F32)
        act = (c * (1.0 / (1.0 + jnp.exp(-c)))).astype(BF16)
        out[:, :wide] = dot(act, whole[...])
        out[:, wide:] = jnp.zeros((samples, 2 * model), F32)
        for f in range(4):
            @pl.when(shard == f)
            def _():
                here = slice(f * b_ada.shape[1], (f + 1) * b_ada.shape[1])
                out[:, here] += b_ada[...].astype(F32)
                for bias, row, at in ((b_qv, 0, 0), (b_proj, 1, 0), (b_fc1, 1, model), (b_fc2, 3, model)):
                    width = bias.shape[1]
                    at += f * width
                    row, at = row + at // (2 * model), wide + at % (2 * model)
                    out[row : row + 1, at : at + width] = bias[...].astype(F32)


def partial_step(pos, w_ada, conds, biases, earlier):
    q, wide = w_ada.shape
    samples, model = conds[0].shape
    return call(
        partial_kernel, pos, (w_ada, *conds, *biases), earlier, [(w_ada.shape, BF16)] + [((samples, wide + 2 * model), F32)] * 4,
        [((4 * q, wide), BF16)],
    )


def line_kernel(pos, own, got_a, got_b, got_c, *rest):
    keep, send, total = rest[-3:]
    section = pos[0]
    samples = own.shape[0]
    each = samples // 2
    model = own.shape[1] // 8
    total[...] = (own[...] + got_a[...]) + (got_b[...] + got_c[...])
    for out, side in ((keep, section), (send, 1 - section)):
        for b in range(each):
            out[:, b * 6 * model : (b + 1) * 6 * model] = total[pl.ds(side * each + b, 1), : 6 * model]
        for row in range(samples):
            at = (6 * each + 2 * row) * model
            out[:, at : at + 2 * model] = total[row : row + 1, 6 * model :]


def line_step(pos, own, got, earlier):
    samples, model = own.shape[0], own.shape[1] // 8
    shape = (1, (3 * samples + 8) * model)
    return call(line_kernel, pos, (own, *got), earlier, [(shape, F32)] * 2, [(own.shape, F32)])


def first_kernel(keep1, other1, keep_m, other_m, own, *messages):
    pieces = 4
    size1, size_m = keep1.shape[0] // pieces, keep_m.shape[0] // pieces
    n1, nm = size1 // 4, size_m // 4
    for p in range(pieces):
        for k in range(4):
            at = k * (n1 + nm)
            for keep, other, first, n, to in (
                (keep1, other1, p * size1 + k * n1, n1, at), (keep_m, other_m, p * size_m + k * nm, nm, at + n1)
            ):
                total = keep[first : first + n, :].astype(F32) + other[first : first + n, :].astype(F32)
                if p == 0:
                    own[to : to + n, :] = total
                else:
                    messages[p - 1][to : to + n, :] = total.astype(BF16)


def first_step(keep1, other1, keep_m, other_m):
    shape = ((keep1.shape[0] + keep_m.shape[0]) // 4, keep1.shape[1])
    return pl.pallas_call(
        first_kernel,
        out_shape=[jax.ShapeDtypeStruct(shape, F32)] + [jax.ShapeDtypeStruct(shape, BF16)] * 3,
        compiler_params=pltpu.CompilerParams(vmem_limit_bytes=VMEM_BYTES),
    )(keep1, other1, keep_m, other_m)


def plane_kernel(samples, pos, keep, other, kept_small, other_small, cond, own, own_small, *rest):
    messages, work = rest[:3], rest[3]
    section = pos[0]
    size, model = own.shape
    for p in range(4):
        rows = slice(p * size, (p + 1) * size)
        total = keep[rows, :].astype(F32) + other[rows, :].astype(F32)
        if p == 0:
            own[...] = total
        else:
            messages[p - 1][:size, :] = total.astype(BF16)
    theirs = other_small[...].astype(F32)
    mine = kept_small[...]
    each = samples // 2
    work[...] = jnp.zeros_like(work)
    for b in range(each):
        for kind in range(6):
            row = b * 8 + kind if kind < 3 else (each + b) * 8 + kind - 3
            work[pl.ds(kind * samples + section * each + b, 1), :] = mine[row : row + 1, :]
            work[pl.ds(kind * samples + (1 - section) * each + b, 1), :] = theirs[row : row + 1, :]
    work[6 * samples : 7 * samples, :] = cond[...].astype(F32)
    both = mine + theirs
    bias_rows = sum(both[(each + b) * 8 + 3 : (each + b) * 8 + 8, :] for b in range(each))
    more_rows = sum(both[b * 8 + 3 : b * 8 + 6, :] for b in range(each))
    at = 7 * samples
    work[at : at + 5, :] = bias_rows
    work[at + 5 : at + 8, :] = more_rows
    work[at + 8 : at + 8 + HIGH, :] = both[2 * each * 8 :, :]
    small = work[...].astype(BF16)
    own_small[...] = small
    for message in messages:
        message[size:, :] = small


def plane_step(pos, keep, other, kept_small, other_small, cond):
    samples, model = cond.shape
    size = keep.shape[0] // 4
    small = -(-(7 * samples + 8 + HIGH) // 16) * 16
    outs = [((size, model), F32), ((small, model), BF16)] + [((size + small, model), BF16)] * 3
    return call(
        functools.partial(plane_kernel, samples), pos, (keep, other, kept_small, other_small, cond), (), outs,
        [((small, model), F32)],
    )


def column_kernel(samples, pos, own, own_small, got_a, got_b, got_c, part, own_out, *rest):
    messages, work = rest[:3], rest[3]
    rank = pos[2]
    size, model = own.shape
    n = size // 4
    got = (got_a, got_b, got_c)
    for j in range(4):
        at = pl.multiple_of((rank ^ j) * n, 16)
        total = own[pl.ds(at, n), :]
        for piece in got:
            total = total + piece[pl.ds(at, n), :].astype(F32)
        if j == 0:
            part[...] = total
        else:
            messages[j - 1][:n, :] = total.astype(BF16)
    smalls = [own_small[...].astype(F32)] + [piece[size:, :].astype(F32) for piece in got]
    work[...] = jnp.zeros_like(work)
    for p in range(4):
        for kind in range(7):
            at = (kind * 4 + p) * samples
            work[at : at + samples, :] = smalls[p][kind * samples : (kind + 1) * samples, :]
    at = 7 * samples
    summed = (smalls[0] + smalls[1]) + (smalls[2] + smalls[3])
    work[4 * at : 4 * at + 8 + HIGH, :] = summed[at : at + 8 + HIGH, :]
    small = work[...].astype(BF16)
    own_out[...] = small
    for message in messages:
        message[n:, :] = small


def column_step(pos, own, own_small, got, samples):
    size, model = own.shape
    small = -(-(28 * samples + 8 + HIGH) // 16) * 16
    outs = [((size // 4, model), F32), ((small, model), BF16)] + [((size // 4 + small, model), BF16)] * 3
    return call(
        functools.partial(column_kernel, samples), pos, (own, own_small, *got), (), outs, [((small, model), F32)]
    )


def finish_kernel(samples, width, pos, own_small, got_a, got_b, got_c,
                  g_ada, g_b_ada, g_b_qv, g_b_proj, g_b_fc1, g_b_fc2, g_table, work, whole, row):
    shard, rank = pos[1], pos[2]
    model = own_small.shape[1]
    each = 4 * samples
    n = got_a.shape[0] - own_small.shape[0]
    pieces = [own_small[...]] + [piece[n:, :] for piece in (got_a, got_b, got_c)]
    for j in range(4):
        for kind in range(7):
            at = pl.multiple_of(kind * 4 * each + (rank ^ j) * each, 16)
            work[pl.ds(at, each), :] = pieces[j][kind * each : (kind + 1) * each, :].astype(F32)
    cond = work[24 * each :, :]
    act = (cond * (1.0 / (1.0 + jnp.exp(-cond)))).astype(BF16)
    for kind in range(6):
        rows = work[kind * 4 * each : (kind + 1) * 4 * each, :]
        whole[...] = dot_cols(act, rows.astype(BF16))
        cols = slice(kind * model, (kind + 1) * model)
        g_ada[:, cols] = whole[pl.ds(pl.multiple_of(shard * width, 16), width), :]
        row[:, cols] = col_sum(rows)
    at = 7 * each
    rows = [piece[at : at + 8 + HIGH, :].astype(F32) for piece in pieces]
    summed = (rows[0] + rows[1]) + (rows[2] + rows[3])
    for c in range(4):
        row[:, (6 + c) * model : (7 + c) * model] = summed[1 + c : 2 + c, :]
    row[:, 10 * model : 11 * model] = summed[5:6, :]
    row[:, 11 * model : 12 * model] = summed[6:7, :]
    row[:, 12 * model : 13 * model] = summed[7:8, :]
    row[:, 13 * model : 14 * model] = summed[0:1, :]
    for f in range(4):
        @pl.when(shard == f)
        def _():
            for out, start in ((g_b_ada, 0), (g_b_fc1, 6), (g_b_qv, 10), (g_b_proj, 12), (g_b_fc2, 13)):
                size = out.shape[1]
                out[...] = row[:, start * model + f * size : start * model + (f + 1) * size]
    heads, entries = g_table.shape
    for high in range(-(-entries // LOW)):
        size = min(LOW, entries - high * LOW)
        for head in range(heads):
            g_table[head : head + 1, high * LOW : high * LOW + size] = summed[
                8 + high : 9 + high, head * LOW : head * LOW + size
            ]


def finish_step(pos, own_small, got, samples, width, heads, entries):
    model = own_small.shape[1]
    sizes = [6 * width, 2 * width, width, 4 * width, width]
    return call(
        functools.partial(finish_kernel, samples, width), pos, (own_small, *got), (),
        [((width, 6 * model), F32)] + [((1, size), F32) for size in sizes] + [((heads, entries), F32)],
        [((7 * 16 * samples, model), F32), ((model, model), F32), ((1, 14 * model), F32)],
    )


def cond_kernel(samples, pos, small, cond, *rest):
    out, w_ada = rest[-2:]
    model = cond.shape[1]
    for p, piece in enumerate(rest[:-2]):
        q = piece.shape[0]
        off = pl.multiple_of((pos[1] ^ p) * q, 16) if q < model else 0
        w_ada[pl.ds(off, q), :] = piece[...]
    total = None
    for kind in range(6):
        rows = small[...].astype(F32)[kind * samples : (kind + 1) * samples, :].astype(BF16)
        part = dot_rows(rows, w_ada[:, kind * model : (kind + 1) * model])
        total = part if total is None else total + part
    c = cond[...].astype(F32)
    gate = 1.0 / (1.0 + jnp.exp(-c))
    out[...] = total * (gate * (1.0 + c * (1.0 - gate)))


def cond_step(pos, small, w_ada, cond):
    model = cond.shape[1]
    return call(
        functools.partial(cond_kernel, cond.shape[0]), pos, (small, cond, *w_ada), (), [(cond.shape, F32)],
        [((model, w_ada[0].shape[1]), BF16)],
    )[0]


def final_kernel(pos, own_a, own_m, other, g_qkv, g_proj, g_fc1, g_fc2):
    section = pos[0]
    q, model = g_proj.shape
    cut = own_a.shape[0]

    def write(first_a, first_m, second_a, second_m):
        for c in range(2):
            g_qkv[:, c * model : (c + 1) * model] = first_a[c * q : (c + 1) * q, :].astype(F32)
        g_qkv[:, 2 * model : 3 * model] = second_a[:q, :].astype(F32)
        g_proj[...] = second_a[q : 2 * q, :].astype(F32)
        for c in range(4):
            g_fc1[:, c * model : (c + 1) * model] = first_m[c * q : (c + 1) * q, :].astype(F32)
        g_fc2[...] = second_m[...].astype(F32)

    other_a, other_m = other.at[:cut, :], other.at[cut:, :]

    @pl.when(section == 0)
    def _():
        write(own_a, own_m, other_a, other_m)

    @pl.when(section == 1)
    def _():
        write(other_a, other_m, own_a, own_m)


def final_step(pos, own_a, own_m, other):
    q, model = own_a.shape[0] // 2, own_a.shape[1]
    return call(
        final_kernel, pos, (own_a, own_m, other), (),
        [((q, 3 * model), F32), ((q, model), F32), ((q, 4 * model), F32), ((4 * q, model), F32)], [],
    )


def halve_kernel(pos, own, got_a, got_b, got_c, keep, send):
    bit = pos[2] & 1
    n = own.shape[0] // 4
    for high in range(2):
        for out, low in ((keep, bit), (send, 1 - bit)):
            rows = pl.ds(pl.multiple_of((2 * high + low) * n, 16), n)
            total = own[rows, :]
            for piece in (got_a, got_b, got_c):
                total = total + piece[rows, :].astype(F32)
            out[high * n : (high + 1) * n, :] = total.astype(out.dtype)


def halve_step(pos, own, got):
    shape = (own.shape[0] // 2, own.shape[1])
    return call(halve_kernel, pos, (own, *got), (), [(shape, F32), (shape, BF16)], [])


def quarter_kernel(pos, kept, got, keep, send):
    bit = pos[2] >> 1
    n = kept.shape[0] // 2
    for out, high in ((keep, bit), (send, 1 - bit)):
        rows = pl.ds(pl.multiple_of(high * n, 16), n)
        out[...] = (kept[rows, :] + got[rows, :].astype(F32)).astype(out.dtype)


def quarter_step(pos, kept, got):
    shape = (kept.shape[0] // 2, kept.shape[1])
    return call(quarter_kernel, pos, (kept, got), (), [(shape, F32), (shape, BF16)], [])


def pack_kernel(qkv, proj, fc1, fc2, out):
    q, model = proj.shape
    for c in range(3):
        out[c * q : (c + 1) * q, :] = qkv[:, c * model : (c + 1) * model]
    out[3 * q : 4 * q, :] = proj[...]
    for c in range(4):
        out[(4 + c) * q : (5 + c) * q, :] = fc1[:, c * model : (c + 1) * model]
    out[8 * q : 12 * q, :] = fc2[...]


def pack_shard(own):
    q, model = own[1].shape
    return pl.pallas_call(
        pack_kernel,
        out_shape=jax.ShapeDtypeStruct((12 * q, model), BF16),
        compiler_params=pltpu.CompilerParams(vmem_limit_bytes=VMEM_BYTES),
    )(*own)


def after(values, others):
    return pl.pallas_call(
        lambda *refs: None,
        out_shape=[jax.ShapeDtypeStruct(v.shape, v.dtype) for v in values],
        in_specs=[pl.BlockSpec(memory_space=pl.ANY)] * (len(values) + len(others)),
        out_specs=[pl.BlockSpec(memory_space=pl.ANY)] * len(values),
        input_output_aliases={i: i for i in range(len(values))},
    )(*values, *others)


def lookup_kernel(table, index, *rest):
    out, work = rest[-2:]
    heads, length = out.shape[0], out.shape[1]
    high_count = table.shape[0] // 8
    values = table[...]
    low_id = lax.broadcasted_iota(jnp.int32, (LOW, length), 0)

    def step(i, carry):
        block = index[pl.ds(pl.multiple_of(i * 8, 8), 8), :]
        for r in range(8):
            entry = block[r : r + 1, :]
            picks = jnp.where(low_id == (entry & (LOW - 1)), 1.0, 0.0).astype(BF16)
            found = dot(values, picks).reshape(high_count, 8, length)
            high = jnp.broadcast_to(entry >> LOW_BITS, (8, length))
            bit = high_count // 2
            while bit:
                chosen = (high & bit) != 0
                found = jnp.where(chosen[None], found[bit : 2 * bit], found[:bit])
                bit //= 2
            for head in range(heads):
                work[head, pl.ds(i * 8 + r, 1), :] = found[0, head : head + 1, :]
        return carry

    lax.fori_loop(0, length // 8, step, 0)
    out[...] = work[...].astype(BF16)


def lookup(table, index, earlier):
    heads, entries = table.shape
    high_count = HIGH
    padded = jnp.pad(table, ((0, 8 - heads), (0, high_count * LOW - entries)))
    rows = jnp.transpose(padded.reshape(8, high_count, LOW), (1, 0, 2)).reshape(high_count * 8, LOW)
    length = index.shape[0]
    return pl.pallas_call(
        lookup_kernel,
        out_shape=jax.ShapeDtypeStruct((heads, length, length), BF16),
        in_specs=[pl.BlockSpec(memory_space=pltpu.VMEM)] * 2 + [pl.BlockSpec(memory_space=pl.ANY)] * len(earlier),
        out_specs=pl.BlockSpec(memory_space=pltpu.VMEM),
        scratch_shapes=[pltpu.VMEM((heads, length, length), F32)],
        cost_estimate=cost(11),
        compiler_params=pltpu.CompilerParams(vmem_limit_bytes=VMEM_BYTES),
    )(rows, index, *earlier)


def swap_section(value):
    return lax.ppermute(value, "section", [(0, 1), (1, 0)])


def pairs_of(count, step):
    return [(i, i ^ step) for i in range(count)]


def by_rank(pieces, rank):
    stack = jnp.stack(pieces)
    count = len(pieces)
    bit = 1
    while bit < count:
        moved = jnp.stack([stack[i ^ bit] for i in range(count)])
        stack = jnp.where((rank & bit) != 0, moved, stack)
        bit *= 2
    return stack


def section_sums(keep, other, shards):
    size = keep.shape[0] // shards
    return [
        keep[p * size : (p + 1) * size].astype(F32) + other[p * size : (p + 1) * size].astype(F32)
        for p in range(shards)
    ]


def low_pieces(sums):
    return [x.astype(BF16) for x in sums[1:]]


def to_peers(messages, axis):
    count = lax.axis_size(axis)
    return [lax.ppermute(messages[p - 1], axis, pairs_of(count, p)) for p in range(1, count)]


def add_pieces(own, got):
    total = own
    for piece in got:
        total = total + piece.astype(F32)
    return total


def replica_parts(total, rank):
    replicas = lax.axis_size("rep")
    parts = total if total.ndim == 3 else total.reshape(replicas, total.shape[0] // replicas, -1)
    low = parts.astype(BF16)
    mine = lax.dynamic_index_in_dim(parts, rank, 0, keepdims=False)
    return mine, [lax.dynamic_index_in_dim(low, rank ^ j, 0, keepdims=False) for j in range(1, replicas)]


def unpack_attention(pack):
    q = pack.shape[0] // 4
    return jnp.concatenate([pack[c * q : (c + 1) * q] for c in range(3)], axis=1), pack[3 * q :]


def unpack_mlp(pack):
    q = pack.shape[0] // 8
    return jnp.concatenate([pack[c * q : (c + 1) * q] for c in range(4)], axis=1), pack[4 * q :]


def pad_rows(value):
    return jnp.pad(value, ((0, -value.shape[0] % 16), (0, 0)))


def from_peers(value, axis):
    return [lax.ppermute(value, axis, pairs_of(lax.axis_size(axis), p)) for p in range(1, lax.axis_size(axis))]


def pair_sum(values):
    while len(values) > 1:
        values = [values[i] + values[i + 1] for i in range(0, len(values), 2)]
    return values[0]


def per_device(inputs, conditioning, cotangent, micro_sizes, relative_bias_index,
               w_ada, w_qkv, w_proj, w_fc1, w_fc2, b_ada, b_qv, b_proj, b_fc1, b_fc2, bias_table):
    section = lax.axis_index("section")
    shard = lax.axis_index("fsdp")
    rank = lax.axis_index("rep")
    shards, replicas = lax.axis_size("fsdp"), lax.axis_size("rep")
    direct = shards == 4 and replicas == 4
    is_first = section == 0
    samples, length, model = inputs.shape
    heads, entries = bias_table.shape[1:]
    half = samples // 2
    z = Sizes(half, length, model, heads, 4 * model, shards if direct else 1)
    pos = jnp.stack([section, shard, rank]).astype(jnp.int32)

    def mine(first, second):
        return jnp.where(is_first, first, second)

    def own_samples(array):
        return lax.dynamic_slice_in_dim(array, section * half, half, 0)

    def in_order(own, other):
        return jnp.where(is_first, jnp.concatenate([own, other]), jnp.concatenate([other, own]))

    live = (jnp.arange(half)[:, None, None] < lax.dynamic_index_in_dim(micro_sizes[0], section, 0)).astype(BF16)
    h0 = own_samples(inputs).reshape(half * length, model)
    grad1 = (own_samples(cotangent) * live).reshape(half * length, model)
    index = relative_bias_index
    own_raw = [w_qkv[0], w_proj[0], w_fc1[0], w_fc2[0]]
    width = model // shards
    if direct:
        conds = [conditioning] + from_peers(conditioning, "fsdp")
        own_pack = pack_shard(own_raw)
        middle_row = own_pack.shape[0] // 2
        got_x = lax.ppermute(own_pack, "fsdp", pairs_of(shards, 1))
        got_y = lax.ppermute(own_pack, "fsdp", pairs_of(shards, 2))
        bias_own = lookup(bias_table[0], index, [own_pack, *conds[1:]])
        w_ada_copy, *partial = partial_step(pos, w_ada[0], conds, (b_ada, b_qv, b_proj, b_fc1, b_fc2), [bias_own])
        got_first = lax.ppermute(got_x[:middle_row], "fsdp", pairs_of(shards, 2))
        got_second = lax.ppermute(got_y[middle_row:], "fsdp", pairs_of(shards, 1))
        own_weights = [own_pack, got_x, got_y, got_first, got_second]
        weights = own_weights + [swap_section(w) for w in own_weights]
        own_line, send_line = line_step(pos, partial[0], after(to_peers(partial[1:], "fsdp"), [got_x, got_y]), [h0, grad1])
    else:
        row = jnp.concatenate([b_ada, b_qv, b_proj, b_fc1, b_fc2], axis=1)
        bias_rows = lax.all_gather(row[0], "fsdp", axis=0)
        whole = [lax.all_gather(w, "fsdp", axis=0, tiled=True) for w in own_raw]
        own_whole = pack_shard(whole)
        weights = [own_whole, swap_section(own_whole)]
        acts = jax.nn.silu(conditioning.astype(F32)).astype(BF16)
        modulation = dot(acts, lax.all_gather(w_ada[0], "fsdp", axis=0, tiled=True))
        bias_own = lookup(bias_table[0], index, [])
        cuts = [b_ada.shape[1], b_qv.shape[1], b_proj.shape[1], b_fc1.shape[1], b_fc2.shape[1]]
        biases, at = [], 0
        for cut in cuts:
            biases.append(bias_rows[:, at : at + cut].reshape(1, -1).astype(F32))
            at += cut
        modulation = modulation + biases[0]
        other_samples = lax.dynamic_slice_in_dim(modulation, (1 - section) * half, half, 0)
        own_line = jnp.concatenate([own_samples(modulation).reshape(1, -1)] + biases[1:], axis=1)
        send_line = jnp.concatenate([other_samples.reshape(1, -1)] + biases[1:], axis=1)
    lines = (own_line, swap_section(send_line))
    bias_heads = (bias_own, swap_section(bias_own))

    if direct:
        w_ada_later = after([w_ada_copy], weights[3:5])[0]
        w_ada_pieces = [w_ada_later] + from_peers(w_ada_later, "fsdp")
    else:
        w_ada_pieces = [lax.all_gather(w_ada[0], "fsdp", axis=0, tiled=True)]
    qkv, probs, att, branch, middle, act, slope, out_branch, h1 = forward_layer(0, z, pos, h0, lines, bias_heads, weights, w_ada_pieces[:1] if direct else [])
    out1, d_h1, small_a1, small_m1, scores1, keep1, send1 = both_ways(1, z, pos, h1, grad1, lines, bias_heads, weights, w_ada_pieces[1:])
    d_middle, small_m0, keep_m0, send_m0 = backward_mlp(0, z, pos, d_h1, middle, lines, act, slope, out_branch, weights, [])
    pieces = z.pieces
    rows = half * length
    other1 = swap_section(send1)
    other_m0 = swap_section(send_m0)
    if direct:
        own_first, *first_messages = first_step(keep1, other1, keep_m0, other_m0)
        earlier = first_messages
    else:
        sums1 = section_sums(keep1, other1[: keep1.shape[0]], pieces)
        sums_m0 = section_sums(keep_m0, other_m0, pieces)
        earlier = []
    d_h0, small_a0, scores0, keep_a0, send_a0 = backward_attention(
        0, z, pos, h0, lines, qkv, probs, att, branch, d_middle, d_h1, weights, earlier
    )
    smalls = (small_a0, small_m0, small_a1, small_m1)
    size_a = keep_a0.shape[0]

    def replica(value, step):
        return lax.ppermute(value, "rep", pairs_of(replicas, step))

    def ordered(own, other, bit):
        return jnp.where(bit == 0, jnp.concatenate([own, other]), jnp.concatenate([other, own]))

    if direct:
        kept_small, send_small = small_step(pos, scores0, scores1, index, smalls, [])
        other_small = swap_section(send_small)
        other_a0 = after([swap_section(send_a0)], [kept_small])[0]
        own_a0, own_small, *messages = plane_step(pos, keep_a0, other_a0, kept_small, other_small, conditioning)
        got = to_peers(messages, "fsdp")
        got_first = after(to_peers(first_messages, "fsdp"), [own_small])
        keep_z, send_z = halve_step(pos, own_first, got_first)
        part0, plane_small, *messages = column_step(pos, own_a0, own_small, got, samples)
        got_z = after([replica(send_z, 1)], [plane_small])[0]
        keep_z, send_z = quarter_step(pos, keep_z, got_z)
        cond_part = cond_step(pos, after([own_small], [send_z])[0], w_ada_pieces, conditioning)
        got = after(to_peers(messages, "rep"), [cond_part])
        size = part0.shape[0]
        high, low = rank >> 1, rank & 1
        quarter0 = add_pieces(part0, [x[:size] for x in got]).astype(BF16)
        got_z, cond_part = after([replica(send_z, 2), cond_part], [quarter0])
        quarter = (keep_z + got_z.astype(F32)).astype(BF16)
        pair = ordered(quarter, replica(quarter, 2), high)
        half_a0 = by_rank([quarter0] + from_peers(quarter0, "rep"), rank).reshape(-1, model)
        n = pair.shape[0] // 2
        quarters = ordered(pair.reshape(1, 2, n, model), replica(pair, 1).reshape(1, 2, n, model), low)
        quarters = jnp.transpose(quarters, (1, 0, 2, 3)).reshape(4, n, model)
        n = 3 * n // 5
        half1 = quarters[:, :n].reshape(-1, model)
        half_m0 = quarters[:, n:].reshape(-1, model)
        g_ada, g_b_ada, g_b_qv, g_b_proj, g_b_fc1, g_b_fc2, g_table = finish_step(
            pos, plane_small, got, samples, width, heads, entries
        )
    else:
        other_a0 = swap_section(send_a0)
        kept_small, send_small = small_step(pos, scores0, scores1, index, smalls, [])
        theirs = swap_section(send_small).astype(F32)
        both = kept_small + theirs
        cut = half * 8

        def d_mod_of(values):
            a, m = values[:cut].reshape(half, 8, model), values[cut : 2 * cut].reshape(half, 8, model)
            return jnp.concatenate([a[:, :3], m[:, :3]], axis=1)

        low = in_order(d_mod_of(kept_small), d_mod_of(theirs)).astype(BF16)
        bias_rows = jnp.sum(both[: 2 * cut].reshape(2, half, 8, model), axis=1)
        summed = jnp.concatenate([bias_rows[1, 3:8], bias_rows[0, 3:6], both[2 * cut :]])
        cond_part = cond_step(pos, jnp.transpose(low, (1, 0, 2)).reshape(-1, model), w_ada_pieces, conditioning)
        kept = jnp.concatenate([low, conditioning[:, None]], axis=1)
        kept = lax.all_gather(kept, ("fsdp", "rep"), axis=0, tiled=True)
        summed = lax.psum(summed, ("fsdp", "rep"))
        act_all = jax.nn.silu(kept[:, 6].astype(F32)).astype(BF16)
        act_cols = lax.dynamic_slice_in_dim(act_all, shard * width, width, 1)
        g_ada = jnp.concatenate([dot_cols(act_cols, kept[:, i]) for i in range(6)], axis=1)
        g_b_ada = jnp.sum(kept[:, :6].astype(F32), axis=0).reshape(-1)
        vectors = [g_b_ada, summed[5:7].reshape(-1), summed[7], summed[1:5].reshape(-1), summed[0]]
        g_b_ada, g_b_qv, g_b_proj, g_b_fc1, g_b_fc2 = [
            lax.dynamic_slice_in_dim(v, shard * (v.shape[0] // shards), v.shape[0] // shards, 0)[None] for v in vectors
        ]
        g_table = jnp.transpose(summed[8:].reshape(HIGH, heads, LOW), (1, 0, 2)).reshape(heads, HIGH * LOW)[:, :entries]
        sums_a0 = section_sums(keep_a0, other_a0[:size_a], z.pieces)
        half_a0, half_m0, half1 = sums_a0[0].astype(BF16), sums_m0[0].astype(BF16), sums1[0].astype(BF16)
    cond_grad = cond_part + swap_section(cond_part)
    cut = half_a0.shape[0]
    half_a1, half_m1 = half1[:cut], half1[cut:]
    grads = final_step(
        pos, mine(half_a0, half_a1), mine(half_m0, half_m1),
        swap_section(mine(jnp.concatenate([half_a1, half_m1]), jnp.concatenate([half_a0, half_m0]))),
    )
    if not direct:
        grads = [lax.psum_scatter(g.astype(BF16), "fsdp", scatter_dimension=0, tiled=True) for g in grads]
        grads = [g.astype(F32) for g in lax.psum(tuple(grads), "rep")]
    g_qkv, g_proj, g_fc1, g_fc2 = grads

    activations = in_order(
        mine(h1, out1).reshape(half, length, model), other1[keep1.shape[0] :].reshape(half, length, model)
    )
    input_grads = in_order(
        mine(d_h0, d_h1.astype(F32)).reshape(half, length, model),
        other_a0[size_a : size_a + rows].astype(F32).reshape(half, length, model),
    )

    return (
        activations[None], input_grads[None], cond_grad,
        g_ada[None], g_qkv[None], g_proj[None], g_fc1[None], g_fc2[None],
        g_b_ada, g_b_qv, g_b_proj, g_b_fc1, g_b_fc2,
        g_table[None],
    )


def solution(mesh):
    batch = ("fsdp", "rep")
    matrix = P("section", "fsdp", None)
    vector = P("section", "fsdp")
    return jax.shard_map(
        per_device,
        mesh=mesh,
        in_specs=(
            P(batch, None, None), P(batch, None), P(batch, None, None), P(batch, None), P(),
            matrix, matrix, matrix, matrix, matrix, vector, vector, vector, vector, vector,
            P("section", None, None),
        ),
        out_specs=(
            P("section", batch, None, None), P("section", batch, None, None), P(batch, None),
            matrix, matrix, matrix, matrix, matrix, vector, vector, vector, vector, vector,
            P("section", None, None),
        ),
        check_vma=False,
    )
```
